32 devices in a mesh: dp: 2 (over x), ctx: 16 (over z, y, core).
Axes of the slice: x: 2, y: 2, z: 4, core: 2. Of those that a mesh axis runs over, the one named last changes fastest.
Arguments:
- query: bfloat16 [24576, 512], P(('dp', 'ctx')), parts along dimension 0, may hold values from -14 to 14
- key: bfloat16 [24576, 128], P(('dp', 'ctx')), parts along dimension 0, may hold values from -12 to 12
- value: bfloat16 [24576, 128], P(('dp', 'ctx')), parts along dimension 0, may hold values from -6 to 6
- d_out: bfloat16 [24576, 512], P(('dp', 'ctx')), parts along dimension 0, may hold values from -6 to 6
- doc_lengths: int32 [64], P('dp'), parts along dimension 0, may hold values from 1 to 768, 12288 in all
Outputs:
- attended: bfloat16 [24576, 512], P(('dp', 'ctx')), parts along dimension 0
- d_query: bfloat16 [24576, 512], P(('dp', 'ctx')), parts along dimension 0
- d_key: bfloat16 [24576, 128], P(('dp', 'ctx')), parts along dimension 0
- d_value: bfloat16 [24576, 128], P(('dp', 'ctx')), parts along dimension 0
The draws below stay inside these ranges and needn't reach their ends.
There are 2 independent parts, one for each index of `dp`. The reference program is written for one: setup_inputs(seed, part) draws one part's arguments, and reference() takes and returns one part's arrays. A program takes and returns all parts, laid end to end along the dimension named above; each array names one. Nothing has to cross between parts.
Inputs may be any that keep to these rules, and one draw needn't show every extreme that they name: `doc_lengths`: the lengths of one session sum to 12288, and one of them is exactly 768.
All inputs are finite; a program needn't handle non-finite values.
Results may differ from the reference program's by a relative error of at most 0.035.
Values may be sent and summed in bfloat16 or wider, within the bound.
No kernel may reach another device: no remote copies, remote signals or barrier semaphores. Data moves between devices by JAX's collectives and lax.ppermute only.
A program may use at most 64 MiB of HBM per device.

```python
import math
import jax
import jax.numpy as jnp
import numpy as np
from jax import lax

HD = 128
QH = 4
CH = 384
REACH = 2
MAXDOC = 768
L = 12288
NDOC = 32


def rough_rows(key, columns):
    values = jax.random.truncated_normal(key, -6.0, 6.0, (L, columns), jnp.float32)
    return values


def draw_query(key, part):
    values = rough_rows(jax.random.fold_in(key, 11), QH * HD)
    return values.astype(jnp.bfloat16)


def draw_key(key, part):
    values = rough_rows(jax.random.fold_in(key, 13), HD)
    return values.astype(jnp.bfloat16)


def shard_levels(key, extent, pieces, low, top_value):
    def one(position, parts):
        heights = jax.random.uniform(jax.random.fold_in(jax.random.fold_in(key, 6), position), (parts,), jnp.float32, low / len(pieces), top_value / len(pieces))
        return jnp.repeat(jnp.exp(heights), extent[position] // parts).reshape((-1,) + (1,) * (len(extent) - position - 1))

    level = one(*pieces[0])
    for cut in pieces[1:]:
        level = level * one(*cut)
    return level


def length_profile(amount, total, reach, skew):
    portions = [(1 << 20) // math.isqrt(rank ** skew) + 1 for rank in range(2, amount + 1)]
    rest, given = total - reach - (amount - 1), [1] * (amount - 1)
    while rest > 0:
        free = [i for i in range(amount - 1) if given[i] < reach]
        mass, remaining = sum([portions[i] for i in free]), rest
        for i in free:
            more = min(reach - given[i], max(1, remaining * portions[i] // mass), rest)
            given[i] = given[i] + more
            rest = rest - more
    return np.array([reach] + given)


def uneven_parts(rng, amount, total, most, skew):
    if amount == 2:
        one = jax.random.randint(rng, (), max(1, total - most), min(most, total - 1) + 1)
        return jnp.stack([one, total - one])
    lengths = jnp.asarray(length_profile(amount, total, most, skew), jnp.int32)
    twos = (amount - 1) // 2
    donor, receiver = lengths[1:1 + 2 * twos:2], lengths[2:2 + 2 * twos:2]
    slack = jnp.minimum(donor - 1, most - receiver)
    moved = jax.random.randint(jax.random.fold_in(rng, 1), (twos,), 0, 1 << 20) % (slack + 1)
    lengths = lengths.at[1:1 + 2 * twos:2].set(donor - moved).at[2:2 + 2 * twos:2].set(receiver + moved)
    return lengths[jax.random.permutation(jax.random.fold_in(rng, 2), amount)]


def bell_draw(rng, dims, scale, limit, cuts=(), kind=jnp.bfloat16):
    level = shard_levels(rng, dims, cuts, -0.22, 0.18) if cuts else 1.0
    array = jax.random.normal(rng, dims, jnp.float32) * scale * level
    return jnp.minimum(jnp.maximum(array, -limit), limit).astype(kind)


def setup_inputs(seed: int = 0, part: int = 0) -> dict:
    key_of = jax.random.split(jax.random.key(seed), 6)
    part_keys = jax.random.split(jax.random.fold_in(key_of[5], part), 6)
    query = draw_query(jax.random.fold_in(jax.random.fold_in(key_of[5], part), 71), part)
    key = draw_key(jax.random.fold_in(jax.random.fold_in(key_of[5], part), 71), part)
    value = bell_draw(part_keys[2], (L, HD), 1.0, 6.0, ((0, 16),))
    d_out = bell_draw(part_keys[3], (L, QH * HD), 1.0, 6.0, ((0, 16),))
    doc_lengths = uneven_parts(part_keys[4], NDOC, L, MAXDOC, 2).astype(jnp.int32)
    return {"query": query, "key": key, "value": value, "d_out": d_out, "doc_lengths": doc_lengths}


masked_score = -1e+30

def to_order(stored):
    count = stored.shape[0] // (2 * CH)
    blocks = stored.reshape(count, 2, CH, stored.shape[1])
    return jnp.concatenate([blocks[:, 0], blocks[::-1, 1]], axis=0).reshape(stored.shape)

def to_stored(ordered):
    count = ordered.shape[0] // (2 * CH)
    blocks = ordered.reshape(2 * count, CH, ordered.shape[1])
    return jnp.stack([blocks[:count], blocks[count:][::-1]], axis=1).reshape(ordered.shape)

def doc_index(positions, doc_lengths):
    starts = jnp.cumsum(doc_lengths) - doc_lengths
    return lax.optimization_barrier(jnp.sum((starts[None, :] <= positions[:, None]).astype(jnp.int32), axis=1)) - 1

def block_terms(query_block, dout_block, keys, values, allowed):
    scale = 1.0 / math.sqrt(HD)
    heads = query_block.shape[1] // HD
    query_heads = query_block.reshape(CH, heads, HD).astype(jnp.float32)
    dout_heads = dout_block.reshape(CH, heads, HD).astype(jnp.float32)
    keys_wide = keys.astype(jnp.float32)
    values_wide = values.astype(jnp.float32)
    scores = jnp.einsum('rhe,ke->hrk', query_heads, keys_wide) * scale
    scores = jnp.where(allowed[None], scores, masked_score)
    row_max = lax.optimization_barrier(jnp.max(scores, axis=2, keepdims=True))
    log_total = row_max + jnp.log(lax.optimization_barrier(jnp.sum(jnp.exp(scores - row_max), axis=2, keepdims=True)))
    weights = jnp.where(allowed[None], jnp.exp(scores - log_total), 0.0).astype(jnp.bfloat16)
    weights_wide = lax.optimization_barrier(weights).astype(jnp.float32)
    attended = jnp.einsum('hrk,ke->rhe', weights_wide, values_wide).astype(jnp.bfloat16)
    attended_wide = lax.optimization_barrier(attended).astype(jnp.float32)
    delta = lax.optimization_barrier(jnp.sum(dout_heads * attended_wide, axis=2))
    dprob = jnp.einsum('rhe,ke->hrk', dout_heads, values_wide)
    dscore = (weights_wide * (dprob - delta.T[:, :, None])).astype(jnp.bfloat16)
    dscore_wide = lax.optimization_barrier(dscore).astype(jnp.float32)
    grad_query = jnp.einsum('hrk,ke->rhe', dscore_wide, keys_wide) * scale
    grad_key = jnp.einsum('hrk,rhe->ke', dscore_wide, query_heads) * scale
    grad_value = jnp.einsum('hrk,rhe->ke', weights_wide, dout_heads)
    features = heads * HD
    return (attended.reshape(CH, features), grad_query.reshape(CH, features).astype(jnp.bfloat16), grad_key, grad_value)

def reference(query, key, value, d_out, doc_lengths):
    total = query.shape[0]
    features = query.shape[1]
    back = REACH * CH
    width = back + CH
    query_ord = to_order(query)
    dout_ord = to_order(d_out)
    key_pad = jnp.concatenate([jnp.zeros((back, HD), key.dtype), to_order(key)], axis=0)
    value_pad = jnp.concatenate([jnp.zeros((back, HD), value.dtype), to_order(value)], axis=0)
    positions = jnp.arange(total + back, dtype=jnp.int32) - back
    docs = doc_index(positions, doc_lengths)

    def step(carry, index):
        key_acc, value_acc = carry
        start = index * CH
        query_block = lax.dynamic_slice_in_dim(query_ord, start, CH, 0)
        dout_block = lax.dynamic_slice_in_dim(dout_ord, start, CH, 0)
        query_pos = lax.dynamic_slice_in_dim(positions, start + back, CH, 0)
        query_doc = lax.dynamic_slice_in_dim(docs, start + back, CH, 0)
        keys = lax.dynamic_slice_in_dim(key_pad, start, width, 0)
        values = lax.dynamic_slice_in_dim(value_pad, start, width, 0)
        key_pos = lax.dynamic_slice_in_dim(positions, start, width, 0)
        key_doc = lax.dynamic_slice_in_dim(docs, start, width, 0)
        allowed = (key_pos[None, :] <= query_pos[:, None]) & (key_doc[None, :] == query_doc[:, None])
        attended, grad_query, grad_key, grad_value = block_terms(query_block, dout_block, keys, values, allowed)
        key_acc = lax.dynamic_update_slice_in_dim(key_acc, lax.dynamic_slice_in_dim(key_acc, start, width, 0) + grad_key, start, 0)
        value_acc = lax.dynamic_update_slice_in_dim(value_acc, lax.dynamic_slice_in_dim(value_acc, start, width, 0) + grad_value, start, 0)
        return ((key_acc, value_acc), (attended, grad_query))
    zeros = jnp.zeros((total + back, HD), jnp.float32)
    (key_acc, value_acc), (attended, grad_query) = lax.scan(step, (zeros, zeros), jnp.arange(total // CH, dtype=jnp.int32))
    return (to_stored(attended.reshape(total, features)), to_stored(grad_query.reshape(total, features)), to_stored(key_acc[back:].astype(jnp.bfloat16)), to_stored(value_acc[back:].astype(jnp.bfloat16)))
```

```python
import functools
import math

import jax
import jax.numpy as jnp
from jax import lax
from jax.experimental import pallas as pl
from jax.experimental.pallas import tpu as pltpu
from jax.sharding import PartitionSpec as P

HD = 128
TQ = 128

masked_score = -1e30
VMEM_LIMIT = 48 * 1024 * 1024


def dot_nt(a, b):
    return lax.dot_general(a, b, (((1,), (1,)), ((), ())), preferred_element_type=jnp.float32)


def dot_nn(a, b):
    return lax.dot_general(a, b, (((1,), (0,)), ((), ())), preferred_element_type=jnp.float32)


def pack_kernel(rows, meta, key, value, near_out, far_out, sems):
    copies = []
    for slot, (out, half) in enumerate(((near_out, meta[1]), (far_out, meta[0]))):
        start = pl.multiple_of(half * rows, rows)
        for part, src in enumerate((key, value)):
            copies.append(
                pltpu.make_async_copy(
                    src.at[pl.ds(start, rows)],
                    out.at[pl.ds(part * rows, rows)],
                    sems.at[2 * slot + part],
                )
            )
    for copy in copies:
        copy.start()
    for copy in copies:
        copy.wait()


def pack_blocks(meta, key, value):
    rows = key.shape[0] // 2
    shape = jax.ShapeDtypeStruct((2 * rows, HD), key.dtype)
    return pl.pallas_call(
        functools.partial(pack_kernel, rows),
        out_shape=(shape, shape),
        grid_spec=pltpu.PrefetchScalarGridSpec(
            num_scalar_prefetch=1,
            grid=(1,),
            in_specs=[pl.BlockSpec(memory_space=pl.ANY)] * 2,
            out_specs=[pl.BlockSpec(memory_space=pl.ANY)] * 2,
            scratch_shapes=[pltpu.SemaphoreType.DMA((4,))],
        ),
        name="pack_blocks",
    )(meta, key, value)


def window_kernel(
    rows,
    heads,
    docs,
    slot,
    meta,
    doc_lengths,
    query,
    dout,
    key_own,
    value_own,
    prev1,
    prev2,
    *refs,
):
    if slot == 1:
        refs = refs[2:]
    (attended, grad_query, own_out, prev1_out, prev2_out) = refs[:5]
    (keys, values, keys_t, values_t, doc_start, scores, dprobs, weights, dscores, dk, dv) = refs[5:]
    step = pl.program_id(0)
    steps = pl.num_programs(0)
    back = 2 * rows
    width = back + TQ
    scale = 1.0 / math.sqrt(HD)
    base2 = scale * math.log2(math.e)
    block_pos = meta[2 + slot] * rows

    @pl.when(step == 0)
    def _():
        keys[0:rows] = prev2[0:rows]
        keys[rows:back] = prev1[0:rows]
        keys[back : back + rows] = key_own[...]
        values[0:rows] = prev2[rows : 2 * rows]
        values[rows:back] = prev1[rows : 2 * rows]
        values[back : back + rows] = value_own[...]
        for tile in range((back + rows) // TQ):
            part = pl.ds(tile * TQ, TQ)
            keys_t[:, part] = jnp.transpose(keys[part, :])
            values_t[:, part] = jnp.transpose(values[part, :])
        dk[...] = jnp.zeros_like(dk)
        dv[...] = jnp.zeros_like(dv)
        at = (
            block_pos
            + lax.broadcasted_iota(jnp.int32, (8, TQ), 0) * TQ
            + lax.broadcasted_iota(jnp.int32, (8, TQ), 1)
        )

        def one(index, carry):
            start, found = carry
            found = jnp.where(at >= start, start, found)
            return (start + doc_lengths[index], found)

        _, found = lax.fori_loop(
            0, docs, one, (jnp.int32(0), jnp.zeros((8, TQ), jnp.int32)), unroll=8
        )
        doc_start[...] = found

    first = pl.multiple_of(step * TQ, TQ)
    window = pl.ds(first, width)
    query_rows = jnp.concatenate([query[:, h * HD : (h + 1) * HD] for h in range(heads)], axis=0)
    dout_rows = jnp.concatenate([dout[:, h * HD : (h + 1) * HD] for h in range(heads)], axis=0)
    scores[...] = dot_nt(keys[window, :], query_rows)
    dprobs[...] = dot_nt(values[window, :], dout_rows)

    window_pos = block_pos - back + first
    low = doc_start[pl.ds(step, 1), :] - window_pos
    high = lax.broadcasted_iota(jnp.int32, (1, TQ), 1) + back
    chunk = TQ
    row_max = jnp.full((1, heads * TQ), masked_score, jnp.float32)
    for start in range(0, width, chunk):
        at = lax.broadcasted_iota(jnp.int32, (chunk, TQ), 0) + start
        allowed = at >= low
        if start >= back:
            allowed = jnp.logical_and(allowed, at <= high)
        allowed = jnp.concatenate([allowed] * heads, axis=1)
        part = jnp.where(allowed, scores[start : start + chunk, :], masked_score)
        scores[start : start + chunk, :] = part
        row_max = jnp.maximum(row_max, jnp.max(part, axis=0, keepdims=True))
    row_max = row_max * base2
    total = jnp.zeros((1, heads * TQ), jnp.float32)
    delta = jnp.zeros((1, heads * TQ), jnp.float32)
    for start in range(0, width, chunk):
        part = jnp.exp2(scores[start : start + chunk, :] * base2 - row_max)
        scores[start : start + chunk, :] = part
        total = total + jnp.sum(part, axis=0, keepdims=True)
        delta = delta + jnp.sum(part * dprobs[start : start + chunk, :], axis=0, keepdims=True)
    inverse = 1.0 / total
    delta = delta * inverse
    for start in range(0, width, chunk):
        part = scores[start : start + chunk, :] * inverse
        weights[start : start + chunk, :] = part.astype(jnp.bfloat16)
        dscores[start : start + chunk, :] = (
            part * (dprobs[start : start + chunk, :] - delta)
        ).astype(jnp.bfloat16)
    dv[window, :] += dot_nn(weights[...], dout_rows)
    dk[window, :] += dot_nn(dscores[...], query_rows)
    attended_t = dot_nn(values_t[:, window], weights[...])
    grad_query_t = dot_nn(keys_t[:, window], dscores[...]) * scale
    for h in range(heads):
        part = slice(h * TQ, (h + 1) * TQ)
        columns = slice(h * HD, (h + 1) * HD)
        attended[:, columns] = jnp.transpose(attended_t[:, part]).astype(attended.dtype)
        grad_query[:, columns] = jnp.transpose(grad_query_t[:, part]).astype(grad_query.dtype)

    @pl.when(step == steps - 1)
    def _():
        prev2_out[0:rows] = (dk[0:rows] * scale).astype(prev2_out.dtype)
        prev2_out[rows : 2 * rows] = dv[0:rows].astype(prev2_out.dtype)
        prev1_out[0:rows] = (dk[rows:back] * scale).astype(prev1_out.dtype)
        prev1_out[rows : 2 * rows] = dv[rows:back].astype(prev1_out.dtype)
        own_out[0:rows] = dk[back : back + rows] * scale
        own_out[rows : 2 * rows] = dv[back : back + rows]


def window_block(slot, meta, doc_lengths, query, dout, key, value, prev1, prev2, filled):
    rows = key.shape[0] // 2
    heads = query.shape[1] // HD
    steps = rows // TQ
    wide = heads * HD
    tall = 3 * rows
    width = 2 * rows + TQ
    q_spec = pl.BlockSpec((TQ, wide), lambda i, meta, docs: (meta[slot] * steps + i, 0))
    own_spec = pl.BlockSpec((rows, HD), lambda i, meta, docs: (meta[slot], 0))
    whole = pl.BlockSpec((2 * rows, HD), lambda i, meta, docs: (0, 0))
    pair = jax.ShapeDtypeStruct((2 * rows, HD), jnp.bfloat16)
    inputs = [query, dout, key, value, prev1, prev2]
    in_specs = [q_spec, q_spec, own_spec, own_spec, whole, whole]
    aliases = {}
    if filled:
        aliases = {2 + len(inputs): 0, 3 + len(inputs): 1}
        inputs += list(filled)
        in_specs += [pl.BlockSpec(memory_space=pl.ANY)] * 2
    flops = 6 * 2 * steps * width * heads * TQ * HD
    return pl.pallas_call(
        functools.partial(window_kernel, rows, heads, doc_lengths.shape[0], slot),
        out_shape=(
            jax.ShapeDtypeStruct(query.shape, query.dtype),
            jax.ShapeDtypeStruct(query.shape, query.dtype),
            jax.ShapeDtypeStruct((2 * rows, HD), jnp.float32),
            pair,
            pair,
        ),
        grid_spec=pltpu.PrefetchScalarGridSpec(
            num_scalar_prefetch=2,
            grid=(steps,),
            in_specs=in_specs,
            out_specs=[q_spec, q_spec, whole, whole, whole],
            scratch_shapes=[
                pltpu.VMEM((tall, HD), jnp.bfloat16),
                pltpu.VMEM((tall, HD), jnp.bfloat16),
                pltpu.VMEM((HD, tall), jnp.bfloat16),
                pltpu.VMEM((HD, tall), jnp.bfloat16),
                pltpu.VMEM((8, TQ), jnp.int32),
                pltpu.VMEM((width, heads * TQ), jnp.float32),
                pltpu.VMEM((width, heads * TQ), jnp.float32),
                pltpu.VMEM((width, heads * TQ), jnp.bfloat16),
                pltpu.VMEM((width, heads * TQ), jnp.bfloat16),
                pltpu.VMEM((tall, HD), jnp.float32),
                pltpu.VMEM((tall, HD), jnp.float32),
            ],
        ),
        input_output_aliases=aliases,
        compiler_params=pltpu.CompilerParams(vmem_limit_bytes=VMEM_LIMIT),
        cost_estimate=pl.CostEstimate(
            flops=2 * flops, bytes_accessed=4 * rows * wide * 2, transcendentals=0
        ),
        name="window_far" if slot == 0 else "window_near",
    )(meta, doc_lengths, *inputs)


def total_kernel(rows, meta, far_own, far_1, far_2, near_own, near_1, grad_key, grad_value):
    far = far_own[...] + far_1[...].astype(jnp.float32) + far_2[...].astype(jnp.float32)
    near = near_own[...] + near_1[...].astype(jnp.float32)
    for total, half in ((far, meta[0]), (near, meta[1])):
        place = pl.ds(pl.multiple_of(half * rows, rows), rows)
        grad_key[place, :] = total[0:rows].astype(grad_key.dtype)
        grad_value[place, :] = total[rows : 2 * rows].astype(grad_value.dtype)


def total_grads(meta, far_own, far_1, far_2, near_own, near_1):
    rows = far_own.shape[0] // 2
    whole = pl.BlockSpec((2 * rows, HD), lambda i, meta: (0, 0))
    shape = jax.ShapeDtypeStruct((2 * rows, HD), jnp.bfloat16)
    return pl.pallas_call(
        functools.partial(total_kernel, rows),
        out_shape=(shape, shape),
        grid_spec=pltpu.PrefetchScalarGridSpec(
            num_scalar_prefetch=1,
            grid=(1,),
            in_specs=[whole] * 5,
            out_specs=[whole] * 2,
        ),
        compiler_params=pltpu.CompilerParams(vmem_limit_bytes=VMEM_LIMIT),
        name="total_grads",
    )(meta, far_own, far_1, far_2, near_own, near_1)


def body(query, key, value, d_out, doc_lengths):
    count = lax.axis_size("ctx")
    device = lax.axis_index("ctx").astype(jnp.int32)
    odd = device % 2
    mirror = 2 * count - 1 - device
    meta = jnp.stack(
        [odd, 1 - odd, jnp.where(odd == 0, device, mirror), jnp.where(odd == 0, mirror, device)]
    ).astype(jnp.int32)

    def holder(block):
        return block if block < count else 2 * count - 1 - block

    def move(array, pairs):
        return lax.ppermute(array, "ctx", pairs)

    near_on = [(holder(b), holder(b + 2)) for b in range(1, 2 * count - 2, 2)]
    far_on = [(holder(b), holder(b + 2)) for b in range(0, 2 * count - 2, 2)]
    swap = [(d, d ^ 1) for d in range(count)]
    near_back = [(t, s) for s, t in near_on]
    far_back = [(t, s) for s, t in far_on]

    near_kv, far_kv = pack_blocks(meta, key, value)
    near_2 = move(near_kv, near_on)
    far_2 = move(far_kv, far_on)
    near_1 = move(far_kv, swap)
    far_1 = move(near_2, swap)

    attended, grad_query, far_own, far_g1, far_g2 = window_block(
        0, meta, doc_lengths, query, d_out, key, value, far_1, far_2, None
    )
    from_far_2 = move(far_g2, far_back)
    relayed = move(far_g1, swap)
    attended, grad_query, near_own, near_g1, near_g2 = window_block(
        1, meta, doc_lengths, query, d_out, key, value, near_1, near_2, (attended, grad_query)
    )
    near_sum = (near_g2.astype(jnp.float32) + relayed.astype(jnp.float32)).astype(jnp.bfloat16)
    from_near_2 = move(near_sum, near_back)
    from_near_1 = move(near_g1, swap)
    grad_key, grad_value = total_grads(
        meta, far_own, from_near_1, from_far_2, near_own, from_near_2
    )
    return (attended, grad_query, grad_key, grad_value)


def solution(mesh):
    rows = P(("dp", "ctx"), None)
    return jax.shard_map(
        body,
        mesh=mesh,
        in_specs=(rows, rows, rows, rows, P("dp")),
        out_specs=(rows, rows, rows, rows),
        check_vma=False,
    )
```

```python
import functools
import math

import jax
import jax.numpy as jnp
from jax import lax
from jax.experimental import pallas as pl
from jax.experimental.pallas import tpu as pltpu
from jax.sharding import PartitionSpec as P

HD = 128
TQ = 128

masked_score = -1e30
VMEM_LIMIT = 24 * 1024 * 1024
SCALE = 1.0 / math.sqrt(HD)
VMEM = pl.BlockSpec(memory_space=pltpu.VMEM)
SMEM = pl.BlockSpec(memory_space=pltpu.SMEM)


def dot_nt(a, b):
    return lax.dot_general(a, b, (((1,), (1,)), ((), ())), preferred_element_type=jnp.float32)


def dot_nn(a, b):
    return lax.dot_general(a, b, (((1,), (0,)), ((), ())), preferred_element_type=jnp.float32)


def half_start(rows, slot):
    odd = lax.axis_index("ctx") % 2
    return pl.multiple_of((odd if slot == 0 else 1 - odd) * rows, rows)


def block_number(count, slot):
    device = lax.axis_index("ctx")
    in_lower = device % 2 == slot
    return jnp.where(in_lower, device, 2 * count - 1 - device)


def pack_kernel(rows, key, value, near_out, far_out):
    for slot, out in ((1, near_out), (0, far_out)):
        place = pl.ds(half_start(rows, slot), rows)
        out[0:rows] = key[place, :]
        out[rows : 2 * rows] = value[place, :]


def pack_blocks(key, value):
    rows = key.shape[0] // 2
    shape = jax.ShapeDtypeStruct((2 * rows, HD), key.dtype)
    return pl.pallas_call(
        functools.partial(pack_kernel, rows),
        out_shape=(shape, shape),
        in_specs=[VMEM] * 2,
        out_specs=[VMEM] * 2,
        name="pack_blocks",
    )(key, value)


def head_rows(array, first, heads):
    return jnp.concatenate(
        [array[pl.ds(first, TQ), h * HD : (h + 1) * HD] for h in range(heads)], axis=0
    )


def scores_kernel(
    rows,
    heads,
    docs,
    count,
    slot,
    doc_lengths,
    query,
    dout,
    own_kv,
    prev1,
    prev2,
    weights,
    dscores,
    prev1_out,
    prev2_out,
    keys,
    values,
    scores,
    dprobs,
    dk,
    dv,
):
    back = 2 * rows
    width = back + TQ
    base2 = SCALE * math.log2(math.e)
    block_pos = block_number(count, slot) * rows
    own_rows = half_start(rows, slot)

    for place, source in enumerate((prev2, prev1, own_kv)):
        keys[place * rows : (place + 1) * rows] = source[0:rows]
        values[place * rows : (place + 1) * rows] = source[rows : 2 * rows]
    at = (
        block_pos
        + lax.broadcasted_iota(jnp.int32, (8, TQ), 0) * TQ
        + lax.broadcasted_iota(jnp.int32, (8, TQ), 1)
    )

    def one(index, carry):
        start, found = carry
        found = jnp.where(at >= start, start, found)
        return (start + doc_lengths[index], found)

    _, doc_start = lax.fori_loop(
        0, docs, one, (jnp.int32(0), jnp.zeros((8, TQ), jnp.int32)), unroll=8
    )

    for step in range(rows // TQ):
        first = step * TQ
        query_rows = head_rows(query, own_rows + first, heads)
        dout_rows = head_rows(dout, own_rows + first, heads)
        scores[...] = dot_nt(keys[first : first + width, :], query_rows)
        dprobs[...] = dot_nt(values[first : first + width, :], dout_rows)

        low = doc_start[step : step + 1, :] - (block_pos - back + first)
        high = lax.broadcasted_iota(jnp.int32, (1, TQ), 1) + back
        chunk = TQ
        row_max = jnp.full((1, heads * TQ), masked_score, jnp.float32)
        for start in range(0, width, chunk):
            at = lax.broadcasted_iota(jnp.int32, (chunk, TQ), 0) + start
            allowed = at >= low
            if start >= back:
                allowed = jnp.logical_and(allowed, at <= high)
            allowed = jnp.concatenate([allowed] * heads, axis=1)
            part = jnp.where(allowed, scores[start : start + chunk, :], masked_score)
            scores[start : start + chunk, :] = part
            row_max = jnp.maximum(row_max, jnp.max(part, axis=0, keepdims=True))
        row_max = row_max * base2
        total = jnp.zeros((1, heads * TQ), jnp.float32)
        delta = jnp.zeros((1, heads * TQ), jnp.float32)
        for start in range(0, width, chunk):
            part = jnp.exp2(scores[start : start + chunk, :] * base2 - row_max)
            scores[start : start + chunk, :] = part
            total = total + jnp.sum(part, axis=0, keepdims=True)
            delta = delta + jnp.sum(part * dprobs[start : start + chunk, :], axis=0, keepdims=True)
        inverse = 1.0 / total
        delta = delta * inverse
        out = step * width
        for start in range(0, width, chunk):
            part = scores[start : start + chunk, :] * inverse
            weights[out + start : out + start + chunk, :] = part.astype(jnp.bfloat16)
            dscores[out + start : out + start + chunk, :] = (
                part * (dprobs[start : start + chunk, :] - delta)
            ).astype(jnp.bfloat16)
        for total_ref, terms, side in ((dv, weights, dout_rows), (dk, dscores, query_rows)):
            term = dot_nn(terms[out : out + back - first, :], side)
            if step == 0:
                total_ref[...] = term
            else:
                total_ref[first:back] += term

    prev2_out[0:rows] = (dk[0:rows] * SCALE).astype(prev2_out.dtype)
    prev2_out[rows:back] = dv[0:rows].astype(prev2_out.dtype)
    prev1_out[0:rows] = (dk[rows:back] * SCALE).astype(prev1_out.dtype)
    prev1_out[rows:back] = dv[rows:back].astype(prev1_out.dtype)


def block_scores(slot, count, doc_lengths, query, dout, own_kv, prev1, prev2):
    rows = query.shape[0] // 2
    heads = query.shape[1] // HD
    steps = rows // TQ
    width = 2 * rows + TQ
    pair = jax.ShapeDtypeStruct((2 * rows, HD), jnp.bfloat16)
    kept = jax.ShapeDtypeStruct((steps * width, heads * TQ), jnp.bfloat16)
    return pl.pallas_call(
        functools.partial(scores_kernel, rows, heads, doc_lengths.shape[0], count, slot),
        out_shape=(kept, kept, pair, pair),
        in_specs=[SMEM] + [VMEM] * 5,
        out_specs=[VMEM] * 4,
        scratch_shapes=[
            pltpu.VMEM((3 * rows, HD), jnp.bfloat16),
            pltpu.VMEM((3 * rows, HD), jnp.bfloat16),
            pltpu.VMEM((width, heads * TQ), jnp.float32),
            pltpu.VMEM((width, heads * TQ), jnp.float32),
            pltpu.VMEM((2 * rows, HD), jnp.float32),
            pltpu.VMEM((2 * rows, HD), jnp.float32),
        ],
        compiler_params=pltpu.CompilerParams(vmem_limit_bytes=VMEM_LIMIT),
        cost_estimate=pl.CostEstimate(
            flops=8 * 2 * steps * width * heads * TQ * HD, bytes_accessed=0, transcendentals=0
        ),
        name="scores_far" if slot == 0 else "scores_near",
    )(doc_lengths, query, dout, own_kv, prev1, prev2)


def outputs_kernel(rows, heads, query, dout, *refs):
    blocks = (refs[0:5], refs[5:10])
    (attended, grad_query, far_own, near_own, keys_t, values_t) = refs[10:]
    back = 2 * rows
    width = back + TQ
    for slot, (own_kv, prev1, prev2, weights, dscores) in enumerate(blocks):
        own_out = (far_own, near_own)[slot]
        own_rows = half_start(rows, slot)
        for place, source in enumerate((prev2, prev1, own_kv)):
            for tile in range(rows // TQ):
                part = slice(place * rows + tile * TQ, place * rows + (tile + 1) * TQ)
                row = tile * TQ
                keys_t[:, part] = jnp.transpose(source[row : row + TQ, :])
                values_t[:, part] = jnp.transpose(source[rows + row : rows + row + TQ, :])
        for step in reversed(range(rows // TQ)):
            first = step * TQ
            out = step * width
            tail = slice(out + back - first, out + width)
            query_rows = head_rows(query, own_rows + first, heads)
            dout_rows = head_rows(dout, own_rows + first, heads)
            for offset, terms, side, factor in (
                (0, dscores, query_rows, SCALE),
                (rows, weights, dout_rows, 1.0),
            ):
                term = dot_nn(terms[tail, :], side) * factor
                place = slice(offset, offset + first + TQ)
                if step == rows // TQ - 1:
                    own_out[place] = term
                else:
                    own_out[place] += term
            window = slice(first, first + width)
            attended_t = dot_nn(values_t[:, window], weights[out : out + width, :])
            grad_query_t = dot_nn(keys_t[:, window], dscores[out : out + width, :]) * SCALE
            place = pl.ds(own_rows + first, TQ)
            for h in range(heads):
                part = slice(h * TQ, (h + 1) * TQ)
                columns = slice(h * HD, (h + 1) * HD)
                attended[place, columns] = jnp.transpose(attended_t[:, part]).astype(
                    attended.dtype
                )
                grad_query[place, columns] = jnp.transpose(grad_query_t[:, part]).astype(
                    grad_query.dtype
                )


def block_outputs(query, dout, far, near):
    rows = query.shape[0] // 2
    heads = query.shape[1] // HD
    steps = rows // TQ
    width = 2 * rows + TQ
    wide = jax.ShapeDtypeStruct(query.shape, query.dtype)
    own = jax.ShapeDtypeStruct((2 * rows, HD), jnp.float32)
    return pl.pallas_call(
        functools.partial(outputs_kernel, rows, heads),
        out_shape=(wide, wide, own, own),
        in_specs=[VMEM] * 12,
        out_specs=[VMEM] * 4,
        scratch_shapes=[
            pltpu.VMEM((HD, 3 * rows), jnp.bfloat16),
            pltpu.VMEM((HD, 3 * rows), jnp.bfloat16),
        ],
        compiler_params=pltpu.CompilerParams(vmem_limit_bytes=VMEM_LIMIT),
        cost_estimate=pl.CostEstimate(
            flops=12 * 2 * steps * width * heads * TQ * HD, bytes_accessed=0, transcendentals=0
        ),
        name="block_outputs",
    )(query, dout, *far, *near)


def total_kernel(rows, far_own, far_1, far_2, near_own, near_1, grad_key, grad_value):
    far = far_own[...] + far_1[...].astype(jnp.float32) + far_2[...].astype(jnp.float32)
    near = near_own[...] + near_1[...].astype(jnp.float32)
    for slot, total in ((0, far), (1, near)):
        place = pl.ds(half_start(rows, slot), rows)
        grad_key[place, :] = total[0:rows].astype(grad_key.dtype)
        grad_value[place, :] = total[rows : 2 * rows].astype(grad_value.dtype)


def total_grads(far_own, far_1, far_2, near_own, near_1):
    rows = far_own.shape[0] // 2
    shape = jax.ShapeDtypeStruct((2 * rows, HD), jnp.bfloat16)
    return pl.pallas_call(
        functools.partial(total_kernel, rows),
        out_shape=(shape, shape),
        in_specs=[VMEM] * 5,
        out_specs=[VMEM] * 2,
        compiler_params=pltpu.CompilerParams(vmem_limit_bytes=VMEM_LIMIT),
        name="total_grads",
    )(far_own, far_1, far_2, near_own, near_1)


def body(query, key, value, d_out, doc_lengths):
    count = lax.axis_size("ctx")

    def holder(block):
        return block if block < count else 2 * count - 1 - block

    def move(array, pairs):
        return lax.ppermute(array, "ctx", pairs)

    near_on = [(holder(b), holder(b + 2)) for b in range(1, 2 * count - 2, 2)]
    far_on = [(holder(b), holder(b + 2)) for b in range(0, 2 * count - 2, 2)]
    swap = [(d, d ^ 1) for d in range(count)]
    near_back = [(t, s) for s, t in near_on]
    far_back = [(t, s) for s, t in far_on]

    near_kv, far_kv = pack_blocks(key, value)
    near_2 = move(near_kv, near_on)
    far_2 = move(far_kv, far_on)
    near_1 = move(far_kv, swap)
    far_1 = move(near_2, swap)

    far_w, far_d, far_g1, far_g2 = block_scores(
        0, count, doc_lengths, query, d_out, far_kv, far_1, far_2
    )
    from_far_2 = move(far_g2, far_back)
    relayed = move(far_g1, swap)
    near_w, near_d, near_g1, near_g2 = block_scores(
        1, count, doc_lengths, query, d_out, near_kv, near_1, near_2
    )
    near_sum = (near_g2.astype(jnp.float32) + relayed.astype(jnp.float32)).astype(jnp.bfloat16)
    from_near_2 = move(near_sum, near_back)
    from_near_1 = move(near_g1, swap)
    attended, grad_query, far_own, near_own = block_outputs(
        query,
        d_out,
        (far_kv, far_1, far_2, far_w, far_d),
        (near_kv, near_1, near_2, near_w, near_d),
    )
    grad_key, grad_value = total_grads(far_own, from_near_1, from_far_2, near_own, from_near_2)
    return (attended, grad_query, grad_key, grad_value)


def solution(mesh):
    rows = P(("dp", "ctx"), None)
    return jax.shard_map(
        body,
        mesh=mesh,
        in_specs=(rows, rows, rows, rows, P("dp")),
        out_specs=(rows, rows, rows, rows),
        check_vma=False,
    )
```

```python
import functools
import math

import jax
import jax.numpy as jnp
from jax import lax
from jax.experimental import pallas as pl
from jax.experimental.pallas import tpu as pltpu
from jax.sharding import PartitionSpec as P

HD = 128
TQ = 128
GROUP = 32

masked_score = -1e30
VMEM_LIMIT = 24 * 1024 * 1024
SCALE = 1.0 / math.sqrt(HD)
VMEM = pl.BlockSpec(memory_space=pltpu.VMEM)
SMEM = pl.BlockSpec(memory_space=pltpu.SMEM)


def dot_nt(a, b):
    return lax.dot_general(a, b, (((1,), (1,)), ((), ())), preferred_element_type=jnp.float32)


def dot_nn(a, b):
    return lax.dot_general(a, b, (((1,), (0,)), ((), ())), preferred_element_type=jnp.float32)


def half_start(rows, slot):
    odd = lax.axis_index("ctx") % 2
    return pl.multiple_of((odd if slot == 0 else 1 - odd) * rows, rows)


def block_number(count, slot):
    device = lax.axis_index("ctx")
    in_lower = device % 2 == slot
    return jnp.where(in_lower, device, 2 * count - 1 - device)


def pack_kernel(rows, key, value, near_out, far_out):
    for slot, out in ((1, near_out), (0, far_out)):
        place = pl.ds(half_start(rows, slot), rows)
        out[0:rows] = key[place, :]
        out[rows : 2 * rows] = value[place, :]


def pack_blocks(key, value):
    rows = key.shape[0] // 2
    shape = jax.ShapeDtypeStruct((2 * rows, HD), key.dtype)
    return pl.pallas_call(
        functools.partial(pack_kernel, rows),
        out_shape=(shape, shape),
        in_specs=[VMEM] * 2,
        out_specs=[VMEM] * 2,
        name="pack_blocks",
    )(key, value)


def prepare_kernel(rows, heads, docs, count, doc_lengths, query, dout, _, *refs):
    for slot in (0, 1):
        query_rows, dout_rows, doc_start = refs[3 * slot : 3 * slot + 3]
        own_rows = half_start(rows, slot)
        for step in range(rows // TQ):
            source = pl.ds(own_rows + step * TQ, TQ)
            for h in range(heads):
                place = slice((step * heads + h) * TQ, (step * heads + h + 1) * TQ)
                columns = slice(h * HD, (h + 1) * HD)
                query_rows[place, :] = query[source, columns]
                dout_rows[place, :] = dout[source, columns]
        at = (
            block_number(count, slot) * rows
            + lax.broadcasted_iota(jnp.int32, (8, TQ), 0) * TQ
            + lax.broadcasted_iota(jnp.int32, (8, TQ), 1)
        )

        def one(index, carry):
            start, found = carry
            found = jnp.where(at >= start, start, found)
            return (start + doc_lengths[index], found)

        _, found = lax.fori_loop(
            0, docs, one, (jnp.int32(0), jnp.zeros((8, TQ), jnp.int32)), unroll=8
        )
        doc_start[...] = found


def prepare(count, doc_lengths, query, dout, after):
    rows = query.shape[0] // 2
    heads = query.shape[1] // HD
    stacked = jax.ShapeDtypeStruct((rows * heads, HD), query.dtype)
    starts = jax.ShapeDtypeStruct((8, TQ), jnp.int32)
    return pl.pallas_call(
        functools.partial(prepare_kernel, rows, heads, doc_lengths.shape[0], count),
        out_shape=(stacked, stacked, starts) * 2,
        in_specs=[SMEM, VMEM, VMEM, pl.BlockSpec(memory_space=pl.ANY)],
        out_specs=[VMEM] * 6,
        compiler_params=pltpu.CompilerParams(vmem_limit_bytes=VMEM_LIMIT),
        cost_estimate=pl.CostEstimate(flops=0, bytes_accessed=4 * 2**20, transcendentals=0),
        name="prepare",
    )(doc_lengths, query, dout, after)


def scores_kernel(
    rows,
    heads,
    count,
    slot,
    query_rows,
    dout_rows,
    doc_start,
    own_kv,
    prev1,
    prev2,
    weights,
    dscores,
    inverses,
    query_scaled,
    dout_scaled,
    prev1_out,
    prev2_out,
    scores,
    dprobs,
    dk,
    dv,
):
    back = 2 * rows
    width = back + TQ
    wide = heads * TQ
    base2 = SCALE * math.log2(math.e)
    block_pos = block_number(count, slot) * rows

    for step in range(rows // TQ):
        first = step * TQ
        tile = slice(step * wide, (step + 1) * wide)
        query_tile = query_rows[tile, :]
        dout_tile = dout_rows[tile, :]
        sources = (
            (prev2, first, rows - first, 0),
            (prev1, 0, rows, rows - first),
            (own_kv, 0, first + TQ, back - first),
        )
        low = doc_start[step : step + 1, :] - (block_pos - back + first)
        high = lax.broadcasted_iota(jnp.int32, (1, TQ), 1) + back
        row_max = jnp.full((8, wide), masked_score, jnp.float32)
        for source, row, length, place in sources:
            product = dot_nt(source[row : row + length, :], query_tile)
            for start in range(0, length, GROUP):
                at = lax.broadcasted_iota(jnp.int32, (GROUP, TQ), 0) + (place + start)
                allowed = at >= low
                if place + start >= back:
                    allowed = jnp.logical_and(allowed, at <= high)
                allowed = jnp.concatenate([allowed] * heads, axis=1)
                part = jnp.where(allowed, product[start : start + GROUP, :], masked_score)
                scores[place + start : place + start + GROUP, :] = part
                for row8 in range(0, GROUP, 8):
                    row_max = jnp.maximum(row_max, part[row8 : row8 + 8, :])
        row_max = jnp.max(row_max, axis=0, keepdims=True) * base2
        total = jnp.zeros((8, wide), jnp.float32)
        delta = jnp.zeros((8, wide), jnp.float32)
        out = step * width
        for source, row, length, place in sources:
            product = dot_nt(source[rows + row : rows + row + length, :], dout_tile)
            for start in range(0, length, GROUP):
                here = slice(place + start, place + start + GROUP)
                there = slice(out + place + start, out + place + start + GROUP)
                dprob = product[start : start + GROUP, :]
                dprobs[here, :] = dprob
                part = jnp.exp2(scores[here, :] * base2 - row_max)
                weights[there, :] = part.astype(jnp.bfloat16)
                term = part * dprob
                for row8 in range(0, GROUP, 8):
                    total = total + part[row8 : row8 + 8, :]
                    delta = delta + term[row8 : row8 + 8, :]
        inverse = 1.0 / jnp.sum(total, axis=0, keepdims=True)
        delta = jnp.sum(delta, axis=0, keepdims=True) * inverse
        inverses[step : step + 1, :] = inverse
        for start in range(0, width, GROUP):
            there = slice(out + start, out + start + GROUP)
            dscores[there, :] = weights[there, :] * (
                dprobs[start : start + GROUP, :] - delta
            ).astype(jnp.bfloat16)
        for h in range(heads):
            part = slice(h * TQ, (h + 1) * TQ)
            place = slice(step * wide + h * TQ, step * wide + (h + 1) * TQ)
            column = jnp.transpose(jnp.broadcast_to(inverse[:, part], (TQ, TQ)))
            query_scaled[place, :] = (query_tile[part].astype(jnp.float32) * column).astype(
                jnp.bfloat16
            )
            dout_scaled[place, :] = (dout_tile[part].astype(jnp.float32) * column).astype(
                jnp.bfloat16
            )
        for total_ref, terms, side in ((dv, weights, dout_scaled), (dk, dscores, query_scaled)):
            term = dot_nn(terms[out : out + back - first, :], side[tile, :])
            if step == 0:
                total_ref[...] = term
            else:
                total_ref[first:back] += term

    prev2_out[0:rows] = (dk[0:rows] * SCALE).astype(prev2_out.dtype)
    prev2_out[rows:back] = dv[0:rows].astype(prev2_out.dtype)
    prev1_out[0:rows] = (dk[rows:back] * SCALE).astype(prev1_out.dtype)
    prev1_out[rows:back] = dv[rows:back].astype(prev1_out.dtype)


def block_scores(slot, count, prepared, own_kv, prev1, prev2):
    rows = own_kv.shape[0] // 2
    heads = prepared[0].shape[0] // rows
    steps = rows // TQ
    width = 2 * rows + TQ
    wide = heads * TQ
    pair = jax.ShapeDtypeStruct((2 * rows, HD), jnp.bfloat16)
    kept = jax.ShapeDtypeStruct((steps * width, wide), jnp.bfloat16)
    inverses = jax.ShapeDtypeStruct((8, wide), jnp.float32)
    stacked = jax.ShapeDtypeStruct((rows * heads, HD), jnp.bfloat16)
    return pl.pallas_call(
        functools.partial(scores_kernel, rows, heads, count, slot),
        out_shape=(kept, kept, inverses, stacked, stacked, pair, pair),
        in_specs=[VMEM] * 6,
        out_specs=[VMEM] * 7,
        scratch_shapes=[
            pltpu.VMEM((width, wide), jnp.float32),
            pltpu.VMEM((width, wide), jnp.float32),
            pltpu.VMEM((2 * rows, HD), jnp.float32),
            pltpu.VMEM((2 * rows, HD), jnp.float32),
        ],
        compiler_params=pltpu.CompilerParams(vmem_limit_bytes=VMEM_LIMIT),
        cost_estimate=pl.CostEstimate(
            flops=4 * 2 * steps * width * heads * TQ * HD, bytes_accessed=0, transcendentals=0
        ),
        name="scores_far" if slot == 0 else "scores_near",
    )(*prepared, own_kv, prev1, prev2)


def outputs_kernel(rows, heads, from_far_2, *refs):
    blocks = (refs[0:8], refs[8:16])
    (attended, grad_query, far_own, near_own, keys_t, values_t) = refs[16:]
    back = 2 * rows
    width = back + TQ
    wide = heads * TQ
    for slot, block in enumerate(blocks):
        (own_kv, prev1, prev2, weights, dscores, inverses, query_scaled, dout_scaled) = block
        own_out = (far_own, near_own)[slot]
        own_rows = half_start(rows, slot)
        for place, source in enumerate((prev2, prev1, own_kv)):
            for tile in range(rows // TQ):
                part = slice(place * rows + tile * TQ, place * rows + (tile + 1) * TQ)
                row = tile * TQ
                keys_t[:, part] = jnp.transpose(source[row : row + TQ, :])
                values_t[:, part] = jnp.transpose(source[rows + row : rows + row + TQ, :])
        for step in reversed(range(rows // TQ)):
            first = step * TQ
            out = step * width
            tile = slice(step * wide, (step + 1) * wide)
            tail = slice(out + back - first, out + width)
            for offset, terms, side, factor in (
                (0, dscores, query_scaled, SCALE),
                (rows, weights, dout_scaled, 1.0),
            ):
                term = dot_nn(terms[tail, :], side[tile, :]) * factor
                place = slice(offset, offset + first + TQ)
                if step < rows // TQ - 1:
                    own_out[place] += term
                elif slot == 0:
                    own_out[place] = term + from_far_2[place].astype(jnp.float32)
                else:
                    own_out[place] = term
            window = slice(first, first + width)
            inverse = inverses[step : step + 1, :]
            attended_t = dot_nn(values_t[:, window], weights[out : out + width, :]) * inverse
            grad_query_t = dot_nn(keys_t[:, window], dscores[out : out + width, :]) * (
                inverse * SCALE
            )
            place = pl.ds(own_rows + first, TQ)
            for h in range(heads):
                part = slice(h * TQ, (h + 1) * TQ)
                columns = slice(h * HD, (h + 1) * HD)
                attended[place, columns] = jnp.transpose(attended_t[:, part]).astype(
                    attended.dtype
                )
                grad_query[place, columns] = jnp.transpose(grad_query_t[:, part]).astype(
                    grad_query.dtype
                )


def block_outputs(query, from_far_2, far, near):
    rows = query.shape[0] // 2
    heads = query.shape[1] // HD
    wide = jax.ShapeDtypeStruct(query.shape, query.dtype)
    own = jax.ShapeDtypeStruct((2 * rows, HD), jnp.float32)
    return pl.pallas_call(
        functools.partial(outputs_kernel, rows, heads),
        out_shape=(wide, wide, own, own),
        in_specs=[VMEM] * 17,
        out_specs=[VMEM] * 4,
        scratch_shapes=[
            pltpu.VMEM((HD, 3 * rows), jnp.bfloat16),
            pltpu.VMEM((HD, 3 * rows), jnp.bfloat16),
        ],
        compiler_params=pltpu.CompilerParams(vmem_limit_bytes=VMEM_LIMIT),
        cost_estimate=pl.CostEstimate(flops=0, bytes_accessed=0, transcendentals=0),
        name="block_outputs",
    )(from_far_2, *far, *near)


def total_kernel(rows, far_own, far_1, near_own, near_1, grad_key, grad_value):
    far = far_own[...] + far_1[...].astype(jnp.float32)
    near = near_own[...] + near_1[...].astype(jnp.float32)
    for slot, total in ((0, far), (1, near)):
        place = pl.ds(half_start(rows, slot), rows)
        grad_key[place, :] = total[0:rows].astype(grad_key.dtype)
        grad_value[place, :] = total[rows : 2 * rows].astype(grad_value.dtype)


def total_grads(far_own, far_1, near_own, near_1):
    rows = far_own.shape[0] // 2
    shape = jax.ShapeDtypeStruct((2 * rows, HD), jnp.bfloat16)
    return pl.pallas_call(
        functools.partial(total_kernel, rows),
        out_shape=(shape, shape),
        in_specs=[VMEM] * 4,
        out_specs=[VMEM] * 2,
        compiler_params=pltpu.CompilerParams(vmem_limit_bytes=VMEM_LIMIT),
        name="total_grads",
    )(far_own, far_1, near_own, near_1)


def body(query, key, value, d_out, doc_lengths):
    count = lax.axis_size("ctx")

    def holder(block):
        return block if block < count else 2 * count - 1 - block

    def move(array, pairs):
        return lax.ppermute(array, "ctx", pairs)

    near_on = [(holder(b), holder(b + 2)) for b in range(1, 2 * count - 2, 2)]
    far_on = [(holder(b), holder(b + 2)) for b in range(0, 2 * count - 2, 2)]
    swap = [(d, d ^ 1) for d in range(count)]
    near_back = [(t, s) for s, t in near_on]
    far_back = [(t, s) for s, t in far_on]

    near_kv, far_kv = pack_blocks(key, value)
    near_2 = move(near_kv, near_on)
    far_2 = move(far_kv, far_on)
    near_1 = move(far_kv, swap)
    prepared = prepare(count, doc_lengths, query, d_out, near_kv)
    near_2, prepared = lax.optimization_barrier((near_2, prepared))
    far_1 = move(near_2, swap)

    *far_kept, far_g1, far_g2 = block_scores(0, count, prepared[0:3], far_kv, far_1, far_2)
    from_far_2 = move(far_g2, far_back)
    relayed = move(far_g1, swap)
    *near_kept, near_g1, near_g2 = block_scores(1, count, prepared[3:6], near_kv, near_1, near_2)
    near_sum = (near_g2.astype(jnp.float32) + relayed.astype(jnp.float32)).astype(jnp.bfloat16)
    from_near_2 = move(near_sum, near_back)
    near_g1, from_far_2 = lax.optimization_barrier((near_g1, from_far_2))
    from_near_1 = move(near_g1, swap)
    attended, grad_query, far_own, near_own = block_outputs(
        query,
        from_far_2,
        (far_kv, far_1, far_2, *far_kept),
        (near_kv, near_1, near_2, *near_kept),
    )
    grad_key, grad_value = total_grads(far_own, from_near_1, near_own, from_near_2)
    return (attended, grad_query, grad_key, grad_value)


def solution(mesh):
    rows = P(("dp", "ctx"), None)
    return jax.shard_map(
        body,
        mesh=mesh,
        in_specs=(rows, rows, rows, rows, P("dp")),
        out_specs=(rows, rows, rows, rows),
        check_vma=False,
    )
```

```python
import functools
import math

import jax
import jax.numpy as jnp
from jax import lax
from jax.experimental import pallas as pl
from jax.experimental.pallas import tpu as pltpu
from jax.sharding import PartitionSpec as P

HD = 128
TQ = 128
GROUP = 32

masked_score = -1e30
VMEM_LIMIT = 24 * 1024 * 1024
SCALE = 1.0 / math.sqrt(HD)
VMEM = pl.BlockSpec(memory_space=pltpu.VMEM)
SMEM = pl.BlockSpec(memory_space=pltpu.SMEM)


def dot_nn(a, b):
    return lax.dot_general(a, b, (((1,), (0,)), ((), ())), preferred_element_type=jnp.float32)


def half_start(rows, slot):
    odd = lax.axis_index("ctx") % 2
    return pl.multiple_of((odd if slot == 0 else 1 - odd) * rows, rows)


def block_number(count, slot):
    device = lax.axis_index("ctx")
    in_lower = device % 2 == slot
    return jnp.where(in_lower, device, 2 * count - 1 - device)


def pack_kernel(rows, key, value, near_out, far_out):
    for slot, out in ((1, near_out), (0, far_out)):
        place = pl.ds(half_start(rows, slot), rows)
        out[0:rows] = key[place, :]
        out[rows : 2 * rows] = value[place, :]


def pack_blocks(key, value):
    rows = key.shape[0] // 2
    shape = jax.ShapeDtypeStruct((2 * rows, HD), key.dtype)
    return pl.pallas_call(
        functools.partial(pack_kernel, rows),
        out_shape=(shape, shape),
        in_specs=[VMEM] * 2,
        out_specs=[VMEM] * 2,
        name="pack_blocks",
    )(key, value)


def prepare_kernel(rows, heads, docs, count, doc_lengths, query, dout, key, value, *refs):
    wide = heads * TQ
    for slot in (0, 1):
        own_kv, query_rows, dout_rows, query_t, dout_t, doc_start = refs[6 * slot : 6 * slot + 6]
        own_rows = half_start(rows, slot)
        own_kv[0:rows] = key[pl.ds(own_rows, rows), :]
        own_kv[rows : 2 * rows] = value[pl.ds(own_rows, rows), :]
        for step in range(rows // TQ):
            source = pl.ds(own_rows + step * TQ, TQ)
            for h in range(heads):
                place = slice(step * wide + h * TQ, step * wide + (h + 1) * TQ)
                columns = slice(h * HD, (h + 1) * HD)
                for wide_ref, rows_ref, t_ref in (
                    (query, query_rows, query_t),
                    (dout, dout_rows, dout_t),
                ):
                    part = wide_ref[source, columns]
                    rows_ref[place, :] = part
                    t_ref[:, place] = jnp.transpose(part)
        at = (
            block_number(count, slot) * rows
            + lax.broadcasted_iota(jnp.int32, (8, TQ), 0) * TQ
            + lax.broadcasted_iota(jnp.int32, (8, TQ), 1)
        )

        def one(index, carry):
            start, found = carry
            found = jnp.where(at >= start, start, found)
            return (start + doc_lengths[index], found)

        _, found = lax.fori_loop(
            0, docs, one, (jnp.int32(0), jnp.zeros((8, TQ), jnp.int32)), unroll=8
        )
        doc_start[...] = found


def prepare(count, doc_lengths, query, dout, key, value):
    rows = query.shape[0] // 2
    heads = query.shape[1] // HD
    pair = jax.ShapeDtypeStruct((2 * rows, HD), key.dtype)
    stacked = jax.ShapeDtypeStruct((rows * heads, HD), query.dtype)
    stacked_t = jax.ShapeDtypeStruct((HD, rows * heads), query.dtype)
    starts = jax.ShapeDtypeStruct((8, TQ), jnp.int32)
    return pl.pallas_call(
        functools.partial(prepare_kernel, rows, heads, doc_lengths.shape[0], count),
        out_shape=(pair, stacked, stacked, stacked_t, stacked_t, starts) * 2,
        in_specs=[SMEM] + [VMEM] * 4,
        out_specs=[VMEM] * 12,
        compiler_params=pltpu.CompilerParams(vmem_limit_bytes=VMEM_LIMIT),
        cost_estimate=pl.CostEstimate(flops=0, bytes_accessed=4 * 2**20, transcendentals=0),
        name="prepare",
    )(doc_lengths, query, dout, key, value)


def scores_kernel(
    rows,
    heads,
    count,
    slot,
    own_kv,
    query_rows,
    dout_rows,
    query_t,
    dout_t,
    doc_start,
    prev1,
    prev2,
    weights,
    dscores,
    inverses,
    query_scaled,
    dout_scaled,
    prev1_out,
    prev2_out,
    all_scores,
    all_dprobs,
    dk,
    dv,
):
    back = 2 * rows
    width = back + TQ
    wide = heads * TQ
    base2 = SCALE * math.log2(math.e)
    block_pos = block_number(count, slot) * rows

    for step in range(rows // TQ):
        first = step * TQ
        tile = slice(step * wide, (step + 1) * wide)
        scores, dprobs = all_scores.at[step], all_dprobs.at[step]
        sources = (
            (prev2, first, rows - first, 0),
            (prev1, 0, rows, rows - first),
            (own_kv, 0, first + TQ, back - first),
        )
        low = doc_start[step : step + 1, :] - (block_pos - back + first)
        high = lax.broadcasted_iota(jnp.int32, (1, TQ), 1) + back
        row_max = [jnp.full((8, TQ), masked_score, jnp.float32)] * heads
        for source, row, length, place in sources:
            product = dot_nn(source[row : row + length, :], query_t[:, tile])
            for start in range(0, length, GROUP):
                at = lax.broadcasted_iota(jnp.int32, (GROUP, TQ), 0) + (place + start)
                allowed = at >= low
                if place + start >= back:
                    allowed = jnp.logical_and(allowed, at <= high)
                here = slice(place + start, place + start + GROUP)
                for h in range(heads):
                    lanes = slice(h * TQ, (h + 1) * TQ)
                    part = jnp.where(allowed, product[start : start + GROUP, lanes], masked_score)
                    scores[here, lanes] = part
                    for row8 in range(0, GROUP, 8):
                        row_max[h] = jnp.maximum(row_max[h], part[row8 : row8 + 8, :])
        row_max = jnp.concatenate(
            [jnp.max(part, axis=0, keepdims=True) * base2 for part in row_max], axis=1
        )
        total = jnp.zeros((8, wide), jnp.float32)
        delta = jnp.zeros((8, wide), jnp.float32)
        out = step * width
        for source, row, length, place in sources:
            product = dot_nn(source[rows + row : rows + row + length, :], dout_t[:, tile])
            for start in range(0, length, GROUP):
                here = slice(place + start, place + start + GROUP)
                there = slice(out + place + start, out + place + start + GROUP)
                dprob = product[start : start + GROUP, :]
                dprobs[here, :] = dprob
                part = jnp.exp2(scores[here, :] * base2 - row_max)
                weights[there, :] = part.astype(jnp.bfloat16)
                term = part * dprob
                for row8 in range(0, GROUP, 8):
                    total = total + part[row8 : row8 + 8, :]
                    delta = delta + term[row8 : row8 + 8, :]
        inverse = 1.0 / jnp.sum(total, axis=0, keepdims=True)
        delta = jnp.sum(delta, axis=0, keepdims=True) * inverse
        inverses[step : step + 1, :] = inverse
        for start in range(0, width, GROUP):
            there = slice(out + start, out + start + GROUP)
            dscores[there, :] = weights[there, :] * (
                dprobs[start : start + GROUP, :] - delta
            ).astype(jnp.bfloat16)
        for h in range(heads):
            part = slice(h * TQ, (h + 1) * TQ)
            place = slice(step * wide + h * TQ, step * wide + (h + 1) * TQ)
            column = jnp.transpose(jnp.broadcast_to(inverse[:, part], (TQ, TQ)))
            for rows_ref, scaled in ((query_rows, query_scaled), (dout_rows, dout_scaled)):
                scaled[place, :] = (rows_ref[place, :].astype(jnp.float32) * column).astype(
                    jnp.bfloat16
                )
        for total_ref, terms, side in ((dv, weights, dout_scaled), (dk, dscores, query_scaled)):
            term = dot_nn(terms[out : out + back - first, :], side[tile, :])
            if step == 0:
                total_ref[...] = term
            else:
                total_ref[first:back] += term

    prev2_out[0:rows] = (dk[0:rows] * SCALE).astype(prev2_out.dtype)
    prev2_out[rows:back] = dv[0:rows].astype(prev2_out.dtype)
    prev1_out[0:rows] = (dk[rows:back] * SCALE).astype(prev1_out.dtype)
    prev1_out[rows:back] = dv[rows:back].astype(prev1_out.dtype)


def block_scores(slot, count, prepared, prev1, prev2):
    rows = prev1.shape[0] // 2
    heads = prepared[1].shape[0] // rows
    steps = rows // TQ
    width = 2 * rows + TQ
    wide = heads * TQ
    pair = jax.ShapeDtypeStruct((2 * rows, HD), jnp.bfloat16)
    kept = jax.ShapeDtypeStruct((steps * width, wide), jnp.bfloat16)
    inverses = jax.ShapeDtypeStruct((8, wide), jnp.float32)
    stacked = jax.ShapeDtypeStruct((rows * heads, HD), jnp.bfloat16)
    return pl.pallas_call(
        functools.partial(scores_kernel, rows, heads, count, slot),
        out_shape=(kept, kept, inverses, stacked, stacked, pair, pair),
        in_specs=[VMEM] * 8,
        out_specs=[VMEM] * 7,
        scratch_shapes=[
            pltpu.VMEM((steps, width, wide), jnp.float32),
            pltpu.VMEM((steps, width, wide), jnp.float32),
            pltpu.VMEM((2 * rows, HD), jnp.float32),
            pltpu.VMEM((2 * rows, HD), jnp.float32),
        ],
        compiler_params=pltpu.CompilerParams(vmem_limit_bytes=VMEM_LIMIT),
        cost_estimate=pl.CostEstimate(
            flops=4 * 2 * steps * width * heads * TQ * HD, bytes_accessed=0, transcendentals=0
        ),
        name="scores_far" if slot == 0 else "scores_near",
    )(*prepared, prev1, prev2)


def outputs_kernel(rows, heads, from_far_2, *refs):
    blocks = (refs[0:8], refs[8:16])
    (attended, grad_query, far_own, near_own, keys_t, values_t) = refs[16:]
    back = 2 * rows
    width = back + TQ
    wide = heads * TQ
    for slot, block in enumerate(blocks):
        (own_kv, prev1, prev2, weights, dscores, inverses, query_scaled, dout_scaled) = block
        own_out = (far_own, near_own)[slot]
        own_rows = half_start(rows, slot)
        for place, source in enumerate((prev2, prev1, own_kv)):
            for tile in range(rows // TQ):
                part = slice(place * rows + tile * TQ, place * rows + (tile + 1) * TQ)
                row = tile * TQ
                keys_t[:, part] = jnp.transpose(source[row : row + TQ, :])
                values_t[:, part] = jnp.transpose(source[rows + row : rows + row + TQ, :])
        for step in reversed(range(rows // TQ)):
            first = step * TQ
            out = step * width
            tile = slice(step * wide, (step + 1) * wide)
            tail = slice(out + back - first, out + width)
            for offset, terms, side, factor in (
                (0, dscores, query_scaled, SCALE),
                (rows, weights, dout_scaled, 1.0),
            ):
                term = dot_nn(terms[tail, :], side[tile, :]) * factor
                place = slice(offset, offset + first + TQ)
                if step < rows // TQ - 1:
                    own_out[place] += term
                elif slot == 0:
                    own_out[place] = term + from_far_2[place].astype(jnp.float32)
                else:
                    own_out[place] = term
            window = slice(first, first + width)
            inverse = inverses[step : step + 1, :]
            attended_t = dot_nn(values_t[:, window], weights[out : out + width, :]) * inverse
            grad_query_t = dot_nn(keys_t[:, window], dscores[out : out + width, :]) * (
                inverse * SCALE
            )
            place = pl.ds(own_rows + first, TQ)
            for h in range(heads):
                part = slice(h * TQ, (h + 1) * TQ)
                columns = slice(h * HD, (h + 1) * HD)
                attended[place, columns] = jnp.transpose(attended_t[:, part]).astype(
                    attended.dtype
                )
                grad_query[place, columns] = jnp.transpose(grad_query_t[:, part]).astype(
                    grad_query.dtype
                )


def block_outputs(query, from_far_2, far, near):
    rows = query.shape[0] // 2
    heads = query.shape[1] // HD
    wide = jax.ShapeDtypeStruct(query.shape, query.dtype)
    own = jax.ShapeDtypeStruct((2 * rows, HD), jnp.float32)
    return pl.pallas_call(
        functools.partial(outputs_kernel, rows, heads),
        out_shape=(wide, wide, own, own),
        in_specs=[VMEM] * 17,
        out_specs=[VMEM] * 4,
        scratch_shapes=[
            pltpu.VMEM((HD, 3 * rows), jnp.bfloat16),
            pltpu.VMEM((HD, 3 * rows), jnp.bfloat16),
        ],
        compiler_params=pltpu.CompilerParams(vmem_limit_bytes=VMEM_LIMIT),
        cost_estimate=pl.CostEstimate(flops=0, bytes_accessed=0, transcendentals=0),
        name="block_outputs",
    )(from_far_2, *far, *near)


def total_kernel(rows, far_own, far_1, near_own, near_1, grad_key, grad_value):
    far = far_own[...] + far_1[...].astype(jnp.float32)
    near = near_own[...] + near_1[...].astype(jnp.float32)
    for slot, total in ((0, far), (1, near)):
        place = pl.ds(half_start(rows, slot), rows)
        grad_key[place, :] = total[0:rows].astype(grad_key.dtype)
        grad_value[place, :] = total[rows : 2 * rows].astype(grad_value.dtype)


def total_grads(far_own, far_1, near_own, near_1):
    rows = far_own.shape[0] // 2
    shape = jax.ShapeDtypeStruct((2 * rows, HD), jnp.bfloat16)
    return pl.pallas_call(
        functools.partial(total_kernel, rows),
        out_shape=(shape, shape),
        in_specs=[VMEM] * 4,
        out_specs=[VMEM] * 2,
        compiler_params=pltpu.CompilerParams(vmem_limit_bytes=VMEM_LIMIT),
        name="total_grads",
    )(far_own, far_1, near_own, near_1)


def body(query, key, value, d_out, doc_lengths):
    count = lax.axis_size("ctx")

    def holder(block):
        return block if block < count else 2 * count - 1 - block

    def move(array, pairs):
        return lax.ppermute(array, "ctx", pairs)

    near_on = [(holder(b), holder(b + 2)) for b in range(1, 2 * count - 2, 2)]
    far_on = [(holder(b), holder(b + 2)) for b in range(0, 2 * count - 2, 2)]
    swap = [(d, d ^ 1) for d in range(count)]
    near_back = [(t, s) for s, t in near_on]
    far_back = [(t, s) for s, t in far_on]

    near_kv, far_kv = pack_blocks(key, value)
    partner_near = move(near_kv, swap)
    far_2 = move(far_kv, far_on)
    far_1 = move(partner_near, far_on)
    near_1 = move(far_kv, swap)
    prepared = prepare(count, doc_lengths, query, d_out, key, value)
    far_1, prepared = lax.optimization_barrier((far_1, prepared))
    near_2 = move(far_1, swap)

    *far_kept, far_g1, far_g2 = block_scores(0, count, prepared[0:6], far_1, far_2)
    from_far_2 = move(far_g2, far_back)
    relayed = move(far_g1, swap)
    *near_kept, near_g1, near_g2 = block_scores(1, count, prepared[6:12], near_1, near_2)
    near_sum = (near_g2.astype(jnp.float32) + relayed.astype(jnp.float32)).astype(jnp.bfloat16)
    from_near_2 = move(near_sum, near_back)
    near_g1, from_far_2 = lax.optimization_barrier((near_g1, from_far_2))
    from_near_1 = move(near_g1, swap)
    attended, grad_query, far_own, near_own = block_outputs(
        query,
        from_far_2,
        (prepared[0], far_1, far_2, *far_kept),
        (prepared[6], near_1, near_2, *near_kept),
    )
    grad_key, grad_value = total_grads(far_own, from_near_1, near_own, from_near_2)
    return (attended, grad_query, grad_key, grad_value)


def solution(mesh):
    rows = P(("dp", "ctx"), None)
    return jax.shard_map(
        body,
        mesh=mesh,
        in_specs=(rows, rows, rows, rows, P("dp")),
        out_specs=(rows, rows, rows, rows),
        check_vma=False,
    )
```

```python
import functools
import math

import jax
import jax.numpy as jnp
from jax import lax
from jax.experimental import pallas as pl
from jax.experimental.pallas import tpu as pltpu
from jax.sharding import PartitionSpec as P

HD = 128
TQ = 128
GROUP = 32

masked_score = -1e30
VMEM_LIMIT = 24 * 1024 * 1024
SCALE = 1.0 / math.sqrt(HD)
VMEM = pl.BlockSpec(memory_space=pltpu.VMEM)
HBM = pl.BlockSpec(memory_space=pltpu.HBM)
CHUNK = 128


def dot_nn(a, b):
    return lax.dot_general(a, b, (((1,), (0,)), ((), ())), preferred_element_type=jnp.float32)


def half_start(rows, slot):
    odd = lax.axis_index("ctx") % 2
    return pl.multiple_of((odd if slot == 0 else 1 - odd) * rows, rows)


def block_number(count, slot):
    device = lax.axis_index("ctx")
    in_lower = device % 2 == slot
    return jnp.where(in_lower, device, 2 * count - 1 - device)


def in_hbm(array):
    return pltpu.with_memory_space_constraint(array, pltpu.HBM)


def load_block(rows, slot, key, value, out, sems):
    place = pl.ds(half_start(rows, slot), rows)
    return [
        pltpu.make_async_copy(key.at[place], out.at[0:rows], sems.at[2 * slot]),
        pltpu.make_async_copy(value.at[place], out.at[rows : 2 * rows], sems.at[2 * slot + 1]),
    ]


def run_copies(copies):
    for copy in copies:
        copy.start()
    for copy in copies:
        copy.wait()


def pack_kernel(rows, key, value, near_out, far_out, sems):
    run_copies(
        load_block(rows, 1, key, value, near_out, sems)
        + load_block(rows, 0, key, value, far_out, sems)
    )


def pack_blocks(key, value):
    rows = key.shape[0] // 2
    shape = jax.ShapeDtypeStruct((2 * rows, HD), key.dtype)
    return pl.pallas_call(
        functools.partial(pack_kernel, rows),
        out_shape=(shape, shape),
        in_specs=[HBM] * 2,
        out_specs=[VMEM] * 2,
        scratch_shapes=[pltpu.SemaphoreType.DMA((4,))],
        name="pack_blocks",
    )(in_hbm(key), in_hbm(value))


def prepare_kernel(rows, heads, docs, count, *refs):
    (doc_hbm, query_hbm, dout_hbm, key, value) = refs[0:5]
    (doc_lengths, query, dout, sems) = refs[17:]
    refs = refs[5:17]
    wide = heads * TQ
    run_copies(
        [
            pltpu.make_async_copy(query_hbm, query, sems.at[4]),
            pltpu.make_async_copy(dout_hbm, dout, sems.at[5]),
            pltpu.make_async_copy(doc_hbm, doc_lengths, sems.at[6]),
        ]
        + load_block(rows, 0, key, value, refs[0], sems)
        + load_block(rows, 1, key, value, refs[6], sems)
    )
    for slot in (0, 1):
        _, query_rows, dout_rows, query_t, dout_t, doc_start = refs[6 * slot : 6 * slot + 6]
        own_rows = half_start(rows, slot)
        for step in range(rows // TQ):
            source = pl.ds(own_rows + step * TQ, TQ)
            for h in range(heads):
                place = slice(step * wide + h * TQ, step * wide + (h + 1) * TQ)
                columns = slice(h * HD, (h + 1) * HD)
                for wide_ref, rows_ref, t_ref in (
                    (query, query_rows, query_t),
                    (dout, dout_rows, dout_t),
                ):
                    part = wide_ref[source, columns]
                    rows_ref[place, :] = part
                    t_ref[:, place] = jnp.transpose(part)
        at = (
            block_number(count, slot) * rows
            + lax.broadcasted_iota(jnp.int32, (8, TQ), 0) * TQ
            + lax.broadcasted_iota(jnp.int32, (8, TQ), 1)
        )

        def one(index, carry):
            start, found = carry
            found = jnp.where(at >= start, start, found)
            return (start + doc_lengths[index], found)

        _, found = lax.fori_loop(
            0, docs, one, (jnp.int32(0), jnp.zeros((8, TQ), jnp.int32)), unroll=8
        )
        doc_start[...] = found


def prepare(count, doc_lengths, query, dout, key, value):
    rows = query.shape[0] // 2
    heads = query.shape[1] // HD
    pair = jax.ShapeDtypeStruct((2 * rows, HD), key.dtype)
    stacked = jax.ShapeDtypeStruct((rows * heads, HD), query.dtype)
    stacked_t = jax.ShapeDtypeStruct((HD, rows * heads), query.dtype)
    starts = jax.ShapeDtypeStruct((8, TQ), jnp.int32)
    return pl.pallas_call(
        functools.partial(prepare_kernel, rows, heads, doc_lengths.shape[0], count),
        out_shape=(pair, stacked, stacked, stacked_t, stacked_t, starts) * 2,
        in_specs=[HBM] * 5,
        out_specs=[VMEM] * 12,
        scratch_shapes=[
            pltpu.SMEM(doc_lengths.shape, doc_lengths.dtype),
            pltpu.VMEM(query.shape, query.dtype),
            pltpu.VMEM(dout.shape, dout.dtype),
            pltpu.SemaphoreType.DMA((7,)),
        ],
        compiler_params=pltpu.CompilerParams(vmem_limit_bytes=VMEM_LIMIT),
        cost_estimate=pl.CostEstimate(flops=0, bytes_accessed=4 * 2**20, transcendentals=0),
        name="prepare",
    )(*(in_hbm(array) for array in (doc_lengths, query, dout, key, value)))


def scores_kernel(
    rows,
    heads,
    count,
    slot,
    own_kv,
    query_rows,
    dout_rows,
    query_t,
    dout_t,
    doc_start,
    prev1,
    prev2,
    weights,
    dscores,
    inverses,
    query_scaled,
    dout_scaled,
    prev1_out,
    prev2_out,
    scores,
    dprobs,
    dk,
    dv,
):
    back = 2 * rows
    width = back + TQ
    wide = heads * TQ
    steps = rows // TQ
    base2 = SCALE * math.log2(math.e)
    block_pos = block_number(count, slot) * rows
    chunks = width // CHUNK

    def source(step, chunk):
        row = step * TQ + chunk * CHUNK
        return (prev2, prev1, own_kv)[row // rows], row % rows

    def score_chunk(step, chunk, row_max):
        low = doc_start[step : step + 1, :] - (block_pos - back + step * TQ)
        high = lax.broadcasted_iota(jnp.int32, (1, TQ), 1) + back
        array, row = source(step, chunk)
        tile = slice(step * wide, (step + 1) * wide)
        product = dot_nn(array[row : row + CHUNK, :], query_t[:, tile])
        for start in range(0, CHUNK, GROUP):
            place = chunk * CHUNK + start
            at = lax.broadcasted_iota(jnp.int32, (GROUP, TQ), 0) + place
            allowed = at >= low
            if place >= back:
                allowed = jnp.logical_and(allowed, at <= high)
            for h in range(heads):
                lanes = slice(h * TQ, (h + 1) * TQ)
                part = jnp.where(allowed, product[start : start + GROUP, lanes], masked_score)
                scores[step, place : place + GROUP, lanes] = part
                for row8 in range(0, GROUP, 8):
                    row_max[h] = jnp.maximum(row_max[h], part[row8 : row8 + 8, :])

    def start_max():
        return [jnp.full((8, TQ), masked_score, jnp.float32)] * heads

    following = start_max()
    for chunk in range(chunks):
        score_chunk(0, chunk, following)
    for step in range(steps):
        tile = slice(step * wide, (step + 1) * wide)
        out = step * width
        row_max = jnp.concatenate(
            [jnp.max(part, axis=0, keepdims=True) * base2 for part in following], axis=1
        )
        following = start_max()
        total = jnp.zeros((8, wide), jnp.float32)
        delta = jnp.zeros((8, wide), jnp.float32)
        for chunk in range(chunks):
            array, row = source(step, chunk)
            product = dot_nn(array[rows + row : rows + row + CHUNK, :], dout_t[:, tile])
            for start in range(0, CHUNK, GROUP):
                place = chunk * CHUNK + start
                there = slice(out + place, out + place + GROUP)
                dprob = product[start : start + GROUP, :]
                dprobs[step, place : place + GROUP, :] = dprob.astype(jnp.bfloat16)
                part = jnp.exp2(scores[step, place : place + GROUP, :] * base2 - row_max)
                weights[there, :] = part.astype(jnp.bfloat16)
                term = part * dprob
                for row8 in range(0, GROUP, 8):
                    total = total + part[row8 : row8 + 8, :]
                    delta = delta + term[row8 : row8 + 8, :]
            if step + 1 < steps:
                score_chunk(step + 1, chunk, following)
        inverse = 1.0 / jnp.sum(total, axis=0, keepdims=True)
        delta = (jnp.sum(delta, axis=0, keepdims=True) * inverse).astype(jnp.bfloat16)
        inverses[step : step + 1, :] = inverse
        for h in range(heads):
            part = slice(h * TQ, (h + 1) * TQ)
            place = slice(step * wide + h * TQ, step * wide + (h + 1) * TQ)
            column = jnp.transpose(jnp.broadcast_to(inverse[:, part], (TQ, TQ)))
            for rows_ref, scaled in ((query_rows, query_scaled), (dout_rows, dout_scaled)):
                scaled[place, :] = (rows_ref[place, :].astype(jnp.float32) * column).astype(
                    jnp.bfloat16
                )
        for chunk in range(chunks):
            place = slice(chunk * CHUNK, (chunk + 1) * CHUNK)
            there = slice(out + chunk * CHUNK, out + (chunk + 1) * CHUNK)
            dscores[there, :] = weights[there, :] * (dprobs[step, place, :] - delta)
            row = step * TQ + chunk * CHUNK
            if row >= back:
                continue
            for total_ref, terms, side in (
                (dv, weights, dout_scaled),
                (dk, dscores, query_scaled),
            ):
                term = dot_nn(terms[there, :], side[tile, :])
                if step == 0 or chunk == chunks - 1:
                    total_ref[row : row + CHUNK] = term
                else:
                    total_ref[row : row + CHUNK] += term

    prev2_out[0:rows] = (dk[0:rows] * SCALE).astype(prev2_out.dtype)
    prev2_out[rows:back] = dv[0:rows].astype(prev2_out.dtype)
    prev1_out[0:rows] = (dk[rows:back] * SCALE).astype(prev1_out.dtype)
    prev1_out[rows:back] = dv[rows:back].astype(prev1_out.dtype)


def block_scores(slot, count, prepared, prev1, prev2):
    rows = prev1.shape[0] // 2
    heads = prepared[1].shape[0] // rows
    steps = rows // TQ
    width = 2 * rows + TQ
    wide = heads * TQ
    pair = jax.ShapeDtypeStruct((2 * rows, HD), jnp.bfloat16)
    kept = jax.ShapeDtypeStruct((steps * width, wide), jnp.bfloat16)
    inverses = jax.ShapeDtypeStruct((8, wide), jnp.float32)
    stacked = jax.ShapeDtypeStruct((rows * heads, HD), jnp.bfloat16)
    return pl.pallas_call(
        functools.partial(scores_kernel, rows, heads, count, slot),
        out_shape=(kept, kept, inverses, stacked, stacked, pair, pair),
        in_specs=[VMEM] * 8,
        out_specs=[VMEM] * 7,
        scratch_shapes=[
            pltpu.VMEM((steps, width, wide), jnp.float32),
            pltpu.VMEM((steps, width, wide), jnp.bfloat16),
            pltpu.VMEM((2 * rows, HD), jnp.float32),
            pltpu.VMEM((2 * rows, HD), jnp.float32),
        ],
        compiler_params=pltpu.CompilerParams(vmem_limit_bytes=VMEM_LIMIT),
        cost_estimate=pl.CostEstimate(
            flops=4 * 2 * steps * width * heads * TQ * HD, bytes_accessed=0, transcendentals=0
        ),
        name="scores_far" if slot == 0 else "scores_near",
    )(*prepared, prev1, prev2)


def outputs_kernel(rows, heads, from_far_2, *refs):
    blocks = (refs[0:8], refs[8:16])
    (attended, grad_query, far_own, near_own, keys_t, values_t) = refs[16:]
    back = 2 * rows
    width = back + TQ
    wide = heads * TQ
    for slot, block in enumerate(blocks):
        (own_kv, prev1, prev2, weights, dscores, inverses, query_scaled, dout_scaled) = block
        own_out = (far_own, near_own)[slot]
        own_rows = half_start(rows, slot)
        for place, source in enumerate((prev2, prev1, own_kv)):
            for tile in range(rows // TQ):
                part = slice(place * rows + tile * TQ, place * rows + (tile + 1) * TQ)
                row = tile * TQ
                keys_t[:, part] = jnp.transpose(source[row : row + TQ, :])
                values_t[:, part] = jnp.transpose(source[rows + row : rows + row + TQ, :])
        for step in reversed(range(rows // TQ)):
            first = step * TQ
            out = step * width
            tile = slice(step * wide, (step + 1) * wide)
            tail = slice(out + back - first, out + width)
            for offset, terms, side, factor in (
                (0, dscores, query_scaled, SCALE),
                (rows, weights, dout_scaled, 1.0),
            ):
                term = dot_nn(terms[tail, :], side[tile, :]) * factor
                place = slice(offset, offset + first + TQ)
                if step < rows // TQ - 1:
                    own_out[place] += term
                elif slot == 0:
                    own_out[place] = term + from_far_2[place].astype(jnp.float32)
                else:
                    own_out[place] = term
            window = slice(first, first + width)
            inverse = inverses[step : step + 1, :]
            attended_t = dot_nn(values_t[:, window], weights[out : out + width, :]) * inverse
            grad_query_t = dot_nn(keys_t[:, window], dscores[out : out + width, :]) * (
                inverse * SCALE
            )
            place = pl.ds(own_rows + first, TQ)
            for h in range(heads):
                part = slice(h * TQ, (h + 1) * TQ)
                columns = slice(h * HD, (h + 1) * HD)
                attended[place, columns] = jnp.transpose(attended_t[:, part]).astype(
                    attended.dtype
                )
                grad_query[place, columns] = jnp.transpose(grad_query_t[:, part]).astype(
                    grad_query.dtype
                )


def block_outputs(query, from_far_2, far, near):
    rows = query.shape[0] // 2
    heads = query.shape[1] // HD
    wide = jax.ShapeDtypeStruct(query.shape, query.dtype)
    own = jax.ShapeDtypeStruct((2 * rows, HD), jnp.float32)
    return pl.pallas_call(
        functools.partial(outputs_kernel, rows, heads),
        out_shape=(wide, wide, own, own),
        in_specs=[VMEM] * 17,
        out_specs=[VMEM] * 4,
        scratch_shapes=[
            pltpu.VMEM((HD, 3 * rows), jnp.bfloat16),
            pltpu.VMEM((HD, 3 * rows), jnp.bfloat16),
        ],
        compiler_params=pltpu.CompilerParams(vmem_limit_bytes=VMEM_LIMIT),
        cost_estimate=pl.CostEstimate(flops=0, bytes_accessed=0, transcendentals=0),
        name="block_outputs",
    )(from_far_2, *far, *near)


def total_kernel(rows, far_own, far_1, near_own, near_1, grad_key, grad_value):
    far = far_own[...] + far_1[...].astype(jnp.float32)
    near = near_own[...] + near_1[...].astype(jnp.float32)
    for slot, total in ((0, far), (1, near)):
        place = pl.ds(half_start(rows, slot), rows)
        grad_key[place, :] = total[0:rows].astype(grad_key.dtype)
        grad_value[place, :] = total[rows : 2 * rows].astype(grad_value.dtype)


def total_grads(far_own, far_1, near_own, near_1):
    rows = far_own.shape[0] // 2
    shape = jax.ShapeDtypeStruct((2 * rows, HD), jnp.bfloat16)
    return pl.pallas_call(
        functools.partial(total_kernel, rows),
        out_shape=(shape, shape),
        in_specs=[VMEM] * 4,
        out_specs=[VMEM] * 2,
        compiler_params=pltpu.CompilerParams(vmem_limit_bytes=VMEM_LIMIT),
        name="total_grads",
    )(far_own, far_1, near_own, near_1)


def body(query, key, value, d_out, doc_lengths):
    count = lax.axis_size("ctx")

    def holder(block):
        return block if block < count else 2 * count - 1 - block

    def move(array, pairs):
        return lax.ppermute(array, "ctx", pairs)

    near_on = [(holder(b), holder(b + 2)) for b in range(1, 2 * count - 2, 2)]
    far_on = [(holder(b), holder(b + 2)) for b in range(0, 2 * count - 2, 2)]
    swap = [(d, d ^ 1) for d in range(count)]
    near_back = [(t, s) for s, t in near_on]
    far_back = [(t, s) for s, t in far_on]

    near_kv, far_kv = pack_blocks(key, value)
    partner_near = move(near_kv, swap)
    far_2 = move(far_kv, far_on)
    far_1 = move(partner_near, far_on)
    near_1 = move(far_kv, swap)
    prepared = prepare(count, doc_lengths, query, d_out, key, value)
    far_1, prepared = lax.optimization_barrier((far_1, prepared))
    near_2 = move(far_1, swap)

    *far_kept, far_g1, far_g2 = block_scores(0, count, prepared[0:6], far_1, far_2)
    from_far_2 = move(far_g2, far_back)
    relayed = move(far_g1, swap)
    *near_kept, near_g1, near_g2 = block_scores(1, count, prepared[6:12], near_1, near_2)
    near_sum = (near_g2.astype(jnp.float32) + relayed.astype(jnp.float32)).astype(jnp.bfloat16)
    from_near_2 = move(near_sum, near_back)
    near_g1, from_far_2 = lax.optimization_barrier((near_g1, from_far_2))
    from_near_1 = move(near_g1, swap)
    attended, grad_query, far_own, near_own = block_outputs(
        query,
        from_far_2,
        (prepared[0], far_1, far_2, *far_kept),
        (prepared[6], near_1, near_2, *near_kept),
    )
    grad_key, grad_value = total_grads(far_own, from_near_1, near_own, from_near_2)
    return (attended, grad_query, grad_key, grad_value)


def solution(mesh):
    rows = P(("dp", "ctx"), None)
    return jax.shard_map(
        body,
        mesh=mesh,
        in_specs=(rows, rows, rows, rows, P("dp")),
        out_specs=(rows, rows, rows, rows),
        check_vma=False,
    )
```

```python
import functools
import math

import jax
import jax.numpy as jnp
from jax import lax
from jax.experimental import pallas as pl
from jax.experimental.pallas import tpu as pltpu
from jax.sharding import PartitionSpec as P

HD = 128
TQ = 128
GROUP = 32

masked_score = -1e30
VMEM_LIMIT = 24 * 1024 * 1024
SCALE = 1.0 / math.sqrt(HD)
VMEM = pl.BlockSpec(memory_space=pltpu.VMEM)
HBM = pl.BlockSpec(memory_space=pltpu.HBM)
CHUNK = 128


def dot_nt(a, b):
    return lax.dot_general(a, b, (((1,), (1,)), ((), ())), preferred_element_type=jnp.float32)


def dot_nn(a, b):
    return lax.dot_general(a, b, (((1,), (0,)), ((), ())), preferred_element_type=jnp.float32)


def half_start(rows, slot):
    odd = lax.axis_index("ctx") % 2
    return pl.multiple_of((odd if slot == 0 else 1 - odd) * rows, rows)


def block_number(count, slot):
    device = lax.axis_index("ctx")
    in_lower = device % 2 == slot
    return jnp.where(in_lower, device, 2 * count - 1 - device)


def in_hbm(array):
    return pltpu.with_memory_space_constraint(array, pltpu.HBM)


def load_block(rows, slot, key, value, out, sems):
    place = pl.ds(half_start(rows, slot), rows)
    return [
        pltpu.make_async_copy(key.at[place], out.at[0:rows], sems.at[2 * slot]),
        pltpu.make_async_copy(value.at[place], out.at[rows : 2 * rows], sems.at[2 * slot + 1]),
    ]


def run_copies(copies):
    for copy in copies:
        copy.start()
    for copy in copies:
        copy.wait()


def pack_kernel(rows, key, value, near_out, far_out, sems):
    run_copies(
        load_block(rows, 1, key, value, near_out, sems)
        + load_block(rows, 0, key, value, far_out, sems)
    )


def pack_blocks(key, value):
    rows = key.shape[0] // 2
    shape = jax.ShapeDtypeStruct((2 * rows, HD), key.dtype)
    return pl.pallas_call(
        functools.partial(pack_kernel, rows),
        out_shape=(shape, shape),
        in_specs=[HBM] * 2,
        out_specs=[VMEM] * 2,
        scratch_shapes=[pltpu.SemaphoreType.DMA((4,))],
        name="pack_blocks",
    )(in_hbm(key), in_hbm(value))


def prepare_kernel(rows, heads, docs, count, *refs):
    (doc_hbm, query_hbm, dout_hbm, key, value) = refs[0:5]
    (doc_lengths, query, dout, sems) = refs[13:]
    refs = refs[5:13]
    wide = heads * TQ
    run_copies(
        [
            pltpu.make_async_copy(query_hbm, query, sems.at[4]),
            pltpu.make_async_copy(dout_hbm, dout, sems.at[5]),
            pltpu.make_async_copy(doc_hbm, doc_lengths, sems.at[6]),
        ]
        + load_block(rows, 0, key, value, refs[0], sems)
        + load_block(rows, 1, key, value, refs[4], sems)
    )
    for slot in (0, 1):
        _, query_t, dout_t, doc_start = refs[4 * slot : 4 * slot + 4]
        own_rows = half_start(rows, slot)
        for step in range(rows // TQ):
            source = pl.ds(own_rows + step * TQ, TQ)
            for h in range(heads):
                place = slice(step * wide + h * TQ, step * wide + (h + 1) * TQ)
                columns = slice(h * HD, (h + 1) * HD)
                query_t[:, place] = jnp.transpose(query[source, columns])
                dout_t[:, place] = jnp.transpose(dout[source, columns])
        at = (
            block_number(count, slot) * rows
            + lax.broadcasted_iota(jnp.int32, (8, TQ), 0) * TQ
            + lax.broadcasted_iota(jnp.int32, (8, TQ), 1)
        )

        def one(index, carry):
            start, found = carry
            found = jnp.where(at >= start, start, found)
            return (start + doc_lengths[index], found)

        _, found = lax.fori_loop(
            0, docs, one, (jnp.int32(0), jnp.zeros((8, TQ), jnp.int32)), unroll=8
        )
        doc_start[...] = found


def prepare(count, doc_lengths, query, dout, key, value):
    rows = query.shape[0] // 2
    heads = query.shape[1] // HD
    pair = jax.ShapeDtypeStruct((2 * rows, HD), key.dtype)
    stacked_t = jax.ShapeDtypeStruct((HD, rows * heads), query.dtype)
    starts = jax.ShapeDtypeStruct((8, TQ), jnp.int32)
    return pl.pallas_call(
        functools.partial(prepare_kernel, rows, heads, doc_lengths.shape[0], count),
        out_shape=(pair, stacked_t, stacked_t, starts) * 2,
        in_specs=[HBM] * 5,
        out_specs=[VMEM] * 8,
        scratch_shapes=[
            pltpu.SMEM(doc_lengths.shape, doc_lengths.dtype),
            pltpu.VMEM(query.shape, query.dtype),
            pltpu.VMEM(dout.shape, dout.dtype),
            pltpu.SemaphoreType.DMA((7,)),
        ],
        compiler_params=pltpu.CompilerParams(vmem_limit_bytes=VMEM_LIMIT),
        cost_estimate=pl.CostEstimate(flops=0, bytes_accessed=4 * 2**20, transcendentals=0),
        name="prepare",
    )(*(in_hbm(array) for array in (doc_lengths, query, dout, key, value)))


def scores_kernel(
    rows,
    heads,
    count,
    slot,
    own_kv,
    query_t,
    dout_t,
    doc_start,
    prev1,
    prev2,
    weights,
    dscores,
    inverses,
    query_scaled,
    dout_scaled,
    prev1_out,
    prev2_out,
    scores,
    dprobs,
    dk,
    dv,
):
    back = 2 * rows
    width = back + TQ
    wide = heads * TQ
    steps = rows // TQ
    base2 = SCALE * math.log2(math.e)
    block_pos = block_number(count, slot) * rows
    chunks = width // CHUNK

    def source(step, chunk):
        row = step * TQ + chunk * CHUNK
        return (prev2, prev1, own_kv)[row // rows], row % rows

    def score_chunk(step, chunk, row_max):
        low = doc_start[step : step + 1, :] - (block_pos - back + step * TQ)
        high = lax.broadcasted_iota(jnp.int32, (1, TQ), 1) + back
        array, row = source(step, chunk)
        tile = slice(step * wide, (step + 1) * wide)
        product = dot_nn(array[row : row + CHUNK, :], query_t[:, tile])
        for start in range(0, CHUNK, GROUP):
            place = chunk * CHUNK + start
            at = lax.broadcasted_iota(jnp.int32, (GROUP, TQ), 0) + place
            allowed = at >= low
            if place >= back:
                allowed = jnp.logical_and(allowed, at <= high)
            for h in range(heads):
                lanes = slice(h * TQ, (h + 1) * TQ)
                part = jnp.where(allowed, product[start : start + GROUP, lanes], masked_score)
                scores[step, place : place + GROUP, lanes] = part
                for row8 in range(0, GROUP, 8):
                    row_max[h] = jnp.maximum(row_max[h], part[row8 : row8 + 8, :])

    def start_max():
        return [jnp.full((8, TQ), masked_score, jnp.float32)] * heads

    following = start_max()
    for chunk in range(chunks):
        score_chunk(0, chunk, following)
    for step in range(steps):
        tile = slice(step * wide, (step + 1) * wide)
        out = step * width
        row_max = jnp.concatenate(
            [jnp.max(part, axis=0, keepdims=True) * base2 for part in following], axis=1
        )
        following = start_max()
        total = jnp.zeros((8, wide), jnp.float32)
        delta = jnp.zeros((8, wide), jnp.float32)
        for chunk in range(chunks):
            array, row = source(step, chunk)
            product = dot_nn(array[rows + row : rows + row + CHUNK, :], dout_t[:, tile])
            for start in range(0, CHUNK, GROUP):
                place = chunk * CHUNK + start
                there = slice(out + place, out + place + GROUP)
                dprob = product[start : start + GROUP, :]
                dprobs[step, place : place + GROUP, :] = dprob.astype(jnp.bfloat16)
                part = jnp.exp2(scores[step, place : place + GROUP, :] * base2 - row_max)
                weights[there, :] = part.astype(jnp.bfloat16)
                term = part * dprob
                for row8 in range(0, GROUP, 8):
                    total = total + part[row8 : row8 + 8, :]
                    delta = delta + term[row8 : row8 + 8, :]
            if step + 1 < steps:
                score_chunk(step + 1, chunk, following)
        inverse = 1.0 / jnp.sum(total, axis=0, keepdims=True)
        delta = (jnp.sum(delta, axis=0, keepdims=True) * inverse).astype(jnp.bfloat16)
        inverses[step : step + 1, :] = inverse
        for array, scaled in ((query_t, query_scaled), (dout_t, dout_scaled)):
            scaled[:, tile] = (array[:, tile].astype(jnp.float32) * inverse).astype(jnp.bfloat16)
        delta = jnp.broadcast_to(delta, (16, wide))
        for start in range(0, width, 16):
            there = slice(out + start, out + start + 16)
            dscores[there, :] = weights[there, :] * (dprobs[step, start : start + 16, :] - delta)
        first = step * TQ
        there = slice(out, out + back - first)
        for total_ref, terms, side in ((dv, weights, dout_scaled), (dk, dscores, query_scaled)):
            term = dot_nt(side[:, tile], terms[there, :])
            if step == 0:
                total_ref[...] = term
            else:
                total_ref[:, first:back] += term

    for out, place in ((prev2_out, slice(0, rows)), (prev1_out, slice(rows, back))):
        out[0:HD] = (dk[:, place] * SCALE).astype(out.dtype)
        out[HD : 2 * HD] = dv[:, place].astype(out.dtype)


def block_scores(slot, count, prepared, prev1, prev2):
    rows = prev1.shape[0] // 2
    heads = prepared[1].shape[1] // rows
    steps = rows // TQ
    width = 2 * rows + TQ
    wide = heads * TQ
    pair = jax.ShapeDtypeStruct((2 * HD, rows), jnp.bfloat16)
    kept = jax.ShapeDtypeStruct((steps * width, wide), jnp.bfloat16)
    inverses = jax.ShapeDtypeStruct((8, wide), jnp.float32)
    stacked = jax.ShapeDtypeStruct((HD, rows * heads), jnp.bfloat16)
    return pl.pallas_call(
        functools.partial(scores_kernel, rows, heads, count, slot),
        out_shape=(kept, kept, inverses, stacked, stacked, pair, pair),
        in_specs=[VMEM] * 6,
        out_specs=[VMEM] * 7,
        scratch_shapes=[
            pltpu.VMEM((steps, width, wide), jnp.float32),
            pltpu.VMEM((steps, width, wide), jnp.bfloat16),
            pltpu.VMEM((HD, 2 * rows), jnp.float32),
            pltpu.VMEM((HD, 2 * rows), jnp.float32),
        ],
        compiler_params=pltpu.CompilerParams(vmem_limit_bytes=VMEM_LIMIT),
        cost_estimate=pl.CostEstimate(
            flops=4 * 2 * steps * width * heads * TQ * HD, bytes_accessed=0, transcendentals=0
        ),
        name="scores_far" if slot == 0 else "scores_near",
    )(*prepared, prev1, prev2)


def outputs_kernel(rows, heads, from_far_2, *refs):
    blocks = (refs[0:8], refs[8:16])
    (attended, grad_query, far_own, near_own, keys_t, values_t) = refs[16:]
    back = 2 * rows
    width = back + TQ
    wide = heads * TQ
    for slot, block in enumerate(blocks):
        (own_kv, prev1, prev2, weights, dscores, inverses, query_scaled, dout_scaled) = block
        own_out = (far_own, near_own)[slot]
        own_rows = half_start(rows, slot)
        for place, source in enumerate((prev2, prev1, own_kv)):
            for tile in range(rows // TQ):
                part = slice(place * rows + tile * TQ, place * rows + (tile + 1) * TQ)
                row = tile * TQ
                keys_t[:, part] = jnp.transpose(source[row : row + TQ, :])
                values_t[:, part] = jnp.transpose(source[rows + row : rows + row + TQ, :])
        for step in reversed(range(rows // TQ)):
            first = step * TQ
            out = step * width
            tile = slice(step * wide, (step + 1) * wide)
            tail = slice(out + back - first, out + width)
            for offset, terms, side, factor in (
                (0, dscores, query_scaled, SCALE),
                (HD, weights, dout_scaled, 1.0),
            ):
                term = dot_nt(side[:, tile], terms[tail, :]) * factor
                side_rows = slice(offset, offset + HD)
                place = slice(0, first + TQ)
                if step < rows // TQ - 1:
                    own_out[side_rows, place] += term
                elif slot == 0:
                    own_out[side_rows, place] = term + from_far_2[side_rows, place].astype(
                        jnp.float32
                    )
                else:
                    own_out[side_rows, place] = term
            window = slice(first, first + width)
            inverse = inverses[step : step + 1, :]
            attended_t = dot_nn(values_t[:, window], weights[out : out + width, :]) * inverse
            grad_query_t = dot_nn(keys_t[:, window], dscores[out : out + width, :]) * (
                inverse * SCALE
            )
            place = pl.ds(own_rows + first, TQ)
            for h in range(heads):
                part = slice(h * TQ, (h + 1) * TQ)
                columns = slice(h * HD, (h + 1) * HD)
                attended[place, columns] = jnp.transpose(attended_t[:, part]).astype(
                    attended.dtype
                )
                grad_query[place, columns] = jnp.transpose(grad_query_t[:, part]).astype(
                    grad_query.dtype
                )


def block_outputs(query, from_far_2, far, near):
    rows = query.shape[0] // 2
    heads = query.shape[1] // HD
    wide = jax.ShapeDtypeStruct(query.shape, query.dtype)
    own = jax.ShapeDtypeStruct((2 * HD, rows), jnp.float32)
    return pl.pallas_call(
        functools.partial(outputs_kernel, rows, heads),
        out_shape=(wide, wide, own, own),
        in_specs=[VMEM] * 17,
        out_specs=[VMEM] * 4,
        scratch_shapes=[
            pltpu.VMEM((HD, 3 * rows), jnp.bfloat16),
            pltpu.VMEM((HD, 3 * rows), jnp.bfloat16),
        ],
        compiler_params=pltpu.CompilerParams(vmem_limit_bytes=VMEM_LIMIT),
        cost_estimate=pl.CostEstimate(flops=0, bytes_accessed=0, transcendentals=0),
        name="block_outputs",
    )(from_far_2, *far, *near)


def total_kernel(rows, far_own, far_1, near_own, near_1, grad_key, grad_value):
    far = far_own[...] + far_1[...].astype(jnp.float32)
    near = near_own[...] + near_1[...].astype(jnp.float32)
    for slot, total in ((0, far), (1, near)):
        place = pl.ds(half_start(rows, slot), rows)
        grad_key[place, :] = jnp.transpose(total[0:HD]).astype(grad_key.dtype)
        grad_value[place, :] = jnp.transpose(total[HD : 2 * HD]).astype(grad_value.dtype)


def total_grads(far_own, far_1, near_own, near_1):
    rows = far_own.shape[1]
    shape = jax.ShapeDtypeStruct((2 * rows, HD), jnp.bfloat16)
    return pl.pallas_call(
        functools.partial(total_kernel, rows),
        out_shape=(shape, shape),
        in_specs=[VMEM] * 4,
        out_specs=[VMEM] * 2,
        compiler_params=pltpu.CompilerParams(vmem_limit_bytes=VMEM_LIMIT),
        name="total_grads",
    )(far_own, far_1, near_own, near_1)


def body(query, key, value, d_out, doc_lengths):
    count = lax.axis_size("ctx")

    def holder(block):
        return block if block < count else 2 * count - 1 - block

    def move(array, pairs):
        return lax.ppermute(array, "ctx", pairs)

    near_on = [(holder(b), holder(b + 2)) for b in range(1, 2 * count - 2, 2)]
    far_on = [(holder(b), holder(b + 2)) for b in range(0, 2 * count - 2, 2)]
    near_to_far = [(holder(b), holder(b + 1)) for b in range(1, 2 * count - 2, 2)]
    swap = [(d, d ^ 1) for d in range(count)]
    near_back = [(t, s) for s, t in near_on]
    far_back = [(t, s) for s, t in far_on]

    near_kv, far_kv = pack_blocks(key, value)
    far_1 = move(near_kv, near_to_far)
    far_2 = move(far_kv, far_on)
    near_1 = move(far_kv, swap)
    prepared = prepare(count, doc_lengths, query, d_out, key, value)
    far_1, prepared = lax.optimization_barrier((far_1, prepared))
    near_2 = move(far_1, swap)

    *far_kept, far_g1, far_g2 = block_scores(0, count, prepared[0:4], far_1, far_2)
    from_far_2 = move(far_g2, far_back)
    relayed = move(far_g1, swap)
    *near_kept, near_g1, near_g2 = block_scores(1, count, prepared[4:8], near_1, near_2)
    near_sum = (near_g2.astype(jnp.float32) + relayed.astype(jnp.float32)).astype(jnp.bfloat16)
    from_near_2 = move(near_sum, near_back)
    near_g1, from_far_2 = lax.optimization_barrier((near_g1, from_far_2))
    from_near_1 = move(near_g1, swap)
    attended, grad_query, far_own, near_own = block_outputs(
        query,
        from_far_2,
        (prepared[0], far_1, far_2, *far_kept),
        (prepared[4], near_1, near_2, *near_kept),
    )
    grad_key, grad_value = total_grads(far_own, from_near_1, near_own, from_near_2)
    return (attended, grad_query, grad_key, grad_value)


def solution(mesh):
    rows = P(("dp", "ctx"), None)
    return jax.shard_map(
        body,
        mesh=mesh,
        in_specs=(rows, rows, rows, rows, P("dp")),
        out_specs=(rows, rows, rows, rows),
        check_vma=False,
    )
```

```python
import functools
import math

import jax
import jax.numpy as jnp
from jax import lax
from jax.experimental import pallas as pl
from jax.experimental.pallas import tpu as pltpu
from jax.sharding import PartitionSpec as P

HD = 128
TQ = 128
GROUP = 32

masked_score = -1e30
VMEM_LIMIT = 24 * 1024 * 1024
SCALE = 1.0 / math.sqrt(HD)
VMEM = pl.BlockSpec(memory_space=pltpu.VMEM)
HBM = pl.BlockSpec(memory_space=pltpu.HBM)
CHUNK = 128


def dot_nt(a, b):
    return lax.dot_general(a, b, (((1,), (1,)), ((), ())), preferred_element_type=jnp.float32)


def dot_nn(a, b):
    return lax.dot_general(a, b, (((1,), (0,)), ((), ())), preferred_element_type=jnp.float32)


def half_start(rows, slot):
    odd = lax.axis_index("ctx") % 2
    return pl.multiple_of((odd if slot == 0 else 1 - odd) * rows, rows)


def block_number(count, slot):
    device = lax.axis_index("ctx")
    in_lower = device % 2 == slot
    return jnp.where(in_lower, device, 2 * count - 1 - device)


def in_hbm(array):
    return pltpu.with_memory_space_constraint(array, pltpu.HBM)


def load_block(rows, slot, key, value, out, sems):
    place = pl.ds(half_start(rows, slot), rows)
    return [
        pltpu.make_async_copy(key.at[place], out.at[0:rows], sems.at[2 * slot]),
        pltpu.make_async_copy(value.at[place], out.at[rows : 2 * rows], sems.at[2 * slot + 1]),
    ]


def run_copies(copies):
    for copy in copies:
        copy.start()
    for copy in copies:
        copy.wait()


def pack_kernel(rows, key, value, near_out, far_out, sems):
    run_copies(
        load_block(rows, 1, key, value, near_out, sems)
        + load_block(rows, 0, key, value, far_out, sems)
    )


def pack_blocks(key, value):
    rows = key.shape[0] // 2
    shape = jax.ShapeDtypeStruct((2 * rows, HD), key.dtype)
    return pl.pallas_call(
        functools.partial(pack_kernel, rows),
        out_shape=(shape, shape),
        in_specs=[HBM] * 2,
        out_specs=[VMEM] * 2,
        scratch_shapes=[pltpu.SemaphoreType.DMA((4,))],
        name="pack_blocks",
    )(in_hbm(key), in_hbm(value))


def prepare_kernel(rows, heads, docs, count, *refs):
    (doc_hbm, query_hbm, dout_hbm, key, value) = refs[0:5]
    (doc_lengths, query, dout, sems) = refs[13:]
    refs = refs[5:13]
    wide = heads * TQ
    run_copies(
        [
            pltpu.make_async_copy(query_hbm, query, sems.at[4]),
            pltpu.make_async_copy(dout_hbm, dout, sems.at[5]),
            pltpu.make_async_copy(doc_hbm, doc_lengths, sems.at[6]),
        ]
        + load_block(rows, 0, key, value, refs[0], sems)
        + load_block(rows, 1, key, value, refs[4], sems)
    )
    for slot in (0, 1):
        _, query_t, dout_t, doc_start = refs[4 * slot : 4 * slot + 4]
        own_rows = half_start(rows, slot)
        for step in range(rows // TQ):
            source = pl.ds(own_rows + step * TQ, TQ)
            for h in range(heads):
                place = slice(step * wide + h * TQ, step * wide + (h + 1) * TQ)
                columns = slice(h * HD, (h + 1) * HD)
                query_t[:, place] = jnp.transpose(query[source, columns])
                dout_t[:, place] = jnp.transpose(dout[source, columns])
        at = (
            block_number(count, slot) * rows
            + lax.broadcasted_iota(jnp.int32, (8, TQ), 0) * TQ
            + lax.broadcasted_iota(jnp.int32, (8, TQ), 1)
        )

        def one(index, carry):
            start, found = carry
            found = jnp.where(at >= start, start, found)
            return (start + doc_lengths[index], found)

        _, found = lax.fori_loop(
            0, docs, one, (jnp.int32(0), jnp.zeros((8, TQ), jnp.int32)), unroll=8
        )
        doc_start[...] = found


def prepare(count, doc_lengths, query, dout, key, value):
    rows = query.shape[0] // 2
    heads = query.shape[1] // HD
    pair = jax.ShapeDtypeStruct((2 * rows, HD), key.dtype)
    stacked_t = jax.ShapeDtypeStruct((HD, rows * heads), query.dtype)
    starts = jax.ShapeDtypeStruct((8, TQ), jnp.int32)
    return pl.pallas_call(
        functools.partial(prepare_kernel, rows, heads, doc_lengths.shape[0], count),
        out_shape=(pair, stacked_t, stacked_t, starts) * 2,
        in_specs=[HBM] * 5,
        out_specs=[VMEM] * 8,
        scratch_shapes=[
            pltpu.SMEM(doc_lengths.shape, doc_lengths.dtype),
            pltpu.VMEM(query.shape, query.dtype),
            pltpu.VMEM(dout.shape, dout.dtype),
            pltpu.SemaphoreType.DMA((7,)),
        ],
        compiler_params=pltpu.CompilerParams(vmem_limit_bytes=VMEM_LIMIT),
        cost_estimate=pl.CostEstimate(flops=0, bytes_accessed=4 * 2**20, transcendentals=0),
        name="prepare",
    )(*(in_hbm(array) for array in (doc_lengths, query, dout, key, value)))


class Window:
    def __init__(self, rows, slot):
        self.tiles = rows // TQ
        self.chunks = 2 * self.tiles + 1
        self.steps = range(self.tiles)
        self.late = [(2 - slot) * self.tiles - step for step in self.steps]
        self.early = [self.chunks - late for late in self.late]
        self.prev = [2 * self.tiles - step for step in self.steps]
        self.own = [self.chunks - prev for prev in self.prev]


def chunk_rows(counts, step, first=0, count=None):
    start = sum(counts[:step]) + first
    count = counts[step] - first if count is None else count
    return slice(start * CHUNK, (start + count) * CHUNK)


def exponentials(jobs, rows, heads, block_pos, scores):
    back = 2 * rows
    wide = heads * TQ
    base2 = SCALE * math.log2(math.e)

    def score(job, index, row_max):
        step, chunks, (query_t, _, doc_start), _, _ = jobs[job]
        chunk, keys, row = chunks[index][0:3]
        low = doc_start[step : step + 1, :] - (block_pos(job) - back + step * TQ)
        high = lax.broadcasted_iota(jnp.int32, (1, TQ), 1) + back
        tile = slice(step * wide, (step + 1) * wide)
        product = dot_nn(keys[row : row + CHUNK, :], query_t[:, tile])
        for start in range(0, CHUNK, GROUP):
            place = chunk * CHUNK + start
            at = lax.broadcasted_iota(jnp.int32, (GROUP, TQ), 0) + place
            allowed = at >= low
            if place >= back:
                allowed = jnp.logical_and(allowed, at <= high)
            for h in range(heads):
                lanes = slice(h * TQ, (h + 1) * TQ)
                part = jnp.where(allowed, product[start : start + GROUP, lanes], masked_score)
                scores[job % 2, place : place + GROUP, lanes] = part
                for row8 in range(0, GROUP, 8):
                    row_max[h] = jnp.maximum(row_max[h], part[row8 : row8 + 8, :])

    def start_max():
        return [jnp.full((8, TQ), masked_score, jnp.float32)] * heads

    following = start_max()
    for index in range(len(jobs[0][1])):
        score(0, index, following)
    for job, (step, chunks, (_, dout_t, _), first_max, end) in enumerate(jobs):
        tile = slice(step * wide, (step + 1) * wide)
        row_max = jnp.concatenate(
            [jnp.max(part, axis=0, keepdims=True) * base2 for part in following], axis=1
        )
        if first_max is not None:
            row_max = jnp.maximum(row_max, first_max)
        following = start_max()
        ahead = len(jobs[job + 1][1]) if job + 1 < len(jobs) else 0
        done = 0
        total = jnp.zeros((8, wide), jnp.float32)
        delta = jnp.zeros((8, wide), jnp.float32)
        for index, (chunk, keys, row, weights, dprobs, kept) in enumerate(chunks):
            product = dot_nn(keys[rows + row : rows + row + CHUNK, :], dout_t[:, tile])
            for start in range(0, CHUNK, GROUP):
                place = chunk * CHUNK + start
                there = slice(kept.start + start, kept.start + start + GROUP)
                dprob = product[start : start + GROUP, :]
                dprobs[there, :] = dprob.astype(jnp.bfloat16)
                part = jnp.exp2(scores[job % 2, place : place + GROUP, :] * base2 - row_max)
                weights[there, :] = part.astype(jnp.bfloat16)
                term = part * dprob
                for row8 in range(0, GROUP, 8):
                    total = total + part[row8 : row8 + 8, :]
                    delta = delta + term[row8 : row8 + 8, :]
            while done * len(chunks) < ahead * (index + 1):
                score(job + 1, done, following)
                done += 1
        end(
            row_max,
            jnp.sum(total, axis=0, keepdims=True),
            jnp.sum(delta, axis=0, keepdims=True),
        )


def early_kernel(rows, heads, count, near_1, *refs):
    inputs, outs, scores = (refs[0:4], refs[4:8]), (refs[8:11], refs[11:14]), refs[14]
    jobs = []
    for slot in (0, 1):
        window = Window(rows, slot)
        own_kv, query_t, dout_t, doc_start = inputs[slot]
        weights, dprobs, stats = outs[slot]
        for step in window.steps:
            chunks = []
            for index in range(window.early[step]):
                chunk = window.late[step] + index
                row = step * TQ + chunk * CHUNK
                keys = own_kv if row >= 2 * rows else near_1
                kept = chunk_rows(window.early, step, index, 1)
                chunks.append((chunk, keys, row % rows, weights, dprobs, kept))

            def end(*found, stats=stats, step=step):
                for kind, value in enumerate(found):
                    stats[8 * kind + step : 8 * kind + step + 1, :] = value

            jobs.append((step, chunks, (query_t, dout_t, doc_start), None, end))
    tiles = rows // TQ
    positions = [block_number(count, slot) * rows for slot in (0, 1)]
    exponentials(jobs, rows, heads, lambda job: positions[job // tiles], scores)


def early_scores(count, prepared, near_1):
    rows = near_1.shape[0] // 2
    heads = prepared[1].shape[1] // rows
    wide = heads * TQ
    out_shape = []
    for slot in (0, 1):
        kept = (sum(Window(rows, slot).early) * CHUNK, wide)
        out_shape += [jax.ShapeDtypeStruct(kept, jnp.bfloat16)] * 2
        out_shape.append(jax.ShapeDtypeStruct((24, wide), jnp.float32))
    return pl.pallas_call(
        functools.partial(early_kernel, rows, heads, count),
        out_shape=out_shape,
        in_specs=[VMEM] * 9,
        out_specs=[VMEM] * 6,
        scratch_shapes=[pltpu.VMEM((2, 2 * rows + TQ, wide), jnp.float32)],
        compiler_params=pltpu.CompilerParams(vmem_limit_bytes=VMEM_LIMIT),
        cost_estimate=pl.CostEstimate(flops=2**31, bytes_accessed=0, transcendentals=0),
        name="early_scores",
    )(near_1, *prepared)


def scaled_by(array, tile, factor):
    return (array[:, tile].astype(jnp.float32) * factor).astype(jnp.bfloat16)


def dscore_rows(dscores, there, weights, dprobs, kept, delta):
    delta = jnp.broadcast_to(delta, (16, delta.shape[1]))
    for start in range(0, there.stop - there.start, 16):
        out = slice(there.start + start, there.start + start + 16)
        place = slice(kept.start + start, kept.start + start + 16)
        dscores[out, :] = weights[place, :] * (dprobs[place, :] - delta)


def scores_kernel(
    rows,
    heads,
    count,
    slot,
    own_kv,
    query_t,
    dout_t,
    doc_start,
    early_w,
    early_dprobs,
    early_stats,
    prev1,
    prev2,
    late_w,
    dscores,
    stats,
    prev1_out,
    prev2_out,
    scores,
    late_dprobs,
    dk,
    dv,
):
    back = 2 * rows
    wide = heads * TQ
    window = Window(rows, slot)
    position = block_number(count, slot) * rows
    jobs = []
    for step in window.steps:
        chunks = []
        for chunk in range(window.late[step]):
            row = step * TQ + chunk * CHUNK
            keys = (prev2, prev1)[row // rows]
            kept = chunk_rows(window.late, step, chunk, 1)
            chunks.append((chunk, keys, row % rows, late_w, late_dprobs, kept))

        def end(row_max, total, delta, step=step):
            tile = slice(step * wide, (step + 1) * wide)
            early = [early_stats[8 * kind + step : 8 * kind + step + 1, :] for kind in range(3)]
            shrink = jnp.exp2(early[0] - row_max)
            late_factor = 1.0 / (total + early[1] * shrink)
            early_factor = late_factor * shrink
            delta = delta * late_factor + early[2] * early_factor
            for kind, value in enumerate((late_factor, early_factor, delta)):
                stats[8 * kind + step : 8 * kind + step + 1, :] = value
            delta = delta.astype(jnp.bfloat16)
            first = step * TQ
            late = window.late[step]
            parts = [(0, late, late_w, late_dprobs, chunk_rows(window.late, step), late_factor)]
            if window.prev[step] > late:
                beyond = window.prev[step] - late
                kept = chunk_rows(window.early, step, 0, beyond)
                parts.append((late, beyond, early_w, early_dprobs, kept, early_factor))
            for start, length, weights, dprobs, kept, factor in parts:
                there = chunk_rows(window.prev, step, start, length)
                dscore_rows(dscores, there, weights, dprobs, kept, delta)
                columns = slice(first + start * CHUNK, first + (start + length) * CHUNK)
                for total_ref, terms, at, side in (
                    (dv, weights, kept, dout_t),
                    (dk, dscores, there, query_t),
                ):
                    term = dot_nt(scaled_by(side, tile, factor), terms[at, :])
                    if step == 0:
                        total_ref[:, columns] = term
                    else:
                        total_ref[:, columns] += term

        first_max = early_stats[step : step + 1, :]
        jobs.append((step, chunks, (query_t, dout_t, doc_start), first_max, end))
    exponentials(jobs, rows, heads, lambda job: position, scores)
    for out, place in ((prev2_out, slice(0, rows)), (prev1_out, slice(rows, back))):
        out[0:HD] = (dk[:, place] * SCALE).astype(out.dtype)
        out[HD : 2 * HD] = dv[:, place].astype(out.dtype)


def block_scores(slot, count, prepared, early, prev1, prev2):
    rows = prev1.shape[0] // 2
    heads = prepared[1].shape[1] // rows
    wide = heads * TQ
    window = Window(rows, slot)
    late = (sum(window.late) * CHUNK, wide)
    pair = jax.ShapeDtypeStruct((2 * HD, rows), jnp.bfloat16)
    return pl.pallas_call(
        functools.partial(scores_kernel, rows, heads, count, slot),
        out_shape=(
            jax.ShapeDtypeStruct(late, jnp.bfloat16),
            jax.ShapeDtypeStruct((sum(window.prev) * CHUNK, wide), jnp.bfloat16),
            jax.ShapeDtypeStruct((24, wide), jnp.float32),
            pair,
            pair,
        ),
        in_specs=[VMEM] * 9,
        out_specs=[VMEM] * 5,
        scratch_shapes=[
            pltpu.VMEM((2, 2 * rows + TQ, wide), jnp.float32),
            pltpu.VMEM(late, jnp.bfloat16),
            pltpu.VMEM((HD, 2 * rows), jnp.float32),
            pltpu.VMEM((HD, 2 * rows), jnp.float32),
        ],
        compiler_params=pltpu.CompilerParams(vmem_limit_bytes=VMEM_LIMIT),
        cost_estimate=pl.CostEstimate(flops=2**32, bytes_accessed=0, transcendentals=0),
        name="scores_far" if slot == 0 else "scores_near",
    )(*prepared, *early, prev1, prev2)


def outputs_kernel(rows, heads, from_far_2, *refs):
    blocks = (refs[0:10], refs[10:20])
    (attended, grad_query, far_own, near_own, keys_t, values_t, own_dscores) = refs[20:]
    wide = heads * TQ
    for slot, block in enumerate(blocks):
        (own_kv, query_t, dout_t, early_w, early_dprobs, prev1, prev2) = block[0:7]
        (late_w, dscores, stats) = block[7:10]
        window = Window(rows, slot)
        own_out = (far_own, near_own)[slot]
        own_rows = half_start(rows, slot)
        for place, source in enumerate((prev2, prev1, own_kv)):
            for tile in range(rows // TQ):
                part = slice(place * rows + tile * TQ, place * rows + (tile + 1) * TQ)
                row = tile * TQ
                keys_t[:, part] = jnp.transpose(source[row : row + TQ, :])
                values_t[:, part] = jnp.transpose(source[rows + row : rows + row + TQ, :])
        for step in reversed(window.steps):
            first = step * TQ
            tile = slice(step * wide, (step + 1) * wide)
            late_factor, early_factor, delta = (
                stats[8 * kind + step : 8 * kind + step + 1, :] for kind in range(3)
            )
            late, prev, own = window.late[step], window.prev[step], window.own[step]
            own_w = chunk_rows(window.early, step, prev - late, own)
            own_d = chunk_rows(window.own, step)
            dscore_rows(
                own_dscores, own_d, early_w, early_dprobs, own_w, delta.astype(jnp.bfloat16)
            )
            for offset, terms, at, side, factor in (
                (0, own_dscores, own_d, query_t, SCALE),
                (HD, early_w, own_w, dout_t, 1.0),
            ):
                term = dot_nt(scaled_by(side, tile, early_factor), terms[at, :]) * factor
                side_rows = slice(offset, offset + HD)
                place = slice(0, first + TQ)
                if step < rows // TQ - 1:
                    own_out[side_rows, place] += term
                elif slot == 0:
                    own_out[side_rows, place] = term + from_far_2[side_rows, place].astype(
                        jnp.float32
                    )
                else:
                    own_out[side_rows, place] = term

            def columns(start, length):
                return slice(first + start * CHUNK, first + (start + length) * CHUNK)

            attended_t = (
                dot_nn(values_t[:, columns(0, late)], late_w[chunk_rows(window.late, step), :])
                * late_factor
                + dot_nn(
                    values_t[:, columns(late, window.early[step])],
                    early_w[chunk_rows(window.early, step), :],
                )
                * early_factor
            )
            late_rows = chunk_rows(window.prev, step, 0, late)
            early_t = dot_nn(keys_t[:, columns(prev, own)], own_dscores[own_d, :])
            if prev > late:
                early_t += dot_nn(
                    keys_t[:, columns(late, prev - late)],
                    dscores[chunk_rows(window.prev, step, late, prev - late), :],
                )
            grad_query_t = dot_nn(keys_t[:, columns(0, late)], dscores[late_rows, :]) * (
                late_factor * SCALE
            ) + early_t * (early_factor * SCALE)
            place = pl.ds(own_rows + first, TQ)
            for h in range(heads):
                part = slice(h * TQ, (h + 1) * TQ)
                head = slice(h * HD, (h + 1) * HD)
                attended[place, head] = jnp.transpose(attended_t[:, part]).astype(attended.dtype)
                grad_query[place, head] = jnp.transpose(grad_query_t[:, part]).astype(
                    grad_query.dtype
                )


def block_outputs(query, from_far_2, far, near):
    rows = query.shape[0] // 2
    heads = query.shape[1] // HD
    shape = jax.ShapeDtypeStruct(query.shape, query.dtype)
    own = jax.ShapeDtypeStruct((2 * HD, rows), jnp.float32)
    return pl.pallas_call(
        functools.partial(outputs_kernel, rows, heads),
        out_shape=(shape, shape, own, own),
        in_specs=[VMEM] * 21,
        out_specs=[VMEM] * 4,
        scratch_shapes=[
            pltpu.VMEM((HD, 3 * rows), jnp.bfloat16),
            pltpu.VMEM((HD, 3 * rows), jnp.bfloat16),
            pltpu.VMEM((sum(Window(rows, 0).own) * CHUNK, heads * TQ), jnp.bfloat16),
        ],
        compiler_params=pltpu.CompilerParams(vmem_limit_bytes=VMEM_LIMIT),
        cost_estimate=pl.CostEstimate(flops=0, bytes_accessed=0, transcendentals=0),
        name="block_outputs",
    )(from_far_2, *far, *near)


def total_kernel(rows, far_own, far_1, near_own, near_1, grad_key, grad_value):
    far = far_own[...] + far_1[...].astype(jnp.float32)
    near = near_own[...] + near_1[...].astype(jnp.float32)
    for slot, total in ((0, far), (1, near)):
        place = pl.ds(half_start(rows, slot), rows)
        grad_key[place, :] = jnp.transpose(total[0:HD]).astype(grad_key.dtype)
        grad_value[place, :] = jnp.transpose(total[HD : 2 * HD]).astype(grad_value.dtype)


def total_grads(far_own, far_1, near_own, near_1):
    rows = far_own.shape[1]
    shape = jax.ShapeDtypeStruct((2 * rows, HD), jnp.bfloat16)
    return pl.pallas_call(
        functools.partial(total_kernel, rows),
        out_shape=(shape, shape),
        in_specs=[VMEM] * 4,
        out_specs=[VMEM] * 2,
        compiler_params=pltpu.CompilerParams(vmem_limit_bytes=VMEM_LIMIT),
        name="total_grads",
    )(far_own, far_1, near_own, near_1)


def body(query, key, value, d_out, doc_lengths):
    count = lax.axis_size("ctx")

    def holder(block):
        return block if block < count else 2 * count - 1 - block

    def move(array, pairs):
        return lax.ppermute(array, "ctx", pairs)

    near_on = [(holder(b), holder(b + 2)) for b in range(1, 2 * count - 2, 2)]
    far_on = [(holder(b), holder(b + 2)) for b in range(0, 2 * count - 2, 2)]
    near_to_far = [(holder(b), holder(b + 1)) for b in range(1, 2 * count - 2, 2)]
    swap = [(d, d ^ 1) for d in range(count)]
    near_back = [(t, s) for s, t in near_on]
    far_back = [(t, s) for s, t in far_on]

    near_kv, far_kv = pack_blocks(key, value)
    far_1 = move(near_kv, near_to_far)
    far_2 = move(far_kv, far_on)
    near_1 = move(far_kv, swap)
    prepared = prepare(count, doc_lengths, query, d_out, key, value)
    far_ready, near_ready = prepared[0:4], prepared[4:8]
    early = early_scores(count, prepared, near_1)
    far_early, near_early = early[0:3], early[3:6]
    far_1, far_early, near_early = lax.optimization_barrier((far_1, far_early, near_early))
    near_2 = move(far_1, swap)

    far_w, far_d, far_stats, far_g1, far_g2 = block_scores(
        0, count, far_ready, far_early, far_1, far_2
    )
    from_far_2 = move(far_g2, far_back)
    relayed = move(far_g1, swap)
    near_w, near_d, near_stats, near_g1, near_g2 = block_scores(
        1, count, near_ready, near_early, near_1, near_2
    )
    near_sum = (near_g2.astype(jnp.float32) + relayed.astype(jnp.float32)).astype(jnp.bfloat16)
    from_near_2 = move(near_sum, near_back)
    near_g1, from_far_2 = lax.optimization_barrier((near_g1, from_far_2))
    from_near_1 = move(near_g1, swap)
    attended, grad_query, far_own, near_own = block_outputs(
        query,
        from_far_2,
        (*far_ready[0:3], *far_early[0:2], far_1, far_2, far_w, far_d, far_stats),
        (*near_ready[0:3], *near_early[0:2], near_1, near_2, near_w, near_d, near_stats),
    )
    grad_key, grad_value = total_grads(far_own, from_near_1, near_own, from_near_2)
    return (attended, grad_query, grad_key, grad_value)


def solution(mesh):
    rows = P(("dp", "ctx"), None)
    return jax.shard_map(
        body,
        mesh=mesh,
        in_specs=(rows, rows, rows, rows, P("dp")),
        out_specs=(rows, rows, rows, rows),
        check_vma=False,
    )
```

```python
import functools
import math

import jax
import jax.numpy as jnp
from jax import lax
from jax.experimental import pallas as pl
from jax.experimental.pallas import tpu as pltpu
from jax.sharding import PartitionSpec as P

HD = 128
TQ = 128
GROUP = 32

masked_score = -1e30
VMEM_LIMIT = 24 * 1024 * 1024
SCALE = 1.0 / math.sqrt(HD)
VMEM = pl.BlockSpec(memory_space=pltpu.VMEM)
HBM = pl.BlockSpec(memory_space=pltpu.HBM)
CHUNK = 128


def dot_nt(a, b):
    return lax.dot_general(a, b, (((1,), (1,)), ((), ())), preferred_element_type=jnp.float32)


def dot_nn(a, b):
    return lax.dot_general(a, b, (((1,), (0,)), ((), ())), preferred_element_type=jnp.float32)


def half_start(rows, slot):
    odd = lax.axis_index("ctx") % 2
    return pl.multiple_of((odd if slot == 0 else 1 - odd) * rows, rows)


def block_number(count, slot):
    device = lax.axis_index("ctx")
    in_lower = device % 2 == slot
    return jnp.where(in_lower, device, 2 * count - 1 - device)


def in_hbm(array):
    return pltpu.with_memory_space_constraint(array, pltpu.HBM)


def load_block(rows, slot, key, value, out, sems):
    place = pl.ds(half_start(rows, slot), rows)
    return [
        pltpu.make_async_copy(key.at[place], out.at[0:rows], sems.at[2 * slot]),
        pltpu.make_async_copy(value.at[place], out.at[rows : 2 * rows], sems.at[2 * slot + 1]),
    ]


def run_copies(copies):
    for copy in copies:
        copy.start()
    for copy in copies:
        copy.wait()


def pack_kernel(rows, key, value, near_out, far_out, sems):
    run_copies(
        load_block(rows, 1, key, value, near_out, sems)
        + load_block(rows, 0, key, value, far_out, sems)
    )


def pack_blocks(key, value):
    rows = key.shape[0] // 2
    shape = jax.ShapeDtypeStruct((2 * rows, HD), key.dtype)
    return pl.pallas_call(
        functools.partial(pack_kernel, rows),
        out_shape=(shape, shape),
        in_specs=[HBM] * 2,
        out_specs=[VMEM] * 2,
        scratch_shapes=[pltpu.SemaphoreType.DMA((4,))],
        name="pack_blocks",
    )(in_hbm(key), in_hbm(value))


def prepare_kernel(rows, heads, docs, count, *refs):
    (doc_hbm, query_hbm, dout_hbm, key, value) = refs[0:5]
    (doc_lengths, query, dout, sems) = refs[13:]
    refs = refs[5:13]
    wide = heads * TQ
    run_copies(
        [
            pltpu.make_async_copy(query_hbm, query, sems.at[4]),
            pltpu.make_async_copy(dout_hbm, dout, sems.at[5]),
            pltpu.make_async_copy(doc_hbm, doc_lengths, sems.at[6]),
        ]
        + load_block(rows, 0, key, value, refs[0], sems)
        + load_block(rows, 1, key, value, refs[4], sems)
    )
    for slot in (0, 1):
        _, query_t, dout_t, doc_start = refs[4 * slot : 4 * slot + 4]
        own_rows = half_start(rows, slot)
        for step in range(rows // TQ):
            source = pl.ds(own_rows + step * TQ, TQ)
            for h in range(heads):
                place = slice(step * wide + h * TQ, step * wide + (h + 1) * TQ)
                columns = slice(h * HD, (h + 1) * HD)
                query_t[:, place] = jnp.transpose(query[source, columns])
                dout_t[:, place] = jnp.transpose(dout[source, columns])
        at = (
            block_number(count, slot) * rows
            + lax.broadcasted_iota(jnp.int32, (8, TQ), 0) * TQ
            + lax.broadcasted_iota(jnp.int32, (8, TQ), 1)
        )

        def one(index, carry):
            start, found = carry
            found = jnp.where(at >= start, start, found)
            return (start + doc_lengths[index], found)

        _, found = lax.fori_loop(
            0, docs, one, (jnp.int32(0), jnp.zeros((8, TQ), jnp.int32)), unroll=8
        )
        doc_start[...] = found


def prepare(count, doc_lengths, query, dout, key, value):
    rows = query.shape[0] // 2
    heads = query.shape[1] // HD
    pair = jax.ShapeDtypeStruct((2 * rows, HD), key.dtype)
    stacked_t = jax.ShapeDtypeStruct((HD, rows * heads), query.dtype)
    starts = jax.ShapeDtypeStruct((8, TQ), jnp.int32)
    return pl.pallas_call(
        functools.partial(prepare_kernel, rows, heads, doc_lengths.shape[0], count),
        out_shape=(pair, stacked_t, stacked_t, starts) * 2,
        in_specs=[HBM] * 5,
        out_specs=[VMEM] * 8,
        scratch_shapes=[
            pltpu.SMEM(doc_lengths.shape, doc_lengths.dtype),
            pltpu.VMEM(query.shape, query.dtype),
            pltpu.VMEM(dout.shape, dout.dtype),
            pltpu.SemaphoreType.DMA((7,)),
        ],
        compiler_params=pltpu.CompilerParams(vmem_limit_bytes=VMEM_LIMIT),
        cost_estimate=pl.CostEstimate(flops=0, bytes_accessed=4 * 2**20, transcendentals=0),
        name="prepare",
    )(*(in_hbm(array) for array in (doc_lengths, query, dout, key, value)))


class Window:
    def __init__(self, rows):
        self.tiles = rows // TQ
        self.chunks = 2 * self.tiles + 1
        self.steps = range(self.tiles)
        self.late = [self.tiles - step for step in self.steps]
        self.early = [self.chunks - late for late in self.late]


def chunk_rows(counts, step, first=0, count=None):
    start = sum(counts[:step]) + first
    count = counts[step] - first if count is None else count
    return slice(start * CHUNK, (start + count) * CHUNK)


def exponentials(jobs, rows, heads, block_pos, scores):
    back = 2 * rows
    wide = heads * TQ
    base2 = SCALE * math.log2(math.e)

    def score(job, index, row_max):
        step, chunks, (query_t, _, doc_start), _, _ = jobs[job]
        chunk, keys, row = chunks[index][0:3]
        low = doc_start[step : step + 1, :] - (block_pos - back + step * TQ)
        high = lax.broadcasted_iota(jnp.int32, (1, TQ), 1) + back
        tile = slice(step * wide, (step + 1) * wide)
        product = dot_nn(keys[row : row + CHUNK, :], query_t[:, tile])
        for start in range(0, CHUNK, GROUP):
            place = chunk * CHUNK + start
            at = lax.broadcasted_iota(jnp.int32, (GROUP, TQ), 0) + place
            allowed = at >= low
            if place >= back:
                allowed = jnp.logical_and(allowed, at <= high)
            for h in range(heads):
                lanes = slice(h * TQ, (h + 1) * TQ)
                part = jnp.where(allowed, product[start : start + GROUP, lanes], masked_score)
                scores[job % 2, place : place + GROUP, lanes] = part
                for row8 in range(0, GROUP, 8):
                    row_max[h] = jnp.maximum(row_max[h], part[row8 : row8 + 8, :])

    def start_max():
        return [jnp.full((8, TQ), masked_score, jnp.float32)] * heads

    following = start_max()
    for index in range(len(jobs[0][1])):
        score(0, index, following)
    for job, (step, chunks, (_, dout_t, _), first_max, end) in enumerate(jobs):
        tile = slice(step * wide, (step + 1) * wide)
        row_max = jnp.concatenate(
            [jnp.max(part, axis=0, keepdims=True) * base2 for part in following], axis=1
        )
        if first_max is not None:
            row_max = jnp.maximum(row_max, first_max)
        following = start_max()
        ahead = len(jobs[job + 1][1]) if job + 1 < len(jobs) else 0
        done = 0
        total = jnp.zeros((8, wide), jnp.float32)
        delta = jnp.zeros((8, wide), jnp.float32)
        for index, (chunk, keys, row, weights, dprobs, kept) in enumerate(chunks):
            product = dot_nn(keys[rows + row : rows + row + CHUNK, :], dout_t[:, tile])
            for start in range(0, CHUNK, GROUP):
                place = chunk * CHUNK + start
                there = slice(kept.start + start, kept.start + start + GROUP)
                dprob = product[start : start + GROUP, :]
                dprobs[there, :] = dprob.astype(jnp.bfloat16)
                part = jnp.exp2(scores[job % 2, place : place + GROUP, :] * base2 - row_max)
                weights[there, :] = part.astype(jnp.bfloat16)
                term = part * dprob
                for row8 in range(0, GROUP, 8):
                    total = total + part[row8 : row8 + 8, :]
                    delta = delta + term[row8 : row8 + 8, :]
            while done * len(chunks) < ahead * (index + 1):
                score(job + 1, done, following)
                done += 1
        end(
            row_max,
            jnp.sum(total, axis=0, keepdims=True),
            jnp.sum(delta, axis=0, keepdims=True),
        )


def early_kernel(
    rows,
    heads,
    count,
    slot,
    own_kv,
    query_t,
    dout_t,
    doc_start,
    prev1,
    weights,
    dprobs,
    stats,
    scores,
):
    window = Window(rows)
    position = block_number(count, slot) * rows
    jobs = []
    for step in window.steps:
        chunks = []
        for index in range(window.early[step]):
            chunk = window.late[step] + index
            row = step * TQ + chunk * CHUNK
            keys = own_kv if row >= 2 * rows else prev1
            kept = chunk_rows(window.early, step, index, 1)
            chunks.append((chunk, keys, row % rows, weights, dprobs, kept))

        def end(*found, step=step):
            for kind, value in enumerate(found):
                stats[8 * kind + step : 8 * kind + step + 1, :] = value

        jobs.append((step, chunks, (query_t, dout_t, doc_start), None, end))
    exponentials(jobs, rows, heads, position, scores)


def early_scores(slot, count, ready, prev1):
    rows = prev1.shape[0] // 2
    heads = ready[1].shape[1] // rows
    wide = heads * TQ
    kept = jax.ShapeDtypeStruct((sum(Window(rows).early) * CHUNK, wide), jnp.bfloat16)
    return pl.pallas_call(
        functools.partial(early_kernel, rows, heads, count, slot),
        out_shape=(kept, kept, jax.ShapeDtypeStruct((24, wide), jnp.float32)),
        in_specs=[VMEM] * 5,
        out_specs=[VMEM] * 3,
        scratch_shapes=[pltpu.VMEM((2, 2 * rows + TQ, wide), jnp.float32)],
        compiler_params=pltpu.CompilerParams(vmem_limit_bytes=VMEM_LIMIT),
        cost_estimate=pl.CostEstimate(flops=0, bytes_accessed=0, transcendentals=0),
        name="early_far" if slot == 0 else "early_near",
    )(*ready, prev1)


def scaled_by(array, tile, factor):
    return (array[:, tile].astype(jnp.float32) * factor).astype(jnp.bfloat16)


def dscore_rows(dscores, there, weights, dprobs, kept, delta):
    delta = jnp.broadcast_to(delta, (16, delta.shape[1]))
    for start in range(0, there.stop - there.start, 16):
        out = slice(there.start + start, there.start + start + 16)
        place = slice(kept.start + start, kept.start + start + 16)
        dscores[out, :] = weights[place, :] * (dprobs[place, :] - delta)


def add_products(step, columns, products):
    for total_ref, side, terms in products:
        term = dot_nt(side, terms)
        if step == 0:
            total_ref[:, columns] = term
        else:
            total_ref[:, columns] += term


def late_kernel(
    rows,
    heads,
    count,
    slot,
    query_t,
    dout_t,
    doc_start,
    early_stats,
    prev2,
    weights,
    dscores,
    stats,
    prev2_out,
    scores,
    dprobs,
    dk,
    dv,
):
    wide = heads * TQ
    window = Window(rows)
    jobs = []
    for step in window.steps:
        chunks = []
        for chunk in range(window.late[step]):
            kept = chunk_rows(window.late, step, chunk, 1)
            chunks.append((chunk, prev2, step * TQ + chunk * CHUNK, weights, dprobs, kept))

        def end(row_max, total, delta, step=step):
            tile = slice(step * wide, (step + 1) * wide)
            early = [early_stats[8 * kind + step : 8 * kind + step + 1, :] for kind in range(3)]
            shrink = jnp.exp2(early[0] - row_max)
            late_factor = 1.0 / (total + early[1] * shrink)
            early_factor = late_factor * shrink
            delta = delta * late_factor + early[2] * early_factor
            for kind, value in enumerate((late_factor, early_factor, delta)):
                stats[8 * kind + step : 8 * kind + step + 1, :] = value
            there = chunk_rows(window.late, step)
            dscore_rows(dscores, there, weights, dprobs, there, delta.astype(jnp.bfloat16))
            add_products(
                step,
                slice(step * TQ, rows),
                (
                    (dv, scaled_by(dout_t, tile, late_factor), weights[there, :]),
                    (dk, scaled_by(query_t, tile, late_factor), dscores[there, :]),
                ),
            )

        first_max = early_stats[step : step + 1, :]
        jobs.append((step, chunks, (query_t, dout_t, doc_start), first_max, end))
    exponentials(jobs, rows, heads, block_number(count, slot) * rows, scores)
    prev2_out[0:HD] = (dk[...] * SCALE).astype(prev2_out.dtype)
    prev2_out[HD : 2 * HD] = dv[...].astype(prev2_out.dtype)


def late_scores(slot, count, ready, early, prev2):
    rows = prev2.shape[0] // 2
    heads = ready[1].shape[1] // rows
    wide = heads * TQ
    late = (sum(Window(rows).late) * CHUNK, wide)
    return pl.pallas_call(
        functools.partial(late_kernel, rows, heads, count, slot),
        out_shape=(
            jax.ShapeDtypeStruct(late, jnp.bfloat16),
            jax.ShapeDtypeStruct(late, jnp.bfloat16),
            jax.ShapeDtypeStruct((24, wide), jnp.float32),
            jax.ShapeDtypeStruct((2 * HD, rows), jnp.bfloat16),
        ),
        in_specs=[VMEM] * 5,
        out_specs=[VMEM] * 4,
        scratch_shapes=[
            pltpu.VMEM((2, rows, wide), jnp.float32),
            pltpu.VMEM(late, jnp.bfloat16),
            pltpu.VMEM((HD, rows), jnp.float32),
            pltpu.VMEM((HD, rows), jnp.float32),
        ],
        compiler_params=pltpu.CompilerParams(vmem_limit_bytes=VMEM_LIMIT),
        cost_estimate=pl.CostEstimate(flops=2**31, bytes_accessed=0, transcendentals=0),
        name="late_far" if slot == 0 else "late_near",
    )(*ready[1:4], early[2], prev2)


def grads_kernel(
    rows, heads, query_t, dout_t, weights, dprobs, stats, dscores, prev1_out, own_out, dk, dv
):
    wide = heads * TQ
    window = Window(rows)
    for step in reversed(window.steps):
        tile = slice(step * wide, (step + 1) * wide)
        factor = stats[8 + step : 8 + step + 1, :]
        delta = stats[16 + step : 16 + step + 1, :].astype(jnp.bfloat16)
        there = chunk_rows(window.early, step)
        dscore_rows(dscores, there, weights, dprobs, there, delta)
        add_products(
            window.tiles - 1 - step,
            slice(0, window.early[step] * CHUNK),
            (
                (dv, scaled_by(dout_t, tile, factor), weights[there, :]),
                (dk, scaled_by(query_t, tile, factor), dscores[there, :]),
            ),
        )
    prev1_out[0:HD] = (dk[:, 0:rows] * SCALE).astype(prev1_out.dtype)
    prev1_out[HD : 2 * HD] = dv[:, 0:rows].astype(prev1_out.dtype)
    own_out[0:HD] = dk[:, rows : 2 * rows] * SCALE
    own_out[HD : 2 * HD] = dv[:, rows : 2 * rows]


def early_grads(slot, ready, early, stats):
    rows = ready[0].shape[0] // 2
    heads = ready[1].shape[1] // rows
    return pl.pallas_call(
        functools.partial(grads_kernel, rows, heads),
        out_shape=(
            jax.ShapeDtypeStruct(early[0].shape, jnp.bfloat16),
            jax.ShapeDtypeStruct((2 * HD, rows), jnp.bfloat16),
            jax.ShapeDtypeStruct((2 * HD, rows), jnp.float32),
        ),
        in_specs=[VMEM] * 5,
        out_specs=[VMEM] * 3,
        scratch_shapes=[pltpu.VMEM((HD, 2 * rows), jnp.float32)] * 2,
        compiler_params=pltpu.CompilerParams(vmem_limit_bytes=VMEM_LIMIT),
        cost_estimate=pl.CostEstimate(flops=2**31, bytes_accessed=0, transcendentals=0),
        name="grads_far" if slot == 0 else "grads_near",
    )(*ready[1:3], *early[0:2], stats)


def outputs_kernel(rows, heads, *refs):
    blocks = (refs[0:8], refs[8:16])
    (attended, grad_query, keys_t, values_t) = refs[16:]
    window = Window(rows)
    for slot, block in enumerate(blocks):
        (own_kv, prev1, prev2, early_w, early_d, late_w, late_d, stats) = block
        own_rows = half_start(rows, slot)
        for place, source in enumerate((prev2, prev1, own_kv)):
            for tile in range(rows // TQ):
                part = slice(place * rows + tile * TQ, place * rows + (tile + 1) * TQ)
                row = tile * TQ
                keys_t[:, part] = jnp.transpose(source[row : row + TQ, :])
                values_t[:, part] = jnp.transpose(source[rows + row : rows + row + TQ, :])
        for step in window.steps:
            late_columns = slice(step * TQ, rows)
            early_columns = slice(rows, 2 * rows + (step + 1) * TQ)
            late_rows = chunk_rows(window.late, step)
            early_rows = chunk_rows(window.early, step)
            place = pl.ds(own_rows + step * TQ, TQ)
            for out, side, late, early, scale in (
                (attended, values_t, late_w, early_w, 1.0),
                (grad_query, keys_t, late_d, early_d, SCALE),
            ):
                found = dot_nn(side[:, late_columns], late[late_rows, :]) * (
                    stats[step : step + 1, :] * scale
                ) + dot_nn(side[:, early_columns], early[early_rows, :]) * (
                    stats[8 + step : 8 + step + 1, :] * scale
                )
                for h in range(heads):
                    part = found[:, h * TQ : (h + 1) * TQ]
                    out[place, h * HD : (h + 1) * HD] = jnp.transpose(part).astype(out.dtype)


def block_outputs(query, far, near):
    rows = query.shape[0] // 2
    heads = query.shape[1] // HD
    shape = jax.ShapeDtypeStruct(query.shape, query.dtype)
    return pl.pallas_call(
        functools.partial(outputs_kernel, rows, heads),
        out_shape=(shape, shape),
        in_specs=[VMEM] * 16,
        out_specs=[VMEM] * 2,
        scratch_shapes=[pltpu.VMEM((HD, 3 * rows), jnp.bfloat16)] * 2,
        compiler_params=pltpu.CompilerParams(vmem_limit_bytes=VMEM_LIMIT),
        cost_estimate=pl.CostEstimate(flops=2**30, bytes_accessed=0, transcendentals=0),
        name="block_outputs",
    )(*far, *near)


def total_kernel(rows, far_own, far_1, far_2, near_own, near_1, grad_key, grad_value):
    far = far_own[...] + far_1[...].astype(jnp.float32) + far_2[...].astype(jnp.float32)
    near = near_own[...] + near_1[...].astype(jnp.float32)
    for slot, total in ((0, far), (1, near)):
        place = pl.ds(half_start(rows, slot), rows)
        grad_key[place, :] = jnp.transpose(total[0:HD]).astype(grad_key.dtype)
        grad_value[place, :] = jnp.transpose(total[HD : 2 * HD]).astype(grad_value.dtype)


def total_grads(*parts):
    rows = parts[0].shape[1]
    shape = jax.ShapeDtypeStruct((2 * rows, HD), jnp.bfloat16)
    return pl.pallas_call(
        functools.partial(total_kernel, rows),
        out_shape=(shape, shape),
        in_specs=[VMEM] * 5,
        out_specs=[VMEM] * 2,
        compiler_params=pltpu.CompilerParams(vmem_limit_bytes=VMEM_LIMIT),
        name="total_grads",
    )(*parts)


def body(query, key, value, d_out, doc_lengths):
    count = lax.axis_size("ctx")

    def holder(block):
        return block if block < count else 2 * count - 1 - block

    def move(array, pairs):
        return lax.ppermute(array, "ctx", pairs)

    near_on = [(holder(b), holder(b + 2)) for b in range(1, 2 * count - 2, 2)]
    far_on = [(holder(b), holder(b + 2)) for b in range(0, 2 * count - 2, 2)]
    near_to_far = [(holder(b), holder(b + 1)) for b in range(1, 2 * count - 2, 2)]
    swap = [(d, d ^ 1) for d in range(count)]
    near_back = [(t, s) for s, t in near_on]
    far_back = [(t, s) for s, t in far_on]

    near_kv, far_kv = pack_blocks(key, value)
    far_1 = move(near_kv, near_to_far)
    near_1 = move(far_kv, swap)
    far_2 = move(far_kv, far_on)
    prepared = prepare(count, doc_lengths, query, d_out, key, value)
    far_ready, near_ready = prepared[0:4], prepared[4:8]
    near_early = early_scores(1, count, near_ready, near_1)
    far_1, near_early = lax.optimization_barrier((far_1, near_early))
    near_2 = move(far_1, swap)
    far_early = early_scores(0, count, far_ready, far_1)

    far_w, far_d, far_stats, far_g2 = late_scores(0, count, far_ready, far_early, far_2)
    from_far_2 = move(far_g2, far_back)
    far_early_d, far_g1, far_own = early_grads(0, far_ready, far_early, far_stats)
    relayed = move(far_g1, swap)
    near_w, near_d, near_stats, near_g2 = late_scores(1, count, near_ready, near_early, near_2)
    near_sum = (near_g2.astype(jnp.float32) + relayed.astype(jnp.float32)).astype(jnp.bfloat16)
    from_near_2 = move(near_sum, near_back)
    near_early_d, near_g1, near_own = early_grads(1, near_ready, near_early, near_stats)
    from_near_1 = move(near_g1, swap)
    attended, grad_query = block_outputs(
        query,
        (far_ready[0], far_1, far_2, far_early[0], far_early_d, far_w, far_d, far_stats),
        (near_ready[0], near_1, near_2, near_early[0], near_early_d, near_w, near_d, near_stats),
    )
    grad_key, grad_value = total_grads(far_own, from_near_1, from_far_2, near_own, from_near_2)
    return (attended, grad_query, grad_key, grad_value)


def solution(mesh):
    rows = P(("dp", "ctx"), None)
    return jax.shard_map(
        body,
        mesh=mesh,
        in_specs=(rows, rows, rows, rows, P("dp")),
        out_specs=(rows, rows, rows, rows),
        check_vma=False,
    )
```

```python
import functools
import math

import jax
import jax.numpy as jnp
from jax import lax
from jax.experimental import pallas as pl
from jax.experimental.pallas import tpu as pltpu
from jax.sharding import PartitionSpec as P

HD = 128
TQ = 128
GROUP = 32

masked_score = -1e30
VMEM_LIMIT = 24 * 1024 * 1024
SCALE = 1.0 / math.sqrt(HD)
VMEM = pl.BlockSpec(memory_space=pltpu.VMEM)
HBM = pl.BlockSpec(memory_space=pltpu.HBM)
CHUNK = 128


def dot_nt(a, b):
    return lax.dot_general(a, b, (((1,), (1,)), ((), ())), preferred_element_type=jnp.float32)


def dot_nn(a, b):
    return lax.dot_general(a, b, (((1,), (0,)), ((), ())), preferred_element_type=jnp.float32)


def half_start(rows, slot):
    odd = lax.axis_index("ctx") % 2
    return pl.multiple_of((odd if slot == 0 else 1 - odd) * rows, rows)


def block_number(count, slot):
    device = lax.axis_index("ctx")
    in_lower = device % 2 == slot
    return jnp.where(in_lower, device, 2 * count - 1 - device)


def in_hbm(array):
    return pltpu.with_memory_space_constraint(array, pltpu.HBM)


def load_block(rows, slot, key, value, out, sems):
    place = pl.ds(half_start(rows, slot), rows)
    return [
        pltpu.make_async_copy(key.at[place], out.at[0:rows], sems.at[2 * slot]),
        pltpu.make_async_copy(value.at[place], out.at[rows : 2 * rows], sems.at[2 * slot + 1]),
    ]


def run_copies(copies):
    for copy in copies:
        copy.start()
    for copy in copies:
        copy.wait()


def pack_kernel(rows, key, value, near_out, far_out, sems):
    run_copies(
        load_block(rows, 1, key, value, near_out, sems)
        + load_block(rows, 0, key, value, far_out, sems)
    )


def pack_blocks(key, value):
    rows = key.shape[0] // 2
    shape = jax.ShapeDtypeStruct((2 * rows, HD), key.dtype)
    return pl.pallas_call(
        functools.partial(pack_kernel, rows),
        out_shape=(shape, shape),
        in_specs=[HBM] * 2,
        out_specs=[VMEM] * 2,
        scratch_shapes=[pltpu.SemaphoreType.DMA((4,))],
        name="pack_blocks",
    )(in_hbm(key), in_hbm(value))


def prepare_kernel(rows, heads, docs, count, *refs):
    (doc_hbm, query_hbm, dout_hbm, key, value) = refs[0:5]
    (doc_lengths, query, dout, sems) = refs[13:]
    refs = refs[5:13]
    wide = heads * TQ
    run_copies(
        [
            pltpu.make_async_copy(query_hbm, query, sems.at[4]),
            pltpu.make_async_copy(dout_hbm, dout, sems.at[5]),
            pltpu.make_async_copy(doc_hbm, doc_lengths, sems.at[6]),
        ]
        + load_block(rows, 0, key, value, refs[0], sems)
        + load_block(rows, 1, key, value, refs[4], sems)
    )
    for slot in (0, 1):
        _, query_t, dout_t, doc_start = refs[4 * slot : 4 * slot + 4]
        own_rows = half_start(rows, slot)
        for step in range(rows // TQ):
            source = pl.ds(own_rows + step * TQ, TQ)
            for h in range(heads):
                place = slice(step * wide + h * TQ, step * wide + (h + 1) * TQ)
                columns = slice(h * HD, (h + 1) * HD)
                query_t[:, place] = jnp.transpose(query[source, columns])
                dout_t[:, place] = jnp.transpose(dout[source, columns])
        at = (
            block_number(count, slot) * rows
            + lax.broadcasted_iota(jnp.int32, (8, TQ), 0) * TQ
            + lax.broadcasted_iota(jnp.int32, (8, TQ), 1)
        )

        def one(index, carry):
            start, found = carry
            found = jnp.where(at >= start, start, found)
            return (start + doc_lengths[index], found)

        _, found = lax.fori_loop(
            0, docs, one, (jnp.int32(0), jnp.zeros((8, TQ), jnp.int32)), unroll=8
        )
        doc_start[...] = found


def prepare(count, doc_lengths, query, dout, key, value):
    rows = query.shape[0] // 2
    heads = query.shape[1] // HD
    pair = jax.ShapeDtypeStruct((2 * rows, HD), key.dtype)
    stacked_t = jax.ShapeDtypeStruct((HD, rows * heads), query.dtype)
    starts = jax.ShapeDtypeStruct((8, TQ), jnp.int32)
    return pl.pallas_call(
        functools.partial(prepare_kernel, rows, heads, doc_lengths.shape[0], count),
        out_shape=(pair, stacked_t, stacked_t, starts) * 2,
        in_specs=[HBM] * 5,
        out_specs=[VMEM] * 8,
        scratch_shapes=[
            pltpu.SMEM(doc_lengths.shape, doc_lengths.dtype),
            pltpu.VMEM(query.shape, query.dtype),
            pltpu.VMEM(dout.shape, dout.dtype),
            pltpu.SemaphoreType.DMA((7,)),
        ],
        compiler_params=pltpu.CompilerParams(vmem_limit_bytes=VMEM_LIMIT),
        cost_estimate=pl.CostEstimate(flops=0, bytes_accessed=4 * 2**20, transcendentals=0),
        name="prepare",
    )(*(in_hbm(array) for array in (doc_lengths, query, dout, key, value)))


class Window:
    def __init__(self, rows, slot):
        self.tiles = rows // TQ
        self.chunks = 2 * self.tiles + 1
        self.steps = range(self.tiles)
        self.first = [self.tiles - step for step in self.steps]
        self.rest = [self.chunks - first for first in self.first]
        self.late = [first + (1 - slot) * self.tiles for first in self.first]
        self.early = [self.chunks - late for late in self.late]


def chunk_rows(counts, step, first=0, count=None):
    start = sum(counts[:step]) + first
    count = counts[step] - first if count is None else count
    return slice(start * CHUNK, (start + count) * CHUNK)


def exponentials(jobs, rows, heads, block_pos, scores):
    back = 2 * rows
    wide = heads * TQ
    base2 = SCALE * math.log2(math.e)

    def score(job, index, row_max):
        step, chunks, (query_t, _, doc_start), _, _ = jobs[job]
        chunk, keys, row = chunks[index][0:3]
        low = doc_start[step : step + 1, :] - (block_pos(job) - back + step * TQ)
        high = lax.broadcasted_iota(jnp.int32, (1, TQ), 1) + back
        tile = slice(step * wide, (step + 1) * wide)
        product = dot_nn(keys[row : row + CHUNK, :], query_t[:, tile])
        for start in range(0, CHUNK, GROUP):
            place = chunk * CHUNK + start
            at = lax.broadcasted_iota(jnp.int32, (GROUP, TQ), 0) + place
            allowed = at >= low
            if place >= back:
                allowed = jnp.logical_and(allowed, at <= high)
            for h in range(heads):
                lanes = slice(h * TQ, (h + 1) * TQ)
                part = jnp.where(allowed, product[start : start + GROUP, lanes], masked_score)
                scores[job % 2, place : place + GROUP, lanes] = part
                for row8 in range(0, GROUP, 8):
                    row_max[h] = jnp.maximum(row_max[h], part[row8 : row8 + 8, :])

    def start_max():
        return [jnp.full((8, TQ), masked_score, jnp.float32)] * heads

    following = start_max()
    for index in range(len(jobs[0][1])):
        score(0, index, following)
    for job, (step, chunks, (_, dout_t, _), first_max, end) in enumerate(jobs):
        tile = slice(step * wide, (step + 1) * wide)
        row_max = jnp.concatenate(
            [jnp.max(part, axis=0, keepdims=True) * base2 for part in following], axis=1
        )
        if first_max is not None:
            row_max = jnp.maximum(row_max, first_max)
        following = start_max()
        ahead = len(jobs[job + 1][1]) if job + 1 < len(jobs) else 0
        done = 0
        total = jnp.zeros((8, wide), jnp.float32)
        delta = jnp.zeros((8, wide), jnp.float32)
        for index, (chunk, keys, row, weights, dprobs, kept) in enumerate(chunks):
            product = dot_nn(keys[rows + row : rows + row + CHUNK, :], dout_t[:, tile])
            for start in range(0, CHUNK, GROUP):
                place = chunk * CHUNK + start
                there = slice(kept.start + start, kept.start + start + GROUP)
                dprob = product[start : start + GROUP, :]
                dprobs[there, :] = dprob.astype(jnp.bfloat16)
                part = jnp.exp2(scores[job % 2, place : place + GROUP, :] * base2 - row_max)
                weights[there, :] = part.astype(jnp.bfloat16)
                term = part * dprob
                for row8 in range(0, GROUP, 8):
                    total = total + part[row8 : row8 + 8, :]
                    delta = delta + term[row8 : row8 + 8, :]
            while done * len(chunks) < ahead * (index + 1):
                score(job + 1, done, following)
                done += 1
        end(
            row_max,
            jnp.sum(total, axis=0, keepdims=True),
            jnp.sum(delta, axis=0, keepdims=True),
        )


def early_kernel(rows, heads, count, near_1, *refs):
    inputs, outs, scores = (refs[0:4], refs[4:8]), (refs[8:11], refs[11:14]), refs[14]
    jobs = []
    for slot in (0, 1):
        window = Window(rows, slot)
        own_kv, query_t, dout_t, doc_start = inputs[slot]
        weights, dprobs, stats = outs[slot]
        for step in window.steps:
            chunks = []
            for index in range(window.early[step]):
                chunk = window.late[step] + index
                row = step * TQ + chunk * CHUNK
                keys = own_kv if row >= 2 * rows else near_1
                kept = chunk_rows(window.early, step, index, 1)
                chunks.append((chunk, keys, row % rows, weights, dprobs, kept))

            def end(*found, stats=stats, step=step):
                for kind, value in enumerate(found):
                    stats[8 * kind + step : 8 * kind + step + 1, :] = value

            jobs.append((step, chunks, (query_t, dout_t, doc_start), None, end))
    tiles = rows // TQ
    positions = [block_number(count, slot) * rows for slot in (0, 1)]
    exponentials(jobs, rows, heads, lambda job: positions[job // tiles], scores)


def early_scores(count, prepared, near_1):
    rows = near_1.shape[0] // 2
    heads = prepared[1].shape[1] // rows
    wide = heads * TQ
    out_shape = []
    for slot in (0, 1):
        kept = (sum(Window(rows, slot).early) * CHUNK, wide)
        out_shape += [jax.ShapeDtypeStruct(kept, jnp.bfloat16)] * 2
        out_shape.append(jax.ShapeDtypeStruct((24, wide), jnp.float32))
    return pl.pallas_call(
        functools.partial(early_kernel, rows, heads, count),
        out_shape=out_shape,
        in_specs=[VMEM] * 9,
        out_specs=[VMEM] * 6,
        scratch_shapes=[pltpu.VMEM((2, 2 * rows + TQ, wide), jnp.float32)],
        compiler_params=pltpu.CompilerParams(vmem_limit_bytes=VMEM_LIMIT),
        cost_estimate=pl.CostEstimate(flops=0, bytes_accessed=0, transcendentals=0),
        name="early_scores",
    )(near_1, *prepared)


def scaled_by(array, tile, factor):
    return (array[:, tile].astype(jnp.float32) * factor).astype(jnp.bfloat16)


def dscore_rows(dscores, there, weights, dprobs, kept, delta):
    delta = jnp.broadcast_to(delta, (16, delta.shape[1]))
    for start in range(0, there.stop - there.start, 16):
        out = slice(there.start + start, there.start + start + 16)
        place = slice(kept.start + start, kept.start + start + 16)
        dscores[out, :] = weights[place, :] * (dprobs[place, :] - delta)


def add_products(new, columns, products):
    for total_ref, side, terms in products:
        term = dot_nt(side, terms)
        if new:
            total_ref[:, columns] = term
        else:
            total_ref[:, columns] += term


def late_kernel(
    rows,
    heads,
    count,
    slot,
    query_t,
    dout_t,
    doc_start,
    early_stats,
    prev1,
    prev2,
    weights,
    dprobs,
    dscores,
    stats,
    prev2_out,
    scores,
    dk,
    dv,
):
    wide = heads * TQ
    window = Window(rows, slot)
    position = block_number(count, slot) * rows
    jobs = []
    for step in window.steps:
        chunks = []
        for chunk in range(window.late[step]):
            row = step * TQ + chunk * CHUNK
            kept = chunk_rows(window.late, step, chunk, 1)
            chunks.append((chunk, (prev2, prev1)[row // rows], row % rows, weights, dprobs, kept))

        def end(row_max, total, delta, step=step):
            tile = slice(step * wide, (step + 1) * wide)
            early = [early_stats[8 * kind + step : 8 * kind + step + 1, :] for kind in range(3)]
            shrink = jnp.exp2(early[0] - row_max)
            late_factor = 1.0 / (total + early[1] * shrink)
            early_factor = late_factor * shrink
            delta = delta * late_factor + early[2] * early_factor
            for kind, value in enumerate((late_factor, early_factor, delta)):
                stats[8 * kind + step : 8 * kind + step + 1, :] = value
            kept = chunk_rows(window.late, step, 0, window.first[step])
            there = chunk_rows(window.first, step)
            dscore_rows(dscores, there, weights, dprobs, kept, delta.astype(jnp.bfloat16))
            add_products(
                step == 0,
                slice(step * TQ, rows),
                (
                    (dv, scaled_by(dout_t, tile, late_factor), weights[kept, :]),
                    (dk, scaled_by(query_t, tile, late_factor), dscores[there, :]),
                ),
            )

        first_max = early_stats[step : step + 1, :]
        jobs.append((step, chunks, (query_t, dout_t, doc_start), first_max, end))
    exponentials(jobs, rows, heads, lambda job: position, scores)
    prev2_out[0:HD] = (dk[...] * SCALE).astype(prev2_out.dtype)
    prev2_out[HD : 2 * HD] = dv[...].astype(prev2_out.dtype)


def late_scores(slot, count, ready, early, prev1, prev2):
    rows = prev2.shape[0] // 2
    heads = ready[1].shape[1] // rows
    wide = heads * TQ
    window = Window(rows, slot)
    late = jax.ShapeDtypeStruct((sum(window.late) * CHUNK, wide), jnp.bfloat16)
    return pl.pallas_call(
        functools.partial(late_kernel, rows, heads, count, slot),
        out_shape=(
            late,
            late,
            jax.ShapeDtypeStruct((sum(window.first) * CHUNK, wide), jnp.bfloat16),
            jax.ShapeDtypeStruct((24, wide), jnp.float32),
            jax.ShapeDtypeStruct((2 * HD, rows), jnp.bfloat16),
        ),
        in_specs=[VMEM] * 6,
        out_specs=[VMEM] * 5,
        scratch_shapes=[
            pltpu.VMEM((2, 2 * rows, wide), jnp.float32),
            pltpu.VMEM((HD, rows), jnp.float32),
            pltpu.VMEM((HD, rows), jnp.float32),
        ],
        compiler_params=pltpu.CompilerParams(vmem_limit_bytes=VMEM_LIMIT),
        cost_estimate=pl.CostEstimate(flops=2**31, bytes_accessed=0, transcendentals=0),
        name="late_far" if slot == 0 else "late_near",
    )(*ready[1:4], early[2], prev1, prev2)


def grads_kernel(rows, heads, slot, query_t, dout_t, stats, *refs):
    (late_w, late_dprobs, early_w, early_dprobs) = refs[0:4] if slot == 0 else (None, None) + refs[0:2]
    (dscores, prev1_out, own_out, dk, dv) = refs[4:] if slot == 0 else refs[2:]
    wide = heads * TQ
    window = Window(rows, slot)
    for step in reversed(window.steps):
        tile = slice(step * wide, (step + 1) * wide)
        late_factor, early_factor, delta = (
            stats[8 * kind + step : 8 * kind + step + 1, :] for kind in range(3)
        )
        beyond = window.late[step] - window.first[step]
        parts = [(beyond, early_w, early_dprobs, chunk_rows(window.early, step), early_factor)]
        if beyond:
            kept = chunk_rows(window.late, step, window.first[step])
            parts.append((0, late_w, late_dprobs, kept, late_factor))
        for start, weights, dprobs, kept, factor in parts:
            length = (kept.stop - kept.start) // CHUNK
            there = chunk_rows(window.rest, step, start, length)
            dscore_rows(dscores, there, weights, dprobs, kept, delta.astype(jnp.bfloat16))
            add_products(
                step == window.tiles - 1,
                slice(start * CHUNK, (start + length) * CHUNK),
                (
                    (dv, scaled_by(dout_t, tile, factor), weights[kept, :]),
                    (dk, scaled_by(query_t, tile, factor), dscores[there, :]),
                ),
            )
    prev1_out[0:HD] = (dk[:, 0:rows] * SCALE).astype(prev1_out.dtype)
    prev1_out[HD : 2 * HD] = dv[:, 0:rows].astype(prev1_out.dtype)
    own_out[0:HD] = dk[:, rows : 2 * rows] * SCALE
    own_out[HD : 2 * HD] = dv[:, rows : 2 * rows]


def rest_grads(slot, ready, early, late):
    rows = ready[0].shape[0] // 2
    heads = ready[1].shape[1] // rows
    rest = (sum(Window(rows, slot).rest) * CHUNK, heads * TQ)
    operands = (*ready[1:3], late[3], *(late[0:2] if slot == 0 else ()), *early[0:2])
    return pl.pallas_call(
        functools.partial(grads_kernel, rows, heads, slot),
        out_shape=(
            jax.ShapeDtypeStruct(rest, jnp.bfloat16),
            jax.ShapeDtypeStruct((2 * HD, rows), jnp.bfloat16),
            jax.ShapeDtypeStruct((2 * HD, rows), jnp.float32),
        ),
        in_specs=[VMEM] * len(operands),
        out_specs=[VMEM] * 3,
        scratch_shapes=[pltpu.VMEM((HD, 2 * rows), jnp.float32)] * 2,
        compiler_params=pltpu.CompilerParams(vmem_limit_bytes=VMEM_LIMIT),
        cost_estimate=pl.CostEstimate(flops=2**31 if slot else 0, bytes_accessed=0, transcendentals=0),
        name="grads_far" if slot == 0 else "grads_near",
    )(*operands)


def outputs_kernel(rows, heads, *refs):
    blocks = (refs[0:8], refs[8:16])
    (attended, grad_query, keys_t, values_t) = refs[16:]
    for slot, block in enumerate(blocks):
        (own_kv, prev1, prev2, early_w, rest_d, late_w, first_d, stats) = block
        window = Window(rows, slot)
        own_rows = half_start(rows, slot)
        for place, source in enumerate((prev2, prev1, own_kv)):
            for tile in range(rows // TQ):
                part = slice(place * rows + tile * TQ, place * rows + (tile + 1) * TQ)
                row = tile * TQ
                keys_t[:, part] = jnp.transpose(source[row : row + TQ, :])
                values_t[:, part] = jnp.transpose(source[rows + row : rows + row + TQ, :])
        for step in window.steps:
            first, late = window.first[step], window.late[step]

            def product(side, terms, counts, start, skip, length):
                columns = slice(step * TQ + start * CHUNK, step * TQ + (start + length) * CHUNK)
                return dot_nn(side[:, columns], terms[chunk_rows(counts, step, skip, length), :])

            early = window.chunks - late
            late_factor = stats[step : step + 1, :]
            early_factor = stats[8 + step : 8 + step + 1, :]
            attended_t = product(values_t, late_w, window.late, 0, 0, late) * late_factor
            attended_t += product(values_t, early_w, window.early, late, 0, early) * early_factor
            late_t = product(keys_t, first_d, window.first, 0, 0, first)
            if late > first:
                late_t += product(keys_t, rest_d, window.rest, first, 0, late - first)
            early_t = product(keys_t, rest_d, window.rest, late, late - first, early)
            grad_query_t = late_t * (late_factor * SCALE) + early_t * (early_factor * SCALE)
            place = pl.ds(own_rows + step * TQ, TQ)
            for out, found in ((attended, attended_t), (grad_query, grad_query_t)):
                for h in range(heads):
                    part = found[:, h * TQ : (h + 1) * TQ]
                    out[place, h * HD : (h + 1) * HD] = jnp.transpose(part).astype(out.dtype)


def block_outputs(query, far, near):
    rows = query.shape[0] // 2
    heads = query.shape[1] // HD
    shape = jax.ShapeDtypeStruct(query.shape, query.dtype)
    return pl.pallas_call(
        functools.partial(outputs_kernel, rows, heads),
        out_shape=(shape, shape),
        in_specs=[VMEM] * 16,
        out_specs=[VMEM] * 2,
        scratch_shapes=[pltpu.VMEM((HD, 3 * rows), jnp.bfloat16)] * 2,
        compiler_params=pltpu.CompilerParams(vmem_limit_bytes=VMEM_LIMIT),
        cost_estimate=pl.CostEstimate(flops=0, bytes_accessed=0, transcendentals=0),
        name="block_outputs",
    )(*far, *near)


def total_kernel(rows, far_own, far_1, far_2, near, grad_key, grad_value):
    far = far_own[...] + far_1[...].astype(jnp.float32) + far_2[...].astype(jnp.float32)
    for slot, total in ((0, far), (1, near[...])):
        place = pl.ds(half_start(rows, slot), rows)
        grad_key[place, :] = jnp.transpose(total[0:HD]).astype(grad_key.dtype)
        grad_value[place, :] = jnp.transpose(total[HD : 2 * HD]).astype(grad_value.dtype)


def total_grads(*parts):
    rows = parts[0].shape[1]
    shape = jax.ShapeDtypeStruct((2 * rows, HD), jnp.bfloat16)
    return pl.pallas_call(
        functools.partial(total_kernel, rows),
        out_shape=(shape, shape),
        in_specs=[VMEM] * 4,
        out_specs=[VMEM] * 2,
        compiler_params=pltpu.CompilerParams(vmem_limit_bytes=VMEM_LIMIT),
        name="total_grads",
    )(*parts)


def body(query, key, value, d_out, doc_lengths):
    count = lax.axis_size("ctx")

    def holder(block):
        return block if block < count else 2 * count - 1 - block

    def move(array, pairs):
        return lax.ppermute(array, "ctx", pairs)

    near_on = [(holder(b), holder(b + 2)) for b in range(1, 2 * count - 2, 2)]
    far_on = [(holder(b), holder(b + 2)) for b in range(0, 2 * count - 2, 2)]
    near_to_far = [(holder(b), holder(b + 1)) for b in range(1, 2 * count - 2, 2)]
    swap = [(d, d ^ 1) for d in range(count)]
    near_back = [(t, s) for s, t in near_on]
    far_back = [(t, s) for s, t in far_on]

    near_kv, far_kv = pack_blocks(key, value)
    far_1 = move(near_kv, near_to_far)
    near_1 = move(far_kv, swap)
    far_2 = move(far_kv, far_on)
    prepared = prepare(count, doc_lengths, query, d_out, key, value)
    far_ready, near_ready = prepared[0:4], prepared[4:8]
    far_early, near_early = (lambda found: (found[0:3], found[3:6]))(
        early_scores(count, prepared, near_1)
    )
    far_late = late_scores(0, count, far_ready, far_early, far_1, far_2)
    from_far_2 = move(far_late[4], far_back)
    far_1, far_stats = lax.optimization_barrier((far_1, far_late[3]))
    near_2 = move(far_1, swap)
    near_2, far_early = lax.optimization_barrier((near_2, far_early))
    far_rest_d, far_g1, far_own = rest_grads(0, far_ready, far_early, far_late)
    relayed = move(far_g1, swap)
    near_late = late_scores(1, count, near_ready, near_early, near_1, near_2)
    near_sum = near_late[4].astype(jnp.float32) + relayed.astype(jnp.float32)
    near_sum, from_far_2 = lax.optimization_barrier((near_sum.astype(jnp.bfloat16), from_far_2))
    from_near_2 = move(near_sum, near_back)
    near_rest_d, near_g1, near_own = rest_grads(1, near_ready, near_early, near_late)
    from_near_1 = move(near_g1, swap)
    attended, grad_query = block_outputs(
        query,
        (far_ready[0], far_1, far_2, far_early[0], far_rest_d, far_late[0], *far_late[2:4]),
        (near_ready[0], near_1, near_2, near_early[0], near_rest_d, near_late[0], *near_late[2:4]),
    )
    near_total = near_own + from_near_2.astype(jnp.float32)
    grad_key, grad_value = total_grads(far_own, from_near_1, from_far_2, near_total)
    return (attended, grad_query, grad_key, grad_value)


def solution(mesh):
    rows = P(("dp", "ctx"), None)
    return jax.shard_map(
        body,
        mesh=mesh,
        in_specs=(rows, rows, rows, rows, P("dp")),
        out_specs=(rows, rows, rows, rows),
        check_vma=False,
    )
```

```python
import functools
import math

import jax
import jax.numpy as jnp
from jax import lax
from jax.experimental import pallas as pl
from jax.experimental.pallas import tpu as pltpu
from jax.sharding import PartitionSpec as P

HD = 128
TQ = 128
GROUP = 32

masked_score = -1e30
VMEM_LIMIT = 24 * 1024 * 1024
SCALE = 1.0 / math.sqrt(HD)
VMEM = pl.BlockSpec(memory_space=pltpu.VMEM)
HBM = pl.BlockSpec(memory_space=pltpu.HBM)
CHUNK = 128


def dot_nt(a, b):
    return lax.dot_general(a, b, (((1,), (1,)), ((), ())), preferred_element_type=jnp.float32)


def dot_nn(a, b):
    return lax.dot_general(a, b, (((1,), (0,)), ((), ())), preferred_element_type=jnp.float32)


def half_start(rows, slot):
    odd = lax.axis_index("ctx") % 2
    return pl.multiple_of((odd if slot == 0 else 1 - odd) * rows, rows)


def block_number(count, slot):
    device = lax.axis_index("ctx")
    in_lower = device % 2 == slot
    return jnp.where(in_lower, device, 2 * count - 1 - device)


def in_hbm(array):
    return pltpu.with_memory_space_constraint(array, pltpu.HBM)


def load_block(rows, slot, key, value, out, sems):
    place = pl.ds(half_start(rows, slot), rows)
    return [
        pltpu.make_async_copy(key.at[place], out.at[0:rows], sems.at[2 * slot]),
        pltpu.make_async_copy(value.at[place], out.at[rows : 2 * rows], sems.at[2 * slot + 1]),
    ]


def run_copies(copies):
    for copy in copies:
        copy.start()
    for copy in copies:
        copy.wait()


def pack_kernel(rows, key, value, near_out, far_out, sems):
    run_copies(
        load_block(rows, 1, key, value, near_out, sems)
        + load_block(rows, 0, key, value, far_out, sems)
    )


def pack_blocks(key, value):
    rows = key.shape[0] // 2
    shape = jax.ShapeDtypeStruct((2 * rows, HD), key.dtype)
    return pl.pallas_call(
        functools.partial(pack_kernel, rows),
        out_shape=(shape, shape),
        in_specs=[HBM] * 2,
        out_specs=[VMEM] * 2,
        scratch_shapes=[pltpu.SemaphoreType.DMA((4,))],
        name="pack_blocks",
    )(in_hbm(key), in_hbm(value))


def prepare_kernel(rows, heads, docs, count, *refs):
    (doc_hbm, query_hbm, dout_hbm, key, value) = refs[0:5]
    (doc_lengths, query, dout, sems) = refs[13:]
    refs = refs[5:13]
    wide = heads * TQ
    run_copies(
        [
            pltpu.make_async_copy(query_hbm, query, sems.at[4]),
            pltpu.make_async_copy(dout_hbm, dout, sems.at[5]),
            pltpu.make_async_copy(doc_hbm, doc_lengths, sems.at[6]),
        ]
        + load_block(rows, 0, key, value, refs[0], sems)
        + load_block(rows, 1, key, value, refs[4], sems)
    )
    for slot in (0, 1):
        _, query_t, dout_t, doc_start = refs[4 * slot : 4 * slot + 4]
        own_rows = half_start(rows, slot)
        for step in range(rows // TQ):
            source = pl.ds(own_rows + step * TQ, TQ)
            for h in range(heads):
                place = slice(step * wide + h * TQ, step * wide + (h + 1) * TQ)
                columns = slice(h * HD, (h + 1) * HD)
                query_t[:, place] = jnp.transpose(query[source, columns])
                dout_t[:, place] = jnp.transpose(dout[source, columns])
        at = (
            block_number(count, slot) * rows
            + lax.broadcasted_iota(jnp.int32, (8, TQ), 0) * TQ
            + lax.broadcasted_iota(jnp.int32, (8, TQ), 1)
        )

        def one(index, carry):
            start, found = carry
            found = jnp.where(at >= start, start, found)
            return (start + doc_lengths[index], found)

        _, found = lax.fori_loop(
            0, docs, one, (jnp.int32(0), jnp.zeros((8, TQ), jnp.int32)), unroll=8
        )
        doc_start[...] = found


def prepare(count, doc_lengths, query, dout, key, value):
    rows = query.shape[0] // 2
    heads = query.shape[1] // HD
    pair = jax.ShapeDtypeStruct((2 * rows, HD), key.dtype)
    stacked_t = jax.ShapeDtypeStruct((HD, rows * heads), query.dtype)
    starts = jax.ShapeDtypeStruct((8, TQ), jnp.int32)
    return pl.pallas_call(
        functools.partial(prepare_kernel, rows, heads, doc_lengths.shape[0], count),
        out_shape=(pair, stacked_t, stacked_t, starts) * 2,
        in_specs=[HBM] * 5,
        out_specs=[VMEM] * 8,
        scratch_shapes=[
            pltpu.SMEM(doc_lengths.shape, doc_lengths.dtype),
            pltpu.VMEM(query.shape, query.dtype),
            pltpu.VMEM(dout.shape, dout.dtype),
            pltpu.SemaphoreType.DMA((7,)),
        ],
        compiler_params=pltpu.CompilerParams(vmem_limit_bytes=VMEM_LIMIT),
        cost_estimate=pl.CostEstimate(flops=0, bytes_accessed=4 * 2**20, transcendentals=0),
        name="prepare",
    )(*(in_hbm(array) for array in (doc_lengths, query, dout, key, value)))


class Window:
    def __init__(self, rows, slot):
        self.tiles = rows // TQ
        self.chunks = 2 * self.tiles + 1
        self.steps = range(self.tiles)
        self.first = [self.tiles - step for step in self.steps]
        self.rest = [self.chunks - first for first in self.first]
        self.late = [first + (1 - slot) * self.tiles for first in self.first]
        self.early = [self.chunks - late for late in self.late]


def chunk_rows(counts, step, first=0, count=None):
    start = sum(counts[:step]) + first
    count = counts[step] - first if count is None else count
    return slice(start * CHUNK, (start + count) * CHUNK)


def exponentials(jobs, rows, heads, block_pos, scores):
    back = 2 * rows
    wide = heads * TQ
    base2 = SCALE * math.log2(math.e)

    def score(job, index, row_max):
        step, chunks, (query_t, _, doc_start), _, _ = jobs[job]
        chunk, keys, row = chunks[index][0:3]
        low = doc_start[step : step + 1, :] - (block_pos(job) - back + step * TQ)
        high = lax.broadcasted_iota(jnp.int32, (1, TQ), 1) + back
        tile = slice(step * wide, (step + 1) * wide)
        product = dot_nn(keys[row : row + CHUNK, :], query_t[:, tile])
        for start in range(0, CHUNK, GROUP):
            place = chunk * CHUNK + start
            at = lax.broadcasted_iota(jnp.int32, (GROUP, TQ), 0) + place
            allowed = at >= low
            if place >= back:
                allowed = jnp.logical_and(allowed, at <= high)
            for h in range(heads):
                lanes = slice(h * TQ, (h + 1) * TQ)
                part = jnp.where(allowed, product[start : start + GROUP, lanes], masked_score)
                scores[job % 2, place : place + GROUP, lanes] = part
                for row8 in range(0, GROUP, 8):
                    row_max[h] = jnp.maximum(row_max[h], part[row8 : row8 + 8, :])

    def start_max():
        return [jnp.full((8, TQ), masked_score, jnp.float32)] * heads

    following = start_max()
    for index in range(len(jobs[0][1])):
        score(0, index, following)
    for job, (step, chunks, (_, dout_t, _), first_max, end) in enumerate(jobs):
        tile = slice(step * wide, (step + 1) * wide)
        row_max = jnp.concatenate(
            [jnp.max(part, axis=0, keepdims=True) * base2 for part in following], axis=1
        )
        if first_max is not None:
            row_max = jnp.maximum(row_max, first_max)
        following = start_max()
        ahead = len(jobs[job + 1][1]) if job + 1 < len(jobs) else 0
        done = 0
        total = jnp.zeros((8, wide), jnp.float32)
        delta = jnp.zeros((8, wide), jnp.float32)
        for index, (chunk, keys, row, weights, dprobs, kept) in enumerate(chunks):
            product = dot_nn(keys[rows + row : rows + row + CHUNK, :], dout_t[:, tile])
            for start in range(0, CHUNK, GROUP):
                place = chunk * CHUNK + start
                there = slice(kept.start + start, kept.start + start + GROUP)
                dprob = product[start : start + GROUP, :]
                dprobs[there, :] = dprob.astype(jnp.bfloat16)
                part = jnp.exp2(scores[job % 2, place : place + GROUP, :] * base2 - row_max)
                weights[there, :] = part.astype(jnp.bfloat16)
                term = part * dprob
                for row8 in range(0, GROUP, 8):
                    total = total + part[row8 : row8 + 8, :]
                    delta = delta + term[row8 : row8 + 8, :]
            while done * len(chunks) < ahead * (index + 1):
                score(job + 1, done, following)
                done += 1
        end(
            row_max,
            jnp.sum(total, axis=0, keepdims=True),
            jnp.sum(delta, axis=0, keepdims=True),
        )


def early_kernel(rows, heads, count, near_1, *refs):
    inputs, outs, scores = (refs[0:4], refs[4:8]), (refs[8:11], refs[11:14]), refs[14]
    jobs = []
    for slot in (0, 1):
        window = Window(rows, slot)
        own_kv, query_t, dout_t, doc_start = inputs[slot]
        weights, dprobs, stats = outs[slot]
        for step in window.steps:
            chunks = []
            for index in range(window.early[step]):
                chunk = window.late[step] + index
                row = step * TQ + chunk * CHUNK
                keys = own_kv if row >= 2 * rows else near_1
                kept = chunk_rows(window.early, step, index, 1)
                chunks.append((chunk, keys, row % rows, weights, dprobs, kept))

            def end(*found, stats=stats, step=step):
                for kind, value in enumerate(found):
                    stats[8 * kind + step : 8 * kind + step + 1, :] = value

            jobs.append((step, chunks, (query_t, dout_t, doc_start), None, end))
    tiles = rows // TQ
    positions = [block_number(count, slot) * rows for slot in (0, 1)]
    exponentials(jobs, rows, heads, lambda job: positions[job // tiles], scores)


def early_scores(count, prepared, near_1):
    rows = near_1.shape[0] // 2
    heads = prepared[1].shape[1] // rows
    wide = heads * TQ
    out_shape = []
    for slot in (0, 1):
        kept = (sum(Window(rows, slot).early) * CHUNK, wide)
        out_shape += [jax.ShapeDtypeStruct(kept, jnp.bfloat16)] * 2
        out_shape.append(jax.ShapeDtypeStruct((24, wide), jnp.float32))
    return pl.pallas_call(
        functools.partial(early_kernel, rows, heads, count),
        out_shape=out_shape,
        in_specs=[VMEM] * 9,
        out_specs=[VMEM] * 6,
        scratch_shapes=[pltpu.VMEM((2, 2 * rows + TQ, wide), jnp.float32)],
        compiler_params=pltpu.CompilerParams(vmem_limit_bytes=VMEM_LIMIT),
        cost_estimate=pl.CostEstimate(flops=0, bytes_accessed=0, transcendentals=0),
        name="early_scores",
    )(near_1, *prepared)


def scaled_by(array, tile, factor):
    return (array[:, tile].astype(jnp.float32) * factor).astype(jnp.bfloat16)


def dscore_rows(dscores, there, weights, dprobs, kept, delta):
    delta = jnp.broadcast_to(delta, (16, delta.shape[1]))
    for start in range(0, there.stop - there.start, 16):
        out = slice(there.start + start, there.start + start + 16)
        place = slice(kept.start + start, kept.start + start + 16)
        dscores[out, :] = weights[place, :] * (dprobs[place, :] - delta)


def add_products(new, columns, products):
    for total_ref, side, terms in products:
        term = dot_nt(side, terms)
        if new:
            total_ref[:, columns] = term
        else:
            total_ref[:, columns] += term


def late_kernel(
    rows,
    heads,
    count,
    slot,
    query_t,
    dout_t,
    doc_start,
    early_stats,
    prev1,
    prev2,
    weights,
    *refs,
):
    (dprobs, dscores, stats, prev2_out, scores, dk, dv) = refs if slot == 0 else refs[-1:] + refs[:-1]
    wide = heads * TQ
    window = Window(rows, slot)
    position = block_number(count, slot) * rows
    jobs = []
    for step in window.steps:
        chunks = []
        for chunk in range(window.late[step]):
            row = step * TQ + chunk * CHUNK
            kept = chunk_rows(window.late, step, chunk, 1)
            chunks.append((chunk, (prev2, prev1)[row // rows], row % rows, weights, dprobs, kept))

        def end(row_max, total, delta, step=step):
            tile = slice(step * wide, (step + 1) * wide)
            early = [early_stats[8 * kind + step : 8 * kind + step + 1, :] for kind in range(3)]
            shrink = jnp.exp2(early[0] - row_max)
            late_factor = 1.0 / (total + early[1] * shrink)
            early_factor = late_factor * shrink
            delta = delta * late_factor + early[2] * early_factor
            for kind, value in enumerate((late_factor, early_factor, delta)):
                stats[8 * kind + step : 8 * kind + step + 1, :] = value
            kept = chunk_rows(window.late, step, 0, window.first[step])
            there = chunk_rows(window.first, step)
            dscore_rows(dscores, there, weights, dprobs, kept, delta.astype(jnp.bfloat16))
            add_products(
                step == 0,
                slice(step * TQ, rows),
                (
                    (dv, scaled_by(dout_t, tile, late_factor), weights[kept, :]),
                    (dk, scaled_by(query_t, tile, late_factor), dscores[there, :]),
                ),
            )

        first_max = early_stats[step : step + 1, :]
        jobs.append((step, chunks, (query_t, dout_t, doc_start), first_max, end))
    exponentials(jobs, rows, heads, lambda job: position, scores)
    prev2_out[0:HD] = (dk[...] * SCALE).astype(prev2_out.dtype)
    prev2_out[HD : 2 * HD] = dv[...].astype(prev2_out.dtype)


def late_scores(slot, count, ready, early, prev1, prev2):
    rows = prev2.shape[0] // 2
    heads = ready[1].shape[1] // rows
    wide = heads * TQ
    window = Window(rows, slot)
    late = jax.ShapeDtypeStruct((sum(window.late) * CHUNK, wide), jnp.bfloat16)
    return pl.pallas_call(
        functools.partial(late_kernel, rows, heads, count, slot),
        out_shape=(
            *([late] * (2 - slot)),
            jax.ShapeDtypeStruct((sum(window.first) * CHUNK, wide), jnp.bfloat16),
            jax.ShapeDtypeStruct((24, wide), jnp.float32),
            jax.ShapeDtypeStruct((2 * HD, rows), jnp.bfloat16),
        ),
        in_specs=[VMEM] * 6,
        out_specs=[VMEM] * (5 - slot),
        scratch_shapes=[
            pltpu.VMEM((2, max(window.late) * CHUNK, wide), jnp.float32),
            pltpu.VMEM((HD, rows), jnp.float32),
            pltpu.VMEM((HD, rows), jnp.float32),
            *([pltpu.VMEM(late.shape, late.dtype)] * slot),
        ],
        compiler_params=pltpu.CompilerParams(vmem_limit_bytes=VMEM_LIMIT),
        cost_estimate=pl.CostEstimate(flops=2**31, bytes_accessed=0, transcendentals=0),
        name="late_far" if slot == 0 else "late_near",
    )(*ready[1:4], early[2], prev1, prev2)


def grads_kernel(rows, heads, slot, query_t, dout_t, stats, *refs):
    (late_w, late_dprobs, early_w, early_dprobs) = refs[0:4] if slot == 0 else (None, None) + refs[0:2]
    (dscores, prev1_out, own_out, dk, dv) = refs[4:] if slot == 0 else refs[2:]
    wide = heads * TQ
    window = Window(rows, slot)
    for step in reversed(window.steps):
        tile = slice(step * wide, (step + 1) * wide)
        late_factor, early_factor, delta = (
            stats[8 * kind + step : 8 * kind + step + 1, :] for kind in range(3)
        )
        beyond = window.late[step] - window.first[step]
        parts = [(beyond, early_w, early_dprobs, chunk_rows(window.early, step), early_factor)]
        if beyond:
            kept = chunk_rows(window.late, step, window.first[step])
            parts.append((0, late_w, late_dprobs, kept, late_factor))
        for start, weights, dprobs, kept, factor in parts:
            length = (kept.stop - kept.start) // CHUNK
            there = chunk_rows(window.rest, step, start, length)
            dscore_rows(dscores, there, weights, dprobs, kept, delta.astype(jnp.bfloat16))
            add_products(
                step == window.tiles - 1,
                slice(start * CHUNK, (start + length) * CHUNK),
                (
                    (dv, scaled_by(dout_t, tile, factor), weights[kept, :]),
                    (dk, scaled_by(query_t, tile, factor), dscores[there, :]),
                ),
            )
    prev1_out[0:HD] = (dk[:, 0:rows] * SCALE).astype(prev1_out.dtype)
    prev1_out[HD : 2 * HD] = dv[:, 0:rows].astype(prev1_out.dtype)
    own_out[0:HD] = dk[:, rows : 2 * rows] * SCALE
    own_out[HD : 2 * HD] = dv[:, rows : 2 * rows]


def rest_grads(slot, ready, early, late):
    rows = ready[0].shape[0] // 2
    heads = ready[1].shape[1] // rows
    rest = (sum(Window(rows, slot).rest) * CHUNK, heads * TQ)
    operands = (*ready[1:3], late[-2], *(late[0:2] if slot == 0 else ()), *early[0:2])
    return pl.pallas_call(
        functools.partial(grads_kernel, rows, heads, slot),
        out_shape=(
            jax.ShapeDtypeStruct(rest, jnp.bfloat16),
            jax.ShapeDtypeStruct((2 * HD, rows), jnp.bfloat16),
            jax.ShapeDtypeStruct((2 * HD, rows), jnp.float32),
        ),
        in_specs=[VMEM] * len(operands),
        out_specs=[VMEM] * 3,
        scratch_shapes=[pltpu.VMEM((HD, 2 * rows), jnp.float32)] * 2,
        compiler_params=pltpu.CompilerParams(vmem_limit_bytes=VMEM_LIMIT),
        cost_estimate=pl.CostEstimate(flops=2**31 if slot else 0, bytes_accessed=0, transcendentals=0),
        name="grads_far" if slot == 0 else "grads_near",
    )(*operands)


def outputs_kernel(rows, heads, *refs):
    blocks = (refs[0:8], refs[8:16])
    (attended, grad_query, keys_t, values_t) = refs[16:]
    for slot, block in enumerate(blocks):
        (own_kv, prev1, prev2, early_w, rest_d, late_w, first_d, stats) = block
        window = Window(rows, slot)
        own_rows = half_start(rows, slot)
        for place, source in enumerate((prev2, prev1, own_kv)):
            for tile in range(rows // TQ):
                part = slice(place * rows + tile * TQ, place * rows + (tile + 1) * TQ)
                row = tile * TQ
                keys_t[:, part] = jnp.transpose(source[row : row + TQ, :])
                values_t[:, part] = jnp.transpose(source[rows + row : rows + row + TQ, :])
        for step in window.steps:
            first, late = window.first[step], window.late[step]

            def product(side, terms, counts, start, skip, length):
                columns = slice(step * TQ + start * CHUNK, step * TQ + (start + length) * CHUNK)
                return dot_nn(side[:, columns], terms[chunk_rows(counts, step, skip, length), :])

            early = window.chunks - late
            late_factor = stats[step : step + 1, :]
            early_factor = stats[8 + step : 8 + step + 1, :]
            attended_t = product(values_t, late_w, window.late, 0, 0, late) * late_factor
            attended_t += product(values_t, early_w, window.early, late, 0, early) * early_factor
            late_t = product(keys_t, first_d, window.first, 0, 0, first)
            if late > first:
                late_t += product(keys_t, rest_d, window.rest, first, 0, late - first)
            early_t = product(keys_t, rest_d, window.rest, late, late - first, early)
            grad_query_t = late_t * (late_factor * SCALE) + early_t * (early_factor * SCALE)
            place = pl.ds(own_rows + step * TQ, TQ)
            for out, found in ((attended, attended_t), (grad_query, grad_query_t)):
                for h in range(heads):
                    part = found[:, h * TQ : (h + 1) * TQ]
                    out[place, h * HD : (h + 1) * HD] = jnp.transpose(part).astype(out.dtype)


def block_outputs(query, far, near):
    rows = query.shape[0] // 2
    heads = query.shape[1] // HD
    shape = jax.ShapeDtypeStruct(query.shape, query.dtype)
    return pl.pallas_call(
        functools.partial(outputs_kernel, rows, heads),
        out_shape=(shape, shape),
        in_specs=[VMEM] * 16,
        out_specs=[VMEM] * 2,
        scratch_shapes=[pltpu.VMEM((HD, 3 * rows), jnp.bfloat16)] * 2,
        compiler_params=pltpu.CompilerParams(vmem_limit_bytes=VMEM_LIMIT),
        cost_estimate=pl.CostEstimate(flops=0, bytes_accessed=0, transcendentals=0),
        name="block_outputs",
    )(*far, *near)


def total_kernel(rows, far_own, far_1, far_2, near, grad_key, grad_value):
    far = far_own[...] + far_1[...].astype(jnp.float32) + far_2[...].astype(jnp.float32)
    for slot, total in ((0, far), (1, near[...])):
        place = pl.ds(half_start(rows, slot), rows)
        grad_key[place, :] = jnp.transpose(total[0:HD]).astype(grad_key.dtype)
        grad_value[place, :] = jnp.transpose(total[HD : 2 * HD]).astype(grad_value.dtype)


def total_grads(*parts):
    rows = parts[0].shape[1]
    shape = jax.ShapeDtypeStruct((2 * rows, HD), jnp.bfloat16)
    return pl.pallas_call(
        functools.partial(total_kernel, rows),
        out_shape=(shape, shape),
        in_specs=[VMEM] * 4,
        out_specs=[VMEM] * 2,
        compiler_params=pltpu.CompilerParams(vmem_limit_bytes=VMEM_LIMIT),
        name="total_grads",
    )(*parts)


def body(query, key, value, d_out, doc_lengths):
    count = lax.axis_size("ctx")

    def holder(block):
        return block if block < count else 2 * count - 1 - block

    def move(array, pairs):
        return lax.ppermute(array, "ctx", pairs)

    near_on = [(holder(b), holder(b + 2)) for b in range(1, 2 * count - 2, 2)]
    far_on = [(holder(b), holder(b + 2)) for b in range(0, 2 * count - 2, 2)]
    near_to_far = [(holder(b), holder(b + 1)) for b in range(1, 2 * count - 2, 2)]
    swap = [(d, d ^ 1) for d in range(count)]
    near_back = [(t, s) for s, t in near_on]
    far_back = [(t, s) for s, t in far_on]

    near_kv, far_kv = pack_blocks(key, value)
    far_1 = move(near_kv, near_to_far)
    near_1 = move(far_kv, swap)
    far_2 = move(far_kv, far_on)
    prepared = prepare(count, doc_lengths, query, d_out, key, value)
    far_ready, near_ready = prepared[0:4], prepared[4:8]
    far_early, near_early = (lambda found: (found[0:3], found[3:6]))(
        early_scores(count, prepared, near_1)
    )
    far_late = late_scores(0, count, far_ready, far_early, far_1, far_2)
    from_far_2 = move(far_late[-1], far_back)
    far_1, far_stats = lax.optimization_barrier((far_1, far_late[-2]))
    near_2 = move(far_1, swap)
    near_2, far_early = lax.optimization_barrier((near_2, far_early))
    far_rest_d, far_g1, far_own = rest_grads(0, far_ready, far_early, far_late)
    relayed = move(far_g1, swap)
    near_late = late_scores(1, count, near_ready, near_early, near_1, near_2)
    near_sum = near_late[-1].astype(jnp.float32) + relayed.astype(jnp.float32)
    from_near_2 = move(near_sum.astype(jnp.bfloat16), near_back)
    near_rest_d, near_g1, near_own = rest_grads(1, near_ready, near_early, near_late)
    near_g1, from_far_2 = lax.optimization_barrier((near_g1, from_far_2))
    from_near_1 = move(near_g1, swap)
    attended, grad_query = block_outputs(
        query,
        (far_ready[0], far_1, far_2, far_early[0], far_rest_d, far_late[0], *far_late[-3:-1]),
        (near_ready[0], near_1, near_2, near_early[0], near_rest_d, near_late[0], *near_late[-3:-1]),
    )
    near_total = near_own + from_near_2.astype(jnp.float32)
    grad_key, grad_value = total_grads(far_own, from_near_1, from_far_2, near_total)
    return (attended, grad_query, grad_key, grad_value)


def solution(mesh):
    rows = P(("dp", "ctx"), None)
    return jax.shard_map(
        body,
        mesh=mesh,
        in_specs=(rows, rows, rows, rows, P("dp")),
        out_specs=(rows, rows, rows, rows),
        check_vma=False,
    )
```

```python
import functools
import math

import jax
import jax.numpy as jnp
from jax import lax
from jax.experimental import pallas as pl
from jax.experimental.pallas import tpu as pltpu
from jax.sharding import PartitionSpec as P

HD = 128
TQ = 128
GROUP = 32

masked_score = -1e30
VMEM_LIMIT = 24 * 1024 * 1024
SCALE = 1.0 / math.sqrt(HD)
VMEM = pl.BlockSpec(memory_space=pltpu.VMEM)
HBM = pl.BlockSpec(memory_space=pltpu.HBM)
CHUNK = 128


def dot_nt(a, b):
    return lax.dot_general(a, b, (((1,), (1,)), ((), ())), preferred_element_type=jnp.float32)


def dot_nn(a, b):
    return lax.dot_general(a, b, (((1,), (0,)), ((), ())), preferred_element_type=jnp.float32)


def half_start(rows, slot):
    odd = lax.axis_index("ctx") % 2
    return pl.multiple_of((odd if slot == 0 else 1 - odd) * rows, rows)


def block_number(count, slot):
    device = lax.axis_index("ctx")
    in_lower = device % 2 == slot
    return jnp.where(in_lower, device, 2 * count - 1 - device)


def in_hbm(array):
    return pltpu.with_memory_space_constraint(array, pltpu.HBM)


def load_block(rows, slot, key, value, out, sems):
    place = pl.ds(half_start(rows, slot), rows)
    return [
        pltpu.make_async_copy(key.at[place], out.at[0:rows], sems.at[2 * slot]),
        pltpu.make_async_copy(value.at[place], out.at[rows : 2 * rows], sems.at[2 * slot + 1]),
    ]


def run_copies(copies):
    for copy in copies:
        copy.start()
    for copy in copies:
        copy.wait()


def prepare_kernel(rows, heads, docs, count, *refs):
    (far_kv, near_kv, doc_hbm, query_hbm, dout_hbm) = refs[0:5]
    (doc_lengths, query, dout, sems) = refs[13:]
    refs = refs[5:13]
    wide = heads * TQ
    run_copies(
        [
            pltpu.make_async_copy(query_hbm, query, sems.at[0]),
            pltpu.make_async_copy(dout_hbm, dout, sems.at[1]),
            pltpu.make_async_copy(doc_hbm, doc_lengths, sems.at[2]),
        ]
    )
    for slot in (0, 1):
        own_kv, query_t, dout_t, doc_start = refs[4 * slot : 4 * slot + 4]
        own_kv[...] = (far_kv, near_kv)[slot][...]
        own_rows = half_start(rows, slot)
        for step in range(rows // TQ):
            source = pl.ds(own_rows + step * TQ, TQ)
            for h in range(heads):
                place = slice(step * wide + h * TQ, step * wide + (h + 1) * TQ)
                columns = slice(h * HD, (h + 1) * HD)
                query_t[:, place] = jnp.transpose(query[source, columns])
                dout_t[:, place] = jnp.transpose(dout[source, columns])
        at = (
            block_number(count, slot) * rows
            + lax.broadcasted_iota(jnp.int32, (8, TQ), 0) * TQ
            + lax.broadcasted_iota(jnp.int32, (8, TQ), 1)
        )

        def one(index, carry):
            start, found = carry
            found = jnp.where(at >= start, start, found)
            return (start + doc_lengths[index], found)

        _, found = lax.fori_loop(
            0, docs, one, (jnp.int32(0), jnp.zeros((8, TQ), jnp.int32)), unroll=8
        )
        doc_start[...] = found


def prepare(count, doc_lengths, query, dout, far_kv, near_kv):
    rows = query.shape[0] // 2
    heads = query.shape[1] // HD
    pair = jax.ShapeDtypeStruct(far_kv.shape, far_kv.dtype)
    stacked_t = jax.ShapeDtypeStruct((HD, rows * heads), query.dtype)
    starts = jax.ShapeDtypeStruct((8, TQ), jnp.int32)
    return pl.pallas_call(
        functools.partial(prepare_kernel, rows, heads, doc_lengths.shape[0], count),
        out_shape=(pair, stacked_t, stacked_t, starts) * 2,
        in_specs=[VMEM] * 2 + [HBM] * 3,
        out_specs=[VMEM] * 8,
        scratch_shapes=[
            pltpu.SMEM(doc_lengths.shape, doc_lengths.dtype),
            pltpu.VMEM(query.shape, query.dtype),
            pltpu.VMEM(dout.shape, dout.dtype),
            pltpu.SemaphoreType.DMA((3,)),
        ],
        compiler_params=pltpu.CompilerParams(vmem_limit_bytes=VMEM_LIMIT),
        cost_estimate=pl.CostEstimate(flops=0, bytes_accessed=4 * 2**20, transcendentals=0),
        name="prepare",
    )(far_kv, near_kv, *(in_hbm(array) for array in (doc_lengths, query, dout)))


class Window:
    def __init__(self, rows, slot):
        self.tiles = rows // TQ
        self.chunks = 2 * self.tiles + 1
        self.steps = range(self.tiles)
        self.first = [self.tiles - step for step in self.steps]
        self.rest = [self.chunks - first for first in self.first]
        self.late = [first + (1 - slot) * self.tiles for first in self.first]
        self.early = [self.chunks - late for late in self.late]


def chunk_rows(counts, step, first=0, count=None):
    start = sum(counts[:step]) + first
    count = counts[step] - first if count is None else count
    return slice(start * CHUNK, (start + count) * CHUNK)


def exponentials(jobs, rows, heads, block_pos, scores):
    back = 2 * rows
    wide = heads * TQ
    base2 = SCALE * math.log2(math.e)

    def score(job, index, row_max):
        step, chunks, (query_t, _, doc_start), _, _ = jobs[job]
        chunk, keys, row = chunks[index][0:3]
        low = doc_start[step : step + 1, :] - (block_pos(job) - back + step * TQ)
        high = lax.broadcasted_iota(jnp.int32, (1, TQ), 1) + back
        tile = slice(step * wide, (step + 1) * wide)
        product = dot_nn(keys[row : row + CHUNK, :], query_t[:, tile])
        for start in range(0, CHUNK, GROUP):
            place = chunk * CHUNK + start
            at = lax.broadcasted_iota(jnp.int32, (GROUP, TQ), 0) + place
            allowed = at >= low
            if place >= back:
                allowed = jnp.logical_and(allowed, at <= high)
            for h in range(heads):
                lanes = slice(h * TQ, (h + 1) * TQ)
                part = jnp.where(allowed, product[start : start + GROUP, lanes], masked_score)
                scores[job % 2, place : place + GROUP, lanes] = part
                for row8 in range(0, GROUP, 8):
                    row_max[h] = jnp.maximum(row_max[h], part[row8 : row8 + 8, :])

    def start_max():
        return [jnp.full((8, TQ), masked_score, jnp.float32)] * heads

    following = start_max()
    for index in range(len(jobs[0][1])):
        score(0, index, following)
    for job, (step, chunks, (_, dout_t, _), first_max, end) in enumerate(jobs):
        tile = slice(step * wide, (step + 1) * wide)
        row_max = jnp.concatenate(
            [jnp.max(part, axis=0, keepdims=True) * base2 for part in following], axis=1
        )
        if first_max is not None:
            row_max = jnp.maximum(row_max, first_max)
        following = start_max()
        ahead = len(jobs[job + 1][1]) if job + 1 < len(jobs) else 0
        done = 0
        total = jnp.zeros((8, wide), jnp.float32)
        delta = jnp.zeros((8, wide), jnp.float32)
        for index, (chunk, keys, row, weights, dprobs, kept) in enumerate(chunks):
            product = dot_nn(keys[rows + row : rows + row + CHUNK, :], dout_t[:, tile])
            for start in range(0, CHUNK, GROUP):
                place = chunk * CHUNK + start
                there = slice(kept.start + start, kept.start + start + GROUP)
                dprob = product[start : start + GROUP, :]
                dprobs[there, :] = dprob.astype(jnp.bfloat16)
                part = jnp.exp2(scores[job % 2, place : place + GROUP, :] * base2 - row_max)
                weights[there, :] = part.astype(jnp.bfloat16)
                term = part * dprob
                for row8 in range(0, GROUP, 8):
                    total = total + part[row8 : row8 + 8, :]
                    delta = delta + term[row8 : row8 + 8, :]
            while done * len(chunks) < ahead * (index + 1):
                score(job + 1, done, following)
                done += 1
        end(
            row_max,
            jnp.sum(total, axis=0, keepdims=True),
            jnp.sum(delta, axis=0, keepdims=True),
        )


def early_kernel(rows, heads, count, slot, own_kv, query_t, dout_t, doc_start, *refs):
    (weights, dprobs, stats, scores) = refs[-4:]
    prev1 = refs[0] if slot == 1 else None
    window = Window(rows, slot)
    position = block_number(count, slot) * rows
    jobs = []
    for step in window.steps:
        chunks = []
        for index in range(window.early[step]):
            chunk = window.late[step] + index
            row = step * TQ + chunk * CHUNK
            keys = own_kv if row >= 2 * rows else prev1
            kept = chunk_rows(window.early, step, index, 1)
            chunks.append((chunk, keys, row % rows, weights, dprobs, kept))

        def end(*found, step=step):
            for kind, value in enumerate(found):
                stats[8 * kind + step : 8 * kind + step + 1, :] = value

        jobs.append((step, chunks, (query_t, dout_t, doc_start), None, end))
    exponentials(jobs, rows, heads, lambda job: position, scores)


def early_scores(slot, count, ready, *prev1):
    rows = ready[0].shape[0] // 2
    heads = ready[1].shape[1] // rows
    wide = heads * TQ
    kept = jax.ShapeDtypeStruct((sum(Window(rows, slot).early) * CHUNK, wide), jnp.bfloat16)
    return pl.pallas_call(
        functools.partial(early_kernel, rows, heads, count, slot),
        out_shape=(kept, kept, jax.ShapeDtypeStruct((24, wide), jnp.float32)),
        in_specs=[VMEM] * (4 + len(prev1)),
        out_specs=[VMEM] * 3,
        scratch_shapes=[pltpu.VMEM((2, 2 * rows + TQ, wide), jnp.float32)],
        compiler_params=pltpu.CompilerParams(vmem_limit_bytes=VMEM_LIMIT),
        cost_estimate=pl.CostEstimate(flops=0 if slot else 2**33, bytes_accessed=0, transcendentals=0),
        name="early_far" if slot == 0 else "early_near",
    )(*ready, *prev1)


def scaled_by(array, tile, factor):
    return (array[:, tile].astype(jnp.float32) * factor).astype(jnp.bfloat16)


def dscore_rows(dscores, there, weights, dprobs, kept, delta):
    delta = jnp.broadcast_to(delta, (16, delta.shape[1]))
    for start in range(0, there.stop - there.start, 16):
        out = slice(there.start + start, there.start + start + 16)
        place = slice(kept.start + start, kept.start + start + 16)
        dscores[out, :] = weights[place, :] * (dprobs[place, :] - delta)


def add_products(new, columns, products):
    for total_ref, side, terms in products:
        term = dot_nt(side, terms)
        if new:
            total_ref[:, columns] = term
        else:
            total_ref[:, columns] += term


def late_kernel(
    rows,
    heads,
    count,
    slot,
    query_t,
    dout_t,
    doc_start,
    early_stats,
    prev1,
    prev2,
    weights,
    *refs,
):
    (dprobs, dscores, stats, prev2_out, scores, dk, dv) = refs if slot == 0 else refs[-1:] + refs[:-1]
    wide = heads * TQ
    window = Window(rows, slot)
    position = block_number(count, slot) * rows
    jobs = []
    for step in window.steps:
        chunks = []
        for chunk in range(window.late[step]):
            row = step * TQ + chunk * CHUNK
            kept = chunk_rows(window.late, step, chunk, 1)
            chunks.append((chunk, (prev2, prev1)[row // rows], row % rows, weights, dprobs, kept))

        def end(row_max, total, delta, step=step):
            tile = slice(step * wide, (step + 1) * wide)
            early = [early_stats[8 * kind + step : 8 * kind + step + 1, :] for kind in range(3)]
            shrink = jnp.exp2(early[0] - row_max)
            late_factor = 1.0 / (total + early[1] * shrink)
            early_factor = late_factor * shrink
            delta = delta * late_factor + early[2] * early_factor
            for kind, value in enumerate((late_factor, early_factor, delta)):
                stats[8 * kind + step : 8 * kind + step + 1, :] = value
            kept = chunk_rows(window.late, step, 0, window.first[step])
            there = chunk_rows(window.first, step)
            dscore_rows(dscores, there, weights, dprobs, kept, delta.astype(jnp.bfloat16))
            add_products(
                step == 0,
                slice(step * TQ, rows),
                (
                    (dv, scaled_by(dout_t, tile, late_factor), weights[kept, :]),
                    (dk, scaled_by(query_t, tile, late_factor), dscores[there, :]),
                ),
            )

        first_max = early_stats[step : step + 1, :]
        jobs.append((step, chunks, (query_t, dout_t, doc_start), first_max, end))
    exponentials(jobs, rows, heads, lambda job: position, scores)
    prev2_out[0:HD] = (dk[...] * SCALE).astype(prev2_out.dtype)
    prev2_out[HD : 2 * HD] = dv[...].astype(prev2_out.dtype)


def late_scores(slot, count, ready, early, prev1, prev2):
    rows = prev2.shape[0] // 2
    heads = ready[1].shape[1] // rows
    wide = heads * TQ
    window = Window(rows, slot)
    late = jax.ShapeDtypeStruct((sum(window.late) * CHUNK, wide), jnp.bfloat16)
    return pl.pallas_call(
        functools.partial(late_kernel, rows, heads, count, slot),
        out_shape=(
            *([late] * (2 - slot)),
            jax.ShapeDtypeStruct((sum(window.first) * CHUNK, wide), jnp.bfloat16),
            jax.ShapeDtypeStruct((24, wide), jnp.float32),
            jax.ShapeDtypeStruct((2 * HD, rows), jnp.bfloat16),
        ),
        in_specs=[VMEM] * 6,
        out_specs=[VMEM] * (5 - slot),
        scratch_shapes=[
            pltpu.VMEM((2, max(window.late) * CHUNK, wide), jnp.float32),
            pltpu.VMEM((HD, rows), jnp.float32),
            pltpu.VMEM((HD, rows), jnp.float32),
            *([pltpu.VMEM(late.shape, late.dtype)] * slot),
        ],
        compiler_params=pltpu.CompilerParams(vmem_limit_bytes=VMEM_LIMIT),
        cost_estimate=pl.CostEstimate(flops=2**31, bytes_accessed=0, transcendentals=0),
        name="late_far" if slot == 0 else "late_near",
    )(*ready[1:4], early[2], prev1, prev2)


def grads_kernel(rows, heads, slot, query_t, dout_t, stats, *refs):
    (late_w, late_dprobs, early_w, early_dprobs) = refs[0:4] if slot == 0 else (None, None) + refs[0:2]
    (dscores, prev1_out, own_out, dk, dv) = refs[4:] if slot == 0 else refs[2:]
    wide = heads * TQ
    window = Window(rows, slot)
    for step in reversed(window.steps):
        tile = slice(step * wide, (step + 1) * wide)
        late_factor, early_factor, delta = (
            stats[8 * kind + step : 8 * kind + step + 1, :] for kind in range(3)
        )
        beyond = window.late[step] - window.first[step]
        parts = [(beyond, early_w, early_dprobs, chunk_rows(window.early, step), early_factor)]
        if beyond:
            kept = chunk_rows(window.late, step, window.first[step])
            parts.append((0, late_w, late_dprobs, kept, late_factor))
        for start, weights, dprobs, kept, factor in parts:
            length = (kept.stop - kept.start) // CHUNK
            there = chunk_rows(window.rest, step, start, length)
            dscore_rows(dscores, there, weights, dprobs, kept, delta.astype(jnp.bfloat16))
            add_products(
                step == window.tiles - 1,
                slice(start * CHUNK, (start + length) * CHUNK),
                (
                    (dv, scaled_by(dout_t, tile, factor), weights[kept, :]),
                    (dk, scaled_by(query_t, tile, factor), dscores[there, :]),
                ),
            )
    prev1_out[0:HD] = (dk[:, 0:rows] * SCALE).astype(prev1_out.dtype)
    prev1_out[HD : 2 * HD] = dv[:, 0:rows].astype(prev1_out.dtype)
    own_out[0:HD] = dk[:, rows : 2 * rows] * SCALE
    own_out[HD : 2 * HD] = dv[:, rows : 2 * rows]


def rest_grads(slot, ready, early, late):
    rows = ready[0].shape[0] // 2
    heads = ready[1].shape[1] // rows
    rest = (sum(Window(rows, slot).rest) * CHUNK, heads * TQ)
    operands = (*ready[1:3], late[-2], *(late[0:2] if slot == 0 else ()), *early[0:2])
    return pl.pallas_call(
        functools.partial(grads_kernel, rows, heads, slot),
        out_shape=(
            jax.ShapeDtypeStruct(rest, jnp.bfloat16),
            jax.ShapeDtypeStruct((2 * HD, rows), jnp.bfloat16),
            jax.ShapeDtypeStruct((2 * HD, rows), jnp.float32),
        ),
        in_specs=[VMEM] * len(operands),
        out_specs=[VMEM] * 3,
        scratch_shapes=[pltpu.VMEM((HD, 2 * rows), jnp.float32)] * 2,
        compiler_params=pltpu.CompilerParams(vmem_limit_bytes=VMEM_LIMIT),
        cost_estimate=pl.CostEstimate(flops=2**31 if slot else 0, bytes_accessed=0, transcendentals=0),
        name="grads_far" if slot == 0 else "grads_near",
    )(*operands)


def outputs_kernel(rows, heads, *refs):
    blocks = (refs[0:8], refs[8:16])
    (attended, grad_query, keys_t, values_t) = refs[16:]
    for slot, block in enumerate(blocks):
        (own_kv, prev1, prev2, early_w, rest_d, late_w, first_d, stats) = block
        window = Window(rows, slot)
        own_rows = half_start(rows, slot)
        for place, source in enumerate((prev2, prev1, own_kv)):
            for tile in range(rows // TQ):
                part = slice(place * rows + tile * TQ, place * rows + (tile + 1) * TQ)
                row = tile * TQ
                keys_t[:, part] = jnp.transpose(source[row : row + TQ, :])
                values_t[:, part] = jnp.transpose(source[rows + row : rows + row + TQ, :])
        for step in window.steps:
            first, late = window.first[step], window.late[step]

            def product(side, terms, counts, start, skip, length):
                columns = slice(step * TQ + start * CHUNK, step * TQ + (start + length) * CHUNK)
                return dot_nn(side[:, columns], terms[chunk_rows(counts, step, skip, length), :])

            early = window.chunks - late
            late_factor = stats[step : step + 1, :]
            early_factor = stats[8 + step : 8 + step + 1, :]
            attended_t = product(values_t, late_w, window.late, 0, 0, late) * late_factor
            attended_t += product(values_t, early_w, window.early, late, 0, early) * early_factor
            late_t = product(keys_t, first_d, window.first, 0, 0, first)
            if late > first:
                late_t += product(keys_t, rest_d, window.rest, first, 0, late - first)
            early_t = product(keys_t, rest_d, window.rest, late, late - first, early)
            grad_query_t = late_t * (late_factor * SCALE) + early_t * (early_factor * SCALE)
            place = pl.ds(own_rows + step * TQ, TQ)
            for out, found in ((attended, attended_t), (grad_query, grad_query_t)):
                for h in range(heads):
                    part = found[:, h * TQ : (h + 1) * TQ]
                    out[place, h * HD : (h + 1) * HD] = jnp.transpose(part).astype(out.dtype)


def block_outputs(query, far, near):
    rows = query.shape[0] // 2
    heads = query.shape[1] // HD
    shape = jax.ShapeDtypeStruct(query.shape, query.dtype)
    return pl.pallas_call(
        functools.partial(outputs_kernel, rows, heads),
        out_shape=(shape, shape),
        in_specs=[VMEM] * 16,
        out_specs=[VMEM] * 2,
        scratch_shapes=[pltpu.VMEM((HD, 3 * rows), jnp.bfloat16)] * 2,
        compiler_params=pltpu.CompilerParams(vmem_limit_bytes=VMEM_LIMIT),
        cost_estimate=pl.CostEstimate(flops=0, bytes_accessed=0, transcendentals=0),
        name="block_outputs",
    )(*far, *near)


def total_kernel(rows, far_own, far_1, far_2, near, grad_key, grad_value):
    far = far_own[...] + far_1[...].astype(jnp.float32) + far_2[...].astype(jnp.float32)
    for slot, total in ((0, far), (1, near[...])):
        place = pl.ds(half_start(rows, slot), rows)
        grad_key[place, :] = jnp.transpose(total[0:HD]).astype(grad_key.dtype)
        grad_value[place, :] = jnp.transpose(total[HD : 2 * HD]).astype(grad_value.dtype)


def total_grads(*parts):
    rows = parts[0].shape[1]
    shape = jax.ShapeDtypeStruct((2 * rows, HD), jnp.bfloat16)
    return pl.pallas_call(
        functools.partial(total_kernel, rows),
        out_shape=(shape, shape),
        in_specs=[VMEM] * 4,
        out_specs=[VMEM] * 2,
        compiler_params=pltpu.CompilerParams(vmem_limit_bytes=VMEM_LIMIT),
        name="total_grads",
    )(*parts)


def body(query, key, value, d_out, doc_lengths):
    count = lax.axis_size("ctx")

    def holder(block):
        return block if block < count else 2 * count - 1 - block

    def move(array, pairs):
        return lax.ppermute(array, "ctx", pairs)

    near_on = [(holder(b), holder(b + 2)) for b in range(1, 2 * count - 2, 2)]
    far_on = [(holder(b), holder(b + 2)) for b in range(0, 2 * count - 2, 2)]
    near_to_far = [(holder(b), holder(b + 1)) for b in range(1, 2 * count - 2, 2)]
    swap = [(d, d ^ 1) for d in range(count)]
    near_back = [(t, s) for s, t in near_on]
    far_back = [(t, s) for s, t in far_on]

    rows = key.shape[0] // 2
    odd = lax.axis_index("ctx") % 2 == 1
    lower = jnp.concatenate([key[:rows], value[:rows]], axis=0)
    upper = jnp.concatenate([key[rows:], value[rows:]], axis=0)
    near_kv, far_kv = jnp.where(odd, lower, upper), jnp.where(odd, upper, lower)
    far_1 = move(near_kv, near_to_far)
    far_2 = move(far_kv, far_on)
    prepared = prepare(count, doc_lengths, query, d_out, far_kv, near_kv)
    far_ready, near_ready = prepared[0:4], prepared[4:8]
    near_1 = move(far_ready[0], swap)
    far_early = early_scores(0, count, far_ready)
    near_early = early_scores(1, count, near_ready, near_1)
    far_1, near_early = lax.optimization_barrier((far_1, near_early))
    far_late = late_scores(0, count, far_ready, far_early, far_1, far_2)
    from_far_2 = move(far_late[-1], far_back)
    far_1, far_stats = lax.optimization_barrier((far_1, far_late[-2]))
    near_2 = move(far_1, swap)
    near_2, far_early = lax.optimization_barrier((near_2, far_early))
    far_rest_d, far_g1, far_own = rest_grads(0, far_ready, far_early, far_late)
    relayed = move(far_g1, swap)
    near_late = late_scores(1, count, near_ready, near_early, near_1, near_2)
    near_sum = near_late[-1].astype(jnp.float32) + relayed.astype(jnp.float32)
    from_near_2 = move(near_sum.astype(jnp.bfloat16), near_back)
    near_rest_d, near_g1, near_own = rest_grads(1, near_ready, near_early, near_late)
    near_g1, from_far_2 = lax.optimization_barrier((near_g1, from_far_2))
    from_near_1 = move(near_g1, swap)
    attended, grad_query = block_outputs(
        query,
        (far_ready[0], far_1, far_2, far_early[0], far_rest_d, far_late[0], *far_late[-3:-1]),
        (near_ready[0], near_1, near_2, near_early[0], near_rest_d, near_late[0], *near_late[-3:-1]),
    )
    near_total = near_own + from_near_2.astype(jnp.float32)
    grad_key, grad_value = total_grads(far_own, from_near_1, from_far_2, near_total)
    return (attended, grad_query, grad_key, grad_value)


def solution(mesh):
    rows = P(("dp", "ctx"), None)
    return jax.shard_map(
        body,
        mesh=mesh,
        in_specs=(rows, rows, rows, rows, P("dp")),
        out_specs=(rows, rows, rows, rows),
        check_vma=False,
    )
```

```python
import functools
import math

import jax
import jax.numpy as jnp
from jax import lax
from jax.experimental import pallas as pl
from jax.experimental.pallas import tpu as pltpu
from jax.sharding import PartitionSpec as P

HD = 128
TQ = 128
GROUP = 32

masked_score = -1e30
VMEM_LIMIT = 24 * 1024 * 1024
SCALE = 1.0 / math.sqrt(HD)
VMEM = pl.BlockSpec(memory_space=pltpu.VMEM)
HBM = pl.BlockSpec(memory_space=pltpu.HBM)
CHUNK = 128


def dot_nt(a, b):
    return lax.dot_general(a, b, (((1,), (1,)), ((), ())), preferred_element_type=jnp.float32)


def dot_nn(a, b):
    return lax.dot_general(a, b, (((1,), (0,)), ((), ())), preferred_element_type=jnp.float32)


def half_start(rows, slot):
    odd = lax.axis_index("ctx") % 2
    return pl.multiple_of((odd if slot == 0 else 1 - odd) * rows, rows)


def block_number(count, slot):
    device = lax.axis_index("ctx")
    in_lower = device % 2 == slot
    return jnp.where(in_lower, device, 2 * count - 1 - device)


def in_hbm(array):
    return pltpu.with_memory_space_constraint(array, pltpu.HBM)


def load_block(rows, slot, key, value, out, sems):
    place = pl.ds(half_start(rows, slot), rows)
    return [
        pltpu.make_async_copy(key.at[place], out.at[0:rows], sems.at[2 * slot]),
        pltpu.make_async_copy(value.at[place], out.at[rows : 2 * rows], sems.at[2 * slot + 1]),
    ]


def run_copies(copies):
    for copy in copies:
        copy.start()
    for copy in copies:
        copy.wait()


def prepare_kernel(rows, heads, docs, count, *refs):
    (far_kv, near_kv, doc_hbm, query_hbm, dout_hbm) = refs[0:5]
    (doc_lengths, query, dout, sems) = refs[13:]
    refs = refs[5:13]
    wide = heads * TQ
    run_copies(
        [
            pltpu.make_async_copy(query_hbm, query, sems.at[0]),
            pltpu.make_async_copy(dout_hbm, dout, sems.at[1]),
            pltpu.make_async_copy(doc_hbm, doc_lengths, sems.at[2]),
        ]
    )
    for slot in (0, 1):
        own_kv, query_t, dout_t, doc_start = refs[4 * slot : 4 * slot + 4]
        own_kv[...] = (far_kv, near_kv)[slot][...]
        own_rows = half_start(rows, slot)
        for step in range(rows // TQ):
            source = pl.ds(own_rows + step * TQ, TQ)
            for h in range(heads):
                place = slice(step * wide + h * TQ, step * wide + (h + 1) * TQ)
                columns = slice(h * HD, (h + 1) * HD)
                query_t[:, place] = jnp.transpose(query[source, columns])
                dout_t[:, place] = jnp.transpose(dout[source, columns])
        at = (
            block_number(count, slot) * rows
            + lax.broadcasted_iota(jnp.int32, (8, TQ), 0) * TQ
            + lax.broadcasted_iota(jnp.int32, (8, TQ), 1)
        )

        def one(index, carry):
            start, found = carry
            found = jnp.where(at >= start, start, found)
            return (start + doc_lengths[index], found)

        _, found = lax.fori_loop(
            0, docs, one, (jnp.int32(0), jnp.zeros((8, TQ), jnp.int32)), unroll=8
        )
        doc_start[...] = found


def prepare(count, doc_lengths, query, dout, far_kv, near_kv):
    rows = query.shape[0] // 2
    heads = query.shape[1] // HD
    pair = jax.ShapeDtypeStruct(far_kv.shape, far_kv.dtype)
    stacked_t = jax.ShapeDtypeStruct((HD, rows * heads), query.dtype)
    starts = jax.ShapeDtypeStruct((8, TQ), jnp.int32)
    return pl.pallas_call(
        functools.partial(prepare_kernel, rows, heads, doc_lengths.shape[0], count),
        out_shape=(pair, stacked_t, stacked_t, starts) * 2,
        in_specs=[VMEM] * 2 + [HBM] * 3,
        out_specs=[VMEM] * 8,
        scratch_shapes=[
            pltpu.SMEM(doc_lengths.shape, doc_lengths.dtype),
            pltpu.VMEM(query.shape, query.dtype),
            pltpu.VMEM(dout.shape, dout.dtype),
            pltpu.SemaphoreType.DMA((3,)),
        ],
        compiler_params=pltpu.CompilerParams(vmem_limit_bytes=VMEM_LIMIT),
        cost_estimate=pl.CostEstimate(flops=0, bytes_accessed=4 * 2**20, transcendentals=0),
        name="prepare",
    )(far_kv, near_kv, *(in_hbm(array) for array in (doc_lengths, query, dout)))


class Window:
    def __init__(self, rows, slot):
        self.tiles = rows // TQ
        self.chunks = 2 * self.tiles + 1
        self.steps = range(self.tiles)
        self.first = [self.tiles - step for step in self.steps]
        self.rest = [self.chunks - first for first in self.first]
        self.late = [first + (1 - slot) * self.tiles for first in self.first]
        self.early = [self.chunks - late for late in self.late]


def chunk_rows(counts, step, first=0, count=None):
    start = sum(counts[:step]) + first
    count = counts[step] - first if count is None else count
    return slice(start * CHUNK, (start + count) * CHUNK)


def exponentials(jobs, rows, heads, block_pos, scores):
    back = 2 * rows
    wide = heads * TQ
    base2 = SCALE * math.log2(math.e)

    def score(job, index, row_max):
        step, chunks, (query_t, _, doc_start), _, _ = jobs[job]
        chunk, keys, row = chunks[index][0:3]
        low = doc_start[step : step + 1, :] - (block_pos(job) - back + step * TQ)
        high = lax.broadcasted_iota(jnp.int32, (1, TQ), 1) + back
        tile = slice(step * wide, (step + 1) * wide)
        product = dot_nn(keys[row : row + CHUNK, :], query_t[:, tile])
        for start in range(0, CHUNK, GROUP):
            place = chunk * CHUNK + start
            at = lax.broadcasted_iota(jnp.int32, (GROUP, TQ), 0) + place
            allowed = at >= low
            if place >= back:
                allowed = jnp.logical_and(allowed, at <= high)
            for h in range(heads):
                lanes = slice(h * TQ, (h + 1) * TQ)
                part = jnp.where(allowed, product[start : start + GROUP, lanes], masked_score)
                scores[job % 2, place : place + GROUP, lanes] = part
                for row8 in range(0, GROUP, 8):
                    row_max[h] = jnp.maximum(row_max[h], part[row8 : row8 + 8, :])

    def start_max():
        return [jnp.full((8, TQ), masked_score, jnp.float32)] * heads

    following = start_max()
    for index in range(len(jobs[0][1])):
        score(0, index, following)
    for job, (step, chunks, (_, dout_t, _), first_max, end) in enumerate(jobs):
        tile = slice(step * wide, (step + 1) * wide)
        row_max = jnp.concatenate(
            [jnp.max(part, axis=0, keepdims=True) * base2 for part in following], axis=1
        )
        if first_max is not None:
            row_max = jnp.maximum(row_max, first_max)
        following = start_max()
        ahead = len(jobs[job + 1][1]) if job + 1 < len(jobs) else 0
        done = 0
        total = [jnp.zeros((8, TQ), jnp.float32)] * heads
        delta = [jnp.zeros((8, TQ), jnp.float32)] * heads
        for index, (chunk, keys, row, weights, dprobs, kept) in enumerate(chunks):
            product = dot_nn(keys[rows + row : rows + row + CHUNK, :], dout_t[:, tile])
            for start in range(0, CHUNK, GROUP):
                place = chunk * CHUNK + start
                there = slice(kept.start + start, kept.start + start + GROUP)
                for h in range(heads):
                    lanes = slice(h * TQ, (h + 1) * TQ)
                    dprob = product[start : start + GROUP, lanes]
                    dprobs[there, lanes] = dprob.astype(jnp.bfloat16)
                    part = scores[job % 2, place : place + GROUP, lanes]
                    part = jnp.exp2(part * base2 - row_max[:, lanes])
                    weights[there, lanes] = part.astype(jnp.bfloat16)
                    term = part * dprob
                    for row8 in range(0, GROUP, 8):
                        total[h] = total[h] + part[row8 : row8 + 8, :]
                        delta[h] = delta[h] + term[row8 : row8 + 8, :]
            while done * len(chunks) < ahead * (index + 1):
                score(job + 1, done, following)
                done += 1
        sums = (
            jnp.concatenate([jnp.sum(part, axis=0, keepdims=True) for part in parts], axis=1)
            for parts in (total, delta)
        )
        end(row_max, *sums)


def early_kernel(rows, heads, count, slot, own_kv, query_t, dout_t, doc_start, *refs):
    (weights, dprobs, stats, scores) = refs[-4:]
    prev1 = refs[0] if slot == 1 else None
    window = Window(rows, slot)
    position = block_number(count, slot) * rows
    jobs = []
    for step in window.steps:
        chunks = []
        for index in range(window.early[step]):
            chunk = window.late[step] + index
            row = step * TQ + chunk * CHUNK
            keys = own_kv if row >= 2 * rows else prev1
            kept = chunk_rows(window.early, step, index, 1)
            chunks.append((chunk, keys, row % rows, weights, dprobs, kept))

        def end(*found, step=step):
            for kind, value in enumerate(found):
                stats[8 * kind + step : 8 * kind + step + 1, :] = value

        jobs.append((step, chunks, (query_t, dout_t, doc_start), None, end))
    exponentials(jobs, rows, heads, lambda job: position, scores)


def early_scores(slot, count, ready, *prev1):
    rows = ready[0].shape[0] // 2
    heads = ready[1].shape[1] // rows
    wide = heads * TQ
    kept = jax.ShapeDtypeStruct((sum(Window(rows, slot).early) * CHUNK, wide), jnp.bfloat16)
    return pl.pallas_call(
        functools.partial(early_kernel, rows, heads, count, slot),
        out_shape=(kept, kept, jax.ShapeDtypeStruct((24, wide), jnp.float32)),
        in_specs=[VMEM] * (4 + len(prev1)),
        out_specs=[VMEM] * 3,
        scratch_shapes=[pltpu.VMEM((2, 2 * rows + TQ, wide), jnp.float32)],
        compiler_params=pltpu.CompilerParams(vmem_limit_bytes=VMEM_LIMIT),
        cost_estimate=pl.CostEstimate(flops=0 if slot else 2**33, bytes_accessed=0, transcendentals=0),
        name="early_far" if slot == 0 else "early_near",
    )(*ready, *prev1)


def scaled_by(array, tile, factor):
    return (array[:, tile].astype(jnp.float32) * factor).astype(jnp.bfloat16)


def dscore_rows(dscores, there, weights, dprobs, kept, delta):
    delta = jnp.broadcast_to(delta, (16, delta.shape[1]))
    for start in range(0, there.stop - there.start, 16):
        out = slice(there.start + start, there.start + start + 16)
        place = slice(kept.start + start, kept.start + start + 16)
        dscores[out, :] = weights[place, :] * (dprobs[place, :] - delta)


def add_products(new, columns, products):
    for total_ref, side, terms in products:
        term = dot_nt(side, terms)
        if new:
            total_ref[:, columns] = term
        else:
            total_ref[:, columns] += term


def late_kernel(
    rows,
    heads,
    count,
    slot,
    query_t,
    dout_t,
    doc_start,
    early_stats,
    prev1,
    prev2,
    weights,
    *refs,
):
    (dprobs, dscores, stats, prev2_out, scores, dk, dv) = refs if slot == 0 else refs[-1:] + refs[:-1]
    wide = heads * TQ
    window = Window(rows, slot)
    position = block_number(count, slot) * rows
    jobs = []
    for step in window.steps:
        chunks = []
        for chunk in range(window.late[step]):
            row = step * TQ + chunk * CHUNK
            kept = chunk_rows(window.late, step, chunk, 1)
            chunks.append((chunk, (prev2, prev1)[row // rows], row % rows, weights, dprobs, kept))

        def end(row_max, total, delta, step=step):
            tile = slice(step * wide, (step + 1) * wide)
            early = [early_stats[8 * kind + step : 8 * kind + step + 1, :] for kind in range(3)]
            shrink = jnp.exp2(early[0] - row_max)
            late_factor = 1.0 / (total + early[1] * shrink)
            early_factor = late_factor * shrink
            delta = delta * late_factor + early[2] * early_factor
            for kind, value in enumerate((late_factor, early_factor, delta)):
                stats[8 * kind + step : 8 * kind + step + 1, :] = value
            kept = chunk_rows(window.late, step, 0, window.first[step])
            there = chunk_rows(window.first, step)
            dscore_rows(dscores, there, weights, dprobs, kept, delta.astype(jnp.bfloat16))
            add_products(
                step == 0,
                slice(step * TQ, rows),
                (
                    (dv, scaled_by(dout_t, tile, late_factor), weights[kept, :]),
                    (dk, scaled_by(query_t, tile, late_factor), dscores[there, :]),
                ),
            )

        first_max = early_stats[step : step + 1, :]
        jobs.append((step, chunks, (query_t, dout_t, doc_start), first_max, end))
    exponentials(jobs, rows, heads, lambda job: position, scores)
    prev2_out[0:HD] = (dk[...] * SCALE).astype(prev2_out.dtype)
    prev2_out[HD : 2 * HD] = dv[...].astype(prev2_out.dtype)


def late_scores(slot, count, ready, early, prev1, prev2):
    rows = prev2.shape[0] // 2
    heads = ready[1].shape[1] // rows
    wide = heads * TQ
    window = Window(rows, slot)
    late = jax.ShapeDtypeStruct((sum(window.late) * CHUNK, wide), jnp.bfloat16)
    return pl.pallas_call(
        functools.partial(late_kernel, rows, heads, count, slot),
        out_shape=(
            *([late] * (2 - slot)),
            jax.ShapeDtypeStruct((sum(window.first) * CHUNK, wide), jnp.bfloat16),
            jax.ShapeDtypeStruct((24, wide), jnp.float32),
            jax.ShapeDtypeStruct((2 * HD, rows), jnp.bfloat16),
        ),
        in_specs=[VMEM] * 6,
        out_specs=[VMEM] * (5 - slot),
        scratch_shapes=[
            pltpu.VMEM((2, max(window.late) * CHUNK, wide), jnp.float32),
            pltpu.VMEM((HD, rows), jnp.float32),
            pltpu.VMEM((HD, rows), jnp.float32),
            *([pltpu.VMEM(late.shape, late.dtype)] * slot),
        ],
        compiler_params=pltpu.CompilerParams(vmem_limit_bytes=VMEM_LIMIT),
        cost_estimate=pl.CostEstimate(flops=2**31, bytes_accessed=0, transcendentals=0),
        name="late_far" if slot == 0 else "late_near",
    )(*ready[1:4], early[2], prev1, prev2)


def grads_kernel(rows, heads, slot, query_t, dout_t, stats, *refs):
    (late_w, late_dprobs, early_w, early_dprobs) = refs[0:4] if slot == 0 else (None, None) + refs[0:2]
    (dscores, prev1_out, own_out, dk, dv) = refs[4:] if slot == 0 else refs[2:]
    wide = heads * TQ
    window = Window(rows, slot)
    for step in reversed(window.steps):
        tile = slice(step * wide, (step + 1) * wide)
        late_factor, early_factor, delta = (
            stats[8 * kind + step : 8 * kind + step + 1, :] for kind in range(3)
        )
        beyond = window.late[step] - window.first[step]
        parts = [(beyond, early_w, early_dprobs, chunk_rows(window.early, step), early_factor)]
        if beyond:
            kept = chunk_rows(window.late, step, window.first[step])
            parts.append((0, late_w, late_dprobs, kept, late_factor))
        for start, weights, dprobs, kept, factor in parts:
            length = (kept.stop - kept.start) // CHUNK
            there = chunk_rows(window.rest, step, start, length)
            dscore_rows(dscores, there, weights, dprobs, kept, delta.astype(jnp.bfloat16))
            add_products(
                step == window.tiles - 1,
                slice(start * CHUNK, (start + length) * CHUNK),
                (
                    (dv, scaled_by(dout_t, tile, factor), weights[kept, :]),
                    (dk, scaled_by(query_t, tile, factor), dscores[there, :]),
                ),
            )
    prev1_out[0:HD] = (dk[:, 0:rows] * SCALE).astype(prev1_out.dtype)
    prev1_out[HD : 2 * HD] = dv[:, 0:rows].astype(prev1_out.dtype)
    own_out[0:HD] = dk[:, rows : 2 * rows] * SCALE
    own_out[HD : 2 * HD] = dv[:, rows : 2 * rows]


def rest_grads(slot, ready, early, late):
    rows = ready[0].shape[0] // 2
    heads = ready[1].shape[1] // rows
    rest = (sum(Window(rows, slot).rest) * CHUNK, heads * TQ)
    operands = (*ready[1:3], late[-2], *(late[0:2] if slot == 0 else ()), *early[0:2])
    return pl.pallas_call(
        functools.partial(grads_kernel, rows, heads, slot),
        out_shape=(
            jax.ShapeDtypeStruct(rest, jnp.bfloat16),
            jax.ShapeDtypeStruct((2 * HD, rows), jnp.bfloat16),
            jax.ShapeDtypeStruct((2 * HD, rows), jnp.float32),
        ),
        in_specs=[VMEM] * len(operands),
        out_specs=[VMEM] * 3,
        scratch_shapes=[pltpu.VMEM((HD, 2 * rows), jnp.float32)] * 2,
        compiler_params=pltpu.CompilerParams(vmem_limit_bytes=VMEM_LIMIT),
        cost_estimate=pl.CostEstimate(flops=2**31 if slot else 0, bytes_accessed=0, transcendentals=0),
        name="grads_far" if slot == 0 else "grads_near",
    )(*operands)


def outputs_kernel(rows, heads, *refs):
    blocks = (refs[0:8], refs[8:16])
    (attended, grad_query, keys_t, values_t) = refs[16:]
    for slot, block in enumerate(blocks):
        (own_kv, prev1, prev2, early_w, rest_d, late_w, first_d, stats) = block
        window = Window(rows, slot)
        own_rows = half_start(rows, slot)
        for place, source in enumerate((prev2, prev1, own_kv)):
            for tile in range(rows // TQ):
                part = slice(place * rows + tile * TQ, place * rows + (tile + 1) * TQ)
                row = tile * TQ
                keys_t[:, part] = jnp.transpose(source[row : row + TQ, :])
                values_t[:, part] = jnp.transpose(source[rows + row : rows + row + TQ, :])
        for step in window.steps:
            first, late = window.first[step], window.late[step]

            def product(side, terms, counts, start, skip, length):
                columns = slice(step * TQ + start * CHUNK, step * TQ + (start + length) * CHUNK)
                return dot_nn(side[:, columns], terms[chunk_rows(counts, step, skip, length), :])

            early = window.chunks - late
            late_factor = stats[step : step + 1, :]
            early_factor = stats[8 + step : 8 + step + 1, :]
            attended_t = product(values_t, late_w, window.late, 0, 0, late) * late_factor
            attended_t += product(values_t, early_w, window.early, late, 0, early) * early_factor
            late_t = product(keys_t, first_d, window.first, 0, 0, first)
            if late > first:
                late_t += product(keys_t, rest_d, window.rest, first, 0, late - first)
            early_t = product(keys_t, rest_d, window.rest, late, late - first, early)
            grad_query_t = late_t * (late_factor * SCALE) + early_t * (early_factor * SCALE)
            place = pl.ds(own_rows + step * TQ, TQ)
            for out, found in ((attended, attended_t), (grad_query, grad_query_t)):
                for h in range(heads):
                    part = found[:, h * TQ : (h + 1) * TQ]
                    out[place, h * HD : (h + 1) * HD] = jnp.transpose(part).astype(out.dtype)


def block_outputs(query, far, near):
    rows = query.shape[0] // 2
    heads = query.shape[1] // HD
    shape = jax.ShapeDtypeStruct(query.shape, query.dtype)
    return pl.pallas_call(
        functools.partial(outputs_kernel, rows, heads),
        out_shape=(shape, shape),
        in_specs=[VMEM] * 16,
        out_specs=[VMEM] * 2,
        scratch_shapes=[pltpu.VMEM((HD, 3 * rows), jnp.bfloat16)] * 2,
        compiler_params=pltpu.CompilerParams(vmem_limit_bytes=VMEM_LIMIT),
        cost_estimate=pl.CostEstimate(flops=0, bytes_accessed=0, transcendentals=0),
        name="block_outputs",
    )(*far, *near)


def total_kernel(rows, far_own, far_1, far_2, near, grad_key, grad_value):
    far = far_own[...] + far_1[...].astype(jnp.float32) + far_2[...].astype(jnp.float32)
    for slot, total in ((0, far), (1, near[...])):
        place = pl.ds(half_start(rows, slot), rows)
        grad_key[place, :] = jnp.transpose(total[0:HD]).astype(grad_key.dtype)
        grad_value[place, :] = jnp.transpose(total[HD : 2 * HD]).astype(grad_value.dtype)


def total_grads(*parts):
    rows = parts[0].shape[1]
    shape = jax.ShapeDtypeStruct((2 * rows, HD), jnp.bfloat16)
    return pl.pallas_call(
        functools.partial(total_kernel, rows),
        out_shape=(shape, shape),
        in_specs=[VMEM] * 4,
        out_specs=[VMEM] * 2,
        compiler_params=pltpu.CompilerParams(vmem_limit_bytes=VMEM_LIMIT),
        name="total_grads",
    )(*parts)


def body(query, key, value, d_out, doc_lengths):
    count = lax.axis_size("ctx")

    def holder(block):
        return block if block < count else 2 * count - 1 - block

    def move(array, pairs):
        return lax.ppermute(array, "ctx", pairs)

    near_on = [(holder(b), holder(b + 2)) for b in range(1, 2 * count - 2, 2)]
    far_on = [(holder(b), holder(b + 2)) for b in range(0, 2 * count - 2, 2)]
    near_to_far = [(holder(b), holder(b + 1)) for b in range(1, 2 * count - 2, 2)]
    swap = [(d, d ^ 1) for d in range(count)]
    near_back = [(t, s) for s, t in near_on]
    far_back = [(t, s) for s, t in far_on]

    rows = key.shape[0] // 2
    odd = lax.axis_index("ctx") % 2 == 1
    lower = jnp.concatenate([key[:rows], value[:rows]], axis=0)
    upper = jnp.concatenate([key[rows:], value[rows:]], axis=0)
    near_kv, far_kv = jnp.where(odd, lower, upper), jnp.where(odd, upper, lower)
    far_1 = move(near_kv, near_to_far)
    far_2 = move(far_kv, far_on)
    prepared = prepare(count, doc_lengths, query, d_out, far_kv, near_kv)
    far_ready, near_ready = prepared[0:4], prepared[4:8]
    near_1 = move(far_ready[0], swap)
    far_early = early_scores(0, count, far_ready)
    near_early = early_scores(1, count, near_ready, near_1)
    far_1, near_early = lax.optimization_barrier((far_1, near_early))
    far_late = late_scores(0, count, far_ready, far_early, far_1, far_2)
    from_far_2 = move(far_late[-1], far_back)
    near_2 = move(far_1, swap)
    far_rest_d, far_g1, far_own = rest_grads(0, far_ready, far_early, far_late)
    relayed = move(far_g1, swap)
    near_late = late_scores(1, count, near_ready, near_early, near_1, near_2)
    near_sum = near_late[-1].astype(jnp.float32) + relayed.astype(jnp.float32)
    from_near_2 = move(near_sum.astype(jnp.bfloat16), near_back)
    near_rest_d, near_g1, near_own = rest_grads(1, near_ready, near_early, near_late)
    near_g1, from_far_2 = lax.optimization_barrier((near_g1, from_far_2))
    from_near_1 = move(near_g1, swap)
    attended, grad_query = block_outputs(
        query,
        (far_ready[0], far_1, far_2, far_early[0], far_rest_d, far_late[0], *far_late[-3:-1]),
        (near_ready[0], near_1, near_2, near_early[0], near_rest_d, near_late[0], *near_late[-3:-1]),
    )
    near_total = near_own + from_near_2.astype(jnp.float32)
    grad_key, grad_value = total_grads(far_own, from_near_1, from_far_2, near_total)
    return (attended, grad_query, grad_key, grad_value)


def solution(mesh):
    rows = P(("dp", "ctx"), None)
    return jax.shard_map(
        body,
        mesh=mesh,
        in_specs=(rows, rows, rows, rows, P("dp")),
        out_specs=(rows, rows, rows, rows),
        check_vma=False,
    )
```

```python
import functools
import math

import jax
import jax.numpy as jnp
from jax import lax
from jax.experimental import pallas as pl
from jax.experimental.pallas import tpu as pltpu
from jax.sharding import PartitionSpec as P

HD = 128
TQ = 128
GROUP = 32

masked_score = -1e30
VMEM_LIMIT = 24 * 1024 * 1024
SCALE = 1.0 / math.sqrt(HD)
VMEM = pl.BlockSpec(memory_space=pltpu.VMEM)
HBM = pl.BlockSpec(memory_space=pltpu.HBM)
CHUNK = 128


def dot_nt(a, b):
    return lax.dot_general(a, b, (((1,), (1,)), ((), ())), preferred_element_type=jnp.float32)


def dot_nn(a, b):
    return lax.dot_general(a, b, (((1,), (0,)), ((), ())), preferred_element_type=jnp.float32)


def half_start(rows, slot):
    odd = lax.axis_index("ctx") % 2
    return pl.multiple_of((odd if slot == 0 else 1 - odd) * rows, rows)


def block_number(count, slot):
    device = lax.axis_index("ctx")
    in_lower = device % 2 == slot
    return jnp.where(in_lower, device, 2 * count - 1 - device)


def in_hbm(array):
    return pltpu.with_memory_space_constraint(array, pltpu.HBM)


def load_block(rows, slot, key, value, out, sems):
    place = pl.ds(half_start(rows, slot), rows)
    return [
        pltpu.make_async_copy(key.at[place], out.at[0:rows], sems.at[2 * slot]),
        pltpu.make_async_copy(value.at[place], out.at[rows : 2 * rows], sems.at[2 * slot + 1]),
    ]


def run_copies(copies):
    for copy in copies:
        copy.start()
    for copy in copies:
        copy.wait()


def prepare_kernel(rows, heads, docs, count, *refs):
    (far_kv, near_kv, doc_hbm, query_hbm, dout_hbm) = refs[0:5]
    (doc_lengths, query, dout, sems) = refs[13:]
    refs = refs[5:13]
    wide = heads * TQ
    run_copies(
        [
            pltpu.make_async_copy(query_hbm, query, sems.at[0]),
            pltpu.make_async_copy(dout_hbm, dout, sems.at[1]),
            pltpu.make_async_copy(doc_hbm, doc_lengths, sems.at[2]),
        ]
    )
    for slot in (0, 1):
        own_kv, query_t, dout_t, doc_start = refs[4 * slot : 4 * slot + 4]
        own_kv[...] = (far_kv, near_kv)[slot][...]
        own_rows = half_start(rows, slot)
        for step in range(rows // TQ):
            source = pl.ds(own_rows + step * TQ, TQ)
            for h in range(heads):
                place = slice(step * wide + h * TQ, step * wide + (h + 1) * TQ)
                columns = slice(h * HD, (h + 1) * HD)
                query_t[:, place] = jnp.transpose(query[source, columns])
                dout_t[:, place] = jnp.transpose(dout[source, columns])
        at = (
            block_number(count, slot) * rows
            + lax.broadcasted_iota(jnp.int32, (8, TQ), 0) * TQ
            + lax.broadcasted_iota(jnp.int32, (8, TQ), 1)
        )

        def one(index, carry):
            start, found = carry
            found = jnp.where(at >= start, start, found)
            return (start + doc_lengths[index], found)

        _, found = lax.fori_loop(
            0, docs, one, (jnp.int32(0), jnp.zeros((8, TQ), jnp.int32)), unroll=8
        )
        doc_start[...] = found


def prepare(count, doc_lengths, query, dout, far_kv, near_kv):
    rows = query.shape[0] // 2
    heads = query.shape[1] // HD
    pair = jax.ShapeDtypeStruct(far_kv.shape, far_kv.dtype)
    stacked_t = jax.ShapeDtypeStruct((HD, rows * heads), query.dtype)
    starts = jax.ShapeDtypeStruct((8, TQ), jnp.int32)
    return pl.pallas_call(
        functools.partial(prepare_kernel, rows, heads, doc_lengths.shape[0], count),
        out_shape=(pair, stacked_t, stacked_t, starts) * 2,
        in_specs=[VMEM] * 2 + [HBM] * 3,
        out_specs=[VMEM] * 8,
        scratch_shapes=[
            pltpu.SMEM(doc_lengths.shape, doc_lengths.dtype),
            pltpu.VMEM(query.shape, query.dtype),
            pltpu.VMEM(dout.shape, dout.dtype),
            pltpu.SemaphoreType.DMA((3,)),
        ],
        compiler_params=pltpu.CompilerParams(vmem_limit_bytes=VMEM_LIMIT),
        cost_estimate=pl.CostEstimate(flops=0, bytes_accessed=4 * 2**20, transcendentals=0),
        name="prepare",
    )(far_kv, near_kv, *(in_hbm(array) for array in (doc_lengths, query, dout)))


class Window:
    def __init__(self, rows, slot):
        self.tiles = rows // TQ
        self.chunks = 2 * self.tiles + 1
        self.steps = range(self.tiles)
        self.first = [self.tiles - step for step in self.steps]
        self.rest = [self.chunks - first for first in self.first]
        self.late = [first + (1 - slot) * self.tiles for first in self.first]
        self.early = [self.chunks - late for late in self.late]


def chunk_rows(counts, step, first=0, count=None):
    start = sum(counts[:step]) + first
    count = counts[step] - first if count is None else count
    return slice(start * CHUNK, (start + count) * CHUNK)


def exponentials(jobs, rows, heads, block_pos, scores):
    back = 2 * rows
    wide = heads * TQ
    base2 = SCALE * math.log2(math.e)

    def score(job, index, row_max):
        step, chunks, (query_t, _, doc_start), _, _ = jobs[job]
        chunk, keys, row = chunks[index][0:3]
        low = doc_start[step : step + 1, :] - (block_pos(job) - back + step * TQ)
        high = lax.broadcasted_iota(jnp.int32, (1, TQ), 1) + back
        tile = slice(step * wide, (step + 1) * wide)
        product = dot_nn(keys[row : row + CHUNK, :], query_t[:, tile])
        for start in range(0, CHUNK, GROUP):
            place = chunk * CHUNK + start
            at = lax.broadcasted_iota(jnp.int32, (GROUP, TQ), 0) + place
            allowed = at >= low
            if place >= back:
                allowed = jnp.logical_and(allowed, at <= high)
            for h in range(heads):
                lanes = slice(h * TQ, (h + 1) * TQ)
                part = jnp.where(allowed, product[start : start + GROUP, lanes], masked_score)
                scores[job % 2, place : place + GROUP, lanes] = part
                for row8 in range(0, GROUP, 8):
                    row_max[h] = jnp.maximum(row_max[h], part[row8 : row8 + 8, :])

    def start_max():
        return [jnp.full((8, TQ), masked_score, jnp.float32)] * heads

    pending = None
    following = start_max()
    for index in range(len(jobs[0][1])):
        score(0, index, following)
    for job, (step, chunks, (_, dout_t, _), first_max, end) in enumerate(jobs):
        tile = slice(step * wide, (step + 1) * wide)
        row_max = jnp.concatenate(
            [jnp.max(part, axis=0, keepdims=True) * base2 for part in following], axis=1
        )
        if first_max is not None:
            row_max = jnp.maximum(row_max, first_max)
        following = start_max()
        ahead = len(jobs[job + 1][1]) if job + 1 < len(jobs) else 0
        done = 0
        total = jnp.zeros((8, wide), jnp.float32)
        delta = jnp.zeros((8, wide), jnp.float32)
        for index, (chunk, keys, row, weights, dprobs, kept) in enumerate(chunks):
            product = dot_nn(keys[rows + row : rows + row + CHUNK, :], dout_t[:, tile])
            for start in range(0, CHUNK, GROUP):
                place = chunk * CHUNK + start
                there = slice(kept.start + start, kept.start + start + GROUP)
                dprob = product[start : start + GROUP, :]
                dprobs[there, :] = dprob.astype(jnp.bfloat16)
                part = jnp.exp2(scores[job % 2, place : place + GROUP, :] * base2 - row_max)
                weights[there, :] = part.astype(jnp.bfloat16)
                term = part * dprob
                for row8 in range(0, GROUP, 8):
                    total = total + part[row8 : row8 + 8, :]
                    delta = delta + term[row8 : row8 + 8, :]
            while done * len(chunks) < ahead * (index + 1):
                score(job + 1, done, following)
                done += 1
            if index == 0 and pending is not None:
                pending()
        sums = [jnp.sum(part, axis=0, keepdims=True) for part in (total, delta)]
        pending = functools.partial(end, row_max, *sums)
    pending()


def early_kernel(rows, heads, count, slot, own_kv, query_t, dout_t, doc_start, *refs):
    (weights, dprobs, stats, scores) = refs[-4:]
    prev1 = refs[0] if slot == 1 else None
    window = Window(rows, slot)
    position = block_number(count, slot) * rows
    jobs = []
    for step in window.steps:
        chunks = []
        for index in range(window.early[step]):
            chunk = window.late[step] + index
            row = step * TQ + chunk * CHUNK
            keys = own_kv if row >= 2 * rows else prev1
            kept = chunk_rows(window.early, step, index, 1)
            chunks.append((chunk, keys, row % rows, weights, dprobs, kept))

        def end(*found, step=step):
            for kind, value in enumerate(found):
                stats[8 * kind + step : 8 * kind + step + 1, :] = value

        jobs.append((step, chunks, (query_t, dout_t, doc_start), None, end))
    exponentials(jobs, rows, heads, lambda job: position, scores)


def early_scores(slot, count, ready, *prev1):
    rows = ready[0].shape[0] // 2
    heads = ready[1].shape[1] // rows
    wide = heads * TQ
    kept = jax.ShapeDtypeStruct((sum(Window(rows, slot).early) * CHUNK, wide), jnp.bfloat16)
    return pl.pallas_call(
        functools.partial(early_kernel, rows, heads, count, slot),
        out_shape=(kept, kept, jax.ShapeDtypeStruct((24, wide), jnp.float32)),
        in_specs=[VMEM] * (4 + len(prev1)),
        out_specs=[VMEM] * 3,
        scratch_shapes=[pltpu.VMEM((2, 2 * rows + TQ, wide), jnp.float32)],
        compiler_params=pltpu.CompilerParams(vmem_limit_bytes=VMEM_LIMIT),
        cost_estimate=pl.CostEstimate(flops=0 if slot else 2**33, bytes_accessed=0, transcendentals=0),
        name="early_far" if slot == 0 else "early_near",
    )(*ready, *prev1)


def scaled_by(array, tile, factor):
    return (array[:, tile].astype(jnp.float32) * factor).astype(jnp.bfloat16)


def dscore_rows(dscores, there, weights, dprobs, kept, delta):
    delta = jnp.broadcast_to(delta, (16, delta.shape[1]))
    for start in range(0, there.stop - there.start, 16):
        out = slice(there.start + start, there.start + start + 16)
        place = slice(kept.start + start, kept.start + start + 16)
        dscores[out, :] = weights[place, :] * (dprobs[place, :] - delta)


def add_products(new, columns, products):
    for total_ref, side, terms in products:
        term = dot_nt(side, terms)
        if new:
            total_ref[:, columns] = term
        else:
            total_ref[:, columns] += term


def late_kernel(
    rows,
    heads,
    count,
    slot,
    query_t,
    dout_t,
    doc_start,
    early_stats,
    prev1,
    prev2,
    weights,
    *refs,
):
    (dprobs, dscores, stats, prev2_out, scores, dk, dv) = refs if slot == 0 else refs[-1:] + refs[:-1]
    wide = heads * TQ
    window = Window(rows, slot)
    position = block_number(count, slot) * rows
    jobs = []
    for step in window.steps:
        chunks = []
        for chunk in range(window.late[step]):
            row = step * TQ + chunk * CHUNK
            kept = chunk_rows(window.late, step, chunk, 1)
            chunks.append((chunk, (prev2, prev1)[row // rows], row % rows, weights, dprobs, kept))

        def end(row_max, total, delta, step=step):
            tile = slice(step * wide, (step + 1) * wide)
            early = [early_stats[8 * kind + step : 8 * kind + step + 1, :] for kind in range(3)]
            shrink = jnp.exp2(early[0] - row_max)
            late_factor = 1.0 / (total + early[1] * shrink)
            early_factor = late_factor * shrink
            delta = delta * late_factor + early[2] * early_factor
            for kind, value in enumerate((late_factor, early_factor, delta)):
                stats[8 * kind + step : 8 * kind + step + 1, :] = value
            kept = chunk_rows(window.late, step, 0, window.first[step])
            there = chunk_rows(window.first, step)
            dscore_rows(dscores, there, weights, dprobs, kept, delta.astype(jnp.bfloat16))
            add_products(
                step == 0,
                slice(step * TQ, rows),
                (
                    (dv, scaled_by(dout_t, tile, late_factor), weights[kept, :]),
                    (dk, scaled_by(query_t, tile, late_factor), dscores[there, :]),
                ),
            )

        first_max = early_stats[step : step + 1, :]
        jobs.append((step, chunks, (query_t, dout_t, doc_start), first_max, end))
    exponentials(jobs, rows, heads, lambda job: position, scores)
    prev2_out[0:HD] = (dk[...] * SCALE).astype(prev2_out.dtype)
    prev2_out[HD : 2 * HD] = dv[...].astype(prev2_out.dtype)


def late_scores(slot, count, ready, early, prev1, prev2):
    rows = prev2.shape[0] // 2
    heads = ready[1].shape[1] // rows
    wide = heads * TQ
    window = Window(rows, slot)
    late = jax.ShapeDtypeStruct((sum(window.late) * CHUNK, wide), jnp.bfloat16)
    return pl.pallas_call(
        functools.partial(late_kernel, rows, heads, count, slot),
        out_shape=(
            *([late] * (2 - slot)),
            jax.ShapeDtypeStruct((sum(window.first) * CHUNK, wide), jnp.bfloat16),
            jax.ShapeDtypeStruct((24, wide), jnp.float32),
            jax.ShapeDtypeStruct((2 * HD, rows), jnp.bfloat16),
        ),
        in_specs=[VMEM] * 6,
        out_specs=[VMEM] * (5 - slot),
        scratch_shapes=[
            pltpu.VMEM((2, max(window.late) * CHUNK, wide), jnp.float32),
            pltpu.VMEM((HD, rows), jnp.float32),
            pltpu.VMEM((HD, rows), jnp.float32),
            *([pltpu.VMEM(late.shape, late.dtype)] * slot),
        ],
        compiler_params=pltpu.CompilerParams(vmem_limit_bytes=VMEM_LIMIT),
        cost_estimate=pl.CostEstimate(flops=2**31, bytes_accessed=0, transcendentals=0),
        name="late_far" if slot == 0 else "late_near",
    )(*ready[1:4], early[2], prev1, prev2)


def grads_kernel(rows, heads, slot, query_t, dout_t, stats, *refs):
    (late_w, late_dprobs, early_w, early_dprobs) = refs[0:4] if slot == 0 else (None, None) + refs[0:2]
    (dscores, prev1_out, own_out, dk, dv) = refs[4:] if slot == 0 else refs[2:]
    wide = heads * TQ
    window = Window(rows, slot)
    for step in reversed(window.steps):
        tile = slice(step * wide, (step + 1) * wide)
        late_factor, early_factor, delta = (
            stats[8 * kind + step : 8 * kind + step + 1, :] for kind in range(3)
        )
        beyond = window.late[step] - window.first[step]
        parts = [(beyond, early_w, early_dprobs, chunk_rows(window.early, step), early_factor)]
        if beyond:
            kept = chunk_rows(window.late, step, window.first[step])
            parts.append((0, late_w, late_dprobs, kept, late_factor))
        for start, weights, dprobs, kept, factor in parts:
            length = (kept.stop - kept.start) // CHUNK
            there = chunk_rows(window.rest, step, start, length)
            dscore_rows(dscores, there, weights, dprobs, kept, delta.astype(jnp.bfloat16))
            add_products(
                step == window.tiles - 1,
                slice(start * CHUNK, (start + length) * CHUNK),
                (
                    (dv, scaled_by(dout_t, tile, factor), weights[kept, :]),
                    (dk, scaled_by(query_t, tile, factor), dscores[there, :]),
                ),
            )
    prev1_out[0:HD] = (dk[:, 0:rows] * SCALE).astype(prev1_out.dtype)
    prev1_out[HD : 2 * HD] = dv[:, 0:rows].astype(prev1_out.dtype)
    own_out[0:HD] = dk[:, rows : 2 * rows] * SCALE
    own_out[HD : 2 * HD] = dv[:, rows : 2 * rows]


def rest_grads(slot, ready, early, late):
    rows = ready[0].shape[0] // 2
    heads = ready[1].shape[1] // rows
    rest = (sum(Window(rows, slot).rest) * CHUNK, heads * TQ)
    operands = (*ready[1:3], late[-2], *(late[0:2] if slot == 0 else ()), *early[0:2])
    return pl.pallas_call(
        functools.partial(grads_kernel, rows, heads, slot),
        out_shape=(
            jax.ShapeDtypeStruct(rest, jnp.bfloat16),
            jax.ShapeDtypeStruct((2 * HD, rows), jnp.bfloat16),
            jax.ShapeDtypeStruct((2 * HD, rows), jnp.float32),
        ),
        in_specs=[VMEM] * len(operands),
        out_specs=[VMEM] * 3,
        scratch_shapes=[pltpu.VMEM((HD, 2 * rows), jnp.float32)] * 2,
        compiler_params=pltpu.CompilerParams(vmem_limit_bytes=VMEM_LIMIT),
        cost_estimate=pl.CostEstimate(flops=2**31 if slot else 0, bytes_accessed=0, transcendentals=0),
        name="grads_far" if slot == 0 else "grads_near",
    )(*operands)


def outputs_kernel(rows, heads, *refs):
    blocks = (refs[0:8], refs[8:16])
    (attended, grad_query, keys_t, values_t) = refs[16:]
    for slot, block in enumerate(blocks):
        (own_kv, prev1, prev2, early_w, rest_d, late_w, first_d, stats) = block
        window = Window(rows, slot)
        own_rows = half_start(rows, slot)
        for place, source in enumerate((prev2, prev1, own_kv)):
            for tile in range(rows // TQ):
                part = slice(place * rows + tile * TQ, place * rows + (tile + 1) * TQ)
                row = tile * TQ
                keys_t[:, part] = jnp.transpose(source[row : row + TQ, :])
                values_t[:, part] = jnp.transpose(source[rows + row : rows + row + TQ, :])
        for step in window.steps:
            first, late = window.first[step], window.late[step]

            def product(side, terms, counts, start, skip, length):
                columns = slice(step * TQ + start * CHUNK, step * TQ + (start + length) * CHUNK)
                return dot_nn(side[:, columns], terms[chunk_rows(counts, step, skip, length), :])

            early = window.chunks - late
            late_factor = stats[step : step + 1, :]
            early_factor = stats[8 + step : 8 + step + 1, :]
            attended_t = product(values_t, late_w, window.late, 0, 0, late) * late_factor
            attended_t += product(values_t, early_w, window.early, late, 0, early) * early_factor
            late_t = product(keys_t, first_d, window.first, 0, 0, first)
            if late > first:
                late_t += product(keys_t, rest_d, window.rest, first, 0, late - first)
            early_t = product(keys_t, rest_d, window.rest, late, late - first, early)
            grad_query_t = late_t * (late_factor * SCALE) + early_t * (early_factor * SCALE)
            place = pl.ds(own_rows + step * TQ, TQ)
            for out, found in ((attended, attended_t), (grad_query, grad_query_t)):
                for h in range(heads):
                    part = found[:, h * TQ : (h + 1) * TQ]
                    out[place, h * HD : (h + 1) * HD] = jnp.transpose(part).astype(out.dtype)


def block_outputs(query, far, near):
    rows = query.shape[0] // 2
    heads = query.shape[1] // HD
    shape = jax.ShapeDtypeStruct(query.shape, query.dtype)
    return pl.pallas_call(
        functools.partial(outputs_kernel, rows, heads),
        out_shape=(shape, shape),
        in_specs=[VMEM] * 16,
        out_specs=[VMEM] * 2,
        scratch_shapes=[pltpu.VMEM((HD, 3 * rows), jnp.bfloat16)] * 2,
        compiler_params=pltpu.CompilerParams(vmem_limit_bytes=VMEM_LIMIT),
        cost_estimate=pl.CostEstimate(flops=0, bytes_accessed=0, transcendentals=0),
        name="block_outputs",
    )(*far, *near)


def total_kernel(rows, far_own, far_1, far_2, near, grad_key, grad_value):
    far = far_own[...] + far_1[...].astype(jnp.float32) + far_2[...].astype(jnp.float32)
    for slot, total in ((0, far), (1, near[...])):
        place = pl.ds(half_start(rows, slot), rows)
        grad_key[place, :] = jnp.transpose(total[0:HD]).astype(grad_key.dtype)
        grad_value[place, :] = jnp.transpose(total[HD : 2 * HD]).astype(grad_value.dtype)


def total_grads(*parts):
    rows = parts[0].shape[1]
    shape = jax.ShapeDtypeStruct((2 * rows, HD), jnp.bfloat16)
    return pl.pallas_call(
        functools.partial(total_kernel, rows),
        out_shape=(shape, shape),
        in_specs=[VMEM] * 4,
        out_specs=[VMEM] * 2,
        compiler_params=pltpu.CompilerParams(vmem_limit_bytes=VMEM_LIMIT),
        name="total_grads",
    )(*parts)


def body(query, key, value, d_out, doc_lengths):
    count = lax.axis_size("ctx")

    def holder(block):
        return block if block < count else 2 * count - 1 - block

    def move(array, pairs):
        return lax.ppermute(array, "ctx", pairs)

    near_on = [(holder(b), holder(b + 2)) for b in range(1, 2 * count - 2, 2)]
    far_on = [(holder(b), holder(b + 2)) for b in range(0, 2 * count - 2, 2)]
    near_to_far = [(holder(b), holder(b + 1)) for b in range(1, 2 * count - 2, 2)]
    swap = [(d, d ^ 1) for d in range(count)]
    near_back = [(t, s) for s, t in near_on]
    far_back = [(t, s) for s, t in far_on]

    rows = key.shape[0] // 2
    odd = lax.axis_index("ctx") % 2 == 1
    lower = jnp.concatenate([key[:rows], value[:rows]], axis=0)
    upper = jnp.concatenate([key[rows:], value[rows:]], axis=0)
    near_kv, far_kv = jnp.where(odd, lower, upper), jnp.where(odd, upper, lower)
    far_1 = move(near_kv, near_to_far)
    far_2 = move(far_kv, far_on)
    prepared = prepare(count, doc_lengths, query, d_out, far_kv, near_kv)
    far_ready, near_ready = prepared[0:4], prepared[4:8]
    near_1 = move(far_ready[0], swap)
    far_early = early_scores(0, count, far_ready)
    near_early = early_scores(1, count, near_ready, near_1)
    far_1, near_early = lax.optimization_barrier((far_1, near_early))
    far_late = late_scores(0, count, far_ready, far_early, far_1, far_2)
    from_far_2 = move(far_late[-1], far_back)
    near_2 = move(far_1, swap)
    far_rest_d, far_g1, far_own = rest_grads(0, far_ready, far_early, far_late)
    relayed = move(far_g1, swap)
    near_late = late_scores(1, count, near_ready, near_early, near_1, near_2)
    near_sum = near_late[-1].astype(jnp.float32) + relayed.astype(jnp.float32)
    from_near_2 = move(near_sum.astype(jnp.bfloat16), near_back)
    near_rest_d, near_g1, near_own = rest_grads(1, near_ready, near_early, near_late)
    near_g1, from_far_2 = lax.optimization_barrier((near_g1, from_far_2))
    from_near_1 = move(near_g1, swap)
    attended, grad_query = block_outputs(
        query,
        (far_ready[0], far_1, far_2, far_early[0], far_rest_d, far_late[0], *far_late[-3:-1]),
        (near_ready[0], near_1, near_2, near_early[0], near_rest_d, near_late[0], *near_late[-3:-1]),
    )
    near_total = near_own + from_near_2.astype(jnp.float32)
    grad_key, grad_value = total_grads(far_own, from_near_1, from_far_2, near_total)
    return (attended, grad_query, grad_key, grad_value)


def solution(mesh):
    rows = P(("dp", "ctx"), None)
    return jax.shard_map(
        body,
        mesh=mesh,
        in_specs=(rows, rows, rows, rows, P("dp")),
        out_specs=(rows, rows, rows, rows),
        check_vma=False,
    )
```

```python
import functools
import math

import jax
import jax.numpy as jnp
from jax import lax
from jax.experimental import pallas as pl
from jax.experimental.pallas import tpu as pltpu
from jax.sharding import PartitionSpec as P

HD = 128
TQ = 128
GROUP = 32

masked_score = -1e30
other_document = -65536.0
VMEM_LIMIT = 24 * 1024 * 1024
SCALE = 1.0 / math.sqrt(HD)
VMEM = pl.BlockSpec(memory_space=pltpu.VMEM)
HBM = pl.BlockSpec(memory_space=pltpu.HBM)
CHUNK = 128


def dot_nt(a, b):
    return lax.dot_general(a, b, (((1,), (1,)), ((), ())), preferred_element_type=jnp.float32)


def dot_nn(a, b):
    return lax.dot_general(a, b, (((1,), (0,)), ((), ())), preferred_element_type=jnp.float32)


def half_start(rows, slot):
    odd = lax.axis_index("ctx") % 2
    return pl.multiple_of((odd if slot == 0 else 1 - odd) * rows, rows)


def block_number(count, slot):
    device = lax.axis_index("ctx")
    in_lower = device % 2 == slot
    return jnp.where(in_lower, device, 2 * count - 1 - device)


def in_hbm(array):
    return pltpu.with_memory_space_constraint(array, pltpu.HBM)


def load_block(rows, slot, key, value, out, sems):
    place = pl.ds(half_start(rows, slot), rows)
    return [
        pltpu.make_async_copy(key.at[place], out.at[0:rows], sems.at[2 * slot]),
        pltpu.make_async_copy(value.at[place], out.at[rows : 2 * rows], sems.at[2 * slot + 1]),
    ]


def run_copies(copies):
    for copy in copies:
        copy.start()
    for copy in copies:
        copy.wait()


def prepare_kernel(rows, heads, docs, count, *refs):
    (far_kv, near_kv, doc_hbm, query_hbm, dout_hbm) = refs[0:5]
    (doc_lengths, query, dout, sems) = refs[13:]
    refs = refs[5:13]
    wide = heads * TQ
    run_copies(
        [
            pltpu.make_async_copy(query_hbm, query, sems.at[0]),
            pltpu.make_async_copy(dout_hbm, dout, sems.at[1]),
            pltpu.make_async_copy(doc_hbm, doc_lengths, sems.at[2]),
        ]
    )
    lane = lax.broadcasted_iota(jnp.int32, (1, HD), 1)

    def one(index, carry):
        start, starts, ends = carry
        end = start + doc_lengths[index]
        starts = jnp.where(lane == index, start, starts)
        return (end, starts, jnp.where(lane == index, end, ends))

    none = jnp.zeros((1, HD), jnp.int32)
    _, starts, ends = lax.fori_loop(0, docs, one, (jnp.int32(0), none, none), unroll=8)
    starts_t, ends_t = (
        jnp.transpose(jnp.broadcast_to(row.astype(jnp.float32), (HD, HD))).astype(jnp.int32)
        for row in (starts, ends)
    )
    for slot in (0, 1):
        own_kv, query_t, dout_t, documents = refs[4 * slot : 4 * slot + 4]
        own_kv[...] = (far_kv, near_kv)[slot][...]
        own_rows = half_start(rows, slot)
        for step in range(rows // TQ):
            source = pl.ds(own_rows + step * TQ, TQ)
            for h in range(heads):
                place = slice(step * wide + h * TQ, step * wide + (h + 1) * TQ)
                columns = slice(h * HD, (h + 1) * HD)
                query_t[0:HD, place] = jnp.transpose(query[source, columns])
                dout_t[:, place] = jnp.transpose(dout[source, columns])
        position = block_number(count, slot) * rows
        for tile in range(3 * rows // TQ):
            at = lax.broadcasted_iota(jnp.int32, (TQ, HD), 0) + (position - 2 * rows + tile * TQ)
            inside = jnp.logical_and(at >= starts, at < ends)
            inside = jnp.logical_or(inside, at < 0)
            documents[tile * TQ : (tile + 1) * TQ, :] = jnp.where(inside, 1.0, 0.0).astype(
                documents.dtype
            )
        for step in range(rows // TQ):
            at = lax.broadcasted_iota(jnp.int32, (HD, TQ), 1) + (position + step * TQ)
            inside = jnp.logical_and(at >= starts_t, at < ends_t)
            other = jnp.where(inside, 0.0, other_document).astype(query_t.dtype)
            for h in range(heads):
                place = slice(step * wide + h * TQ, step * wide + (h + 1) * TQ)
                query_t[HD : 2 * HD, place] = other


def prepare(count, doc_lengths, query, dout, far_kv, near_kv):
    rows = query.shape[0] // 2
    heads = query.shape[1] // HD
    pair = jax.ShapeDtypeStruct(far_kv.shape, far_kv.dtype)
    stacked_t = jax.ShapeDtypeStruct((HD, rows * heads), query.dtype)
    query_shape = jax.ShapeDtypeStruct((2 * HD, rows * heads), query.dtype)
    documents = jax.ShapeDtypeStruct((3 * rows, HD), query.dtype)
    assert doc_lengths.shape[0] <= HD
    return pl.pallas_call(
        functools.partial(prepare_kernel, rows, heads, doc_lengths.shape[0], count),
        out_shape=(pair, query_shape, stacked_t, documents) * 2,
        in_specs=[VMEM] * 2 + [HBM] * 3,
        out_specs=[VMEM] * 8,
        scratch_shapes=[
            pltpu.SMEM(doc_lengths.shape, doc_lengths.dtype),
            pltpu.VMEM(query.shape, query.dtype),
            pltpu.VMEM(dout.shape, dout.dtype),
            pltpu.SemaphoreType.DMA((3,)),
        ],
        compiler_params=pltpu.CompilerParams(vmem_limit_bytes=VMEM_LIMIT),
        cost_estimate=pl.CostEstimate(flops=0, bytes_accessed=4 * 2**20, transcendentals=0),
        name="prepare",
    )(far_kv, near_kv, *(in_hbm(array) for array in (doc_lengths, query, dout)))


class Window:
    def __init__(self, rows, slot):
        self.tiles = rows // TQ
        self.chunks = 2 * self.tiles + 1
        self.steps = range(self.tiles)
        self.first = [self.tiles - step for step in self.steps]
        self.late = [first + (1 - slot) * self.tiles for first in self.first]
        self.early = [self.chunks - late for late in self.late]
        self.middle = [late - first for late, first in zip(self.late, self.first)]


def chunk_rows(counts, step, first=0, count=None):
    start = sum(counts[:step]) + first
    count = counts[step] - first if count is None else count
    return slice(start * CHUNK, (start + count) * CHUNK)


def exponentials(jobs, rows, heads, scores):
    back = 2 * rows
    wide = heads * TQ
    base2 = SCALE * math.log2(math.e)

    def score(job, index, row_max):
        step, chunks, (query_t, _, documents), _, _ = jobs[job]
        chunk, keys, row = chunks[index][0:3]
        tile = slice(step * wide, (step + 1) * wide)
        window = slice(step * TQ + chunk * CHUNK, step * TQ + (chunk + 1) * CHUNK)
        product = dot_nn(
            jnp.concatenate([keys[row : row + CHUNK, :], documents[window, :]], axis=1),
            query_t[:, tile],
        )
        for start in range(0, CHUNK, GROUP):
            place = chunk * CHUNK + start
            for h in range(heads):
                lanes = slice(h * TQ, (h + 1) * TQ)
                part = product[start : start + GROUP, lanes]
                if place >= back:
                    key_at = lax.broadcasted_iota(jnp.int32, (GROUP, TQ), 0) + (place - back)
                    query_at = lax.broadcasted_iota(jnp.int32, (GROUP, TQ), 1)
                    part = jnp.where(key_at <= query_at, part, masked_score)
                scores[job % 2, place : place + GROUP, lanes] = part
                for row8 in range(0, GROUP, 8):
                    row_max[h] = jnp.maximum(row_max[h], part[row8 : row8 + 8, :])

    def start_max():
        return [jnp.full((8, TQ), masked_score, jnp.float32)] * heads

    pending = None
    following = start_max()
    for index in range(len(jobs[0][1])):
        score(0, index, following)
    for job, (step, chunks, (_, dout_t, _), first_max, end) in enumerate(jobs):
        tile = slice(step * wide, (step + 1) * wide)
        row_max = jnp.concatenate(
            [jnp.max(part, axis=0, keepdims=True) * base2 for part in following], axis=1
        )
        if first_max is not None:
            row_max = jnp.maximum(row_max, first_max)
        following = start_max()
        ahead = len(jobs[job + 1][1]) if job + 1 < len(jobs) else 0
        done = 0
        total = jnp.zeros((8, wide), jnp.float32)
        delta = jnp.zeros((8, wide), jnp.float32)
        for index, (chunk, keys, row, weights, dprobs, kept) in enumerate(chunks):
            product = dot_nn(keys[rows + row : rows + row + CHUNK, :], dout_t[:, tile])
            for start in range(0, CHUNK, GROUP):
                place = chunk * CHUNK + start
                there = slice(kept.start + start, kept.start + start + GROUP)
                dprob = product[start : start + GROUP, :]
                dprobs[there, :] = dprob.astype(jnp.bfloat16)
                part = jnp.exp2(scores[job % 2, place : place + GROUP, :] * base2 - row_max)
                weights[there, :] = part.astype(jnp.bfloat16)
                term = part * dprob
                for row8 in range(0, GROUP, 8):
                    total = total + part[row8 : row8 + 8, :]
                    delta = delta + term[row8 : row8 + 8, :]
            while done * len(chunks) < ahead * (index + 1):
                score(job + 1, done, following)
                done += 1
            if index == 0 and pending is not None:
                pending()
        sums = [jnp.sum(part, axis=0, keepdims=True) for part in (total, delta)]
        pending = functools.partial(end, row_max, *sums)
    pending()


def early_kernel(rows, heads, slot, own_kv, query_t, dout_t, documents, *refs):
    (weights, dprobs, stats, scores) = refs[-4:]
    prev1 = refs[0] if slot == 1 else None
    window = Window(rows, slot)
    jobs = []
    for step in window.steps:
        chunks = []
        for index in range(window.early[step]):
            chunk = window.late[step] + index
            row = step * TQ + chunk * CHUNK
            keys = own_kv if row >= 2 * rows else prev1
            kept = chunk_rows(window.early, step, index, 1)
            chunks.append((chunk, keys, row % rows, weights, dprobs, kept))

        def end(*found, step=step):
            for kind, value in enumerate(found):
                stats[8 * kind + step : 8 * kind + step + 1, :] = value

        jobs.append((step, chunks, (query_t, dout_t, documents), None, end))
    exponentials(jobs, rows, heads, scores)


def early_scores(slot, ready, *prev1):
    rows = ready[0].shape[0] // 2
    heads = ready[1].shape[1] // rows
    wide = heads * TQ
    kept = jax.ShapeDtypeStruct((sum(Window(rows, slot).early) * CHUNK, wide), jnp.bfloat16)
    return pl.pallas_call(
        functools.partial(early_kernel, rows, heads, slot),
        out_shape=(kept, kept, jax.ShapeDtypeStruct((24, wide), jnp.float32)),
        in_specs=[VMEM] * (4 + len(prev1)),
        out_specs=[VMEM] * 3,
        scratch_shapes=[pltpu.VMEM((2, 2 * rows + TQ, wide), jnp.float32)],
        compiler_params=pltpu.CompilerParams(vmem_limit_bytes=VMEM_LIMIT),
        cost_estimate=pl.CostEstimate(flops=0 if slot else 2**33, bytes_accessed=0, transcendentals=0),
        name="early_far" if slot == 0 else "early_near",
    )(*ready, *prev1)


def scaled_by(array, tile, factor):
    return (array[0:HD, tile].astype(jnp.float32) * factor).astype(jnp.bfloat16)


def dscore_rows(dscores, there, weights, dprobs, kept, delta):
    delta = jnp.broadcast_to(delta, (16, delta.shape[1]))
    for start in range(0, there.stop - there.start, 16):
        out = slice(there.start + start, there.start + start + 16)
        place = slice(kept.start + start, kept.start + start + 16)
        dscores[out, :] = weights[place, :] * (dprobs[place, :] - delta)


def add_products(new, columns, products):
    for total_ref, side, terms in products:
        term = dot_nt(side, terms)
        if new:
            total_ref[:, columns] = term
        else:
            total_ref[:, columns] += term


def late_kernel(
    rows,
    heads,
    slot,
    query_t,
    dout_t,
    documents,
    early_stats,
    prev1,
    prev2,
    weights,
    *refs,
):
    (dprobs, dscores, stats, prev2_out, scores, dk, dv) = refs if slot == 0 else refs[-1:] + refs[:-1]
    wide = heads * TQ
    window = Window(rows, slot)
    jobs = []
    for step in window.steps:
        chunks = []
        for chunk in range(window.late[step]):
            row = step * TQ + chunk * CHUNK
            kept = chunk_rows(window.late, step, chunk, 1)
            chunks.append((chunk, (prev2, prev1)[row // rows], row % rows, weights, dprobs, kept))

        def end(row_max, total, delta, step=step):
            tile = slice(step * wide, (step + 1) * wide)
            early = [early_stats[8 * kind + step : 8 * kind + step + 1, :] for kind in range(3)]
            shrink = jnp.exp2(early[0] - row_max)
            late_factor = 1.0 / (total + early[1] * shrink)
            early_factor = late_factor * shrink
            delta = delta * late_factor + early[2] * early_factor
            for kind, value in enumerate((late_factor, early_factor, delta)):
                stats[8 * kind + step : 8 * kind + step + 1, :] = value
            kept = chunk_rows(window.late, step, 0, window.first[step])
            there = chunk_rows(window.first, step)
            dscore_rows(dscores, there, weights, dprobs, kept, delta.astype(jnp.bfloat16))
            add_products(
                step == 0,
                slice(step * TQ, rows),
                (
                    (dv, scaled_by(dout_t, tile, late_factor), weights[kept, :]),
                    (dk, scaled_by(query_t, tile, late_factor), dscores[there, :]),
                ),
            )

        first_max = early_stats[step : step + 1, :]
        jobs.append((step, chunks, (query_t, dout_t, documents), first_max, end))
    exponentials(jobs, rows, heads, scores)
    prev2_out[0:HD] = (dk[...] * SCALE).astype(prev2_out.dtype)
    prev2_out[HD : 2 * HD] = dv[...].astype(prev2_out.dtype)


def late_scores(slot, ready, early, prev1, prev2):
    rows = prev2.shape[0] // 2
    heads = ready[1].shape[1] // rows
    wide = heads * TQ
    window = Window(rows, slot)
    late = jax.ShapeDtypeStruct((sum(window.late) * CHUNK, wide), jnp.bfloat16)
    return pl.pallas_call(
        functools.partial(late_kernel, rows, heads, slot),
        out_shape=(
            *([late] * (2 - slot)),
            jax.ShapeDtypeStruct((sum(window.first) * CHUNK, wide), jnp.bfloat16),
            jax.ShapeDtypeStruct((24, wide), jnp.float32),
            jax.ShapeDtypeStruct((2 * HD, rows), jnp.bfloat16),
        ),
        in_specs=[VMEM] * 6,
        out_specs=[VMEM] * (5 - slot),
        scratch_shapes=[
            pltpu.VMEM((2, max(window.late) * CHUNK, wide), jnp.float32),
            pltpu.VMEM((HD, rows), jnp.float32),
            pltpu.VMEM((HD, rows), jnp.float32),
            *([pltpu.VMEM(late.shape, late.dtype)] * slot),
        ],
        compiler_params=pltpu.CompilerParams(vmem_limit_bytes=VMEM_LIMIT),
        cost_estimate=pl.CostEstimate(flops=2**31, bytes_accessed=0, transcendentals=0),
        name="late_far" if slot == 0 else "late_near",
    )(*ready[1:4], early[2], prev1, prev2)


def grads_kernel(rows, heads, slots, *refs):
    wide = heads * TQ
    outs = list(refs[5 * len(slots) : -2])
    (dk, dv) = refs[-2:]
    for part, (slot, late) in enumerate(slots):
        (query_t, dout_t, stats, weights, dprobs) = refs[5 * part : 5 * part + 5]
        dscores = outs.pop(0)
        window = Window(rows, slot)
        counts = window.middle if late else window.early
        for step in reversed(window.steps):
            tile = slice(step * wide, (step + 1) * wide)
            late_factor, early_factor, delta = (
                stats[8 * kind + step : 8 * kind + step + 1, :] for kind in range(3)
            )
            factor = late_factor if late else early_factor
            there = chunk_rows(counts, step)
            kept = chunk_rows(window.late, step, window.first[step]) if late else there
            dscore_rows(dscores, there, weights, dprobs, kept, delta.astype(jnp.bfloat16))
            add_products(
                step == window.tiles - 1,
                slice(0, counts[step] * CHUNK),
                (
                    (dv, scaled_by(dout_t, tile, factor), weights[kept, :]),
                    (dk, scaled_by(query_t, tile, factor), dscores[there, :]),
                ),
            )
        for block in range(counts[-1] // window.tiles):
            out = outs.pop(0)
            place = slice(block * rows, (block + 1) * rows)
            out[0:HD] = (dk[:, place] * SCALE).astype(out.dtype)
            out[HD : 2 * HD] = dv[:, place].astype(out.dtype)


def rest_grads(name, cost, parts):
    rows = parts[0][2][0].shape[0] // 2
    heads = parts[0][2][1].shape[1] // rows
    operands, out_shape = [], []
    for slot, late, (_, query_t, dout_t, _, stats, weights, dprobs), sent in parts:
        window = Window(rows, slot)
        kept = (sum(window.middle if late else window.early) * CHUNK, heads * TQ)
        operands += [query_t, dout_t, stats, weights, dprobs]
        out_shape.append(jax.ShapeDtypeStruct(kept, jnp.bfloat16))
        for one in sent:
            kind = jnp.bfloat16 if one else jnp.float32
            out_shape.append(jax.ShapeDtypeStruct((2 * HD, rows), kind))
    slots = tuple(part[0:2] for part in parts)
    return pl.pallas_call(
        functools.partial(grads_kernel, rows, heads, slots),
        out_shape=out_shape,
        in_specs=[VMEM] * len(operands),
        out_specs=[VMEM] * len(out_shape),
        scratch_shapes=[pltpu.VMEM((HD, 2 * rows), jnp.float32)] * 2,
        compiler_params=pltpu.CompilerParams(vmem_limit_bytes=VMEM_LIMIT),
        cost_estimate=pl.CostEstimate(flops=cost, bytes_accessed=0, transcendentals=0),
        name=name,
    )(*operands)


def outputs_kernel(rows, heads, *refs):
    blocks = (refs[0:9], refs[9:17])
    (attended, grad_query, keys_t, values_t) = refs[17:]
    for slot, block in enumerate(blocks):
        (own_kv, prev1, prev2, early_w, early_d, late_w, first_d, stats) = block[0:8]
        window = Window(rows, slot)
        own_rows = half_start(rows, slot)
        for place, source in enumerate((prev2, prev1, own_kv)):
            for tile in range(rows // TQ):
                part = slice(place * rows + tile * TQ, place * rows + (tile + 1) * TQ)
                row = tile * TQ
                keys_t[:, part] = jnp.transpose(source[row : row + TQ, :])
                values_t[:, part] = jnp.transpose(source[rows + row : rows + row + TQ, :])
        for step in window.steps:
            first, late = window.first[step], window.late[step]

            def product(side, terms, counts, start, skip, length):
                columns = slice(step * TQ + start * CHUNK, step * TQ + (start + length) * CHUNK)
                return dot_nn(side[:, columns], terms[chunk_rows(counts, step, skip, length), :])

            early = window.chunks - late
            late_factor = stats[step : step + 1, :]
            early_factor = stats[8 + step : 8 + step + 1, :]
            attended_t = product(values_t, late_w, window.late, 0, 0, late) * late_factor
            attended_t += product(values_t, early_w, window.early, late, 0, early) * early_factor
            late_t = product(keys_t, first_d, window.first, 0, 0, first)
            if late > first:
                late_t += product(keys_t, block[8], window.middle, first, 0, late - first)
            early_t = product(keys_t, early_d, window.early, late, 0, early)
            grad_query_t = late_t * (late_factor * SCALE) + early_t * (early_factor * SCALE)
            place = pl.ds(own_rows + step * TQ, TQ)
            for out, found in ((attended, attended_t), (grad_query, grad_query_t)):
                for h in range(heads):
                    part = found[:, h * TQ : (h + 1) * TQ]
                    out[place, h * HD : (h + 1) * HD] = jnp.transpose(part).astype(out.dtype)


def block_outputs(query, far, near):
    rows = query.shape[0] // 2
    heads = query.shape[1] // HD
    shape = jax.ShapeDtypeStruct(query.shape, query.dtype)
    return pl.pallas_call(
        functools.partial(outputs_kernel, rows, heads),
        out_shape=(shape, shape),
        in_specs=[VMEM] * 17,
        out_specs=[VMEM] * 2,
        scratch_shapes=[pltpu.VMEM((HD, 3 * rows), jnp.bfloat16)] * 2,
        compiler_params=pltpu.CompilerParams(vmem_limit_bytes=VMEM_LIMIT),
        cost_estimate=pl.CostEstimate(flops=0, bytes_accessed=0, transcendentals=0),
        name="block_outputs",
    )(*far, *near)


def total_kernel(rows, far_own, far_1, far_2, near, grad_key, grad_value):
    far = far_own[...] + far_1[...].astype(jnp.float32) + far_2[...].astype(jnp.float32)
    for slot, total in ((0, far), (1, near[...])):
        place = pl.ds(half_start(rows, slot), rows)
        grad_key[place, :] = jnp.transpose(total[0:HD]).astype(grad_key.dtype)
        grad_value[place, :] = jnp.transpose(total[HD : 2 * HD]).astype(grad_value.dtype)


def total_grads(*parts):
    rows = parts[0].shape[1]
    shape = jax.ShapeDtypeStruct((2 * rows, HD), jnp.bfloat16)
    return pl.pallas_call(
        functools.partial(total_kernel, rows),
        out_shape=(shape, shape),
        in_specs=[VMEM] * 4,
        out_specs=[VMEM] * 2,
        compiler_params=pltpu.CompilerParams(vmem_limit_bytes=VMEM_LIMIT),
        name="total_grads",
    )(*parts)


def body(query, key, value, d_out, doc_lengths):
    count = lax.axis_size("ctx")

    def holder(block):
        return block if block < count else 2 * count - 1 - block

    def move(array, pairs):
        return lax.ppermute(array, "ctx", pairs)

    near_on = [(holder(b), holder(b + 2)) for b in range(1, 2 * count - 2, 2)]
    far_on = [(holder(b), holder(b + 2)) for b in range(0, 2 * count - 2, 2)]
    near_to_far = [(holder(b), holder(b + 1)) for b in range(1, 2 * count - 2, 2)]
    swap = [(d, d ^ 1) for d in range(count)]
    near_back = [(t, s) for s, t in near_on]
    far_back = [(t, s) for s, t in far_on]

    rows = key.shape[0] // 2
    odd = lax.axis_index("ctx") % 2 == 1
    lower = jnp.concatenate([key[:rows], value[:rows]], axis=0)
    upper = jnp.concatenate([key[rows:], value[rows:]], axis=0)
    near_kv, far_kv = jnp.where(odd, lower, upper), jnp.where(odd, upper, lower)
    far_1 = move(near_kv, near_to_far)
    far_2 = move(far_kv, far_on)
    prepared = prepare(count, doc_lengths, query, d_out, far_kv, near_kv)
    far_ready, near_ready = prepared[0:4], prepared[4:8]
    near_1 = move(far_ready[0], swap)
    far_early = early_scores(0, far_ready)
    near_early = early_scores(1, near_ready, near_1)
    far_1, near_early = lax.optimization_barrier((far_1, near_early))
    far_late = late_scores(0, far_ready, far_early, far_1, far_2)
    from_far_2 = move(far_late[-1], far_back)
    near_2 = move(far_1, swap)
    near_2, far_stats = lax.optimization_barrier((near_2, far_late[-2]))
    far_middle_d, far_g1 = rest_grads(
        "grads_far", 0, [(0, True, (*far_ready, far_stats, *far_late[0:2]), (True,))]
    )
    relayed = move(far_g1, swap)
    near_late = late_scores(1, near_ready, near_early, near_1, near_2)
    near_sum = near_late[-1].astype(jnp.float32) + relayed.astype(jnp.float32)
    from_near_2 = move(near_sum.astype(jnp.bfloat16), near_back)
    near_early_d, near_g1, near_own, far_early_d, far_own = rest_grads(
        "grads_near",
        2**31,
        [
            (1, False, (*near_ready, near_late[-2], *near_early[0:2]), (True, False)),
            (0, False, (*far_ready, far_late[-2], *far_early[0:2]), (False,)),
        ],
    )
    near_g1, from_far_2 = lax.optimization_barrier((near_g1, from_far_2))
    from_near_1 = move(near_g1, swap)
    attended, grad_query = block_outputs(
        query,
        (far_ready[0], far_1, far_2, far_early[0], far_early_d, far_late[0], *far_late[-3:-1], far_middle_d),
        (near_ready[0], near_1, near_2, near_early[0], near_early_d, near_late[0], *near_late[-3:-1]),
    )
    near_total = near_own + from_near_2.astype(jnp.float32)
    grad_key, grad_value = total_grads(far_own, from_near_1, from_far_2, near_total)
    return (attended, grad_query, grad_key, grad_value)


def solution(mesh):
    rows = P(("dp", "ctx"), None)
    return jax.shard_map(
        body,
        mesh=mesh,
        in_specs=(rows, rows, rows, rows, P("dp")),
        out_specs=(rows, rows, rows, rows),
        check_vma=False,
    )
```

```python
import functools
import math

import jax
import jax.numpy as jnp
from jax import lax
from jax.experimental import pallas as pl
from jax.experimental.pallas import tpu as pltpu
from jax.sharding import PartitionSpec as P

HD = 128
TQ = 128
GROUP = 32

masked_score = -1e30
other_document = -65536.0
VMEM_LIMIT = 24 * 1024 * 1024
SCALE = 1.0 / math.sqrt(HD)
VMEM = pl.BlockSpec(memory_space=pltpu.VMEM)
HBM = pl.BlockSpec(memory_space=pltpu.HBM)
CHUNK = 128
RUN = 3


def dot_nt(a, b):
    return lax.dot_general(a, b, (((1,), (1,)), ((), ())), preferred_element_type=jnp.float32)


def dot_nn(a, b):
    return lax.dot_general(a, b, (((1,), (0,)), ((), ())), preferred_element_type=jnp.float32)


def half_start(rows, slot):
    odd = lax.axis_index("ctx") % 2
    return pl.multiple_of((odd if slot == 0 else 1 - odd) * rows, rows)


def block_number(count, slot):
    device = lax.axis_index("ctx")
    in_lower = device % 2 == slot
    return jnp.where(in_lower, device, 2 * count - 1 - device)


def in_hbm(array):
    return pltpu.with_memory_space_constraint(array, pltpu.HBM)


def load_block(rows, slot, key, value, out, sems):
    place = pl.ds(half_start(rows, slot), rows)
    return [
        pltpu.make_async_copy(key.at[place], out.at[0:rows], sems.at[2 * slot]),
        pltpu.make_async_copy(value.at[place], out.at[rows : 2 * rows], sems.at[2 * slot + 1]),
    ]


def run_copies(copies):
    for copy in copies:
        copy.start()
    for copy in copies:
        copy.wait()


def prepare_kernel(rows, heads, docs, count, *refs):
    (far_kv, near_kv, doc_hbm, query_hbm, dout_hbm) = refs[0:5]
    (doc_lengths, query, dout, sems) = refs[13:]
    refs = refs[5:13]
    wide = heads * TQ
    run_copies(
        [
            pltpu.make_async_copy(query_hbm, query, sems.at[0]),
            pltpu.make_async_copy(dout_hbm, dout, sems.at[1]),
            pltpu.make_async_copy(doc_hbm, doc_lengths, sems.at[2]),
        ]
    )
    lane = lax.broadcasted_iota(jnp.int32, (1, HD), 1)

    def one(index, carry):
        start, starts, ends = carry
        end = start + doc_lengths[index]
        starts = jnp.where(lane == index, start, starts)
        return (end, starts, jnp.where(lane == index, end, ends))

    none = jnp.zeros((1, HD), jnp.int32)
    _, starts, ends = lax.fori_loop(0, docs, one, (jnp.int32(0), none, none), unroll=8)
    starts_t, ends_t = (
        jnp.transpose(jnp.broadcast_to(row.astype(jnp.float32), (HD, HD))).astype(jnp.int32)
        for row in (starts, ends)
    )
    for slot in (0, 1):
        own_kv, query_t, dout_t, documents = refs[4 * slot : 4 * slot + 4]
        own_kv[...] = (far_kv, near_kv)[slot][...]
        own_rows = half_start(rows, slot)
        for step in range(rows // TQ):
            source = pl.ds(own_rows + step * TQ, TQ)
            for h in range(heads):
                place = slice(step * wide + h * TQ, step * wide + (h + 1) * TQ)
                columns = slice(h * HD, (h + 1) * HD)
                query_t[0:HD, place] = jnp.transpose(query[source, columns])
                dout_t[:, place] = jnp.transpose(dout[source, columns])
        position = block_number(count, slot) * rows
        for tile in range(3 * rows // TQ):
            at = lax.broadcasted_iota(jnp.int32, (TQ, HD), 0) + (position - 2 * rows + tile * TQ)
            inside = jnp.logical_and(at >= starts, at < ends)
            inside = jnp.logical_or(inside, at < 0)
            documents[tile * TQ : (tile + 1) * TQ, :] = jnp.where(inside, 1.0, 0.0).astype(
                documents.dtype
            )
        for step in range(rows // TQ):
            at = lax.broadcasted_iota(jnp.int32, (HD, TQ), 1) + (position + step * TQ)
            inside = jnp.logical_and(at >= starts_t, at < ends_t)
            other = jnp.where(inside, 0.0, other_document).astype(query_t.dtype)
            for h in range(heads):
                place = slice(step * wide + h * TQ, step * wide + (h + 1) * TQ)
                query_t[HD : 2 * HD, place] = other


def prepare(count, doc_lengths, query, dout, far_kv, near_kv):
    rows = query.shape[0] // 2
    heads = query.shape[1] // HD
    pair = jax.ShapeDtypeStruct(far_kv.shape, far_kv.dtype)
    stacked_t = jax.ShapeDtypeStruct((HD, rows * heads), query.dtype)
    query_shape = jax.ShapeDtypeStruct((2 * HD, rows * heads), query.dtype)
    documents = jax.ShapeDtypeStruct((3 * rows, HD), query.dtype)
    assert doc_lengths.shape[0] <= HD
    return pl.pallas_call(
        functools.partial(prepare_kernel, rows, heads, doc_lengths.shape[0], count),
        out_shape=(pair, query_shape, stacked_t, documents) * 2,
        in_specs=[VMEM] * 2 + [HBM] * 3,
        out_specs=[VMEM] * 8,
        scratch_shapes=[
            pltpu.SMEM(doc_lengths.shape, doc_lengths.dtype),
            pltpu.VMEM(query.shape, query.dtype),
            pltpu.VMEM(dout.shape, dout.dtype),
            pltpu.SemaphoreType.DMA((3,)),
        ],
        compiler_params=pltpu.CompilerParams(vmem_limit_bytes=VMEM_LIMIT),
        cost_estimate=pl.CostEstimate(flops=0, bytes_accessed=4 * 2**20, transcendentals=0),
        name="prepare",
    )(far_kv, near_kv, *(in_hbm(array) for array in (doc_lengths, query, dout)))


class Window:
    def __init__(self, rows, slot):
        self.tiles = rows // TQ
        self.chunks = 2 * self.tiles + 1
        self.steps = range(self.tiles)
        self.first = [self.tiles - step for step in self.steps]
        self.late = [first + (1 - slot) * self.tiles for first in self.first]
        self.early = [self.chunks - late for late in self.late]
        self.middle = [late - first for late, first in zip(self.late, self.first)]


def chunk_rows(counts, step, first=0, count=None):
    start = sum(counts[:step]) + first
    count = counts[step] - first if count is None else count
    return slice(start * CHUNK, (start + count) * CHUNK)


def run_length(run):
    return run[-1].stop - run[-1].start


def runs_of(chunks):
    runs = []
    for chunk in chunks:
        if runs:
            last = runs[-1]
            length = run_length(last)
            if last[1] is chunk[1] and last[2] + length == chunk[2] and length < RUN * CHUNK:
                runs[-1] = (*last[:-1], slice(last[-1].start, chunk[-1].stop))
                continue
        runs.append(chunk)
    return runs


def exponentials(jobs, rows, heads, scores):
    back = 2 * rows
    wide = heads * TQ
    base2 = SCALE * math.log2(math.e)

    def score(job, index, row_max):
        step, chunks, (query_t, _, documents), _, _ = jobs[job]
        chunk, keys, row = chunks[index][0:3]
        tile = slice(step * wide, (step + 1) * wide)
        length = run_length(chunks[index])
        window = slice(step * TQ + chunk * CHUNK, step * TQ + chunk * CHUNK + length)
        product = dot_nn(
            jnp.concatenate([keys[row : row + length, :], documents[window, :]], axis=1),
            query_t[:, tile],
        )
        for start in range(0, length, GROUP):
            place = chunk * CHUNK + start
            for h in range(heads):
                lanes = slice(h * TQ, (h + 1) * TQ)
                part = product[start : start + GROUP, lanes]
                if place >= back:
                    key_at = lax.broadcasted_iota(jnp.int32, (GROUP, TQ), 0) + (place - back)
                    query_at = lax.broadcasted_iota(jnp.int32, (GROUP, TQ), 1)
                    part = jnp.where(key_at <= query_at, part, masked_score)
                scores[job % 2, place : place + GROUP, lanes] = part
                for row8 in range(0, GROUP, 8):
                    row_max[h] = jnp.maximum(row_max[h], part[row8 : row8 + 8, :])

    def start_max():
        return [jnp.full((8, TQ), masked_score, jnp.float32)] * heads

    pending = None
    following = start_max()
    for index in range(len(jobs[0][1])):
        score(0, index, following)
    for job, (step, chunks, (_, dout_t, _), first_max, end) in enumerate(jobs):
        tile = slice(step * wide, (step + 1) * wide)
        row_max = jnp.concatenate(
            [jnp.max(part, axis=0, keepdims=True) * base2 for part in following], axis=1
        )
        if first_max is not None:
            row_max = jnp.maximum(row_max, first_max)
        following = start_max()
        ahead = len(jobs[job + 1][1]) if job + 1 < len(jobs) else 0
        done = 0
        total = jnp.zeros((8, wide), jnp.float32)
        delta = jnp.zeros((8, wide), jnp.float32)
        for index, (chunk, keys, row, weights, dprobs, kept) in enumerate(chunks):
            length = kept.stop - kept.start
            product = dot_nn(keys[rows + row : rows + row + length, :], dout_t[:, tile])
            for start in range(0, length, GROUP):
                place = chunk * CHUNK + start
                there = slice(kept.start + start, kept.start + start + GROUP)
                dprob = product[start : start + GROUP, :]
                dprobs[there, :] = dprob.astype(jnp.bfloat16)
                part = jnp.exp2(scores[job % 2, place : place + GROUP, :] * base2 - row_max)
                weights[there, :] = part.astype(jnp.bfloat16)
                term = part * dprob
                for row8 in range(0, GROUP, 8):
                    total = total + part[row8 : row8 + 8, :]
                    delta = delta + term[row8 : row8 + 8, :]
            while done * len(chunks) < ahead * (index + 1):
                score(job + 1, done, following)
                done += 1
            if index == 0 and pending is not None:
                pending()
        sums = [jnp.sum(part, axis=0, keepdims=True) for part in (total, delta)]
        pending = functools.partial(end, row_max, *sums)
    pending()


def early_kernel(rows, heads, slot, own_kv, query_t, dout_t, documents, *refs):
    (weights, dprobs, stats, scores) = refs[-4:]
    prev1 = refs[0] if slot == 1 else None
    window = Window(rows, slot)
    jobs = []
    for step in window.steps:
        chunks = []
        for index in range(window.early[step]):
            chunk = window.late[step] + index
            row = step * TQ + chunk * CHUNK
            keys = own_kv if row >= 2 * rows else prev1
            kept = chunk_rows(window.early, step, index, 1)
            chunks.append((chunk, keys, row % rows, weights, dprobs, kept))

        def end(*found, step=step):
            for kind, value in enumerate(found):
                stats[8 * kind + step : 8 * kind + step + 1, :] = value

        jobs.append((step, runs_of(chunks), (query_t, dout_t, documents), None, end))
    exponentials(jobs, rows, heads, scores)


def early_scores(slot, ready, *prev1):
    rows = ready[0].shape[0] // 2
    heads = ready[1].shape[1] // rows
    wide = heads * TQ
    kept = jax.ShapeDtypeStruct((sum(Window(rows, slot).early) * CHUNK, wide), jnp.bfloat16)
    return pl.pallas_call(
        functools.partial(early_kernel, rows, heads, slot),
        out_shape=(kept, kept, jax.ShapeDtypeStruct((24, wide), jnp.float32)),
        in_specs=[VMEM] * (4 + len(prev1)),
        out_specs=[VMEM] * 3,
        scratch_shapes=[pltpu.VMEM((2, 2 * rows + TQ, wide), jnp.float32)],
        compiler_params=pltpu.CompilerParams(vmem_limit_bytes=VMEM_LIMIT),
        cost_estimate=pl.CostEstimate(flops=0 if slot else 2**33, bytes_accessed=0, transcendentals=0),
        name="early_far" if slot == 0 else "early_near",
    )(*ready, *prev1)


def scaled_by(array, tile, factor):
    return (array[0:HD, tile].astype(jnp.float32) * factor).astype(jnp.bfloat16)


def dscore_rows(dscores, there, weights, dprobs, kept, delta):
    delta = jnp.broadcast_to(delta, (16, delta.shape[1]))
    for start in range(0, there.stop - there.start, 16):
        out = slice(there.start + start, there.start + start + 16)
        place = slice(kept.start + start, kept.start + start + 16)
        dscores[out, :] = weights[place, :] * (dprobs[place, :] - delta)


def add_products(new, columns, products):
    for total_ref, side, terms in products:
        term = dot_nt(side, terms)
        if new:
            total_ref[:, columns] = term
        else:
            total_ref[:, columns] += term


def late_kernel(
    rows,
    heads,
    slot,
    query_t,
    dout_t,
    documents,
    early_stats,
    prev1,
    prev2,
    weights,
    *refs,
):
    (dprobs, dscores, stats, prev2_out, scores, dk, dv) = refs if slot == 0 else refs[-1:] + refs[:-1]
    wide = heads * TQ
    window = Window(rows, slot)
    jobs = []
    for step in window.steps:
        chunks = []
        for chunk in range(window.late[step]):
            row = step * TQ + chunk * CHUNK
            kept = chunk_rows(window.late, step, chunk, 1)
            chunks.append((chunk, (prev2, prev1)[row // rows], row % rows, weights, dprobs, kept))

        def end(row_max, total, delta, step=step):
            tile = slice(step * wide, (step + 1) * wide)
            early = [early_stats[8 * kind + step : 8 * kind + step + 1, :] for kind in range(3)]
            shrink = jnp.exp2(early[0] - row_max)
            late_factor = 1.0 / (total + early[1] * shrink)
            early_factor = late_factor * shrink
            delta = delta * late_factor + early[2] * early_factor
            for kind, value in enumerate((late_factor, early_factor, delta)):
                stats[8 * kind + step : 8 * kind + step + 1, :] = value
            kept = chunk_rows(window.late, step, 0, window.first[step])
            there = chunk_rows(window.first, step)
            dscore_rows(dscores, there, weights, dprobs, kept, delta.astype(jnp.bfloat16))
            add_products(
                step == 0,
                slice(step * TQ, rows),
                (
                    (dv, scaled_by(dout_t, tile, late_factor), weights[kept, :]),
                    (dk, scaled_by(query_t, tile, late_factor), dscores[there, :]),
                ),
            )

        first_max = early_stats[step : step + 1, :]
        jobs.append((step, runs_of(chunks), (query_t, dout_t, documents), first_max, end))
    exponentials(jobs, rows, heads, scores)
    prev2_out[0:HD] = (dk[...] * SCALE).astype(prev2_out.dtype)
    prev2_out[HD : 2 * HD] = dv[...].astype(prev2_out.dtype)


def late_scores(slot, ready, early, prev1, prev2):
    rows = prev2.shape[0] // 2
    heads = ready[1].shape[1] // rows
    wide = heads * TQ
    window = Window(rows, slot)
    late = jax.ShapeDtypeStruct((sum(window.late) * CHUNK, wide), jnp.bfloat16)
    return pl.pallas_call(
        functools.partial(late_kernel, rows, heads, slot),
        out_shape=(
            *([late] * (2 - slot)),
            jax.ShapeDtypeStruct((sum(window.first) * CHUNK, wide), jnp.bfloat16),
            jax.ShapeDtypeStruct((24, wide), jnp.float32),
            jax.ShapeDtypeStruct((2 * HD, rows), jnp.bfloat16),
        ),
        in_specs=[VMEM] * 6,
        out_specs=[VMEM] * (5 - slot),
        scratch_shapes=[
            pltpu.VMEM((2, max(window.late) * CHUNK, wide), jnp.float32),
            pltpu.VMEM((HD, rows), jnp.float32),
            pltpu.VMEM((HD, rows), jnp.float32),
            *([pltpu.VMEM(late.shape, late.dtype)] * slot),
        ],
        compiler_params=pltpu.CompilerParams(vmem_limit_bytes=VMEM_LIMIT),
        cost_estimate=pl.CostEstimate(flops=2**31, bytes_accessed=0, transcendentals=0),
        name="late_far" if slot == 0 else "late_near",
    )(*ready[1:4], early[2], prev1, prev2)


def grads_kernel(rows, heads, slots, *refs):
    wide = heads * TQ
    outs = list(refs[5 * len(slots) : -2])
    (dk, dv) = refs[-2:]
    for part, (slot, late) in enumerate(slots):
        (query_t, dout_t, stats, weights, dprobs) = refs[5 * part : 5 * part + 5]
        dscores = outs.pop(0)
        window = Window(rows, slot)
        counts = window.middle if late else window.early
        for step in reversed(window.steps):
            tile = slice(step * wide, (step + 1) * wide)
            late_factor, early_factor, delta = (
                stats[8 * kind + step : 8 * kind + step + 1, :] for kind in range(3)
            )
            factor = late_factor if late else early_factor
            there = chunk_rows(counts, step)
            kept = chunk_rows(window.late, step, window.first[step]) if late else there
            dscore_rows(dscores, there, weights, dprobs, kept, delta.astype(jnp.bfloat16))
            add_products(
                step == window.tiles - 1,
                slice(0, counts[step] * CHUNK),
                (
                    (dv, scaled_by(dout_t, tile, factor), weights[kept, :]),
                    (dk, scaled_by(query_t, tile, factor), dscores[there, :]),
                ),
            )
        for block in range(counts[-1] // window.tiles):
            out = outs.pop(0)
            place = slice(block * rows, (block + 1) * rows)
            out[0:HD] = (dk[:, place] * SCALE).astype(out.dtype)
            out[HD : 2 * HD] = dv[:, place].astype(out.dtype)


def rest_grads(name, cost, parts):
    rows = parts[0][2][0].shape[0] // 2
    heads = parts[0][2][1].shape[1] // rows
    operands, out_shape = [], []
    for slot, late, (_, query_t, dout_t, _, stats, weights, dprobs), sent in parts:
        window = Window(rows, slot)
        kept = (sum(window.middle if late else window.early) * CHUNK, heads * TQ)
        operands += [query_t, dout_t, stats, weights, dprobs]
        out_shape.append(jax.ShapeDtypeStruct(kept, jnp.bfloat16))
        for one in sent:
            kind = jnp.bfloat16 if one else jnp.float32
            out_shape.append(jax.ShapeDtypeStruct((2 * HD, rows), kind))
    slots = tuple(part[0:2] for part in parts)
    return pl.pallas_call(
        functools.partial(grads_kernel, rows, heads, slots),
        out_shape=out_shape,
        in_specs=[VMEM] * len(operands),
        out_specs=[VMEM] * len(out_shape),
        scratch_shapes=[pltpu.VMEM((HD, 2 * rows), jnp.float32)] * 2,
        compiler_params=pltpu.CompilerParams(vmem_limit_bytes=VMEM_LIMIT),
        cost_estimate=pl.CostEstimate(flops=cost, bytes_accessed=0, transcendentals=0),
        name=name,
    )(*operands)


def outputs_kernel(rows, heads, *refs):
    blocks = (refs[0:9], refs[9:17])
    (attended, grad_query, keys_t, values_t) = refs[17:]
    for slot, block in enumerate(blocks):
        (own_kv, prev1, prev2, early_w, early_d, late_w, first_d, stats) = block[0:8]
        window = Window(rows, slot)
        own_rows = half_start(rows, slot)
        for place, source in enumerate((prev2, prev1, own_kv)):
            for tile in range(rows // TQ):
                part = slice(place * rows + tile * TQ, place * rows + (tile + 1) * TQ)
                row = tile * TQ
                keys_t[:, part] = jnp.transpose(source[row : row + TQ, :])
                values_t[:, part] = jnp.transpose(source[rows + row : rows + row + TQ, :])
        for step in window.steps:
            first, late = window.first[step], window.late[step]

            def product(side, terms, counts, start, skip, length):
                columns = slice(step * TQ + start * CHUNK, step * TQ + (start + length) * CHUNK)
                return dot_nn(side[:, columns], terms[chunk_rows(counts, step, skip, length), :])

            early = window.chunks - late
            late_factor = stats[step : step + 1, :]
            early_factor = stats[8 + step : 8 + step + 1, :]
            attended_t = product(values_t, late_w, window.late, 0, 0, late) * late_factor
            attended_t += product(values_t, early_w, window.early, late, 0, early) * early_factor
            late_t = product(keys_t, first_d, window.first, 0, 0, first)
            if late > first:
                late_t += product(keys_t, block[8], window.middle, first, 0, late - first)
            early_t = product(keys_t, early_d, window.early, late, 0, early)
            grad_query_t = late_t * (late_factor * SCALE) + early_t * (early_factor * SCALE)
            place = pl.ds(own_rows + step * TQ, TQ)
            for out, found in ((attended, attended_t), (grad_query, grad_query_t)):
                for h in range(heads):
                    part = found[:, h * TQ : (h + 1) * TQ]
                    out[place, h * HD : (h + 1) * HD] = jnp.transpose(part).astype(out.dtype)


def block_outputs(query, far, near):
    rows = query.shape[0] // 2
    heads = query.shape[1] // HD
    shape = jax.ShapeDtypeStruct(query.shape, query.dtype)
    return pl.pallas_call(
        functools.partial(outputs_kernel, rows, heads),
        out_shape=(shape, shape),
        in_specs=[VMEM] * 17,
        out_specs=[VMEM] * 2,
        scratch_shapes=[pltpu.VMEM((HD, 3 * rows), jnp.bfloat16)] * 2,
        compiler_params=pltpu.CompilerParams(vmem_limit_bytes=VMEM_LIMIT),
        cost_estimate=pl.CostEstimate(flops=0, bytes_accessed=0, transcendentals=0),
        name="block_outputs",
    )(*far, *near)


def total_kernel(rows, far_own, far_1, far_2, near, grad_key, grad_value):
    far = far_own[...] + far_1[...].astype(jnp.float32) + far_2[...].astype(jnp.float32)
    for slot, total in ((0, far), (1, near[...])):
        place = pl.ds(half_start(rows, slot), rows)
        grad_key[place, :] = jnp.transpose(total[0:HD]).astype(grad_key.dtype)
        grad_value[place, :] = jnp.transpose(total[HD : 2 * HD]).astype(grad_value.dtype)


def total_grads(*parts):
    rows = parts[0].shape[1]
    shape = jax.ShapeDtypeStruct((2 * rows, HD), jnp.bfloat16)
    return pl.pallas_call(
        functools.partial(total_kernel, rows),
        out_shape=(shape, shape),
        in_specs=[VMEM] * 4,
        out_specs=[VMEM] * 2,
        compiler_params=pltpu.CompilerParams(vmem_limit_bytes=VMEM_LIMIT),
        name="total_grads",
    )(*parts)


def body(query, key, value, d_out, doc_lengths):
    count = lax.axis_size("ctx")

    def holder(block):
        return block if block < count else 2 * count - 1 - block

    def move(array, pairs):
        return lax.ppermute(array, "ctx", pairs)

    near_on = [(holder(b), holder(b + 2)) for b in range(1, 2 * count - 2, 2)]
    far_on = [(holder(b), holder(b + 2)) for b in range(0, 2 * count - 2, 2)]
    near_to_far = [(holder(b), holder(b + 1)) for b in range(1, 2 * count - 2, 2)]
    swap = [(d, d ^ 1) for d in range(count)]
    near_back = [(t, s) for s, t in near_on]
    far_back = [(t, s) for s, t in far_on]

    rows = key.shape[0] // 2
    odd = lax.axis_index("ctx") % 2 == 1
    lower = jnp.concatenate([key[:rows], value[:rows]], axis=0)
    upper = jnp.concatenate([key[rows:], value[rows:]], axis=0)
    near_kv, far_kv = jnp.where(odd, lower, upper), jnp.where(odd, upper, lower)
    far_1 = move(near_kv, near_to_far)
    far_2 = move(far_kv, far_on)
    prepared = prepare(count, doc_lengths, query, d_out, far_kv, near_kv)
    far_ready, near_ready = prepared[0:4], prepared[4:8]
    near_1 = move(far_ready[0], swap)
    far_early = early_scores(0, far_ready)
    near_early = early_scores(1, near_ready, near_1)
    far_1, near_early = lax.optimization_barrier((far_1, near_early))
    far_late = late_scores(0, far_ready, far_early, far_1, far_2)
    from_far_2 = move(far_late[-1], far_back)
    near_2 = move(far_1, swap)
    near_2, far_stats = lax.optimization_barrier((near_2, far_late[-2]))
    far_middle_d, far_g1 = rest_grads(
        "grads_far", 0, [(0, True, (*far_ready, far_stats, *far_late[0:2]), (True,))]
    )
    relayed = move(far_g1, swap)
    near_late = late_scores(1, near_ready, near_early, near_1, near_2)
    near_sum = near_late[-1].astype(jnp.float32) + relayed.astype(jnp.float32)
    from_near_2 = move(near_sum.astype(jnp.bfloat16), near_back)
    near_early_d, near_g1, near_own, far_early_d, far_own = rest_grads(
        "grads_near",
        2**31,
        [
            (1, False, (*near_ready, near_late[-2], *near_early[0:2]), (True, False)),
            (0, False, (*far_ready, far_late[-2], *far_early[0:2]), (False,)),
        ],
    )
    near_g1, from_far_2 = lax.optimization_barrier((near_g1, from_far_2))
    from_near_1 = move(near_g1, swap)
    attended, grad_query = block_outputs(
        query,
        (far_ready[0], far_1, far_2, far_early[0], far_early_d, far_late[0], *far_late[-3:-1], far_middle_d),
        (near_ready[0], near_1, near_2, near_early[0], near_early_d, near_late[0], *near_late[-3:-1]),
    )
    near_total = near_own + from_near_2.astype(jnp.float32)
    grad_key, grad_value = total_grads(far_own, from_near_1, from_far_2, near_total)
    return (attended, grad_query, grad_key, grad_value)


def solution(mesh):
    rows = P(("dp", "ctx"), None)
    return jax.shard_map(
        body,
        mesh=mesh,
        in_specs=(rows, rows, rows, rows, P("dp")),
        out_specs=(rows, rows, rows, rows),
        check_vma=False,
    )
```

```python
import functools
import math

import jax
import jax.numpy as jnp
from jax import lax
from jax.experimental import pallas as pl
from jax.experimental.pallas import tpu as pltpu
from jax.sharding import PartitionSpec as P

HD = 128
TQ = 128
GROUP = 32

masked_score = -1e30
other_document = -65536.0
VMEM_LIMIT = 24 * 1024 * 1024
SCALE = 1.0 / math.sqrt(HD)
VMEM = pl.BlockSpec(memory_space=pltpu.VMEM)
HBM = pl.BlockSpec(memory_space=pltpu.HBM)
CHUNK = 128
RUN = 3


def dot_nt(a, b):
    return lax.dot_general(a, b, (((1,), (1,)), ((), ())), preferred_element_type=jnp.float32)


def dot_nn(a, b):
    return lax.dot_general(a, b, (((1,), (0,)), ((), ())), preferred_element_type=jnp.float32)


def half_start(rows, slot):
    odd = lax.axis_index("ctx") % 2
    return pl.multiple_of((odd if slot == 0 else 1 - odd) * rows, rows)


def block_number(count, slot):
    device = lax.axis_index("ctx")
    in_lower = device % 2 == slot
    return jnp.where(in_lower, device, 2 * count - 1 - device)


def in_hbm(array):
    return pltpu.with_memory_space_constraint(array, pltpu.HBM)


def load_block(rows, slot, key, value, out, sems):
    place = pl.ds(half_start(rows, slot), rows)
    return [
        pltpu.make_async_copy(key.at[place], out.at[0:rows], sems.at[2 * slot]),
        pltpu.make_async_copy(value.at[place], out.at[rows : 2 * rows], sems.at[2 * slot + 1]),
    ]


def run_copies(copies):
    for copy in copies:
        copy.start()
    for copy in copies:
        copy.wait()


def prepare_kernel(rows, heads, docs, count, *refs):
    (far_kv, near_kv, doc_hbm, query_hbm, dout_hbm) = refs[0:5]
    (doc_lengths, query, dout, sems) = refs[13:]
    refs = refs[5:13]
    wide = heads * TQ
    run_copies(
        [
            pltpu.make_async_copy(query_hbm, query, sems.at[0]),
            pltpu.make_async_copy(dout_hbm, dout, sems.at[1]),
            pltpu.make_async_copy(doc_hbm, doc_lengths, sems.at[2]),
        ]
    )
    lane = lax.broadcasted_iota(jnp.int32, (1, HD), 1)

    def one(index, carry):
        start, starts, ends = carry
        end = start + doc_lengths[index]
        starts = jnp.where(lane == index, start, starts)
        return (end, starts, jnp.where(lane == index, end, ends))

    none = jnp.zeros((1, HD), jnp.int32)
    _, starts, ends = lax.fori_loop(0, docs, one, (jnp.int32(0), none, none), unroll=8)
    starts_t, ends_t = (
        jnp.transpose(jnp.broadcast_to(row.astype(jnp.float32), (HD, HD))).astype(jnp.int32)
        for row in (starts, ends)
    )
    for slot in (0, 1):
        own_kv, query_t, dout_t, documents = refs[4 * slot : 4 * slot + 4]
        own_kv[...] = (far_kv, near_kv)[slot][...]
        own_rows = half_start(rows, slot)
        for step in range(rows // TQ):
            source = pl.ds(own_rows + step * TQ, TQ)
            for h in range(heads):
                place = slice(step * wide + h * TQ, step * wide + (h + 1) * TQ)
                columns = slice(h * HD, (h + 1) * HD)
                query_t[0:HD, place] = jnp.transpose(query[source, columns])
                dout_t[:, place] = jnp.transpose(dout[source, columns])
        position = block_number(count, slot) * rows
        for tile in range(3 * rows // TQ):
            at = lax.broadcasted_iota(jnp.int32, (TQ, HD), 0) + (position - 2 * rows + tile * TQ)
            inside = jnp.logical_and(at >= starts, at < ends)
            inside = jnp.logical_or(inside, at < 0)
            documents[tile * TQ : (tile + 1) * TQ, :] = jnp.where(inside, 1.0, 0.0).astype(
                documents.dtype
            )
        for step in range(rows // TQ):
            at = lax.broadcasted_iota(jnp.int32, (HD, TQ), 1) + (position + step * TQ)
            inside = jnp.logical_and(at >= starts_t, at < ends_t)
            other = jnp.where(inside, 0.0, other_document).astype(query_t.dtype)
            for h in range(heads):
                place = slice(step * wide + h * TQ, step * wide + (h + 1) * TQ)
                query_t[HD : 2 * HD, place] = other


def prepare(count, doc_lengths, query, dout, far_kv, near_kv):
    rows = query.shape[0] // 2
    heads = query.shape[1] // HD
    pair = jax.ShapeDtypeStruct(far_kv.shape, far_kv.dtype)
    stacked_t = jax.ShapeDtypeStruct((HD, rows * heads), query.dtype)
    query_shape = jax.ShapeDtypeStruct((2 * HD, rows * heads), query.dtype)
    documents = jax.ShapeDtypeStruct((3 * rows, HD), query.dtype)
    assert doc_lengths.shape[0] <= HD
    return pl.pallas_call(
        functools.partial(prepare_kernel, rows, heads, doc_lengths.shape[0], count),
        out_shape=(pair, query_shape, stacked_t, documents) * 2,
        in_specs=[VMEM] * 2 + [HBM] * 3,
        out_specs=[VMEM] * 8,
        scratch_shapes=[
            pltpu.SMEM(doc_lengths.shape, doc_lengths.dtype),
            pltpu.VMEM(query.shape, query.dtype),
            pltpu.VMEM(dout.shape, dout.dtype),
            pltpu.SemaphoreType.DMA((3,)),
        ],
        compiler_params=pltpu.CompilerParams(vmem_limit_bytes=VMEM_LIMIT),
        cost_estimate=pl.CostEstimate(flops=0, bytes_accessed=4 * 2**20, transcendentals=0),
        name="prepare",
    )(far_kv, near_kv, *(in_hbm(array) for array in (doc_lengths, query, dout)))


class Window:
    def __init__(self, rows, slot):
        self.tiles = rows // TQ
        self.chunks = 2 * self.tiles + 1
        self.steps = range(self.tiles)
        self.late = [self.tiles - step for step in self.steps]
        self.middle = [(1 - slot) * self.tiles for step in self.steps]
        self.early = [
            self.chunks - late - middle for late, middle in zip(self.late, self.middle)
        ]


def chunk_rows(counts, step, first=0, count=None):
    start = sum(counts[:step]) + first
    count = counts[step] - first if count is None else count
    return slice(start * CHUNK, (start + count) * CHUNK)


def run_length(run):
    return run[-1].stop - run[-1].start


def runs_of(chunks):
    runs = []
    for chunk in chunks:
        if runs:
            last = runs[-1]
            length = run_length(last)
            if last[1] is chunk[1] and last[2] + length == chunk[2] and length < RUN * CHUNK:
                runs[-1] = (*last[:-1], slice(last[-1].start, chunk[-1].stop))
                continue
        runs.append(chunk)
    return runs


def exponentials(jobs, rows, heads, scores):
    back = 2 * rows
    wide = heads * TQ
    base2 = SCALE * math.log2(math.e)

    def score(job, index, row_max):
        step, chunks, (query_t, _, documents), _, _ = jobs[job]
        chunk, keys, row = chunks[index][0:3]
        tile = slice(step * wide, (step + 1) * wide)
        length = run_length(chunks[index])
        window = slice(step * TQ + chunk * CHUNK, step * TQ + chunk * CHUNK + length)
        product = dot_nn(
            jnp.concatenate([keys[row : row + length, :], documents[window, :]], axis=1),
            query_t[:, tile],
        )
        for start in range(0, length, GROUP):
            place = chunk * CHUNK + start
            for h in range(heads):
                lanes = slice(h * TQ, (h + 1) * TQ)
                part = product[start : start + GROUP, lanes]
                if place >= back:
                    key_at = lax.broadcasted_iota(jnp.int32, (GROUP, TQ), 0) + (place - back)
                    query_at = lax.broadcasted_iota(jnp.int32, (GROUP, TQ), 1)
                    part = jnp.where(key_at <= query_at, part, masked_score)
                scores[job % 2, place : place + GROUP, lanes] = part
                for row8 in range(0, GROUP, 8):
                    row_max[h] = jnp.maximum(row_max[h], part[row8 : row8 + 8, :])

    def start_max():
        return [jnp.full((8, TQ), masked_score, jnp.float32)] * heads

    pending = None
    following = start_max()
    for index in range(len(jobs[0][1])):
        score(0, index, following)
    for job, (step, chunks, (_, dout_t, _), first_max, end) in enumerate(jobs):
        tile = slice(step * wide, (step + 1) * wide)
        row_max = jnp.concatenate(
            [jnp.max(part, axis=0, keepdims=True) * base2 for part in following], axis=1
        )
        if first_max is not None:
            row_max = jnp.maximum(row_max, first_max)
        following = start_max()
        ahead = len(jobs[job + 1][1]) if job + 1 < len(jobs) else 0
        done = 0
        total = jnp.zeros((8, wide), jnp.float32)
        delta = jnp.zeros((8, wide), jnp.float32)
        for index, (chunk, keys, row, weights, dprobs, kept) in enumerate(chunks):
            length = kept.stop - kept.start
            product = dot_nn(keys[rows + row : rows + row + length, :], dout_t[:, tile])
            for start in range(0, length, GROUP):
                place = chunk * CHUNK + start
                there = slice(kept.start + start, kept.start + start + GROUP)
                dprob = product[start : start + GROUP, :]
                dprobs[there, :] = dprob.astype(jnp.bfloat16)
                part = jnp.exp2(scores[job % 2, place : place + GROUP, :] * base2 - row_max)
                weights[there, :] = part.astype(jnp.bfloat16)
                term = part * dprob
                for row8 in range(0, GROUP, 8):
                    total = total + part[row8 : row8 + 8, :]
                    delta = delta + term[row8 : row8 + 8, :]
            while done * len(chunks) < ahead * (index + 1):
                score(job + 1, done, following)
                done += 1
            if index == 0 and pending is not None:
                pending()
        sums = [jnp.sum(part, axis=0, keepdims=True) for part in (total, delta)]
        pending = functools.partial(end, row_max, *sums)
    pending()


def group_kernel(rows, heads, slot, middle, query_t, dout_t, documents, *refs):
    (weights, dprobs, stats, scores) = refs[-4:]
    prev1 = refs[0] if middle or slot == 1 else None
    own_kv = None if middle else refs[slot]
    window = Window(rows, slot)
    counts = window.middle if middle else window.early
    jobs = []
    for step in window.steps:
        chunks = []
        for index in range(counts[step]):
            chunk = window.late[step] + (0 if middle else window.middle[step]) + index
            row = step * TQ + chunk * CHUNK
            keys = own_kv if row >= 2 * rows else prev1
            kept = chunk_rows(counts, step, index, 1)
            chunks.append((chunk, keys, row % rows, weights, dprobs, kept))

        def end(*found, step=step):
            for kind, value in enumerate(found):
                stats[8 * kind + step : 8 * kind + step + 1, :] = value

        first_max = refs[1][step : step + 1, :] if middle else None
        jobs.append((step, runs_of(chunks), (query_t, dout_t, documents), first_max, end))
    exponentials(jobs, rows, heads, scores)


def group_scores(slot, middle, ready, *operands):
    rows = ready[0].shape[0] // 2
    heads = ready[1].shape[1] // rows
    wide = heads * TQ
    window = Window(rows, slot)
    counts = window.middle if middle else window.early
    kept = jax.ShapeDtypeStruct((sum(counts) * CHUNK, wide), jnp.bfloat16)
    cost = (0 if slot else 2**33) if not middle else 0
    return pl.pallas_call(
        functools.partial(group_kernel, rows, heads, slot, middle),
        out_shape=(kept, kept, jax.ShapeDtypeStruct((24, wide), jnp.float32)),
        in_specs=[VMEM] * (3 + len(operands)),
        out_specs=[VMEM] * 3,
        scratch_shapes=[pltpu.VMEM((2, 2 * rows + TQ, wide), jnp.float32)],
        compiler_params=pltpu.CompilerParams(vmem_limit_bytes=VMEM_LIMIT),
        cost_estimate=pl.CostEstimate(flops=cost, bytes_accessed=0, transcendentals=0),
        name="middle_far" if middle else "early_far" if slot == 0 else "early_near",
    )(*ready[1:4], *operands)


def scaled_by(array, tile, factor):
    return (array[0:HD, tile].astype(jnp.float32) * factor).astype(jnp.bfloat16)


def dscore_rows(dscores, there, weights, dprobs, kept, delta):
    delta = jnp.broadcast_to(delta, (16, delta.shape[1]))
    for start in range(0, there.stop - there.start, 16):
        out = slice(there.start + start, there.start + start + 16)
        place = slice(kept.start + start, kept.start + start + 16)
        dscores[out, :] = weights[place, :] * (dprobs[place, :] - delta)


def add_products(new, columns, products):
    for total_ref, side, terms in products:
        term = dot_nt(side, terms)
        if new:
            total_ref[:, columns] = term
        else:
            total_ref[:, columns] += term


def late_kernel(rows, heads, slot, query_t, dout_t, documents, prev2, *refs):
    groups = refs[0 : 2 - slot]
    (weights, dscores, stats, prev2_out, scores, dprobs, dk, dv) = refs[2 - slot :]
    wide = heads * TQ
    window = Window(rows, slot)
    jobs = []
    for step in window.steps:
        chunks = []
        for chunk in range(window.late[step]):
            kept = chunk_rows(window.late, step, chunk, 1)
            chunks.append((chunk, prev2, step * TQ + chunk * CHUNK, weights, dprobs, kept))

        def end(row_max, total, delta, step=step):
            tile = slice(step * wide, (step + 1) * wide)
            rows_of = [
                [group[8 * kind + step : 8 * kind + step + 1, :] for kind in range(3)]
                for group in groups
            ]
            shrinks = [jnp.exp2(found[0] - row_max) for found in rows_of]
            for found, shrink in zip(rows_of, shrinks):
                total = total + found[1] * shrink
                delta = delta + found[2] * shrink
            late_factor = 1.0 / total
            delta = delta * late_factor
            factors = [late_factor * shrink for shrink in shrinks]
            for kind, value in enumerate((late_factor, factors[0], delta, factors[-1])):
                stats[8 * kind + step : 8 * kind + step + 1, :] = value
            there = chunk_rows(window.late, step)
            dscore_rows(dscores, there, weights, dprobs, there, delta.astype(jnp.bfloat16))
            add_products(
                step == 0,
                slice(step * TQ, rows),
                (
                    (dv, scaled_by(dout_t, tile, late_factor), weights[there, :]),
                    (dk, scaled_by(query_t, tile, late_factor), dscores[there, :]),
                ),
            )

        first_max = groups[-1][step : step + 1, :]
        jobs.append((step, runs_of(chunks), (query_t, dout_t, documents), first_max, end))
    exponentials(jobs, rows, heads, scores)
    prev2_out[0:HD] = (dk[...] * SCALE).astype(prev2_out.dtype)
    prev2_out[HD : 2 * HD] = dv[...].astype(prev2_out.dtype)


def late_scores(slot, ready, groups, prev2):
    rows = prev2.shape[0] // 2
    heads = ready[1].shape[1] // rows
    wide = heads * TQ
    late = jax.ShapeDtypeStruct((sum(Window(rows, slot).late) * CHUNK, wide), jnp.bfloat16)
    return pl.pallas_call(
        functools.partial(late_kernel, rows, heads, slot),
        out_shape=(
            late,
            late,
            jax.ShapeDtypeStruct((32, wide), jnp.float32),
            jax.ShapeDtypeStruct((2 * HD, rows), jnp.bfloat16),
        ),
        in_specs=[VMEM] * (4 + len(groups)),
        out_specs=[VMEM] * 4,
        scratch_shapes=[
            pltpu.VMEM((2, rows, wide), jnp.float32),
            pltpu.VMEM(late.shape, late.dtype),
            pltpu.VMEM((HD, rows), jnp.float32),
            pltpu.VMEM((HD, rows), jnp.float32),
        ],
        compiler_params=pltpu.CompilerParams(vmem_limit_bytes=VMEM_LIMIT),
        cost_estimate=pl.CostEstimate(flops=2**31, bytes_accessed=0, transcendentals=0),
        name="late_far" if slot == 0 else "late_near",
    )(*ready[1:4], prev2, *groups)


def grads_kernel(rows, heads, slots, *refs):
    wide = heads * TQ
    outs = list(refs[5 * len(slots) : -2])
    (dk, dv) = refs[-2:]
    for part, (slot, middle) in enumerate(slots):
        (query_t, dout_t, stats, weights, dprobs) = refs[5 * part : 5 * part + 5]
        dscores = outs.pop(0)
        window = Window(rows, slot)
        counts = window.middle if middle else window.early
        for step in reversed(window.steps):
            tile = slice(step * wide, (step + 1) * wide)
            _, early_factor, delta, middle_factor = (
                stats[8 * kind + step : 8 * kind + step + 1, :] for kind in range(4)
            )
            factor = middle_factor if middle else early_factor
            there = chunk_rows(counts, step)
            dscore_rows(dscores, there, weights, dprobs, there, delta.astype(jnp.bfloat16))
            add_products(
                step == window.tiles - 1,
                slice(0, counts[step] * CHUNK),
                (
                    (dv, scaled_by(dout_t, tile, factor), weights[there, :]),
                    (dk, scaled_by(query_t, tile, factor), dscores[there, :]),
                ),
            )
        for block in range(counts[-1] // window.tiles):
            out = outs.pop(0)
            place = slice(block * rows, (block + 1) * rows)
            out[0:HD] = (dk[:, place] * SCALE).astype(out.dtype)
            out[HD : 2 * HD] = dv[:, place].astype(out.dtype)


def rest_grads(name, cost, parts):
    rows = parts[0][2][0].shape[0] // 2
    heads = parts[0][2][1].shape[1] // rows
    operands, out_shape = [], []
    for slot, middle, (_, query_t, dout_t, _, stats, weights, dprobs), sent in parts:
        window = Window(rows, slot)
        kept = (sum(window.middle if middle else window.early) * CHUNK, heads * TQ)
        operands += [query_t, dout_t, stats, weights, dprobs]
        out_shape.append(jax.ShapeDtypeStruct(kept, jnp.bfloat16))
        for one in sent:
            kind = jnp.bfloat16 if one else jnp.float32
            out_shape.append(jax.ShapeDtypeStruct((2 * HD, rows), kind))
    slots = tuple(part[0:2] for part in parts)
    return pl.pallas_call(
        functools.partial(grads_kernel, rows, heads, slots),
        out_shape=out_shape,
        in_specs=[VMEM] * len(operands),
        out_specs=[VMEM] * len(out_shape),
        scratch_shapes=[pltpu.VMEM((HD, 2 * rows), jnp.float32)] * 2,
        compiler_params=pltpu.CompilerParams(vmem_limit_bytes=VMEM_LIMIT),
        cost_estimate=pl.CostEstimate(flops=cost, bytes_accessed=0, transcendentals=0),
        name=name,
    )(*operands)


def outputs_kernel(rows, heads, *refs):
    blocks = (refs[0:3], refs[3:6], refs[6:9], refs[9]), (refs[10:13], refs[13:15], refs[15:17], refs[17])
    (attended, grad_query, keys_t, values_t) = refs[18:]
    for slot, (sources, weights, dscores, stats) in enumerate(blocks):
        window = Window(rows, slot)
        groups = [(window.late, 0), (window.early, 1)]
        if slot == 0:
            groups.insert(1, (window.middle, 3))
        own_rows = half_start(rows, slot)
        for place, source in enumerate(sources):
            for tile in range(rows // TQ):
                part = slice(place * rows + tile * TQ, place * rows + (tile + 1) * TQ)
                row = tile * TQ
                keys_t[:, part] = jnp.transpose(source[row : row + TQ, :])
                values_t[:, part] = jnp.transpose(source[rows + row : rows + row + TQ, :])
        for step in window.steps:
            place = pl.ds(own_rows + step * TQ, TQ)
            for out, side, terms, scale in (
                (attended, values_t, weights, 1.0),
                (grad_query, keys_t, dscores, SCALE),
            ):
                found = None
                start = step * TQ
                for (counts, kind), term in zip(groups, terms):
                    columns = slice(start, start + counts[step] * CHUNK)
                    start = columns.stop
                    factor = stats[8 * kind + step : 8 * kind + step + 1, :] * scale
                    part = dot_nn(side[:, columns], term[chunk_rows(counts, step), :]) * factor
                    found = part if found is None else found + part
                for h in range(heads):
                    part = found[:, h * TQ : (h + 1) * TQ]
                    out[place, h * HD : (h + 1) * HD] = jnp.transpose(part).astype(out.dtype)


def block_outputs(query, far, near):
    rows = query.shape[0] // 2
    heads = query.shape[1] // HD
    shape = jax.ShapeDtypeStruct(query.shape, query.dtype)
    return pl.pallas_call(
        functools.partial(outputs_kernel, rows, heads),
        out_shape=(shape, shape),
        in_specs=[VMEM] * 18,
        out_specs=[VMEM] * 2,
        scratch_shapes=[pltpu.VMEM((HD, 3 * rows), jnp.bfloat16)] * 2,
        compiler_params=pltpu.CompilerParams(vmem_limit_bytes=VMEM_LIMIT),
        cost_estimate=pl.CostEstimate(flops=0, bytes_accessed=0, transcendentals=0),
        name="block_outputs",
    )(*far, *near)


def total_kernel(rows, far_own, far_1, far_2, near, grad_key, grad_value):
    far = far_own[...] + far_1[...].astype(jnp.float32) + far_2[...].astype(jnp.float32)
    for slot, total in ((0, far), (1, near[...])):
        place = pl.ds(half_start(rows, slot), rows)
        grad_key[place, :] = jnp.transpose(total[0:HD]).astype(grad_key.dtype)
        grad_value[place, :] = jnp.transpose(total[HD : 2 * HD]).astype(grad_value.dtype)


def total_grads(*parts):
    rows = parts[0].shape[1]
    shape = jax.ShapeDtypeStruct((2 * rows, HD), jnp.bfloat16)
    return pl.pallas_call(
        functools.partial(total_kernel, rows),
        out_shape=(shape, shape),
        in_specs=[VMEM] * 4,
        out_specs=[VMEM] * 2,
        compiler_params=pltpu.CompilerParams(vmem_limit_bytes=VMEM_LIMIT),
        name="total_grads",
    )(*parts)


def body(query, key, value, d_out, doc_lengths):
    count = lax.axis_size("ctx")

    def holder(block):
        return block if block < count else 2 * count - 1 - block

    def move(array, pairs):
        return lax.ppermute(array, "ctx", pairs)

    near_on = [(holder(b), holder(b + 2)) for b in range(1, 2 * count - 2, 2)]
    far_on = [(holder(b), holder(b + 2)) for b in range(0, 2 * count - 2, 2)]
    near_to_far = [(holder(b), holder(b + 1)) for b in range(1, 2 * count - 2, 2)]
    swap = [(d, d ^ 1) for d in range(count)]
    near_back = [(t, s) for s, t in near_on]
    far_back = [(t, s) for s, t in far_on]

    rows = key.shape[0] // 2
    odd = lax.axis_index("ctx") % 2 == 1
    lower = jnp.concatenate([key[:rows], value[:rows]], axis=0)
    upper = jnp.concatenate([key[rows:], value[rows:]], axis=0)
    near_kv, far_kv = jnp.where(odd, lower, upper), jnp.where(odd, upper, lower)
    far_1 = move(near_kv, near_to_far)
    far_2 = move(far_kv, far_on)
    prepared = prepare(count, doc_lengths, query, d_out, far_kv, near_kv)
    far_ready, near_ready = prepared[0:4], prepared[4:8]
    near_1 = move(far_ready[0], swap)
    far_early = group_scores(0, False, far_ready, far_ready[0])
    near_early = group_scores(1, False, near_ready, near_1, near_ready[0])
    far_1, near_early = lax.optimization_barrier((far_1, near_early))
    far_middle = group_scores(0, True, far_ready, far_1, far_early[2])
    far_late = late_scores(0, far_ready, (far_early[2], far_middle[2]), far_2)
    from_far_2 = move(far_late[3], far_back)
    near_2 = move(far_1, swap)
    near_2, far_stats = lax.optimization_barrier((near_2, far_late[2]))
    far_middle_d, far_g1 = rest_grads(
        "grads_far", 0, [(0, True, (*far_ready, far_stats, *far_middle[0:2]), (True,))]
    )
    relayed = move(far_g1, swap)
    near_late = late_scores(1, near_ready, (near_early[2],), near_2)
    near_sum = near_late[3].astype(jnp.float32) + relayed.astype(jnp.float32)
    from_near_2 = move(near_sum.astype(jnp.bfloat16), near_back)
    near_early_d, near_g1, near_own, far_early_d, far_own = rest_grads(
        "grads_near",
        2**31,
        [
            (1, False, (*near_ready, near_late[2], *near_early[0:2]), (True, False)),
            (0, False, (*far_ready, far_late[2], *far_early[0:2]), (False,)),
        ],
    )
    near_g1, from_far_2 = lax.optimization_barrier((near_g1, from_far_2))
    from_near_1 = move(near_g1, swap)
    attended, grad_query = block_outputs(
        query,
        (
            *(far_2, far_1, far_ready[0]),
            *(far_late[0], far_middle[0], far_early[0]),
            *(far_late[1], far_middle_d, far_early_d),
            far_late[2],
        ),
        (
            *(near_2, near_1, near_ready[0]),
            *(near_late[0], near_early[0]),
            *(near_late[1], near_early_d),
            near_late[2],
        ),
    )
    near_total = near_own + from_near_2.astype(jnp.float32)
    grad_key, grad_value = total_grads(far_own, from_near_1, from_far_2, near_total)
    return (attended, grad_query, grad_key, grad_value)


def solution(mesh):
    rows = P(("dp", "ctx"), None)
    return jax.shard_map(
        body,
        mesh=mesh,
        in_specs=(rows, rows, rows, rows, P("dp")),
        out_specs=(rows, rows, rows, rows),
        check_vma=False,
    )
```

```python
import functools
import math

import jax
import jax.numpy as jnp
from jax import lax
from jax.experimental import pallas as pl
from jax.experimental.pallas import tpu as pltpu
from jax.sharding import PartitionSpec as P

HD = 128
TQ = 128
GROUP = 32

masked_score = -1e30
other_document = -65536.0
VMEM_LIMIT = 24 * 1024 * 1024
SCALE = 1.0 / math.sqrt(HD)
VMEM = pl.BlockSpec(memory_space=pltpu.VMEM)
HBM = pl.BlockSpec(memory_space=pltpu.HBM)
CHUNK = 128
RUN = 3


def dot_nt(a, b):
    return lax.dot_general(a, b, (((1,), (1,)), ((), ())), preferred_element_type=jnp.float32)


def dot_nn(a, b):
    return lax.dot_general(a, b, (((1,), (0,)), ((), ())), preferred_element_type=jnp.float32)


def half_start(rows, slot):
    odd = lax.axis_index("ctx") % 2
    return pl.multiple_of((odd if slot == 0 else 1 - odd) * rows, rows)


def block_number(count, slot):
    device = lax.axis_index("ctx")
    in_lower = device % 2 == slot
    return jnp.where(in_lower, device, 2 * count - 1 - device)


def in_hbm(array):
    return pltpu.with_memory_space_constraint(array, pltpu.HBM)


def load_block(rows, slot, key, value, out, sems):
    place = pl.ds(half_start(rows, slot), rows)
    return [
        pltpu.make_async_copy(key.at[place], out.at[0:rows], sems.at[2 * slot]),
        pltpu.make_async_copy(value.at[place], out.at[rows : 2 * rows], sems.at[2 * slot + 1]),
    ]


def run_copies(copies):
    for copy in copies:
        copy.start()
    for copy in copies:
        copy.wait()


def prepare_kernel(rows, heads, docs, count, *refs):
    (far_kv, near_kv, doc_hbm, query_hbm, dout_hbm) = refs[0:5]
    (doc_lengths, query, dout, sems) = refs[13:]
    refs = refs[5:13]
    wide = heads * TQ
    run_copies(
        [
            pltpu.make_async_copy(query_hbm, query, sems.at[0]),
            pltpu.make_async_copy(dout_hbm, dout, sems.at[1]),
            pltpu.make_async_copy(doc_hbm, doc_lengths, sems.at[2]),
        ]
    )
    lane = lax.broadcasted_iota(jnp.int32, (1, HD), 1)

    def one(index, carry):
        start, starts, ends = carry
        end = start + doc_lengths[index]
        starts = jnp.where(lane == index, start, starts)
        return (end, starts, jnp.where(lane == index, end, ends))

    none = jnp.zeros((1, HD), jnp.int32)
    _, starts, ends = lax.fori_loop(0, docs, one, (jnp.int32(0), none, none), unroll=8)
    starts_t, ends_t = (
        jnp.transpose(jnp.broadcast_to(row.astype(jnp.float32), (HD, HD))).astype(jnp.int32)
        for row in (starts, ends)
    )
    for slot in (0, 1):
        own_kv, query_t, dout_t, documents = refs[4 * slot : 4 * slot + 4]
        own_kv[...] = (far_kv, near_kv)[slot][...]
        own_rows = half_start(rows, slot)
        for step in range(rows // TQ):
            source = pl.ds(own_rows + step * TQ, TQ)
            for h in range(heads):
                place = slice(step * wide + h * TQ, step * wide + (h + 1) * TQ)
                columns = slice(h * HD, (h + 1) * HD)
                query_t[0:HD, place] = jnp.transpose(query[source, columns])
                dout_t[:, place] = jnp.transpose(dout[source, columns])
        position = block_number(count, slot) * rows
        for tile in range(3 * rows // TQ):
            at = lax.broadcasted_iota(jnp.int32, (TQ, HD), 0) + (position - 2 * rows + tile * TQ)
            inside = jnp.logical_and(at >= starts, at < ends)
            inside = jnp.logical_or(inside, at < 0)
            documents[tile * TQ : (tile + 1) * TQ, :] = jnp.where(inside, 1.0, 0.0).astype(
                documents.dtype
            )
        for step in range(rows // TQ):
            at = lax.broadcasted_iota(jnp.int32, (HD, TQ), 1) + (position + step * TQ)
            inside = jnp.logical_and(at >= starts_t, at < ends_t)
            other = jnp.where(inside, 0.0, other_document).astype(query_t.dtype)
            for h in range(heads):
                place = slice(step * wide + h * TQ, step * wide + (h + 1) * TQ)
                query_t[HD : 2 * HD, place] = other


def prepare(count, doc_lengths, query, dout, far_kv, near_kv):
    rows = query.shape[0] // 2
    heads = query.shape[1] // HD
    pair = jax.ShapeDtypeStruct(far_kv.shape, far_kv.dtype)
    stacked_t = jax.ShapeDtypeStruct((HD, rows * heads), query.dtype)
    query_shape = jax.ShapeDtypeStruct((2 * HD, rows * heads), query.dtype)
    documents = jax.ShapeDtypeStruct((3 * rows, HD), query.dtype)
    assert doc_lengths.shape[0] <= HD
    return pl.pallas_call(
        functools.partial(prepare_kernel, rows, heads, doc_lengths.shape[0], count),
        out_shape=(pair, query_shape, stacked_t, documents) * 2,
        in_specs=[VMEM] * 2 + [HBM] * 3,
        out_specs=[VMEM] * 8,
        scratch_shapes=[
            pltpu.SMEM(doc_lengths.shape, doc_lengths.dtype),
            pltpu.VMEM(query.shape, query.dtype),
            pltpu.VMEM(dout.shape, dout.dtype),
            pltpu.SemaphoreType.DMA((3,)),
        ],
        compiler_params=pltpu.CompilerParams(vmem_limit_bytes=VMEM_LIMIT),
        cost_estimate=pl.CostEstimate(flops=0, bytes_accessed=4 * 2**20, transcendentals=0),
        name="prepare",
    )(far_kv, near_kv, *(in_hbm(array) for array in (doc_lengths, query, dout)))


class Window:
    def __init__(self, rows, slot):
        self.tiles = rows // TQ
        self.chunks = 2 * self.tiles + 1
        self.steps = range(self.tiles)
        self.late = [self.tiles - step for step in self.steps]
        self.middle = [(1 - slot) * self.tiles for step in self.steps]
        self.early = [
            self.chunks - late - middle for late, middle in zip(self.late, self.middle)
        ]


def chunk_rows(counts, step, first=0, count=None):
    start = sum(counts[:step]) + first
    count = counts[step] - first if count is None else count
    return slice(start * CHUNK, (start + count) * CHUNK)


def run_length(run):
    return run[-1].stop - run[-1].start


def runs_of(chunks):
    runs = []
    for chunk in chunks:
        if runs:
            last = runs[-1]
            length = run_length(last)
            if last[1] is chunk[1] and last[2] + length == chunk[2] and length < RUN * CHUNK:
                runs[-1] = (*last[:-1], slice(last[-1].start, chunk[-1].stop))
                continue
        runs.append(chunk)
    return runs


def exponentials(jobs, rows, heads, scores):
    back = 2 * rows
    wide = heads * TQ
    base2 = SCALE * math.log2(math.e)

    def score(job, index, row_max):
        step, chunks, (query_t, _, documents), _, _ = jobs[job]
        chunk, keys, row = chunks[index][0:3]
        tile = slice(step * wide, (step + 1) * wide)
        length = run_length(chunks[index])
        window = slice(step * TQ + chunk * CHUNK, step * TQ + chunk * CHUNK + length)
        product = dot_nn(
            jnp.concatenate([keys[row : row + length, :], documents[window, :]], axis=1),
            query_t[:, tile],
        )
        for start in range(0, length, GROUP):
            place = chunk * CHUNK + start
            for h in range(heads):
                lanes = slice(h * TQ, (h + 1) * TQ)
                part = product[start : start + GROUP, lanes]
                if place >= back:
                    key_at = lax.broadcasted_iota(jnp.int32, (GROUP, TQ), 0) + (place - back)
                    query_at = lax.broadcasted_iota(jnp.int32, (GROUP, TQ), 1)
                    part = jnp.where(key_at <= query_at, part, masked_score)
                scores[job % 2, place : place + GROUP, lanes] = part
                for row8 in range(0, GROUP, 8):
                    row_max[h] = jnp.maximum(row_max[h], part[row8 : row8 + 8, :])

    def start_max():
        return [jnp.full((8, TQ), masked_score, jnp.float32)] * heads

    pending = None
    following = start_max()
    for index in range(len(jobs[0][1])):
        score(0, index, following)
    for job, (step, chunks, (_, dout_t, _), first_max, end) in enumerate(jobs):
        tile = slice(step * wide, (step + 1) * wide)
        row_max = jnp.concatenate(
            [jnp.max(part, axis=0, keepdims=True) * base2 for part in following], axis=1
        )
        if first_max is not None:
            row_max = jnp.maximum(row_max, first_max)
        following = start_max()
        ahead = len(jobs[job + 1][1]) if job + 1 < len(jobs) else 0
        done = 0
        total = jnp.zeros((8, wide), jnp.float32)
        delta = jnp.zeros((8, wide), jnp.float32)
        for index, (chunk, keys, row, weights, dprobs, kept) in enumerate(chunks):
            length = kept.stop - kept.start
            product = dot_nn(keys[rows + row : rows + row + length, :], dout_t[:, tile])
            for start in range(0, length, GROUP):
                place = chunk * CHUNK + start
                there = slice(kept.start + start, kept.start + start + GROUP)
                dprob = product[start : start + GROUP, :]
                dprobs[there, :] = dprob.astype(jnp.bfloat16)
                part = jnp.exp2(scores[job % 2, place : place + GROUP, :] * base2 - row_max)
                weights[there, :] = part.astype(jnp.bfloat16)
                term = part * dprob
                for row8 in range(0, GROUP, 8):
                    total = total + part[row8 : row8 + 8, :]
                    delta = delta + term[row8 : row8 + 8, :]
            while done * len(chunks) < ahead * (index + 1):
                score(job + 1, done, following)
                done += 1
            if index == 0 and pending is not None:
                pending()
        sums = [jnp.sum(part, axis=0, keepdims=True) for part in (total, delta)]
        pending = functools.partial(end, row_max, *sums)
    pending()


def group_kernel(rows, heads, slot, middle, query_t, dout_t, documents, *refs):
    (weights, dprobs, stats, scores) = refs[-4:]
    prev1 = refs[0] if middle or slot == 1 else None
    own_kv = None if middle else refs[slot]
    window = Window(rows, slot)
    counts = window.middle if middle else window.early
    jobs = []
    for step in window.steps:
        chunks = []
        for index in range(counts[step]):
            chunk = window.late[step] + (0 if middle else window.middle[step]) + index
            row = step * TQ + chunk * CHUNK
            keys = own_kv if row >= 2 * rows else prev1
            kept = chunk_rows(counts, step, index, 1)
            chunks.append((chunk, keys, row % rows, weights, dprobs, kept))

        def end(*found, step=step):
            for kind, value in enumerate(found):
                stats[8 * kind + step : 8 * kind + step + 1, :] = value

        first_max = refs[1][step : step + 1, :] if middle else None
        jobs.append((step, runs_of(chunks), (query_t, dout_t, documents), first_max, end))
    exponentials(jobs, rows, heads, scores)


def group_scores(slot, middle, ready, *operands):
    rows = ready[0].shape[0] // 2
    heads = ready[1].shape[1] // rows
    wide = heads * TQ
    window = Window(rows, slot)
    counts = window.middle if middle else window.early
    kept = jax.ShapeDtypeStruct((sum(counts) * CHUNK, wide), jnp.bfloat16)
    cost = (0 if slot else 2**33) if not middle else 0
    return pl.pallas_call(
        functools.partial(group_kernel, rows, heads, slot, middle),
        out_shape=(kept, kept, jax.ShapeDtypeStruct((24, wide), jnp.float32)),
        in_specs=[VMEM] * (3 + len(operands)),
        out_specs=[VMEM] * 3,
        scratch_shapes=[pltpu.VMEM((2, 2 * rows + TQ, wide), jnp.float32)],
        compiler_params=pltpu.CompilerParams(vmem_limit_bytes=VMEM_LIMIT),
        cost_estimate=pl.CostEstimate(flops=cost, bytes_accessed=0, transcendentals=0),
        name="middle_far" if middle else "early_far" if slot == 0 else "early_near",
    )(*ready[1:4], *operands)


def scaled_by(array, tile, factor):
    return (array[0:HD, tile].astype(jnp.float32) * factor).astype(jnp.bfloat16)


def dscore_rows(dscores, there, weights, dprobs, kept, delta):
    delta = jnp.broadcast_to(delta, (16, delta.shape[1]))
    for start in range(0, there.stop - there.start, 16):
        out = slice(there.start + start, there.start + start + 16)
        place = slice(kept.start + start, kept.start + start + 16)
        dscores[out, :] = weights[place, :] * (dprobs[place, :] - delta)


def add_products(new, columns, products):
    for total_ref, side, terms in products:
        term = dot_nt(side, terms)
        if new:
            total_ref[:, columns] = term
        else:
            total_ref[:, columns] += term


def late_kernel(rows, heads, slot, query_t, dout_t, documents, prev2, *refs):
    groups = refs[0 : 2 - slot]
    (weights, dscores, stats, prev2_out, scores, dprobs, dk, dv) = refs[2 - slot :]
    wide = heads * TQ
    window = Window(rows, slot)
    jobs = []
    for step in window.steps:
        chunks = []
        for chunk in range(window.late[step]):
            kept = chunk_rows(window.late, step, chunk, 1)
            chunks.append((chunk, prev2, step * TQ + chunk * CHUNK, weights, dprobs, kept))

        def end(row_max, total, delta, step=step):
            tile = slice(step * wide, (step + 1) * wide)
            rows_of = [
                [group[8 * kind + step : 8 * kind + step + 1, :] for kind in range(3)]
                for group in groups
            ]
            shrinks = [jnp.exp2(found[0] - row_max) for found in rows_of]
            for found, shrink in zip(rows_of, shrinks):
                total = total + found[1] * shrink
                delta = delta + found[2] * shrink
            late_factor = 1.0 / total
            delta = delta * late_factor
            factors = [late_factor * shrink for shrink in shrinks]
            for kind, value in enumerate((late_factor, factors[0], delta, factors[-1])):
                stats[8 * kind + step : 8 * kind + step + 1, :] = value
            there = chunk_rows(window.late, step)
            dscore_rows(dscores, there, weights, dprobs, there, delta.astype(jnp.bfloat16))
            add_products(
                step == 0,
                slice(step * TQ, rows),
                (
                    (dv, scaled_by(dout_t, tile, late_factor), weights[there, :]),
                    (dk, scaled_by(query_t, tile, late_factor), dscores[there, :]),
                ),
            )

        first_max = groups[-1][step : step + 1, :]
        jobs.append((step, runs_of(chunks), (query_t, dout_t, documents), first_max, end))
    exponentials(jobs, rows, heads, scores)
    prev2_out[0:HD] = (dk[...] * SCALE).astype(prev2_out.dtype)
    prev2_out[HD : 2 * HD] = dv[...].astype(prev2_out.dtype)


def late_scores(slot, ready, groups, prev2):
    rows = prev2.shape[0] // 2
    heads = ready[1].shape[1] // rows
    wide = heads * TQ
    late = jax.ShapeDtypeStruct((sum(Window(rows, slot).late) * CHUNK, wide), jnp.bfloat16)
    return pl.pallas_call(
        functools.partial(late_kernel, rows, heads, slot),
        out_shape=(
            late,
            late,
            jax.ShapeDtypeStruct((32, wide), jnp.float32),
            jax.ShapeDtypeStruct((2 * HD, rows), jnp.bfloat16),
        ),
        in_specs=[VMEM] * (4 + len(groups)),
        out_specs=[VMEM] * 4,
        scratch_shapes=[
            pltpu.VMEM((2, rows, wide), jnp.float32),
            pltpu.VMEM(late.shape, late.dtype),
            pltpu.VMEM((HD, rows), jnp.float32),
            pltpu.VMEM((HD, rows), jnp.float32),
        ],
        compiler_params=pltpu.CompilerParams(vmem_limit_bytes=VMEM_LIMIT),
        cost_estimate=pl.CostEstimate(flops=2**31, bytes_accessed=0, transcendentals=0),
        name="late_far" if slot == 0 else "late_near",
    )(*ready[1:4], prev2, *groups)


def gated_kernel(rows, heads, slots, core, *refs):
    here = lax.axis_index("ctx") % 2 == core
    count = 5 * len(slots)
    given = len(refs) - count - 2 - 2 * len(slots)
    pl.when(here)(lambda: grads_kernel(rows, heads, slots, *refs[0:count], *refs[count + given :]))

    if given:

        @pl.when(jnp.logical_not(here))
        def _():
            for source, out in zip(refs[count : count + given], refs[count + given :]):
                out[...] = source[...]


def grads_kernel(rows, heads, slots, *refs):
    wide = heads * TQ
    outs = list(refs[5 * len(slots) : -2])
    (dk, dv) = refs[-2:]
    for part, (slot, middle) in enumerate(slots):
        (query_t, dout_t, stats, weights, dprobs) = refs[5 * part : 5 * part + 5]
        dscores = outs.pop(0)
        window = Window(rows, slot)
        counts = window.middle if middle else window.early
        for step in reversed(window.steps):
            tile = slice(step * wide, (step + 1) * wide)
            _, early_factor, delta, middle_factor = (
                stats[8 * kind + step : 8 * kind + step + 1, :] for kind in range(4)
            )
            factor = middle_factor if middle else early_factor
            there = chunk_rows(counts, step)
            dscore_rows(dscores, there, weights, dprobs, there, delta.astype(jnp.bfloat16))
            add_products(
                step == window.tiles - 1,
                slice(0, counts[step] * CHUNK),
                (
                    (dv, scaled_by(dout_t, tile, factor), weights[there, :]),
                    (dk, scaled_by(query_t, tile, factor), dscores[there, :]),
                ),
            )
        for block in range(counts[-1] // window.tiles):
            out = outs.pop(0)
            place = slice(block * rows, (block + 1) * rows)
            out[0:HD] = (dk[:, place] * SCALE).astype(out.dtype)
            out[HD : 2 * HD] = dv[:, place].astype(out.dtype)


def rest_grads(name, cost, parts, core=None, given=()):
    rows = parts[0][2][0].shape[0] // 2
    heads = parts[0][2][1].shape[1] // rows
    operands, out_shape = [], []
    for slot, middle, (_, query_t, dout_t, _, stats, weights, dprobs), sent in parts:
        window = Window(rows, slot)
        kept = (sum(window.middle if middle else window.early) * CHUNK, heads * TQ)
        operands += [query_t, dout_t, stats, weights, dprobs]
        out_shape.append(jax.ShapeDtypeStruct(kept, jnp.bfloat16))
        for one in sent:
            kind = jnp.bfloat16 if one else jnp.float32
            out_shape.append(jax.ShapeDtypeStruct((2 * HD, rows), kind))
    slots = tuple(part[0:2] for part in parts)
    operands += given
    kernel = functools.partial(grads_kernel, rows, heads, slots)
    if core is not None:
        kernel = functools.partial(gated_kernel, rows, heads, slots, core)
    return pl.pallas_call(
        kernel,
        out_shape=out_shape,
        in_specs=[VMEM] * len(operands),
        out_specs=[VMEM] * len(out_shape),
        scratch_shapes=[pltpu.VMEM((HD, 2 * rows), jnp.float32)] * 2,
        compiler_params=pltpu.CompilerParams(vmem_limit_bytes=VMEM_LIMIT),
        cost_estimate=pl.CostEstimate(flops=cost, bytes_accessed=0, transcendentals=0),
        name=name,
    )(*operands)


def outputs_kernel(rows, heads, *refs):
    blocks = (refs[0:3], refs[3:6], refs[6:9], refs[9]), (refs[10:13], refs[13:15], refs[15:17], refs[17])
    (attended, grad_query, keys_t, values_t) = refs[18:]
    for slot, (sources, weights, dscores, stats) in enumerate(blocks):
        window = Window(rows, slot)
        groups = [(window.late, 0), (window.early, 1)]
        if slot == 0:
            groups.insert(1, (window.middle, 3))
        own_rows = half_start(rows, slot)
        for place, source in enumerate(sources):
            for tile in range(rows // TQ):
                part = slice(place * rows + tile * TQ, place * rows + (tile + 1) * TQ)
                row = tile * TQ
                keys_t[:, part] = jnp.transpose(source[row : row + TQ, :])
                values_t[:, part] = jnp.transpose(source[rows + row : rows + row + TQ, :])
        for step in window.steps:
            place = pl.ds(own_rows + step * TQ, TQ)
            for out, side, terms, scale in (
                (attended, values_t, weights, 1.0),
                (grad_query, keys_t, dscores, SCALE),
            ):
                found = None
                start = step * TQ
                for (counts, kind), term in zip(groups, terms):
                    columns = slice(start, start + counts[step] * CHUNK)
                    start = columns.stop
                    factor = stats[8 * kind + step : 8 * kind + step + 1, :] * scale
                    part = dot_nn(side[:, columns], term[chunk_rows(counts, step), :]) * factor
                    found = part if found is None else found + part
                for h in range(heads):
                    part = found[:, h * TQ : (h + 1) * TQ]
                    out[place, h * HD : (h + 1) * HD] = jnp.transpose(part).astype(out.dtype)


def block_outputs(query, far, near):
    rows = query.shape[0] // 2
    heads = query.shape[1] // HD
    shape = jax.ShapeDtypeStruct(query.shape, query.dtype)
    return pl.pallas_call(
        functools.partial(outputs_kernel, rows, heads),
        out_shape=(shape, shape),
        in_specs=[VMEM] * 18,
        out_specs=[VMEM] * 2,
        scratch_shapes=[pltpu.VMEM((HD, 3 * rows), jnp.bfloat16)] * 2,
        compiler_params=pltpu.CompilerParams(vmem_limit_bytes=VMEM_LIMIT),
        cost_estimate=pl.CostEstimate(flops=0, bytes_accessed=0, transcendentals=0),
        name="block_outputs",
    )(*far, *near)


def total_kernel(rows, far_own, far_1, far_2, near, grad_key, grad_value):
    far = far_own[...] + far_1[...].astype(jnp.float32) + far_2[...].astype(jnp.float32)
    for slot, total in ((0, far), (1, near[...])):
        place = pl.ds(half_start(rows, slot), rows)
        grad_key[place, :] = jnp.transpose(total[0:HD]).astype(grad_key.dtype)
        grad_value[place, :] = jnp.transpose(total[HD : 2 * HD]).astype(grad_value.dtype)


def total_grads(*parts):
    rows = parts[0].shape[1]
    shape = jax.ShapeDtypeStruct((2 * rows, HD), jnp.bfloat16)
    return pl.pallas_call(
        functools.partial(total_kernel, rows),
        out_shape=(shape, shape),
        in_specs=[VMEM] * 4,
        out_specs=[VMEM] * 2,
        compiler_params=pltpu.CompilerParams(vmem_limit_bytes=VMEM_LIMIT),
        name="total_grads",
    )(*parts)


def body(query, key, value, d_out, doc_lengths):
    count = lax.axis_size("ctx")

    def holder(block):
        return block if block < count else 2 * count - 1 - block

    def move(array, pairs):
        return lax.ppermute(array, "ctx", pairs)

    near_on = [(holder(b), holder(b + 2)) for b in range(1, 2 * count - 2, 2)]
    far_on = [(holder(b), holder(b + 2)) for b in range(0, 2 * count - 2, 2)]
    near_to_far = [(holder(b), holder(b + 1)) for b in range(1, 2 * count - 2, 2)]
    swap = [(d, d ^ 1) for d in range(count)]
    near_back = [(t, s) for s, t in near_on]
    far_back = [(t, s) for s, t in far_on]

    rows = key.shape[0] // 2
    odd = lax.axis_index("ctx") % 2 == 1
    lower = jnp.concatenate([key[:rows], value[:rows]], axis=0)
    upper = jnp.concatenate([key[rows:], value[rows:]], axis=0)
    near_kv, far_kv = jnp.where(odd, lower, upper), jnp.where(odd, upper, lower)
    far_1 = move(near_kv, near_to_far)
    far_2 = move(far_kv, far_on)
    prepared = prepare(count, doc_lengths, query, d_out, far_kv, near_kv)
    far_ready, near_ready = prepared[0:4], prepared[4:8]
    near_1 = move(far_ready[0], swap)
    far_early = group_scores(0, False, far_ready, far_ready[0])
    near_early = group_scores(1, False, near_ready, near_1, near_ready[0])
    far_1, near_early = lax.optimization_barrier((far_1, near_early))
    far_middle = group_scores(0, True, far_ready, far_1, far_early[2])
    far_late = late_scores(0, far_ready, (far_early[2], far_middle[2]), far_2)
    near_2 = move(far_1, swap)
    middle = [(0, True, (*far_ready, far_late[2], *far_middle[0:2]), (True,))]
    odd_grads = rest_grads("grads_far_odd", 0, middle, 1)
    far_g2, odd_grads = lax.optimization_barrier((far_late[3], odd_grads))
    from_far_2 = move(far_g2, far_back)
    near_2, odd_grads = lax.optimization_barrier((near_2, odd_grads))
    far_middle_d, far_g1 = rest_grads("grads_far", 0, middle, 0, odd_grads)
    relayed = move(far_g1, swap)
    near_late = late_scores(1, near_ready, (near_early[2],), near_2)
    near_sum = near_late[3].astype(jnp.float32) + relayed.astype(jnp.float32)
    from_near_2 = move(near_sum.astype(jnp.bfloat16), near_back)
    near_early_d, near_g1, near_own, far_early_d, far_own = rest_grads(
        "grads_near",
        2**31,
        [
            (1, False, (*near_ready, near_late[2], *near_early[0:2]), (True, False)),
            (0, False, (*far_ready, far_late[2], *far_early[0:2]), (False,)),
        ],
    )
    near_g1, from_far_2 = lax.optimization_barrier((near_g1, from_far_2))
    from_near_1 = move(near_g1, swap)
    attended, grad_query = block_outputs(
        query,
        (
            *(far_2, far_1, far_ready[0]),
            *(far_late[0], far_middle[0], far_early[0]),
            *(far_late[1], far_middle_d, far_early_d),
            far_late[2],
        ),
        (
            *(near_2, near_1, near_ready[0]),
            *(near_late[0], near_early[0]),
            *(near_late[1], near_early_d),
            near_late[2],
        ),
    )
    near_total = near_own + from_near_2.astype(jnp.float32)
    grad_key, grad_value = total_grads(far_own, from_near_1, from_far_2, near_total)
    return (attended, grad_query, grad_key, grad_value)


def solution(mesh):
    rows = P(("dp", "ctx"), None)
    return jax.shard_map(
        body,
        mesh=mesh,
        in_specs=(rows, rows, rows, rows, P("dp")),
        out_specs=(rows, rows, rows, rows),
        check_vma=False,
    )
```

```python
import functools
import math

import jax
import jax.numpy as jnp
from jax import lax
from jax.experimental import pallas as pl
from jax.experimental.pallas import tpu as pltpu
from jax.sharding import PartitionSpec as P

HD = 128
TQ = 128
GROUP = 32

masked_score = -1e30
other_document = -65536.0
VMEM_LIMIT = 24 * 1024 * 1024
SCALE = 1.0 / math.sqrt(HD)
VMEM = pl.BlockSpec(memory_space=pltpu.VMEM)
HBM = pl.BlockSpec(memory_space=pltpu.HBM)
CHUNK = 128
RUN = 3


def dot_nt(a, b):
    return lax.dot_general(a, b, (((1,), (1,)), ((), ())), preferred_element_type=jnp.float32)


def dot_nn(a, b):
    return lax.dot_general(a, b, (((1,), (0,)), ((), ())), preferred_element_type=jnp.float32)


def half_start(rows, slot):
    odd = lax.axis_index("ctx") % 2
    return pl.multiple_of((odd if slot == 0 else 1 - odd) * rows, rows)


def block_number(count, slot):
    device = lax.axis_index("ctx")
    in_lower = device % 2 == slot
    return jnp.where(in_lower, device, 2 * count - 1 - device)


def in_hbm(array):
    return pltpu.with_memory_space_constraint(array, pltpu.HBM)


def load_block(rows, slot, key, value, out, sems):
    place = pl.ds(half_start(rows, slot), rows)
    return [
        pltpu.make_async_copy(key.at[place], out.at[0:rows], sems.at[2 * slot]),
        pltpu.make_async_copy(value.at[place], out.at[rows : 2 * rows], sems.at[2 * slot + 1]),
    ]


def run_copies(copies):
    for copy in copies:
        copy.start()
    for copy in copies:
        copy.wait()


def prepare_kernel(rows, heads, docs, count, *refs):
    (far_kv, near_kv, doc_hbm, query_hbm, dout_hbm) = refs[0:5]
    (doc_lengths, query, dout, sems) = refs[13:]
    refs = refs[5:13]
    wide = heads * TQ
    run_copies(
        [
            pltpu.make_async_copy(query_hbm, query, sems.at[0]),
            pltpu.make_async_copy(dout_hbm, dout, sems.at[1]),
            pltpu.make_async_copy(doc_hbm, doc_lengths, sems.at[2]),
        ]
    )
    lane = lax.broadcasted_iota(jnp.int32, (1, HD), 1)

    def one(index, carry):
        start, starts, ends = carry
        end = start + doc_lengths[index]
        starts = jnp.where(lane == index, start, starts)
        return (end, starts, jnp.where(lane == index, end, ends))

    none = jnp.zeros((1, HD), jnp.int32)
    _, starts, ends = lax.fori_loop(0, docs, one, (jnp.int32(0), none, none), unroll=8)
    starts_t, ends_t = (
        jnp.transpose(jnp.broadcast_to(row.astype(jnp.float32), (HD, HD))).astype(jnp.int32)
        for row in (starts, ends)
    )
    for slot in (0, 1):
        own_kv, query_t, dout_t, documents = refs[4 * slot : 4 * slot + 4]
        own_kv[...] = (far_kv, near_kv)[slot][...]
        own_rows = half_start(rows, slot)
        for step in range(rows // TQ):
            source = pl.ds(own_rows + step * TQ, TQ)
            for h in range(heads):
                place = slice(step * wide + h * TQ, step * wide + (h + 1) * TQ)
                columns = slice(h * HD, (h + 1) * HD)
                query_t[0:HD, place] = jnp.transpose(query[source, columns])
                dout_t[:, place] = jnp.transpose(dout[source, columns])
        position = block_number(count, slot) * rows
        for tile in range(3 * rows // TQ):
            at = lax.broadcasted_iota(jnp.int32, (TQ, HD), 0) + (position - 2 * rows + tile * TQ)
            inside = jnp.logical_and(at >= starts, at < ends)
            inside = jnp.logical_or(inside, at < 0)
            documents[tile * TQ : (tile + 1) * TQ, :] = jnp.where(inside, 1.0, 0.0).astype(
                documents.dtype
            )
        for step in range(rows // TQ):
            at = lax.broadcasted_iota(jnp.int32, (HD, TQ), 1) + (position + step * TQ)
            inside = jnp.logical_and(at >= starts_t, at < ends_t)
            other = jnp.where(inside, 0.0, other_document).astype(query_t.dtype)
            for h in range(heads):
                place = slice(step * wide + h * TQ, step * wide + (h + 1) * TQ)
                query_t[HD : 2 * HD, place] = other


def prepare(count, doc_lengths, query, dout, far_kv, near_kv):
    rows = query.shape[0] // 2
    heads = query.shape[1] // HD
    pair = jax.ShapeDtypeStruct(far_kv.shape, far_kv.dtype)
    stacked_t = jax.ShapeDtypeStruct((HD, rows * heads), query.dtype)
    query_shape = jax.ShapeDtypeStruct((2 * HD, rows * heads), query.dtype)
    documents = jax.ShapeDtypeStruct((3 * rows, HD), query.dtype)
    assert doc_lengths.shape[0] <= HD
    return pl.pallas_call(
        functools.partial(prepare_kernel, rows, heads, doc_lengths.shape[0], count),
        out_shape=(pair, query_shape, stacked_t, documents) * 2,
        in_specs=[VMEM] * 2 + [HBM] * 3,
        out_specs=[VMEM] * 8,
        scratch_shapes=[
            pltpu.SMEM(doc_lengths.shape, doc_lengths.dtype),
            pltpu.VMEM(query.shape, query.dtype),
            pltpu.VMEM(dout.shape, dout.dtype),
            pltpu.SemaphoreType.DMA((3,)),
        ],
        compiler_params=pltpu.CompilerParams(vmem_limit_bytes=VMEM_LIMIT),
        cost_estimate=pl.CostEstimate(flops=0, bytes_accessed=4 * 2**20, transcendentals=0),
        name="prepare",
    )(far_kv, near_kv, *(in_hbm(array) for array in (doc_lengths, query, dout)))


class Window:
    def __init__(self, rows, slot):
        self.tiles = rows // TQ
        self.chunks = 2 * self.tiles + 1
        self.steps = range(self.tiles)
        self.late = [self.tiles - step for step in self.steps]
        self.middle = [(1 - slot) * self.tiles for step in self.steps]
        self.early = [
            self.chunks - late - middle for late, middle in zip(self.late, self.middle)
        ]


def chunk_rows(counts, step, first=0, count=None):
    start = sum(counts[:step]) + first
    count = counts[step] - first if count is None else count
    return slice(start * CHUNK, (start + count) * CHUNK)


def run_length(run):
    return run[-1].stop - run[-1].start


def runs_of(chunks):
    runs = []
    for chunk in chunks:
        if runs:
            last = runs[-1]
            length = run_length(last)
            if last[1] is chunk[1] and last[2] + length == chunk[2] and length < RUN * CHUNK:
                runs[-1] = (*last[:-1], slice(last[-1].start, chunk[-1].stop))
                continue
        runs.append(chunk)
    return runs


def exponentials(jobs, rows, heads, scores, scores_first=False):
    back = 2 * rows
    wide = heads * TQ
    base2 = SCALE * math.log2(math.e)

    def score(job, index, row_max):
        step, chunks, (query_t, _, documents), _, _ = jobs[job]
        chunk, keys, row = chunks[index][0:3]
        tile = slice(step * wide, (step + 1) * wide)
        length = run_length(chunks[index])
        window = slice(step * TQ + chunk * CHUNK, step * TQ + chunk * CHUNK + length)
        product = dot_nn(
            jnp.concatenate([keys[row : row + length, :], documents[window, :]], axis=1),
            query_t[:, tile],
        )
        for start in range(0, length, GROUP):
            place = chunk * CHUNK + start
            for h in range(heads):
                lanes = slice(h * TQ, (h + 1) * TQ)
                part = product[start : start + GROUP, lanes]
                if place >= back:
                    key_at = lax.broadcasted_iota(jnp.int32, (GROUP, TQ), 0) + (place - back)
                    query_at = lax.broadcasted_iota(jnp.int32, (GROUP, TQ), 1)
                    part = jnp.where(key_at <= query_at, part, masked_score)
                scores[job % scores.shape[0], place : place + GROUP, lanes] = part
                for row8 in range(0, GROUP, 8):
                    row_max[h] = jnp.maximum(row_max[h], part[row8 : row8 + 8, :])

    def start_max():
        return [jnp.full((8, TQ), masked_score, jnp.float32)] * heads

    pending = None
    every = [start_max() for _ in jobs]
    for job in range(len(jobs) if scores_first else 1):
        for index in range(len(jobs[job][1])):
            score(job, index, every[job])
    for job, (step, chunks, (_, dout_t, _), first_max, end) in enumerate(jobs):
        tile = slice(step * wide, (step + 1) * wide)
        row_max = jnp.concatenate(
            [jnp.max(part, axis=0, keepdims=True) * base2 for part in every[job]], axis=1
        )
        if first_max is not None:
            row_max = jnp.maximum(row_max, first_max)
        ahead = len(jobs[job + 1][1]) if job + 1 < len(jobs) and not scores_first else 0
        done = 0
        total = jnp.zeros((8, wide), jnp.float32)
        delta = jnp.zeros((8, wide), jnp.float32)
        for index, (chunk, keys, row, weights, dprobs, kept) in enumerate(chunks):
            length = kept.stop - kept.start
            product = dot_nn(keys[rows + row : rows + row + length, :], dout_t[:, tile])
            for start in range(0, length, GROUP):
                place = chunk * CHUNK + start
                there = slice(kept.start + start, kept.start + start + GROUP)
                dprob = product[start : start + GROUP, :]
                dprobs[there, :] = dprob.astype(jnp.bfloat16)
                part = jnp.exp2(scores[job % scores.shape[0], place : place + GROUP, :] * base2 - row_max)
                weights[there, :] = part.astype(jnp.bfloat16)
                term = part * dprob
                for row8 in range(0, GROUP, 8):
                    total = total + part[row8 : row8 + 8, :]
                    delta = delta + term[row8 : row8 + 8, :]
            while done * len(chunks) < ahead * (index + 1):
                score(job + 1, done, every[job + 1])
                done += 1
            if index == 0 and pending is not None:
                pending()
        sums = [jnp.sum(part, axis=0, keepdims=True) for part in (total, delta)]
        pending = functools.partial(end, row_max, *sums)
    pending()


def group_kernel(rows, heads, slot, middle, query_t, dout_t, documents, *refs):
    (weights, dprobs, stats, scores) = refs[-4:]
    prev1 = refs[0] if middle or slot == 1 else None
    own_kv = None if middle else refs[slot]
    window = Window(rows, slot)
    counts = window.middle if middle else window.early
    jobs = []
    for step in window.steps:
        chunks = []
        for index in range(counts[step]):
            chunk = window.late[step] + (0 if middle else window.middle[step]) + index
            row = step * TQ + chunk * CHUNK
            keys = own_kv if row >= 2 * rows else prev1
            kept = chunk_rows(counts, step, index, 1)
            chunks.append((chunk, keys, row % rows, weights, dprobs, kept))

        def end(*found, step=step):
            for kind, value in enumerate(found):
                stats[8 * kind + step : 8 * kind + step + 1, :] = value

        first_max = refs[1][step : step + 1, :] if middle else None
        jobs.append((step, runs_of(chunks), (query_t, dout_t, documents), first_max, end))
    exponentials(jobs, rows, heads, scores)


def group_scores(slot, middle, ready, *operands):
    rows = ready[0].shape[0] // 2
    heads = ready[1].shape[1] // rows
    wide = heads * TQ
    window = Window(rows, slot)
    counts = window.middle if middle else window.early
    kept = jax.ShapeDtypeStruct((sum(counts) * CHUNK, wide), jnp.bfloat16)
    cost = (0 if slot else 2**33) if not middle else 0
    return pl.pallas_call(
        functools.partial(group_kernel, rows, heads, slot, middle),
        out_shape=(kept, kept, jax.ShapeDtypeStruct((24, wide), jnp.float32)),
        in_specs=[VMEM] * (3 + len(operands)),
        out_specs=[VMEM] * 3,
        scratch_shapes=[pltpu.VMEM((2, 2 * rows + TQ, wide), jnp.float32)],
        compiler_params=pltpu.CompilerParams(vmem_limit_bytes=VMEM_LIMIT),
        cost_estimate=pl.CostEstimate(flops=cost, bytes_accessed=0, transcendentals=0),
        name="middle_far" if middle else "early_far" if slot == 0 else "early_near",
    )(*ready[1:4], *operands)


def scaled_by(array, tile, factor):
    return (array[0:HD, tile].astype(jnp.float32) * factor).astype(jnp.bfloat16)


def dscore_rows(dscores, there, weights, dprobs, kept, delta):
    delta = jnp.broadcast_to(delta, (16, delta.shape[1]))
    for start in range(0, there.stop - there.start, 16):
        out = slice(there.start + start, there.start + start + 16)
        place = slice(kept.start + start, kept.start + start + 16)
        dscores[out, :] = weights[place, :] * (dprobs[place, :] - delta)


def add_products(new, columns, products):
    for total_ref, side, terms in products:
        term = dot_nt(side, terms)
        if new:
            total_ref[:, columns] = term
        else:
            total_ref[:, columns] += term


def late_kernel(rows, heads, slot, query_t, dout_t, documents, prev2, *refs):
    groups = refs[0 : 2 - slot]
    (weights, dscores, stats, prev2_out, scores, dprobs, dk, dv) = refs[2 - slot :]
    wide = heads * TQ
    window = Window(rows, slot)
    jobs = []
    for step in window.steps:
        chunks = []
        for chunk in range(window.late[step]):
            kept = chunk_rows(window.late, step, chunk, 1)
            chunks.append((chunk, prev2, step * TQ + chunk * CHUNK, weights, dprobs, kept))

        def end(row_max, total, delta, step=step):
            tile = slice(step * wide, (step + 1) * wide)
            rows_of = [
                [group[8 * kind + step : 8 * kind + step + 1, :] for kind in range(3)]
                for group in groups
            ]
            shrinks = [jnp.exp2(found[0] - row_max) for found in rows_of]
            for found, shrink in zip(rows_of, shrinks):
                total = total + found[1] * shrink
                delta = delta + found[2] * shrink
            late_factor = 1.0 / total
            delta = delta * late_factor
            factors = [late_factor * shrink for shrink in shrinks]
            for kind, value in enumerate((late_factor, factors[0], delta, factors[-1])):
                stats[8 * kind + step : 8 * kind + step + 1, :] = value
            there = chunk_rows(window.late, step)
            dscore_rows(dscores, there, weights, dprobs, there, delta.astype(jnp.bfloat16))
            add_products(
                step == 0,
                slice(step * TQ, rows),
                (
                    (dv, scaled_by(dout_t, tile, late_factor), weights[there, :]),
                    (dk, scaled_by(query_t, tile, late_factor), dscores[there, :]),
                ),
            )

        first_max = groups[-1][step : step + 1, :]
        jobs.append((step, runs_of(chunks), (query_t, dout_t, documents), first_max, end))
    exponentials(jobs, rows, heads, scores, True)
    prev2_out[0:HD] = (dk[...] * SCALE).astype(prev2_out.dtype)
    prev2_out[HD : 2 * HD] = dv[...].astype(prev2_out.dtype)


def late_scores(slot, ready, groups, prev2):
    rows = prev2.shape[0] // 2
    heads = ready[1].shape[1] // rows
    wide = heads * TQ
    late = jax.ShapeDtypeStruct((sum(Window(rows, slot).late) * CHUNK, wide), jnp.bfloat16)
    return pl.pallas_call(
        functools.partial(late_kernel, rows, heads, slot),
        out_shape=(
            late,
            late,
            jax.ShapeDtypeStruct((32, wide), jnp.float32),
            jax.ShapeDtypeStruct((2 * HD, rows), jnp.bfloat16),
        ),
        in_specs=[VMEM] * (4 + len(groups)),
        out_specs=[VMEM] * 4,
        scratch_shapes=[
            pltpu.VMEM((rows // TQ, rows, wide), jnp.float32),
            pltpu.VMEM(late.shape, late.dtype),
            pltpu.VMEM((HD, rows), jnp.float32),
            pltpu.VMEM((HD, rows), jnp.float32),
        ],
        compiler_params=pltpu.CompilerParams(vmem_limit_bytes=VMEM_LIMIT),
        cost_estimate=pl.CostEstimate(flops=2**31, bytes_accessed=0, transcendentals=0),
        name="late_far" if slot == 0 else "late_near",
    )(*ready[1:4], prev2, *groups)


def grads_kernel(rows, heads, slots, *refs):
    wide = heads * TQ
    outs = list(refs[5 * len(slots) : -2])
    (dk, dv) = refs[-2:]
    for part, (slot, middle) in enumerate(slots):
        (query_t, dout_t, stats, weights, dprobs) = refs[5 * part : 5 * part + 5]
        dscores = outs.pop(0)
        window = Window(rows, slot)
        counts = window.middle if middle else window.early
        for step in reversed(window.steps):
            tile = slice(step * wide, (step + 1) * wide)
            _, early_factor, delta, middle_factor = (
                stats[8 * kind + step : 8 * kind + step + 1, :] for kind in range(4)
            )
            factor = middle_factor if middle else early_factor
            there = chunk_rows(counts, step)
            dscore_rows(dscores, there, weights, dprobs, there, delta.astype(jnp.bfloat16))
            add_products(
                step == window.tiles - 1,
                slice(0, counts[step] * CHUNK),
                (
                    (dv, scaled_by(dout_t, tile, factor), weights[there, :]),
                    (dk, scaled_by(query_t, tile, factor), dscores[there, :]),
                ),
            )
        for block in range(counts[-1] // window.tiles):
            out = outs.pop(0)
            place = slice(block * rows, (block + 1) * rows)
            out[0:HD] = (dk[:, place] * SCALE).astype(out.dtype)
            out[HD : 2 * HD] = dv[:, place].astype(out.dtype)


def rest_grads(name, cost, parts):
    rows = parts[0][2][0].shape[0] // 2
    heads = parts[0][2][1].shape[1] // rows
    operands, out_shape = [], []
    for slot, middle, (_, query_t, dout_t, _, stats, weights, dprobs), sent in parts:
        window = Window(rows, slot)
        kept = (sum(window.middle if middle else window.early) * CHUNK, heads * TQ)
        operands += [query_t, dout_t, stats, weights, dprobs]
        out_shape.append(jax.ShapeDtypeStruct(kept, jnp.bfloat16))
        for one in sent:
            kind = jnp.bfloat16 if one else jnp.float32
            out_shape.append(jax.ShapeDtypeStruct((2 * HD, rows), kind))
    slots = tuple(part[0:2] for part in parts)
    return pl.pallas_call(
        functools.partial(grads_kernel, rows, heads, slots),
        out_shape=out_shape,
        in_specs=[VMEM] * len(operands),
        out_specs=[VMEM] * len(out_shape),
        scratch_shapes=[pltpu.VMEM((HD, 2 * rows), jnp.float32)] * 2,
        compiler_params=pltpu.CompilerParams(vmem_limit_bytes=VMEM_LIMIT),
        cost_estimate=pl.CostEstimate(flops=cost, bytes_accessed=0, transcendentals=0),
        name=name,
    )(*operands)


def outputs_kernel(rows, heads, *refs):
    blocks = (refs[0:3], refs[3:6], refs[6:9], refs[9]), (refs[10:13], refs[13:15], refs[15:17], refs[17])
    (attended_hbm, grad_query_hbm, attended, grad_query, keys_t, values_t, sems) = refs[18:]
    copies = []
    for slot, (sources, weights, dscores, stats) in enumerate(blocks):
        window = Window(rows, slot)
        groups = [(window.late, 0), (window.early, 1)]
        if slot == 0:
            groups.insert(1, (window.middle, 3))
        own_rows = half_start(rows, slot)
        for place, source in enumerate(sources):
            for tile in range(rows // TQ):
                part = slice(place * rows + tile * TQ, place * rows + (tile + 1) * TQ)
                row = tile * TQ
                keys_t[:, part] = jnp.transpose(source[row : row + TQ, :])
                values_t[:, part] = jnp.transpose(source[rows + row : rows + row + TQ, :])
        for step in window.steps:
            place = pl.ds(own_rows + step * TQ, TQ)
            for out, side, terms, scale in (
                (0, values_t, weights, 1.0),
                (1, keys_t, dscores, SCALE),
            ):
                found = None
                start = step * TQ
                for (counts, kind), term in zip(groups, terms):
                    columns = slice(start, start + counts[step] * CHUNK)
                    start = columns.stop
                    factor = stats[8 * kind + step : 8 * kind + step + 1, :] * scale
                    part = dot_nn(side[:, columns], term[chunk_rows(counts, step), :]) * factor
                    found = part if found is None else found + part
                target = (attended_hbm, grad_query_hbm)[out]
                source = (attended, grad_query)[out]
                for h in range(heads):
                    part = jnp.transpose(found[:, h * TQ : (h + 1) * TQ])
                    source[place, h * HD : (h + 1) * HD] = part.astype(source.dtype)
                copy = pltpu.make_async_copy(
                    source.at[place], target.at[place], sems.at[slot, step, out]
                )
                copy.start()
                copies.append(copy)
    for copy in copies:
        copy.wait()


def block_outputs(query, far, near):
    rows = query.shape[0] // 2
    heads = query.shape[1] // HD
    shape = jax.ShapeDtypeStruct(query.shape, query.dtype)
    return pl.pallas_call(
        functools.partial(outputs_kernel, rows, heads),
        out_shape=(shape, shape),
        in_specs=[VMEM] * 18,
        out_specs=[HBM] * 2,
        scratch_shapes=[pltpu.VMEM(query.shape, query.dtype)] * 2
        + [pltpu.VMEM((HD, 3 * rows), jnp.bfloat16)] * 2
        + [pltpu.SemaphoreType.DMA((2, rows // TQ, 2))],
        compiler_params=pltpu.CompilerParams(vmem_limit_bytes=VMEM_LIMIT),
        cost_estimate=pl.CostEstimate(flops=0, bytes_accessed=0, transcendentals=0),
        name="block_outputs",
    )(*far, *near)


def total_kernel(rows, far_own, far_1, far_2, near, grad_key, grad_value):
    far = far_own[...] + far_1[...].astype(jnp.float32) + far_2[...].astype(jnp.float32)
    for slot, total in ((0, far), (1, near[...])):
        place = pl.ds(half_start(rows, slot), rows)
        grad_key[place, :] = jnp.transpose(total[0:HD]).astype(grad_key.dtype)
        grad_value[place, :] = jnp.transpose(total[HD : 2 * HD]).astype(grad_value.dtype)


def total_grads(*parts):
    rows = parts[0].shape[1]
    shape = jax.ShapeDtypeStruct((2 * rows, HD), jnp.bfloat16)
    return pl.pallas_call(
        functools.partial(total_kernel, rows),
        out_shape=(shape, shape),
        in_specs=[VMEM] * 4,
        out_specs=[VMEM] * 2,
        compiler_params=pltpu.CompilerParams(vmem_limit_bytes=VMEM_LIMIT),
        name="total_grads",
    )(*parts)


def body(query, key, value, d_out, doc_lengths):
    count = lax.axis_size("ctx")

    def holder(block):
        return block if block < count else 2 * count - 1 - block

    def move(array, pairs):
        return lax.ppermute(array, "ctx", pairs)

    near_on = [(holder(b), holder(b + 2)) for b in range(1, 2 * count - 2, 2)]
    far_on = [(holder(b), holder(b + 2)) for b in range(0, 2 * count - 2, 2)]
    near_to_far = [(holder(b), holder(b + 1)) for b in range(1, 2 * count - 2, 2)]
    swap = [(d, d ^ 1) for d in range(count)]
    near_back = [(t, s) for s, t in near_on]
    far_back = [(t, s) for s, t in far_on]

    rows = key.shape[0] // 2
    odd = lax.axis_index("ctx") % 2 == 1
    lower = jnp.concatenate([key[:rows], value[:rows]], axis=0)
    upper = jnp.concatenate([key[rows:], value[rows:]], axis=0)
    near_kv, far_kv = jnp.where(odd, lower, upper), jnp.where(odd, upper, lower)
    far_1 = move(near_kv, near_to_far)
    far_2 = move(far_kv, far_on)
    prepared = prepare(count, doc_lengths, query, d_out, far_kv, near_kv)
    far_ready, near_ready = prepared[0:4], prepared[4:8]
    near_1 = move(far_ready[0], swap)
    far_early = group_scores(0, False, far_ready, far_ready[0])
    near_early = group_scores(1, False, near_ready, near_1, near_ready[0])
    far_1, near_early = lax.optimization_barrier((far_1, near_early))
    far_middle = group_scores(0, True, far_ready, far_1, far_early[2])
    far_late = late_scores(0, far_ready, (far_early[2], far_middle[2]), far_2)
    from_far_2 = move(far_late[3], far_back)
    near_2 = move(far_1, swap)
    near_2, far_stats = lax.optimization_barrier((near_2, far_late[2]))
    far_middle_d, far_g1 = rest_grads(
        "grads_far", 0, [(0, True, (*far_ready, far_stats, *far_middle[0:2]), (True,))]
    )
    relayed = move(far_g1, swap)
    near_late = late_scores(1, near_ready, (near_early[2],), near_2)
    near_sum = near_late[3].astype(jnp.float32) + relayed.astype(jnp.float32)
    from_near_2 = move(near_sum.astype(jnp.bfloat16), near_back)
    near_early_d, near_g1, near_own, far_early_d, far_own = rest_grads(
        "grads_near",
        2**31,
        [
            (1, False, (*near_ready, near_late[2], *near_early[0:2]), (True, False)),
            (0, False, (*far_ready, far_late[2], *far_early[0:2]), (False,)),
        ],
    )
    near_g1, from_far_2 = lax.optimization_barrier((near_g1, from_far_2))
    from_near_1 = move(near_g1, swap)
    attended, grad_query = block_outputs(
        query,
        (
            *(far_2, far_1, far_ready[0]),
            *(far_late[0], far_middle[0], far_early[0]),
            *(far_late[1], far_middle_d, far_early_d),
            far_late[2],
        ),
        (
            *(near_2, near_1, near_ready[0]),
            *(near_late[0], near_early[0]),
            *(near_late[1], near_early_d),
            near_late[2],
        ),
    )
    near_total = near_own + from_near_2.astype(jnp.float32)
    grad_key, grad_value = total_grads(far_own, from_near_1, from_far_2, near_total)
    return (attended, grad_query, grad_key, grad_value)


def solution(mesh):
    rows = P(("dp", "ctx"), None)
    return jax.shard_map(
        body,
        mesh=mesh,
        in_specs=(rows, rows, rows, rows, P("dp")),
        out_specs=(rows, rows, rows, rows),
        check_vma=False,
    )
```

```python
import functools
import math

import jax
import jax.numpy as jnp
from jax import lax
from jax.experimental import pallas as pl
from jax.experimental.pallas import tpu as pltpu
from jax.sharding import PartitionSpec as P

HD = 128
TQ = 128
GROUP = 16

masked_score = -1e30
other_document = -65536.0
VMEM_LIMIT = 24 * 1024 * 1024
SCALE = 1.0 / math.sqrt(HD)
VMEM = pl.BlockSpec(memory_space=pltpu.VMEM)
HBM = pl.BlockSpec(memory_space=pltpu.HBM)
CHUNK = 128
RUN = 3


def dot_nt(a, b):
    return lax.dot_general(a, b, (((1,), (1,)), ((), ())), preferred_element_type=jnp.float32)


def dot_nn(a, b):
    return lax.dot_general(a, b, (((1,), (0,)), ((), ())), preferred_element_type=jnp.float32)


def half_start(rows, slot):
    odd = lax.axis_index("ctx") % 2
    return pl.multiple_of((odd if slot == 0 else 1 - odd) * rows, rows)


def block_number(count, slot):
    device = lax.axis_index("ctx")
    in_lower = device % 2 == slot
    return jnp.where(in_lower, device, 2 * count - 1 - device)


def in_hbm(array):
    return pltpu.with_memory_space_constraint(array, pltpu.HBM)


def load_block(rows, slot, key, value, out, sems):
    place = pl.ds(half_start(rows, slot), rows)
    return [
        pltpu.make_async_copy(key.at[place], out.at[0:rows], sems.at[2 * slot]),
        pltpu.make_async_copy(value.at[place], out.at[rows : 2 * rows], sems.at[2 * slot + 1]),
    ]


def run_copies(copies):
    for copy in copies:
        copy.start()
    for copy in copies:
        copy.wait()


def prepare_kernel(rows, heads, docs, count, *refs):
    (far_kv, near_kv, doc_hbm, query_hbm, dout_hbm) = refs[0:5]
    (doc_lengths, query, dout, sems) = refs[13:]
    refs = refs[5:13]
    wide = heads * TQ
    run_copies(
        [
            pltpu.make_async_copy(query_hbm, query, sems.at[0]),
            pltpu.make_async_copy(dout_hbm, dout, sems.at[1]),
            pltpu.make_async_copy(doc_hbm, doc_lengths, sems.at[2]),
        ]
    )
    lane = lax.broadcasted_iota(jnp.int32, (1, HD), 1)

    def one(index, carry):
        start, starts, ends = carry
        end = start + doc_lengths[index]
        starts = jnp.where(lane == index, start, starts)
        return (end, starts, jnp.where(lane == index, end, ends))

    none = jnp.zeros((1, HD), jnp.int32)
    _, starts, ends = lax.fori_loop(0, docs, one, (jnp.int32(0), none, none), unroll=8)
    starts_t, ends_t = (
        jnp.transpose(jnp.broadcast_to(row.astype(jnp.float32), (HD, HD))).astype(jnp.int32)
        for row in (starts, ends)
    )
    for slot in (0, 1):
        own_kv, query_t, dout_t, documents = refs[4 * slot : 4 * slot + 4]
        own_kv[...] = (far_kv, near_kv)[slot][...]
        own_rows = half_start(rows, slot)
        for step in range(rows // TQ):
            source = pl.ds(own_rows + step * TQ, TQ)
            for h in range(heads):
                place = slice(step * wide + h * TQ, step * wide + (h + 1) * TQ)
                columns = slice(h * HD, (h + 1) * HD)
                query_t[0:HD, place] = jnp.transpose(query[source, columns])
                dout_t[:, place] = jnp.transpose(dout[source, columns])
        position = block_number(count, slot) * rows
        for tile in range(3 * rows // TQ):
            at = lax.broadcasted_iota(jnp.int32, (TQ, HD), 0) + (position - 2 * rows + tile * TQ)
            inside = jnp.logical_and(at >= starts, at < ends)
            inside = jnp.logical_or(inside, at < 0)
            documents[tile * TQ : (tile + 1) * TQ, :] = jnp.where(inside, 1.0, 0.0).astype(
                documents.dtype
            )
        for step in range(rows // TQ):
            at = lax.broadcasted_iota(jnp.int32, (HD, TQ), 1) + (position + step * TQ)
            inside = jnp.logical_and(at >= starts_t, at < ends_t)
            other = jnp.where(inside, 0.0, other_document).astype(query_t.dtype)
            for h in range(heads):
                place = slice(step * wide + h * TQ, step * wide + (h + 1) * TQ)
                query_t[HD : 2 * HD, place] = other


def prepare(count, doc_lengths, query, dout, far_kv, near_kv):
    rows = query.shape[0] // 2
    heads = query.shape[1] // HD
    pair = jax.ShapeDtypeStruct(far_kv.shape, far_kv.dtype)
    stacked_t = jax.ShapeDtypeStruct((HD, rows * heads), query.dtype)
    query_shape = jax.ShapeDtypeStruct((2 * HD, rows * heads), query.dtype)
    documents = jax.ShapeDtypeStruct((3 * rows, HD), query.dtype)
    assert doc_lengths.shape[0] <= HD
    return pl.pallas_call(
        functools.partial(prepare_kernel, rows, heads, doc_lengths.shape[0], count),
        out_shape=(pair, query_shape, stacked_t, documents) * 2,
        in_specs=[VMEM] * 2 + [HBM] * 3,
        out_specs=[VMEM] * 8,
        scratch_shapes=[
            pltpu.SMEM(doc_lengths.shape, doc_lengths.dtype),
            pltpu.VMEM(query.shape, query.dtype),
            pltpu.VMEM(dout.shape, dout.dtype),
            pltpu.SemaphoreType.DMA((3,)),
        ],
        compiler_params=pltpu.CompilerParams(vmem_limit_bytes=VMEM_LIMIT),
        cost_estimate=pl.CostEstimate(flops=0, bytes_accessed=4 * 2**20, transcendentals=0),
        name="prepare",
    )(far_kv, near_kv, *(in_hbm(array) for array in (doc_lengths, query, dout)))


class Window:
    def __init__(self, rows, slot):
        self.tiles = rows // TQ
        self.chunks = 2 * self.tiles + 1
        self.steps = range(self.tiles)
        self.late = [self.tiles - step for step in self.steps]
        self.middle = [(1 - slot) * self.tiles for step in self.steps]
        self.early = [
            self.chunks - late - middle for late, middle in zip(self.late, self.middle)
        ]


def chunk_rows(counts, step, first=0, count=None):
    start = sum(counts[:step]) + first
    count = counts[step] - first if count is None else count
    return slice(start * CHUNK, (start + count) * CHUNK)


def run_length(run):
    return run[-1].stop - run[-1].start


def runs_of(chunks):
    runs = []
    for chunk in chunks:
        if runs:
            last = runs[-1]
            length = run_length(last)
            if last[1] is chunk[1] and last[2] + length == chunk[2] and length < RUN * CHUNK:
                runs[-1] = (*last[:-1], slice(last[-1].start, chunk[-1].stop))
                continue
        runs.append(chunk)
    return runs


def exponentials(jobs, rows, heads, scores, scores_first=False):
    back = 2 * rows
    wide = heads * TQ
    base2 = SCALE * math.log2(math.e)

    def score(job, index, row_max):
        step, chunks, (query_t, _, documents), _, _ = jobs[job]
        chunk, keys, row = chunks[index][0:3]
        tile = slice(step * wide, (step + 1) * wide)
        length = run_length(chunks[index])
        window = slice(step * TQ + chunk * CHUNK, step * TQ + chunk * CHUNK + length)
        product = dot_nn(
            jnp.concatenate([keys[row : row + length, :], documents[window, :]], axis=1),
            query_t[:, tile],
        )
        for start in range(0, length, GROUP):
            place = chunk * CHUNK + start
            for h in range(heads):
                lanes = slice(h * TQ, (h + 1) * TQ)
                part = product[start : start + GROUP, lanes]
                if place >= back:
                    key_at = lax.broadcasted_iota(jnp.int32, (GROUP, TQ), 0) + (place - back)
                    query_at = lax.broadcasted_iota(jnp.int32, (GROUP, TQ), 1)
                    part = jnp.where(key_at <= query_at, part, masked_score)
                scores[job % scores.shape[0], place : place + GROUP, lanes] = part
                for row8 in range(0, GROUP, 8):
                    row_max[h] = jnp.maximum(row_max[h], part[row8 : row8 + 8, :])

    def start_max():
        return [jnp.full((8, TQ), masked_score, jnp.float32)] * heads

    pending = None
    every = [start_max() for _ in jobs]
    for job in range(len(jobs) if scores_first else 1):
        for index in range(len(jobs[job][1])):
            score(job, index, every[job])
    for job, (step, chunks, (_, dout_t, _), first_max, end) in enumerate(jobs):
        tile = slice(step * wide, (step + 1) * wide)
        row_max = jnp.concatenate(
            [jnp.max(part, axis=0, keepdims=True) * base2 for part in every[job]], axis=1
        )
        if first_max is not None:
            row_max = jnp.maximum(row_max, first_max)
        ahead = len(jobs[job + 1][1]) if job + 1 < len(jobs) and not scores_first else 0
        done = 0
        total = jnp.zeros((8, wide), jnp.float32)
        delta = jnp.zeros((8, wide), jnp.float32)
        for index, (chunk, keys, row, weights, dprobs, kept) in enumerate(chunks):
            length = kept.stop - kept.start
            product = dot_nn(keys[rows + row : rows + row + length, :], dout_t[:, tile])
            for start in range(0, length, GROUP):
                place = chunk * CHUNK + start
                there = slice(kept.start + start, kept.start + start + GROUP)
                dprob = product[start : start + GROUP, :]
                dprobs[there, :] = dprob.astype(jnp.bfloat16)
                part = jnp.exp2(scores[job % scores.shape[0], place : place + GROUP, :] * base2 - row_max)
                weights[there, :] = part.astype(jnp.bfloat16)
                term = part * dprob
                for row8 in range(0, GROUP, 8):
                    total = total + part[row8 : row8 + 8, :]
                    delta = delta + term[row8 : row8 + 8, :]
            while done * len(chunks) < ahead * (index + 1):
                score(job + 1, done, every[job + 1])
                done += 1
            if index == 0 and pending is not None:
                pending()
        sums = [jnp.sum(part, axis=0, keepdims=True) for part in (total, delta)]
        pending = functools.partial(end, row_max, *sums)
    pending()


def group_kernel(rows, heads, slot, middle, query_t, dout_t, documents, *refs):
    (weights, dprobs, stats, scores) = refs[-4:]
    prev1 = refs[0] if middle or slot == 1 else None
    own_kv = None if middle else refs[slot]
    window = Window(rows, slot)
    counts = window.middle if middle else window.early
    jobs = []
    for step in window.steps:
        chunks = []
        for index in range(counts[step]):
            chunk = window.late[step] + (0 if middle else window.middle[step]) + index
            row = step * TQ + chunk * CHUNK
            keys = own_kv if row >= 2 * rows else prev1
            kept = chunk_rows(counts, step, index, 1)
            chunks.append((chunk, keys, row % rows, weights, dprobs, kept))

        def end(*found, step=step):
            for kind, value in enumerate(found):
                stats[8 * kind + step : 8 * kind + step + 1, :] = value

        first_max = refs[1][step : step + 1, :] if middle else None
        jobs.append((step, runs_of(chunks), (query_t, dout_t, documents), first_max, end))
    exponentials(jobs, rows, heads, scores)


def group_scores(slot, middle, ready, *operands):
    rows = ready[0].shape[0] // 2
    heads = ready[1].shape[1] // rows
    wide = heads * TQ
    window = Window(rows, slot)
    counts = window.middle if middle else window.early
    kept = jax.ShapeDtypeStruct((sum(counts) * CHUNK, wide), jnp.bfloat16)
    cost = (0 if slot else 2**33) if not middle else 0
    return pl.pallas_call(
        functools.partial(group_kernel, rows, heads, slot, middle),
        out_shape=(kept, kept, jax.ShapeDtypeStruct((24, wide), jnp.float32)),
        in_specs=[VMEM] * (3 + len(operands)),
        out_specs=[VMEM] * 3,
        scratch_shapes=[pltpu.VMEM((2, 2 * rows + TQ, wide), jnp.float32)],
        compiler_params=pltpu.CompilerParams(vmem_limit_bytes=VMEM_LIMIT),
        cost_estimate=pl.CostEstimate(flops=cost, bytes_accessed=0, transcendentals=0),
        name="middle_far" if middle else "early_far" if slot == 0 else "early_near",
    )(*ready[1:4], *operands)


def scaled_by(array, tile, factor):
    return (array[0:HD, tile].astype(jnp.float32) * factor).astype(jnp.bfloat16)


def dscore_rows(dscores, there, weights, dprobs, kept, delta):
    delta = jnp.broadcast_to(delta, (16, delta.shape[1]))
    for start in range(0, there.stop - there.start, 16):
        out = slice(there.start + start, there.start + start + 16)
        place = slice(kept.start + start, kept.start + start + 16)
        dscores[out, :] = weights[place, :] * (dprobs[place, :] - delta)


def add_products(new, columns, products):
    for total_ref, side, terms in products:
        term = dot_nt(side, terms)
        if new:
            total_ref[:, columns] = term
        else:
            total_ref[:, columns] += term


def late_kernel(rows, heads, slot, query_t, dout_t, documents, prev2, *refs):
    groups = refs[0 : 2 - slot]
    (weights, dscores, stats, prev2_out, scores, dprobs, dk, dv) = refs[2 - slot :]
    wide = heads * TQ
    window = Window(rows, slot)
    jobs = []
    for step in window.steps:
        chunks = []
        for chunk in range(window.late[step]):
            kept = chunk_rows(window.late, step, chunk, 1)
            chunks.append((chunk, prev2, step * TQ + chunk * CHUNK, weights, dprobs, kept))

        def end(row_max, total, delta, step=step):
            tile = slice(step * wide, (step + 1) * wide)
            rows_of = [
                [group[8 * kind + step : 8 * kind + step + 1, :] for kind in range(3)]
                for group in groups
            ]
            shrinks = [jnp.exp2(found[0] - row_max) for found in rows_of]
            for found, shrink in zip(rows_of, shrinks):
                total = total + found[1] * shrink
                delta = delta + found[2] * shrink
            late_factor = 1.0 / total
            delta = delta * late_factor
            factors = [late_factor * shrink for shrink in shrinks]
            for kind, value in enumerate((late_factor, factors[0], delta, factors[-1])):
                stats[8 * kind + step : 8 * kind + step + 1, :] = value
            there = chunk_rows(window.late, step)
            dscore_rows(dscores, there, weights, dprobs, there, delta.astype(jnp.bfloat16))
            add_products(
                step == 0,
                slice(step * TQ, rows),
                (
                    (dv, scaled_by(dout_t, tile, late_factor), weights[there, :]),
                    (dk, scaled_by(query_t, tile, late_factor), dscores[there, :]),
                ),
            )

        first_max = groups[-1][step : step + 1, :]
        jobs.append((step, runs_of(chunks), (query_t, dout_t, documents), first_max, end))
    exponentials(jobs, rows, heads, scores, True)
    prev2_out[0:HD] = (dk[...] * SCALE).astype(prev2_out.dtype)
    prev2_out[HD : 2 * HD] = dv[...].astype(prev2_out.dtype)


def late_scores(slot, ready, groups, prev2):
    rows = prev2.shape[0] // 2
    heads = ready[1].shape[1] // rows
    wide = heads * TQ
    late = jax.ShapeDtypeStruct((sum(Window(rows, slot).late) * CHUNK, wide), jnp.bfloat16)
    return pl.pallas_call(
        functools.partial(late_kernel, rows, heads, slot),
        out_shape=(
            late,
            late,
            jax.ShapeDtypeStruct((32, wide), jnp.float32),
            jax.ShapeDtypeStruct((2 * HD, rows), jnp.bfloat16),
        ),
        in_specs=[VMEM] * (4 + len(groups)),
        out_specs=[VMEM] * 4,
        scratch_shapes=[
            pltpu.VMEM((rows // TQ, rows, wide), jnp.float32),
            pltpu.VMEM(late.shape, late.dtype),
            pltpu.VMEM((HD, rows), jnp.float32),
            pltpu.VMEM((HD, rows), jnp.float32),
        ],
        compiler_params=pltpu.CompilerParams(vmem_limit_bytes=VMEM_LIMIT),
        cost_estimate=pl.CostEstimate(flops=2**31, bytes_accessed=0, transcendentals=0),
        name="late_far" if slot == 0 else "late_near",
    )(*ready[1:4], prev2, *groups)


def grads_kernel(rows, heads, slots, *refs):
    wide = heads * TQ
    outs = list(refs[5 * len(slots) : -2])
    (dk, dv) = refs[-2:]
    for part, (slot, middle) in enumerate(slots):
        (query_t, dout_t, stats, weights, dprobs) = refs[5 * part : 5 * part + 5]
        dscores = outs.pop(0)
        window = Window(rows, slot)
        counts = window.middle if middle else window.early
        for step in reversed(window.steps):
            tile = slice(step * wide, (step + 1) * wide)
            _, early_factor, delta, middle_factor = (
                stats[8 * kind + step : 8 * kind + step + 1, :] for kind in range(4)
            )
            factor = middle_factor if middle else early_factor
            there = chunk_rows(counts, step)
            dscore_rows(dscores, there, weights, dprobs, there, delta.astype(jnp.bfloat16))
            add_products(
                step == window.tiles - 1,
                slice(0, counts[step] * CHUNK),
                (
                    (dv, scaled_by(dout_t, tile, factor), weights[there, :]),
                    (dk, scaled_by(query_t, tile, factor), dscores[there, :]),
                ),
            )
        for block in range(counts[-1] // window.tiles):
            out = outs.pop(0)
            place = slice(block * rows, (block + 1) * rows)
            out[0:HD] = (dk[:, place] * SCALE).astype(out.dtype)
            out[HD : 2 * HD] = dv[:, place].astype(out.dtype)


def rest_grads(name, cost, parts):
    rows = parts[0][2][0].shape[0] // 2
    heads = parts[0][2][1].shape[1] // rows
    operands, out_shape = [], []
    for slot, middle, (_, query_t, dout_t, _, stats, weights, dprobs), sent in parts:
        window = Window(rows, slot)
        kept = (sum(window.middle if middle else window.early) * CHUNK, heads * TQ)
        operands += [query_t, dout_t, stats, weights, dprobs]
        out_shape.append(jax.ShapeDtypeStruct(kept, jnp.bfloat16))
        for one in sent:
            kind = jnp.bfloat16 if one else jnp.float32
            out_shape.append(jax.ShapeDtypeStruct((2 * HD, rows), kind))
    slots = tuple(part[0:2] for part in parts)
    return pl.pallas_call(
        functools.partial(grads_kernel, rows, heads, slots),
        out_shape=out_shape,
        in_specs=[VMEM] * len(operands),
        out_specs=[VMEM] * len(out_shape),
        scratch_shapes=[pltpu.VMEM((HD, 2 * rows), jnp.float32)] * 2,
        compiler_params=pltpu.CompilerParams(vmem_limit_bytes=VMEM_LIMIT),
        cost_estimate=pl.CostEstimate(flops=cost, bytes_accessed=0, transcendentals=0),
        name=name,
    )(*operands)


def outputs_kernel(rows, heads, *refs):
    blocks = (refs[0:3], refs[3:6], refs[6:9], refs[9]), (refs[10:13], refs[13:15], refs[15:17], refs[17])
    (attended_hbm, grad_query_hbm, attended, grad_query, keys_t, values_t, sems) = refs[18:]
    copies = []
    for slot, (sources, weights, dscores, stats) in enumerate(blocks):
        window = Window(rows, slot)
        groups = [(window.late, 0), (window.early, 1)]
        if slot == 0:
            groups.insert(1, (window.middle, 3))
        own_rows = half_start(rows, slot)
        for place, source in enumerate(sources):
            for tile in range(rows // TQ):
                part = slice(place * rows + tile * TQ, place * rows + (tile + 1) * TQ)
                row = tile * TQ
                keys_t[:, part] = jnp.transpose(source[row : row + TQ, :])
                values_t[:, part] = jnp.transpose(source[rows + row : rows + row + TQ, :])
        for step in window.steps:
            place = pl.ds(own_rows + step * TQ, TQ)
            for out, side, terms, scale in (
                (0, values_t, weights, 1.0),
                (1, keys_t, dscores, SCALE),
            ):
                found = None
                start = step * TQ
                for (counts, kind), term in zip(groups, terms):
                    columns = slice(start, start + counts[step] * CHUNK)
                    start = columns.stop
                    factor = stats[8 * kind + step : 8 * kind + step + 1, :] * scale
                    part = dot_nn(side[:, columns], term[chunk_rows(counts, step), :]) * factor
                    found = part if found is None else found + part
                target = (attended_hbm, grad_query_hbm)[out]
                source = (attended, grad_query)[out]
                for h in range(heads):
                    part = jnp.transpose(found[:, h * TQ : (h + 1) * TQ])
                    source[place, h * HD : (h + 1) * HD] = part.astype(source.dtype)
                copy = pltpu.make_async_copy(
                    source.at[place], target.at[place], sems.at[slot, step, out]
                )
                copy.start()
                copies.append(copy)
    for copy in copies:
        copy.wait()


def block_outputs(query, far, near):
    rows = query.shape[0] // 2
    heads = query.shape[1] // HD
    shape = jax.ShapeDtypeStruct(query.shape, query.dtype)
    return pl.pallas_call(
        functools.partial(outputs_kernel, rows, heads),
        out_shape=(shape, shape),
        in_specs=[VMEM] * 18,
        out_specs=[HBM] * 2,
        scratch_shapes=[pltpu.VMEM(query.shape, query.dtype)] * 2
        + [pltpu.VMEM((HD, 3 * rows), jnp.bfloat16)] * 2
        + [pltpu.SemaphoreType.DMA((2, rows // TQ, 2))],
        compiler_params=pltpu.CompilerParams(vmem_limit_bytes=VMEM_LIMIT),
        cost_estimate=pl.CostEstimate(flops=0, bytes_accessed=0, transcendentals=0),
        name="block_outputs",
    )(*far, *near)


def total_kernel(rows, far_own, far_1, far_2, near, grad_key, grad_value):
    far = far_own[...] + far_1[...].astype(jnp.float32) + far_2[...].astype(jnp.float32)
    for slot, total in ((0, far), (1, near[...])):
        place = pl.ds(half_start(rows, slot), rows)
        grad_key[place, :] = jnp.transpose(total[0:HD]).astype(grad_key.dtype)
        grad_value[place, :] = jnp.transpose(total[HD : 2 * HD]).astype(grad_value.dtype)


def total_grads(*parts):
    rows = parts[0].shape[1]
    shape = jax.ShapeDtypeStruct((2 * rows, HD), jnp.bfloat16)
    return pl.pallas_call(
        functools.partial(total_kernel, rows),
        out_shape=(shape, shape),
        in_specs=[VMEM] * 4,
        out_specs=[VMEM] * 2,
        compiler_params=pltpu.CompilerParams(vmem_limit_bytes=VMEM_LIMIT),
        name="total_grads",
    )(*parts)


def body(query, key, value, d_out, doc_lengths):
    count = lax.axis_size("ctx")

    def holder(block):
        return block if block < count else 2 * count - 1 - block

    def move(array, pairs):
        return lax.ppermute(array, "ctx", pairs)

    near_on = [(holder(b), holder(b + 2)) for b in range(1, 2 * count - 2, 2)]
    far_on = [(holder(b), holder(b + 2)) for b in range(0, 2 * count - 2, 2)]
    near_to_far = [(holder(b), holder(b + 1)) for b in range(1, 2 * count - 2, 2)]
    swap = [(d, d ^ 1) for d in range(count)]
    near_back = [(t, s) for s, t in near_on]
    far_back = [(t, s) for s, t in far_on]

    rows = key.shape[0] // 2
    odd = lax.axis_index("ctx") % 2 == 1
    lower = jnp.concatenate([key[:rows], value[:rows]], axis=0)
    upper = jnp.concatenate([key[rows:], value[rows:]], axis=0)
    near_kv, far_kv = jnp.where(odd, lower, upper), jnp.where(odd, upper, lower)
    far_1 = move(near_kv, near_to_far)
    far_2 = move(far_kv, far_on)
    prepared = prepare(count, doc_lengths, query, d_out, far_kv, near_kv)
    far_ready, near_ready = prepared[0:4], prepared[4:8]
    near_1 = move(far_ready[0], swap)
    far_early = group_scores(0, False, far_ready, far_ready[0])
    near_early = group_scores(1, False, near_ready, near_1, near_ready[0])
    far_1, near_early = lax.optimization_barrier((far_1, near_early))
    far_middle = group_scores(0, True, far_ready, far_1, far_early[2])
    far_late = late_scores(0, far_ready, (far_early[2], far_middle[2]), far_2)
    from_far_2 = move(far_late[3], far_back)
    near_2 = move(far_1, swap)
    near_2, far_stats = lax.optimization_barrier((near_2, far_late[2]))
    far_middle_d, far_g1 = rest_grads(
        "grads_far", 0, [(0, True, (*far_ready, far_stats, *far_middle[0:2]), (True,))]
    )
    relayed = move(far_g1, swap)
    near_late = late_scores(1, near_ready, (near_early[2],), near_2)
    near_sum = near_late[3].astype(jnp.float32) + relayed.astype(jnp.float32)
    from_near_2 = move(near_sum.astype(jnp.bfloat16), near_back)
    near_early_d, near_g1, near_own, far_early_d, far_own = rest_grads(
        "grads_near",
        2**31,
        [
            (1, False, (*near_ready, near_late[2], *near_early[0:2]), (True, False)),
            (0, False, (*far_ready, far_late[2], *far_early[0:2]), (False,)),
        ],
    )
    near_g1, from_far_2 = lax.optimization_barrier((near_g1, from_far_2))
    from_near_1 = move(near_g1, swap)
    attended, grad_query = block_outputs(
        query,
        (
            *(far_2, far_1, far_ready[0]),
            *(far_late[0], far_middle[0], far_early[0]),
            *(far_late[1], far_middle_d, far_early_d),
            far_late[2],
        ),
        (
            *(near_2, near_1, near_ready[0]),
            *(near_late[0], near_early[0]),
            *(near_late[1], near_early_d),
            near_late[2],
        ),
    )
    near_total = near_own + from_near_2.astype(jnp.float32)
    grad_key, grad_value = total_grads(far_own, from_near_1, from_far_2, near_total)
    return (attended, grad_query, grad_key, grad_value)


def solution(mesh):
    rows = P(("dp", "ctx"), None)
    return jax.shard_map(
        body,
        mesh=mesh,
        in_specs=(rows, rows, rows, rows, P("dp")),
        out_specs=(rows, rows, rows, rows),
        check_vma=False,
    )
```

```python
import functools
import math

import jax
import jax.numpy as jnp
from jax import lax
from jax.experimental import pallas as pl
from jax.experimental.pallas import tpu as pltpu
from jax.sharding import PartitionSpec as P

HD = 128
TQ = 128
GROUP = 16

masked_score = -1e30
other_document = -65536.0
VMEM_LIMIT = 24 * 1024 * 1024
SCALE = 1.0 / math.sqrt(HD)
VMEM = pl.BlockSpec(memory_space=pltpu.VMEM)
HBM = pl.BlockSpec(memory_space=pltpu.HBM)
CHUNK = 128
RUN = 3


def dot_nt(a, b):
    return lax.dot_general(a, b, (((1,), (1,)), ((), ())), preferred_element_type=jnp.float32)


def dot_nn(a, b):
    return lax.dot_general(a, b, (((1,), (0,)), ((), ())), preferred_element_type=jnp.float32)


def half_start(rows, slot):
    odd = lax.axis_index("ctx") % 2
    return pl.multiple_of((odd if slot == 0 else 1 - odd) * rows, rows)


def block_number(count, slot):
    device = lax.axis_index("ctx")
    in_lower = device % 2 == slot
    return jnp.where(in_lower, device, 2 * count - 1 - device)


def in_hbm(array):
    return pltpu.with_memory_space_constraint(array, pltpu.HBM)


def run_copies(copies):
    for copy in copies:
        copy.start()
    for copy in copies:
        copy.wait()


def prepare_kernel(rows, heads, docs, count, *refs):
    (far_kv, near_kv, doc_hbm, query_hbm, dout_hbm) = refs[0:5]
    (doc_lengths, query, dout, sems) = refs[13:]
    refs = refs[5:13]
    wide = heads * TQ
    run_copies(
        [
            pltpu.make_async_copy(query_hbm, query, sems.at[0]),
            pltpu.make_async_copy(dout_hbm, dout, sems.at[1]),
            pltpu.make_async_copy(doc_hbm, doc_lengths, sems.at[2]),
        ]
    )
    lane = lax.broadcasted_iota(jnp.int32, (1, HD), 1)

    def one(index, carry):
        start, starts, ends = carry
        end = start + doc_lengths[index]
        starts = jnp.where(lane == index, start, starts)
        return (end, starts, jnp.where(lane == index, end, ends))

    none = jnp.zeros((1, HD), jnp.int32)
    _, starts, ends = lax.fori_loop(0, docs, one, (jnp.int32(0), none, none), unroll=8)
    starts_t, ends_t = (
        jnp.transpose(jnp.broadcast_to(row.astype(jnp.float32), (HD, HD))).astype(jnp.int32)
        for row in (starts, ends)
    )
    for slot in (0, 1):
        own_kv, query_t, dout_t, documents = refs[4 * slot : 4 * slot + 4]
        own_kv[...] = (far_kv, near_kv)[slot][...]
        own_rows = half_start(rows, slot)
        for step in range(rows // TQ):
            source = pl.ds(own_rows + step * TQ, TQ)
            for h in range(heads):
                place = slice(step * wide + h * TQ, step * wide + (h + 1) * TQ)
                columns = slice(h * HD, (h + 1) * HD)
                query_t[0:HD, place] = jnp.transpose(query[source, columns])
                dout_t[:, place] = jnp.transpose(dout[source, columns])
        position = block_number(count, slot) * rows
        for tile in range(3 * rows // TQ):
            at = lax.broadcasted_iota(jnp.int32, (TQ, HD), 0) + (position - 2 * rows + tile * TQ)
            inside = jnp.logical_and(at >= starts, at < ends)
            inside = jnp.logical_or(inside, at < 0)
            documents[tile * TQ : (tile + 1) * TQ, :] = jnp.where(inside, 1.0, 0.0).astype(
                documents.dtype
            )
        for step in range(rows // TQ):
            at = lax.broadcasted_iota(jnp.int32, (HD, TQ), 1) + (position + step * TQ)
            inside = jnp.logical_and(at >= starts_t, at < ends_t)
            other = jnp.where(inside, 0.0, other_document).astype(query_t.dtype)
            for h in range(heads):
                place = slice(step * wide + h * TQ, step * wide + (h + 1) * TQ)
                query_t[HD : 2 * HD, place] = other


def prepare(count, doc_lengths, query, dout, far_kv, near_kv):
    rows = query.shape[0] // 2
    heads = query.shape[1] // HD
    pair = jax.ShapeDtypeStruct(far_kv.shape, far_kv.dtype)
    stacked_t = jax.ShapeDtypeStruct((HD, rows * heads), query.dtype)
    query_shape = jax.ShapeDtypeStruct((2 * HD, rows * heads), query.dtype)
    documents = jax.ShapeDtypeStruct((3 * rows, HD), query.dtype)
    assert doc_lengths.shape[0] <= HD
    return pl.pallas_call(
        functools.partial(prepare_kernel, rows, heads, doc_lengths.shape[0], count),
        out_shape=(pair, query_shape, stacked_t, documents) * 2,
        in_specs=[VMEM] * 2 + [HBM] * 3,
        out_specs=[VMEM] * 8,
        scratch_shapes=[
            pltpu.SMEM(doc_lengths.shape, doc_lengths.dtype),
            pltpu.VMEM(query.shape, query.dtype),
            pltpu.VMEM(dout.shape, dout.dtype),
            pltpu.SemaphoreType.DMA((3,)),
        ],
        compiler_params=pltpu.CompilerParams(vmem_limit_bytes=VMEM_LIMIT),
        cost_estimate=pl.CostEstimate(flops=0, bytes_accessed=4 * 2**20, transcendentals=0),
        name="prepare",
    )(far_kv, near_kv, *(in_hbm(array) for array in (doc_lengths, query, dout)))


class Window:
    def __init__(self, rows, slot):
        self.tiles = rows // TQ
        self.chunks = 2 * self.tiles + 1
        self.steps = range(self.tiles)
        self.late = [self.tiles - step for step in self.steps]
        self.middle = [(1 - slot) * self.tiles for step in self.steps]
        self.early = [
            self.chunks - late - middle for late, middle in zip(self.late, self.middle)
        ]


def chunk_rows(counts, step, first=0, count=None):
    start = sum(counts[:step]) + first
    count = counts[step] - first if count is None else count
    return slice(start * CHUNK, (start + count) * CHUNK)


def run_length(run):
    return run[-1].stop - run[-1].start


def runs_of(chunks):
    runs = []
    for chunk in chunks:
        if runs:
            last = runs[-1]
            length = run_length(last)
            if last[1] is chunk[1] and last[2] + length == chunk[2] and length < RUN * CHUNK:
                runs[-1] = (*last[:-1], slice(last[-1].start, chunk[-1].stop))
                continue
        runs.append(chunk)
    return runs


def exponentials(jobs, rows, heads, scores, scores_first=False):
    back = 2 * rows
    wide = heads * TQ
    base2 = SCALE * math.log2(math.e)

    def score(job, index, row_max):
        step, chunks, (query_t, _, documents), _, _ = jobs[job]
        chunk, keys, row = chunks[index][0:3]
        tile = slice(step * wide, (step + 1) * wide)
        length = run_length(chunks[index])
        window = slice(step * TQ + chunk * CHUNK, step * TQ + chunk * CHUNK + length)
        product = dot_nn(
            jnp.concatenate([keys[row : row + length, :], documents[window, :]], axis=1),
            query_t[:, tile],
        )
        for start in range(0, length, GROUP):
            place = chunk * CHUNK + start
            for h in range(heads):
                lanes = slice(h * TQ, (h + 1) * TQ)
                part = product[start : start + GROUP, lanes]
                if place >= back:
                    key_at = lax.broadcasted_iota(jnp.int32, (GROUP, TQ), 0) + (place - back)
                    query_at = lax.broadcasted_iota(jnp.int32, (GROUP, TQ), 1)
                    part = jnp.where(key_at <= query_at, part, masked_score)
                scores[job % scores.shape[0], place : place + GROUP, lanes] = part
                for row8 in range(0, GROUP, 8):
                    row_max[h] = jnp.maximum(row_max[h], part[row8 : row8 + 8, :])

    def start_max():
        return [jnp.full((8, TQ), masked_score, jnp.float32)] * heads

    pending = None
    every = [start_max() for _ in jobs]
    for job in range(len(jobs) if scores_first else 1):
        for index in range(len(jobs[job][1])):
            score(job, index, every[job])
    for job, (step, chunks, (_, dout_t, _), first_max, end) in enumerate(jobs):
        tile = slice(step * wide, (step + 1) * wide)
        row_max = jnp.concatenate(
            [jnp.max(part, axis=0, keepdims=True) * base2 for part in every[job]], axis=1
        )
        if first_max is not None:
            row_max = jnp.maximum(row_max, first_max)
        ahead = len(jobs[job + 1][1]) if job + 1 < len(jobs) and not scores_first else 0
        done = 0
        total = jnp.zeros((8, wide), jnp.float32)
        delta = jnp.zeros((8, wide), jnp.float32)
        for index, (chunk, keys, row, weights, dprobs, kept) in enumerate(chunks):
            length = kept.stop - kept.start
            product = dot_nn(keys[rows + row : rows + row + length, :], dout_t[:, tile])
            for start in range(0, length, GROUP):
                place = chunk * CHUNK + start
                there = slice(kept.start + start, kept.start + start + GROUP)
                dprob = product[start : start + GROUP, :]
                dprobs[there, :] = dprob.astype(jnp.bfloat16)
                part = jnp.exp2(scores[job % scores.shape[0], place : place + GROUP, :] * base2 - row_max)
                weights[there, :] = part.astype(jnp.bfloat16)
                term = part * dprob
                for row8 in range(0, GROUP, 8):
                    total = total + part[row8 : row8 + 8, :]
                    delta = delta + term[row8 : row8 + 8, :]
            while done * len(chunks) < ahead * (index + 1):
                score(job + 1, done, every[job + 1])
                done += 1
            if index == 0 and pending is not None:
                pending()
        sums = [jnp.sum(part, axis=0, keepdims=True) for part in (total, delta)]
        pending = functools.partial(end, row_max, *sums)
    pending()


def group_kernel(rows, heads, slot, middle, query_t, dout_t, documents, *refs):
    (weights, dprobs, stats, scores) = refs[-4:]
    prev1 = refs[0] if middle or slot == 1 else None
    own_kv = None if middle else refs[slot]
    window = Window(rows, slot)
    counts = window.middle if middle else window.early
    jobs = []
    for step in window.steps:
        chunks = []
        for index in range(counts[step]):
            chunk = window.late[step] + (0 if middle else window.middle[step]) + index
            row = step * TQ + chunk * CHUNK
            keys = own_kv if row >= 2 * rows else prev1
            kept = chunk_rows(counts, step, index, 1)
            chunks.append((chunk, keys, row % rows, weights, dprobs, kept))

        def end(*found, step=step):
            for kind, value in enumerate(found):
                stats[8 * kind + step : 8 * kind + step + 1, :] = value

        first_max = refs[1][step : step + 1, :] if middle else None
        jobs.append((step, runs_of(chunks), (query_t, dout_t, documents), first_max, end))
    exponentials(jobs, rows, heads, scores)


def group_scores(slot, middle, ready, *operands):
    rows = ready[0].shape[0] // 2
    heads = ready[1].shape[1] // rows
    wide = heads * TQ
    window = Window(rows, slot)
    counts = window.middle if middle else window.early
    kept = jax.ShapeDtypeStruct((sum(counts) * CHUNK, wide), jnp.bfloat16)
    cost = (0 if slot else 2**33) if not middle else 0
    return pl.pallas_call(
        functools.partial(group_kernel, rows, heads, slot, middle),
        out_shape=(kept, kept, jax.ShapeDtypeStruct((24, wide), jnp.float32)),
        in_specs=[VMEM] * (3 + len(operands)),
        out_specs=[VMEM] * 3,
        scratch_shapes=[pltpu.VMEM((2, 2 * rows + TQ, wide), jnp.float32)],
        compiler_params=pltpu.CompilerParams(vmem_limit_bytes=VMEM_LIMIT),
        cost_estimate=pl.CostEstimate(flops=cost, bytes_accessed=0, transcendentals=0),
        name="middle_far" if middle else "early_far" if slot == 0 else "early_near",
    )(*ready[1:4], *operands)


def scaled_by(array, tile, factor):
    return (array[0:HD, tile].astype(jnp.float32) * factor).astype(jnp.bfloat16)


def dscore_rows(dscores, there, weights, dprobs, kept, delta):
    delta = jnp.broadcast_to(delta, (16, delta.shape[1]))
    for start in range(0, there.stop - there.start, 16):
        out = slice(there.start + start, there.start + start + 16)
        place = slice(kept.start + start, kept.start + start + 16)
        dscores[out, :] = weights[place, :] * (dprobs[place, :] - delta)


def add_products(new, columns, products):
    for total_ref, side, terms in products:
        term = dot_nt(side, terms)
        if new:
            total_ref[:, columns] = term
        else:
            total_ref[:, columns] += term


def late_kernel(rows, heads, slot, query_t, dout_t, documents, prev2, *refs):
    groups = refs[0 : 2 - slot]
    (weights, dscores, stats, prev2_out, scores, dprobs) = refs[2 - slot :]
    wide = heads * TQ
    window = Window(rows, slot)
    jobs = []
    key_terms, value_terms = [], []
    for step in window.steps:
        chunks = []
        for chunk in range(window.late[step]):
            kept = chunk_rows(window.late, step, chunk, 1)
            chunks.append((chunk, prev2, step * TQ + chunk * CHUNK, weights, dprobs, kept))

        def end(row_max, total, delta, step=step):
            tile = slice(step * wide, (step + 1) * wide)
            rows_of = [
                [group[8 * kind + step : 8 * kind + step + 1, :] for kind in range(3)]
                for group in groups
            ]
            shrinks = [jnp.exp2(found[0] - row_max) for found in rows_of]
            for found, shrink in zip(rows_of, shrinks):
                total = total + found[1] * shrink
                delta = delta + found[2] * shrink
            late_factor = 1.0 / total
            delta = delta * late_factor
            factors = [late_factor * shrink for shrink in shrinks]
            for kind, value in enumerate((late_factor, factors[0], delta, factors[-1])):
                stats[8 * kind + step : 8 * kind + step + 1, :] = value
            there = chunk_rows(window.late, step)
            dscore_rows(dscores, there, weights, dprobs, there, delta.astype(jnp.bfloat16))
            value_terms.append(dot_nt(scaled_by(dout_t, tile, late_factor), weights[there, :]))
            key_terms.append(dot_nt(scaled_by(query_t, tile, late_factor), dscores[there, :]))

        first_max = groups[-1][step : step + 1, :]
        jobs.append((step, runs_of(chunks), (query_t, dout_t, documents), first_max, end))
    exponentials(jobs, rows, heads, scores, True)
    for first, terms, scale in ((0, key_terms, SCALE), (HD, value_terms, 1.0)):
        for tile in range(window.tiles):
            parts = [
                terms[step][:, (tile - step) * TQ : (tile - step + 1) * TQ]
                for step in range(tile + 1)
            ]
            prev2_out[first : first + HD, tile * TQ : (tile + 1) * TQ] = (
                sum(parts[1:], parts[0]) * scale
            ).astype(prev2_out.dtype)


def late_scores(slot, ready, groups, prev2):
    rows = prev2.shape[0] // 2
    heads = ready[1].shape[1] // rows
    wide = heads * TQ
    late = jax.ShapeDtypeStruct((sum(Window(rows, slot).late) * CHUNK, wide), jnp.bfloat16)
    return pl.pallas_call(
        functools.partial(late_kernel, rows, heads, slot),
        out_shape=(
            late,
            late,
            jax.ShapeDtypeStruct((32, wide), jnp.float32),
            jax.ShapeDtypeStruct((2 * HD, rows), jnp.bfloat16),
        ),
        in_specs=[VMEM] * (4 + len(groups)),
        out_specs=[VMEM] * 4,
        scratch_shapes=[
            pltpu.VMEM((rows // TQ, rows, wide), jnp.float32),
            pltpu.VMEM(late.shape, late.dtype),
        ],
        compiler_params=pltpu.CompilerParams(vmem_limit_bytes=VMEM_LIMIT),
        cost_estimate=pl.CostEstimate(flops=2**31, bytes_accessed=0, transcendentals=0),
        name="late_far" if slot == 0 else "late_near",
    )(*ready[1:4], prev2, *groups)


def grads_kernel(rows, heads, slots, *refs):
    wide = heads * TQ
    outs = list(refs[5 * len(slots) : -2])
    (dk, dv) = refs[-2:]
    for part, (slot, middle) in enumerate(slots):
        (query_t, dout_t, stats, weights, dprobs) = refs[5 * part : 5 * part + 5]
        dscores = outs.pop(0)
        window = Window(rows, slot)
        counts = window.middle if middle else window.early
        for step in reversed(window.steps):
            tile = slice(step * wide, (step + 1) * wide)
            _, early_factor, delta, middle_factor = (
                stats[8 * kind + step : 8 * kind + step + 1, :] for kind in range(4)
            )
            factor = middle_factor if middle else early_factor
            there = chunk_rows(counts, step)
            dscore_rows(dscores, there, weights, dprobs, there, delta.astype(jnp.bfloat16))
            add_products(
                step == window.tiles - 1,
                slice(0, counts[step] * CHUNK),
                (
                    (dv, scaled_by(dout_t, tile, factor), weights[there, :]),
                    (dk, scaled_by(query_t, tile, factor), dscores[there, :]),
                ),
            )
        for block in range(counts[-1] // window.tiles):
            out = outs.pop(0)
            place = slice(block * rows, (block + 1) * rows)
            out[0:HD] = (dk[:, place] * SCALE).astype(out.dtype)
            out[HD : 2 * HD] = dv[:, place].astype(out.dtype)


def rest_grads(name, cost, parts):
    rows = parts[0][2][0].shape[0] // 2
    heads = parts[0][2][1].shape[1] // rows
    operands, out_shape = [], []
    for slot, middle, (_, query_t, dout_t, _, stats, weights, dprobs), sent in parts:
        window = Window(rows, slot)
        kept = (sum(window.middle if middle else window.early) * CHUNK, heads * TQ)
        operands += [query_t, dout_t, stats, weights, dprobs]
        out_shape.append(jax.ShapeDtypeStruct(kept, jnp.bfloat16))
        for one in sent:
            kind = jnp.bfloat16 if one else jnp.float32
            out_shape.append(jax.ShapeDtypeStruct((2 * HD, rows), kind))
    slots = tuple(part[0:2] for part in parts)
    return pl.pallas_call(
        functools.partial(grads_kernel, rows, heads, slots),
        out_shape=out_shape,
        in_specs=[VMEM] * len(operands),
        out_specs=[VMEM] * len(out_shape),
        scratch_shapes=[pltpu.VMEM((HD, 2 * rows), jnp.float32)] * 2,
        compiler_params=pltpu.CompilerParams(vmem_limit_bytes=VMEM_LIMIT),
        cost_estimate=pl.CostEstimate(flops=cost, bytes_accessed=0, transcendentals=0),
        name=name,
    )(*operands)


def outputs_kernel(rows, heads, *refs):
    blocks = (refs[0:3], refs[3:6], refs[6:9], refs[9]), (refs[10:13], refs[13:15], refs[15:17], refs[17])
    (attended_hbm, grad_query_hbm, attended, grad_query, keys_t, values_t, sems) = refs[18:]
    copies = []
    for slot, (sources, weights, dscores, stats) in enumerate(blocks):
        window = Window(rows, slot)
        groups = [(window.late, 0), (window.early, 1)]
        if slot == 0:
            groups.insert(1, (window.middle, 3))
        own_rows = half_start(rows, slot)
        for place, source in enumerate(sources):
            for tile in range(rows // TQ):
                part = slice(place * rows + tile * TQ, place * rows + (tile + 1) * TQ)
                row = tile * TQ
                keys_t[:, part] = jnp.transpose(source[row : row + TQ, :])
                values_t[:, part] = jnp.transpose(source[rows + row : rows + row + TQ, :])
        for step in window.steps:
            place = pl.ds(own_rows + step * TQ, TQ)
            for out, side, terms, scale in (
                (0, values_t, weights, 1.0),
                (1, keys_t, dscores, SCALE),
            ):
                found = None
                start = step * TQ
                for (counts, kind), term in zip(groups, terms):
                    columns = slice(start, start + counts[step] * CHUNK)
                    start = columns.stop
                    factor = stats[8 * kind + step : 8 * kind + step + 1, :] * scale
                    part = dot_nn(side[:, columns], term[chunk_rows(counts, step), :]) * factor
                    found = part if found is None else found + part
                target = (attended_hbm, grad_query_hbm)[out]
                source = (attended, grad_query)[out]
                for h in range(heads):
                    part = jnp.transpose(found[:, h * TQ : (h + 1) * TQ])
                    source[place, h * HD : (h + 1) * HD] = part.astype(source.dtype)
                copy = pltpu.make_async_copy(
                    source.at[place], target.at[place], sems.at[slot, step, out]
                )
                copy.start()
                copies.append(copy)
    for copy in copies:
        copy.wait()


def block_outputs(query, far, near):
    rows = query.shape[0] // 2
    heads = query.shape[1] // HD
    shape = jax.ShapeDtypeStruct(query.shape, query.dtype)
    return pl.pallas_call(
        functools.partial(outputs_kernel, rows, heads),
        out_shape=(shape, shape),
        in_specs=[VMEM] * 18,
        out_specs=[HBM] * 2,
        scratch_shapes=[pltpu.VMEM(query.shape, query.dtype)] * 2
        + [pltpu.VMEM((HD, 3 * rows), jnp.bfloat16)] * 2
        + [pltpu.SemaphoreType.DMA((2, rows // TQ, 2))],
        compiler_params=pltpu.CompilerParams(vmem_limit_bytes=VMEM_LIMIT),
        cost_estimate=pl.CostEstimate(flops=0, bytes_accessed=0, transcendentals=0),
        name="block_outputs",
    )(*far, *near)


def total_kernel(rows, far_own, far_1, far_2, near, grad_key, grad_value):
    far = far_own[...] + far_1[...].astype(jnp.float32) + far_2[...].astype(jnp.float32)
    for slot, total in ((0, far), (1, near[...])):
        place = pl.ds(half_start(rows, slot), rows)
        grad_key[place, :] = jnp.transpose(total[0:HD]).astype(grad_key.dtype)
        grad_value[place, :] = jnp.transpose(total[HD : 2 * HD]).astype(grad_value.dtype)


def total_grads(*parts):
    rows = parts[0].shape[1]
    shape = jax.ShapeDtypeStruct((2 * rows, HD), jnp.bfloat16)
    return pl.pallas_call(
        functools.partial(total_kernel, rows),
        out_shape=(shape, shape),
        in_specs=[VMEM] * 4,
        out_specs=[VMEM] * 2,
        compiler_params=pltpu.CompilerParams(vmem_limit_bytes=VMEM_LIMIT),
        name="total_grads",
    )(*parts)


def body(query, key, value, d_out, doc_lengths):
    count = lax.axis_size("ctx")

    def holder(block):
        return block if block < count else 2 * count - 1 - block

    def move(array, pairs):
        return lax.ppermute(array, "ctx", pairs)

    near_on = [(holder(b), holder(b + 2)) for b in range(1, 2 * count - 2, 2)]
    far_on = [(holder(b), holder(b + 2)) for b in range(0, 2 * count - 2, 2)]
    near_to_far = [(holder(b), holder(b + 1)) for b in range(1, 2 * count - 2, 2)]
    swap = [(d, d ^ 1) for d in range(count)]
    near_back = [(t, s) for s, t in near_on]
    far_back = [(t, s) for s, t in far_on]

    rows = key.shape[0] // 2
    odd = lax.axis_index("ctx") % 2 == 1
    lower = jnp.concatenate([key[:rows], value[:rows]], axis=0)
    upper = jnp.concatenate([key[rows:], value[rows:]], axis=0)
    near_kv, far_kv = jnp.where(odd, lower, upper), jnp.where(odd, upper, lower)
    far_1 = move(near_kv, near_to_far)
    far_2 = move(far_kv, far_on)
    prepared = prepare(count, doc_lengths, query, d_out, far_kv, near_kv)
    far_ready, near_ready = prepared[0:4], prepared[4:8]
    near_1 = move(far_ready[0], swap)
    far_early = group_scores(0, False, far_ready, far_ready[0])
    near_early = group_scores(1, False, near_ready, near_1, near_ready[0])
    far_1, near_early = lax.optimization_barrier((far_1, near_early))
    far_middle = group_scores(0, True, far_ready, far_1, far_early[2])
    far_late = late_scores(0, far_ready, (far_early[2], far_middle[2]), far_2)
    from_far_2 = move(far_late[3], far_back)
    near_2 = move(far_1, swap)
    near_2, far_stats = lax.optimization_barrier((near_2, far_late[2]))
    far_middle_d, far_g1 = rest_grads(
        "grads_far", 0, [(0, True, (*far_ready, far_stats, *far_middle[0:2]), (True,))]
    )
    relayed = move(far_g1, swap)
    near_late = late_scores(1, near_ready, (near_early[2],), near_2)
    near_sum = near_late[3].astype(jnp.float32) + relayed.astype(jnp.float32)
    from_near_2 = move(near_sum.astype(jnp.bfloat16), near_back)
    near_early_d, near_g1, near_own, far_early_d, far_own = rest_grads(
        "grads_near",
        2**31,
        [
            (1, False, (*near_ready, near_late[2], *near_early[0:2]), (True, False)),
            (0, False, (*far_ready, far_late[2], *far_early[0:2]), (False,)),
        ],
    )
    near_g1, from_far_2 = lax.optimization_barrier((near_g1, from_far_2))
    from_near_1 = move(near_g1, swap)
    attended, grad_query = block_outputs(
        query,
        (
            *(far_2, far_1, far_ready[0]),
            *(far_late[0], far_middle[0], far_early[0]),
            *(far_late[1], far_middle_d, far_early_d),
            far_late[2],
        ),
        (
            *(near_2, near_1, near_ready[0]),
            *(near_late[0], near_early[0]),
            *(near_late[1], near_early_d),
            near_late[2],
        ),
    )
    near_total = near_own + from_near_2.astype(jnp.float32)
    grad_key, grad_value = total_grads(far_own, from_near_1, from_far_2, near_total)
    return (attended, grad_query, grad_key, grad_value)


def solution(mesh):
    rows = P(("dp", "ctx"), None)
    return jax.shard_map(
        body,
        mesh=mesh,
        in_specs=(rows, rows, rows, rows, P("dp")),
        out_specs=(rows, rows, rows, rows),
        check_vma=False,
    )
```

```python
import functools
import math

import jax
import jax.numpy as jnp
from jax import lax
from jax.experimental import pallas as pl
from jax.experimental.pallas import tpu as pltpu
from jax.sharding import PartitionSpec as P

HD = 128
TQ = 128
GROUP = 16

masked_score = -1e30
other_document = -65536.0
VMEM_LIMIT = 24 * 1024 * 1024
SCALE = 1.0 / math.sqrt(HD)
VMEM = pl.BlockSpec(memory_space=pltpu.VMEM)
HBM = pl.BlockSpec(memory_space=pltpu.HBM)
CHUNK = 128
RUN = 3


def dot_nt(a, b):
    return lax.dot_general(a, b, (((1,), (1,)), ((), ())), preferred_element_type=jnp.float32)


def dot_nn(a, b):
    return lax.dot_general(a, b, (((1,), (0,)), ((), ())), preferred_element_type=jnp.float32)


def half_start(rows, slot):
    odd = lax.axis_index("ctx") % 2
    return pl.multiple_of((odd if slot == 0 else 1 - odd) * rows, rows)


def block_number(count, slot):
    device = lax.axis_index("ctx")
    in_lower = device % 2 == slot
    return jnp.where(in_lower, device, 2 * count - 1 - device)


def in_hbm(array):
    return pltpu.with_memory_space_constraint(array, pltpu.HBM)


def run_copies(copies):
    for copy in copies:
        copy.start()
    for copy in copies:
        copy.wait()


def prepare_kernel(rows, heads, docs, count, *refs):
    (far_kv, near_kv, doc_hbm, query_hbm, dout_hbm) = refs[0:5]
    (doc_lengths, query, dout, sems) = refs[13:]
    refs = refs[5:13]
    wide = heads * TQ
    run_copies(
        [
            pltpu.make_async_copy(query_hbm, query, sems.at[0]),
            pltpu.make_async_copy(dout_hbm, dout, sems.at[1]),
            pltpu.make_async_copy(doc_hbm, doc_lengths, sems.at[2]),
        ]
    )
    lane = lax.broadcasted_iota(jnp.int32, (1, HD), 1)

    def one(index, carry):
        start, starts, ends = carry
        end = start + doc_lengths[index]
        starts = jnp.where(lane == index, start, starts)
        return (end, starts, jnp.where(lane == index, end, ends))

    none = jnp.zeros((1, HD), jnp.int32)
    _, starts, ends = lax.fori_loop(0, docs, one, (jnp.int32(0), none, none), unroll=8)
    starts_t, ends_t = (
        jnp.transpose(jnp.broadcast_to(row.astype(jnp.float32), (HD, HD))).astype(jnp.int32)
        for row in (starts, ends)
    )
    for slot in (0, 1):
        own_kv, query_t, dout_t, documents = refs[4 * slot : 4 * slot + 4]
        own_kv[...] = (far_kv, near_kv)[slot][...]
        own_rows = half_start(rows, slot)
        for step in range(rows // TQ):
            source = pl.ds(own_rows + step * TQ, TQ)
            for h in range(heads):
                place = slice(step * wide + h * TQ, step * wide + (h + 1) * TQ)
                columns = slice(h * HD, (h + 1) * HD)
                query_t[0:HD, place] = jnp.transpose(query[source, columns])
                dout_t[:, place] = jnp.transpose(dout[source, columns])
        position = block_number(count, slot) * rows
        for tile in range(3 * rows // TQ):
            at = lax.broadcasted_iota(jnp.int32, (TQ, HD), 0) + (position - 2 * rows + tile * TQ)
            inside = jnp.logical_and(at >= starts, at < ends)
            inside = jnp.logical_or(inside, at < 0)
            documents[tile * TQ : (tile + 1) * TQ, :] = jnp.where(inside, 1.0, 0.0).astype(
                documents.dtype
            )
        for step in range(rows // TQ):
            at = lax.broadcasted_iota(jnp.int32, (HD, TQ), 1) + (position + step * TQ)
            inside = jnp.logical_and(at >= starts_t, at < ends_t)
            other = jnp.where(inside, 0.0, other_document).astype(query_t.dtype)
            for h in range(heads):
                place = slice(step * wide + h * TQ, step * wide + (h + 1) * TQ)
                query_t[HD : 2 * HD, place] = other


def prepare(count, doc_lengths, query, dout, far_kv, near_kv):
    rows = query.shape[0] // 2
    heads = query.shape[1] // HD
    pair = jax.ShapeDtypeStruct(far_kv.shape, far_kv.dtype)
    stacked_t = jax.ShapeDtypeStruct((HD, rows * heads), query.dtype)
    query_shape = jax.ShapeDtypeStruct((2 * HD, rows * heads), query.dtype)
    documents = jax.ShapeDtypeStruct((3 * rows, HD), query.dtype)
    assert doc_lengths.shape[0] <= HD
    return pl.pallas_call(
        functools.partial(prepare_kernel, rows, heads, doc_lengths.shape[0], count),
        out_shape=(pair, query_shape, stacked_t, documents) * 2,
        in_specs=[VMEM] * 2 + [HBM] * 3,
        out_specs=[VMEM] * 8,
        scratch_shapes=[
            pltpu.SMEM(doc_lengths.shape, doc_lengths.dtype),
            pltpu.VMEM(query.shape, query.dtype),
            pltpu.VMEM(dout.shape, dout.dtype),
            pltpu.SemaphoreType.DMA((3,)),
        ],
        compiler_params=pltpu.CompilerParams(vmem_limit_bytes=VMEM_LIMIT),
        cost_estimate=pl.CostEstimate(flops=0, bytes_accessed=4 * 2**20, transcendentals=0),
        name="prepare",
    )(far_kv, near_kv, *(in_hbm(array) for array in (doc_lengths, query, dout)))


class Window:
    def __init__(self, rows, slot):
        self.tiles = rows // TQ
        self.chunks = 2 * self.tiles + 1
        self.steps = range(self.tiles)
        self.late = [self.tiles - step for step in self.steps]
        self.middle = [(1 - slot) * self.tiles for step in self.steps]
        self.early = [
            self.chunks - late - middle for late, middle in zip(self.late, self.middle)
        ]


def chunk_rows(counts, step, first=0, count=None):
    start = sum(counts[:step]) + first
    count = counts[step] - first if count is None else count
    return slice(start * CHUNK, (start + count) * CHUNK)


def run_length(run):
    return run[-1].stop - run[-1].start


def runs_of(chunks):
    runs = []
    for chunk in chunks:
        if runs:
            last = runs[-1]
            length = run_length(last)
            if last[1] is chunk[1] and last[2] + length == chunk[2] and length < RUN * CHUNK:
                runs[-1] = (*last[:-1], slice(last[-1].start, chunk[-1].stop))
                continue
        runs.append(chunk)
    return runs


def exponentials(jobs, rows, heads, scores, scores_first=False):
    back = 2 * rows
    wide = heads * TQ
    base2 = SCALE * math.log2(math.e)

    def score(job, index, row_max):
        step, chunks, (query_t, _, documents), _, _ = jobs[job]
        chunk, keys, row = chunks[index][0:3]
        tile = slice(step * wide, (step + 1) * wide)
        length = run_length(chunks[index])
        window = slice(step * TQ + chunk * CHUNK, step * TQ + chunk * CHUNK + length)
        product = dot_nn(
            jnp.concatenate([keys[row : row + length, :], documents[window, :]], axis=1),
            query_t[:, tile],
        )
        for start in range(0, length, GROUP):
            place = chunk * CHUNK + start
            for h in range(heads):
                lanes = slice(h * TQ, (h + 1) * TQ)
                part = product[start : start + GROUP, lanes]
                if place >= back:
                    key_at = lax.broadcasted_iota(jnp.int32, (GROUP, TQ), 0) + (place - back)
                    query_at = lax.broadcasted_iota(jnp.int32, (GROUP, TQ), 1)
                    part = jnp.where(key_at <= query_at, part, masked_score)
                scores[job % scores.shape[0], place : place + GROUP, lanes] = part
                for row8 in range(0, GROUP, 8):
                    row_max[h] = jnp.maximum(row_max[h], part[row8 : row8 + 8, :])

    def start_max():
        return [jnp.full((8, TQ), masked_score, jnp.float32)] * heads

    pending = None
    every = [start_max() for _ in jobs]
    for job in range(len(jobs) if scores_first else 1):
        for index in range(len(jobs[job][1])):
            score(job, index, every[job])
    for job, (step, chunks, (_, dout_t, _), first_max, end) in enumerate(jobs):
        tile = slice(step * wide, (step + 1) * wide)
        row_max = jnp.concatenate(
            [jnp.max(part, axis=0, keepdims=True) * base2 for part in every[job]], axis=1
        )
        if first_max is not None:
            row_max = jnp.maximum(row_max, first_max)
        ahead = len(jobs[job + 1][1]) if job + 1 < len(jobs) and not scores_first else 0
        done = 0
        total = jnp.zeros((8, wide), jnp.float32)
        delta = jnp.zeros((8, wide), jnp.float32)
        for index, (chunk, keys, row, weights, dprobs, kept) in enumerate(chunks):
            length = kept.stop - kept.start
            product = dot_nn(keys[rows + row : rows + row + length, :], dout_t[:, tile])
            for start in range(0, length, GROUP):
                place = chunk * CHUNK + start
                there = slice(kept.start + start, kept.start + start + GROUP)
                dprob = product[start : start + GROUP, :]
                dprobs[there, :] = dprob.astype(jnp.bfloat16)
                part = jnp.exp2(scores[job % scores.shape[0], place : place + GROUP, :] * base2 - row_max)
                weights[there, :] = part.astype(jnp.bfloat16)
                term = part * dprob
                for row8 in range(0, GROUP, 8):
                    total = total + part[row8 : row8 + 8, :]
                    delta = delta + term[row8 : row8 + 8, :]
            while done * len(chunks) < ahead * (index + 1):
                score(job + 1, done, every[job + 1])
                done += 1
            if index == 0 and pending is not None:
                pending()
        sums = [jnp.sum(part, axis=0, keepdims=True) for part in (total, delta)]
        pending = functools.partial(end, row_max, *sums)
    pending()


def group_kernel(rows, heads, slot, middle, query_t, dout_t, documents, *refs):
    (weights, dprobs, stats, scores) = refs[-4:]
    prev1 = refs[0] if middle or slot == 1 else None
    own_kv = None if middle else refs[slot]
    window = Window(rows, slot)
    counts = window.middle if middle else window.early
    jobs = []
    for step in window.steps:
        chunks = []
        for index in range(counts[step]):
            chunk = window.late[step] + (0 if middle else window.middle[step]) + index
            row = step * TQ + chunk * CHUNK
            keys = own_kv if row >= 2 * rows else prev1
            kept = chunk_rows(counts, step, index, 1)
            chunks.append((chunk, keys, row % rows, weights, dprobs, kept))

        def end(*found, step=step):
            for kind, value in enumerate(found):
                stats[8 * kind + step : 8 * kind + step + 1, :] = value

        first_max = refs[1][step : step + 1, :] if middle else None
        jobs.append((step, runs_of(chunks), (query_t, dout_t, documents), first_max, end))
    exponentials(jobs, rows, heads, scores)


def group_scores(slot, middle, ready, *operands):
    rows = ready[0].shape[0] // 2
    heads = ready[1].shape[1] // rows
    wide = heads * TQ
    window = Window(rows, slot)
    counts = window.middle if middle else window.early
    kept = jax.ShapeDtypeStruct((sum(counts) * CHUNK, wide), jnp.bfloat16)
    cost = (0 if slot else 2**33) if not middle else 0
    return pl.pallas_call(
        functools.partial(group_kernel, rows, heads, slot, middle),
        out_shape=(kept, kept, jax.ShapeDtypeStruct((24, wide), jnp.float32)),
        in_specs=[VMEM] * (3 + len(operands)),
        out_specs=[VMEM] * 3,
        scratch_shapes=[pltpu.VMEM((2, 2 * rows + TQ, wide), jnp.float32)],
        compiler_params=pltpu.CompilerParams(vmem_limit_bytes=VMEM_LIMIT),
        cost_estimate=pl.CostEstimate(flops=cost, bytes_accessed=0, transcendentals=0),
        name="middle_far" if middle else "early_far" if slot == 0 else "early_near",
    )(*ready[1:4], *operands)


def scaled_by(array, tile, factor):
    return (array[0:HD, tile].astype(jnp.float32) * factor).astype(jnp.bfloat16)


def dscore_rows(dscores, there, weights, dprobs, kept, delta):
    delta = jnp.broadcast_to(delta, (16, delta.shape[1]))
    for start in range(0, there.stop - there.start, 16):
        out = slice(there.start + start, there.start + start + 16)
        place = slice(kept.start + start, kept.start + start + 16)
        dscores[out, :] = weights[place, :] * (dprobs[place, :] - delta)


def add_products(new, columns, products):
    for total_ref, side, terms in products:
        term = dot_nt(side, terms)
        if new:
            total_ref[:, columns] = term
        else:
            total_ref[:, columns] += term


def late_kernel(rows, heads, slot, query_t, dout_t, documents, prev2, *refs):
    groups = refs[0 : 2 - slot]
    (weights, dscores, stats, prev2_out, scores, dprobs) = refs[2 - slot :]
    wide = heads * TQ
    window = Window(rows, slot)
    jobs = []
    key_terms, value_terms = [], []
    for step in window.steps:
        chunks = []
        for chunk in range(window.late[step]):
            kept = chunk_rows(window.late, step, chunk, 1)
            chunks.append((chunk, prev2, step * TQ + chunk * CHUNK, weights, dprobs, kept))

        def end(row_max, total, delta, step=step):
            tile = slice(step * wide, (step + 1) * wide)
            rows_of = [
                [group[8 * kind + step : 8 * kind + step + 1, :] for kind in range(3)]
                for group in groups
            ]
            shrinks = [jnp.exp2(found[0] - row_max) for found in rows_of]
            for found, shrink in zip(rows_of, shrinks):
                total = total + found[1] * shrink
                delta = delta + found[2] * shrink
            late_factor = 1.0 / total
            delta = delta * late_factor
            factors = [late_factor * shrink for shrink in shrinks]
            for kind, value in enumerate((late_factor, factors[0], delta, factors[-1])):
                stats[8 * kind + step : 8 * kind + step + 1, :] = value
            there = chunk_rows(window.late, step)
            dscore_rows(dscores, there, weights, dprobs, there, delta.astype(jnp.bfloat16))
            value_terms.append(dot_nt(scaled_by(dout_t, tile, late_factor), weights[there, :]))
            key_terms.append(dot_nt(scaled_by(query_t, tile, late_factor), dscores[there, :]))

        first_max = groups[-1][step : step + 1, :]
        jobs.append((step, runs_of(chunks), (query_t, dout_t, documents), first_max, end))
    exponentials(jobs, rows, heads, scores, True)
    for first, terms, scale in ((0, key_terms, SCALE), (HD, value_terms, 1.0)):
        for tile in range(window.tiles):
            parts = [
                terms[step][:, (tile - step) * TQ : (tile - step + 1) * TQ]
                for step in range(tile + 1)
            ]
            prev2_out[first : first + HD, tile * TQ : (tile + 1) * TQ] = (
                sum(parts[1:], parts[0]) * scale
            ).astype(prev2_out.dtype)


def late_scores(slot, ready, groups, prev2):
    rows = prev2.shape[0] // 2
    heads = ready[1].shape[1] // rows
    wide = heads * TQ
    late = jax.ShapeDtypeStruct((sum(Window(rows, slot).late) * CHUNK, wide), jnp.bfloat16)
    return pl.pallas_call(
        functools.partial(late_kernel, rows, heads, slot),
        out_shape=(
            late,
            late,
            jax.ShapeDtypeStruct((32, wide), jnp.float32),
            jax.ShapeDtypeStruct((2 * HD, rows), jnp.bfloat16),
        ),
        in_specs=[VMEM] * (4 + len(groups)),
        out_specs=[VMEM] * 4,
        scratch_shapes=[
            pltpu.VMEM((rows // TQ, rows, wide), jnp.float32),
            pltpu.VMEM(late.shape, late.dtype),
        ],
        compiler_params=pltpu.CompilerParams(vmem_limit_bytes=VMEM_LIMIT),
        cost_estimate=pl.CostEstimate(flops=2**31, bytes_accessed=0, transcendentals=0),
        name="late_far" if slot == 0 else "late_near",
    )(*ready[1:4], prev2, *groups)


def grads_kernel(rows, heads, slots, *refs):
    wide = heads * TQ
    outs = list(refs[5 * len(slots) : -2])
    (dk, dv) = refs[-2:]
    for part, (slot, middle) in enumerate(slots):
        (query_t, dout_t, stats, weights, dprobs) = refs[5 * part : 5 * part + 5]
        dscores = outs.pop(0)
        window = Window(rows, slot)
        counts = window.middle if middle else window.early
        for step in reversed(window.steps):
            tile = slice(step * wide, (step + 1) * wide)
            _, early_factor, delta, middle_factor = (
                stats[8 * kind + step : 8 * kind + step + 1, :] for kind in range(4)
            )
            factor = middle_factor if middle else early_factor
            there = chunk_rows(counts, step)
            dscore_rows(dscores, there, weights, dprobs, there, delta.astype(jnp.bfloat16))
            add_products(
                step == window.tiles - 1,
                slice(0, counts[step] * CHUNK),
                (
                    (dv, scaled_by(dout_t, tile, factor), weights[there, :]),
                    (dk, scaled_by(query_t, tile, factor), dscores[there, :]),
                ),
            )
        for block in range(counts[-1] // window.tiles):
            out = outs.pop(0)
            place = slice(block * rows, (block + 1) * rows)
            out[0:HD] = (dk[:, place] * SCALE).astype(out.dtype)
            out[HD : 2 * HD] = dv[:, place].astype(out.dtype)


def rest_grads(name, cost, parts):
    rows = parts[0][2][0].shape[0] // 2
    heads = parts[0][2][1].shape[1] // rows
    operands, out_shape = [], []
    for slot, middle, (_, query_t, dout_t, _, stats, weights, dprobs), sent in parts:
        window = Window(rows, slot)
        kept = (sum(window.middle if middle else window.early) * CHUNK, heads * TQ)
        operands += [query_t, dout_t, stats, weights, dprobs]
        out_shape.append(jax.ShapeDtypeStruct(kept, jnp.bfloat16))
        for one in sent:
            kind = jnp.bfloat16 if one else jnp.float32
            out_shape.append(jax.ShapeDtypeStruct((2 * HD, rows), kind))
    slots = tuple(part[0:2] for part in parts)
    return pl.pallas_call(
        functools.partial(grads_kernel, rows, heads, slots),
        out_shape=out_shape,
        in_specs=[VMEM] * len(operands),
        out_specs=[VMEM] * len(out_shape),
        scratch_shapes=[pltpu.VMEM((HD, 2 * rows), jnp.float32)] * 2,
        compiler_params=pltpu.CompilerParams(vmem_limit_bytes=VMEM_LIMIT),
        cost_estimate=pl.CostEstimate(flops=cost, bytes_accessed=0, transcendentals=0),
        name=name,
    )(*operands)


def outputs_kernel(rows, heads, *refs):
    blocks = (refs[0:3], refs[3:6], refs[6:9], refs[9]), (refs[10:13], refs[13:15], refs[15:17], refs[17])
    (attended_hbm, grad_query_hbm, attended, grad_query, keys_t, values_t, sems) = refs[18:]
    copies = []
    for slot, (sources, weights, dscores, stats) in enumerate(blocks):
        window = Window(rows, slot)
        groups = [(window.late, 0), (window.early, 1)]
        if slot == 0:
            groups.insert(1, (window.middle, 3))
        own_rows = half_start(rows, slot)
        for place, source in enumerate(sources):
            for tile in range(rows // TQ):
                part = slice(place * rows + tile * TQ, place * rows + (tile + 1) * TQ)
                row = tile * TQ
                keys_t[:, part] = jnp.transpose(source[row : row + TQ, :])
                values_t[:, part] = jnp.transpose(source[rows + row : rows + row + TQ, :])
        for step in window.steps:
            place = pl.ds(own_rows + step * TQ, TQ)
            for out, side, terms, scale in (
                (0, values_t, weights, 1.0),
                (1, keys_t, dscores, SCALE),
            ):
                found = None
                start = step * TQ
                for (counts, kind), term in zip(groups, terms):
                    columns = slice(start, start + counts[step] * CHUNK)
                    start = columns.stop
                    factor = stats[8 * kind + step : 8 * kind + step + 1, :] * scale
                    part = dot_nn(side[:, columns], term[chunk_rows(counts, step), :]) * factor
                    found = part if found is None else found + part
                target = (attended_hbm, grad_query_hbm)[out]
                source = (attended, grad_query)[out]
                for h in range(heads):
                    part = jnp.transpose(found[:, h * TQ : (h + 1) * TQ])
                    source[place, h * HD : (h + 1) * HD] = part.astype(source.dtype)
                copy = pltpu.make_async_copy(
                    source.at[place], target.at[place], sems.at[slot, step, out]
                )
                copy.start()
                copies.append(copy)
    for copy in copies:
        copy.wait()


def block_outputs(query, far, near):
    rows = query.shape[0] // 2
    heads = query.shape[1] // HD
    shape = jax.ShapeDtypeStruct(query.shape, query.dtype)
    return pl.pallas_call(
        functools.partial(outputs_kernel, rows, heads),
        out_shape=(shape, shape),
        in_specs=[VMEM] * 18,
        out_specs=[HBM] * 2,
        scratch_shapes=[pltpu.VMEM(query.shape, query.dtype)] * 2
        + [pltpu.VMEM((HD, 3 * rows), jnp.bfloat16)] * 2
        + [pltpu.SemaphoreType.DMA((2, rows // TQ, 2))],
        compiler_params=pltpu.CompilerParams(vmem_limit_bytes=VMEM_LIMIT),
        cost_estimate=pl.CostEstimate(flops=0, bytes_accessed=0, transcendentals=0),
        name="block_outputs",
    )(*far, *near)


def total_kernel(rows, far_own, far_1, far_2, near, grad_key, grad_value):
    far = far_own[...] + far_1[...].astype(jnp.float32) + far_2[...].astype(jnp.float32)
    for slot, total in ((0, far), (1, near[...])):
        place = pl.ds(half_start(rows, slot), rows)
        grad_key[place, :] = jnp.transpose(total[0:HD]).astype(grad_key.dtype)
        grad_value[place, :] = jnp.transpose(total[HD : 2 * HD]).astype(grad_value.dtype)


def total_grads(*parts):
    rows = parts[0].shape[1]
    shape = jax.ShapeDtypeStruct((2 * rows, HD), jnp.bfloat16)
    return pl.pallas_call(
        functools.partial(total_kernel, rows),
        out_shape=(shape, shape),
        in_specs=[VMEM] * 4,
        out_specs=[VMEM] * 2,
        compiler_params=pltpu.CompilerParams(vmem_limit_bytes=VMEM_LIMIT),
        name="total_grads",
    )(*parts)


def body(query, key, value, d_out, doc_lengths):
    count = lax.axis_size("ctx")

    def holder(block):
        return block if block < count else 2 * count - 1 - block

    def move(array, pairs):
        return lax.ppermute(array, "ctx", pairs)

    near_on = [(holder(b), holder(b + 2)) for b in range(1, 2 * count - 2, 2)]
    far_on = [(holder(b), holder(b + 2)) for b in range(0, 2 * count - 2, 2)]
    near_to_far = [(holder(b), holder(b + 1)) for b in range(1, 2 * count - 2, 2)]
    swap = [(d, d ^ 1) for d in range(count)]
    near_back = [(t, s) for s, t in near_on]
    far_back = [(t, s) for s, t in far_on]

    rows = key.shape[0] // 2
    odd = lax.axis_index("ctx") % 2 == 1
    near_kv, far_kv = (
        jnp.concatenate([jnp.where(first, part[:rows], part[rows:]) for part in (key, value)], axis=0)
        for first in (odd, jnp.logical_not(odd))
    )
    far_1 = move(near_kv, near_to_far)
    far_2 = move(far_kv, far_on)
    prepared = prepare(count, doc_lengths, query, d_out, far_kv, near_kv)
    far_ready, near_ready = prepared[0:4], prepared[4:8]
    near_1 = move(far_ready[0], swap)
    far_early = group_scores(0, False, far_ready, far_ready[0])
    near_early = group_scores(1, False, near_ready, near_1, near_ready[0])
    far_1, near_early = lax.optimization_barrier((far_1, near_early))
    far_middle = group_scores(0, True, far_ready, far_1, far_early[2])
    far_late = late_scores(0, far_ready, (far_early[2], far_middle[2]), far_2)
    from_far_2 = move(far_late[3], far_back)
    near_2 = move(far_1, swap)
    near_2, far_stats = lax.optimization_barrier((near_2, far_late[2]))
    far_middle_d, far_g1 = rest_grads(
        "grads_far", 0, [(0, True, (*far_ready, far_stats, *far_middle[0:2]), (True,))]
    )
    relayed = move(far_g1, swap)
    near_late = late_scores(1, near_ready, (near_early[2],), near_2)
    near_sum = near_late[3].astype(jnp.float32) + relayed.astype(jnp.float32)
    from_near_2 = move(near_sum.astype(jnp.bfloat16), near_back)
    near_early_d, near_g1, near_own, far_early_d, far_own = rest_grads(
        "grads_near",
        2**31,
        [
            (1, False, (*near_ready, near_late[2], *near_early[0:2]), (True, False)),
            (0, False, (*far_ready, far_late[2], *far_early[0:2]), (False,)),
        ],
    )
    near_g1, from_far_2 = lax.optimization_barrier((near_g1, from_far_2))
    from_near_1 = move(near_g1, swap)
    attended, grad_query = block_outputs(
        query,
        (
            *(far_2, far_1, far_ready[0]),
            *(far_late[0], far_middle[0], far_early[0]),
            *(far_late[1], far_middle_d, far_early_d),
            far_late[2],
        ),
        (
            *(near_2, near_1, near_ready[0]),
            *(near_late[0], near_early[0]),
            *(near_late[1], near_early_d),
            near_late[2],
        ),
    )
    near_total = near_own + from_near_2.astype(jnp.float32)
    grad_key, grad_value = total_grads(far_own, from_near_1, from_far_2, near_total)
    return (attended, grad_query, grad_key, grad_value)


def solution(mesh):
    rows = P(("dp", "ctx"), None)
    return jax.shard_map(
        body,
        mesh=mesh,
        in_specs=(rows, rows, rows, rows, P("dp")),
        out_specs=(rows, rows, rows, rows),
        check_vma=False,
    )
```

```python
import functools
import math

import jax
import jax.numpy as jnp
from jax import lax
from jax.experimental import pallas as pl
from jax.experimental.pallas import tpu as pltpu
from jax.sharding import PartitionSpec as P

HD = 128
TQ = 128
GROUP = 16

masked_score = -1e30
other_document = -65536.0
VMEM_LIMIT = 24 * 1024 * 1024
SCALE = 1.0 / math.sqrt(HD)
VMEM = pl.BlockSpec(memory_space=pltpu.VMEM)
HBM = pl.BlockSpec(memory_space=pltpu.HBM)
CHUNK = 128
RUN = 3


def dot_nt(a, b):
    return lax.dot_general(a, b, (((1,), (1,)), ((), ())), preferred_element_type=jnp.float32)


def dot_nn(a, b):
    return lax.dot_general(a, b, (((1,), (0,)), ((), ())), preferred_element_type=jnp.float32)


def half_start(rows, slot):
    odd = lax.axis_index("ctx") % 2
    return pl.multiple_of((odd if slot == 0 else 1 - odd) * rows, rows)


def block_number(count, slot):
    device = lax.axis_index("ctx")
    in_lower = device % 2 == slot
    return jnp.where(in_lower, device, 2 * count - 1 - device)


def in_hbm(array):
    return pltpu.with_memory_space_constraint(array, pltpu.HBM)


def run_copies(copies):
    for copy in copies:
        copy.start()
    for copy in copies:
        copy.wait()


def prepare_kernel(rows, heads, docs, count, *refs):
    (far_kv, near_kv, doc_hbm, query_hbm, dout_hbm) = refs[0:5]
    (doc_lengths, query, dout, sems) = refs[13:]
    refs = refs[5:13]
    wide = heads * TQ
    run_copies(
        [
            pltpu.make_async_copy(query_hbm, query, sems.at[0]),
            pltpu.make_async_copy(dout_hbm, dout, sems.at[1]),
            pltpu.make_async_copy(doc_hbm, doc_lengths, sems.at[2]),
        ]
    )
    lane = lax.broadcasted_iota(jnp.int32, (1, HD), 1)

    def one(index, carry):
        start, starts, ends = carry
        end = start + doc_lengths[index]
        starts = jnp.where(lane == index, start, starts)
        return (end, starts, jnp.where(lane == index, end, ends))

    none = jnp.zeros((1, HD), jnp.int32)
    _, starts, ends = lax.fori_loop(0, docs, one, (jnp.int32(0), none, none), unroll=8)
    starts_t, ends_t = (
        jnp.transpose(jnp.broadcast_to(row.astype(jnp.float32), (HD, HD))).astype(jnp.int32)
        for row in (starts, ends)
    )
    for slot in (0, 1):
        own_kv, query_t, dout_t, documents = refs[4 * slot : 4 * slot + 4]
        own_kv[...] = (far_kv, near_kv)[slot][...]
        own_rows = half_start(rows, slot)
        for step in range(rows // TQ):
            source = pl.ds(own_rows + step * TQ, TQ)
            for h in range(heads):
                place = slice(step * wide + h * TQ, step * wide + (h + 1) * TQ)
                columns = slice(h * HD, (h + 1) * HD)
                query_t[0:HD, place] = jnp.transpose(query[source, columns])
                dout_t[:, place] = jnp.transpose(dout[source, columns])
        position = block_number(count, slot) * rows
        for tile in range(3 * rows // TQ):
            at = lax.broadcasted_iota(jnp.int32, (TQ, HD), 0) + (position - 2 * rows + tile * TQ)
            inside = jnp.logical_and(at >= starts, at < ends)
            inside = jnp.logical_or(inside, at < 0)
            documents[tile * TQ : (tile + 1) * TQ, :] = jnp.where(inside, 1.0, 0.0).astype(
                documents.dtype
            )
        for step in range(rows // TQ):
            at = lax.broadcasted_iota(jnp.int32, (HD, TQ), 1) + (position + step * TQ)
            inside = jnp.logical_and(at >= starts_t, at < ends_t)
            other = jnp.where(inside, 0.0, other_document).astype(query_t.dtype)
            for h in range(heads):
                place = slice(step * wide + h * TQ, step * wide + (h + 1) * TQ)
                query_t[HD : 2 * HD, place] = other


def prepare(count, doc_lengths, query, dout, far_kv, near_kv):
    rows = query.shape[0] // 2
    heads = query.shape[1] // HD
    pair = jax.ShapeDtypeStruct(far_kv.shape, far_kv.dtype)
    stacked_t = jax.ShapeDtypeStruct((HD, rows * heads), query.dtype)
    query_shape = jax.ShapeDtypeStruct((2 * HD, rows * heads), query.dtype)
    documents = jax.ShapeDtypeStruct((3 * rows, HD), query.dtype)
    assert doc_lengths.shape[0] <= HD
    return pl.pallas_call(
        functools.partial(prepare_kernel, rows, heads, doc_lengths.shape[0], count),
        out_shape=(pair, query_shape, stacked_t, documents) * 2,
        in_specs=[VMEM] * 2 + [HBM] * 3,
        out_specs=[VMEM] * 8,
        scratch_shapes=[
            pltpu.SMEM(doc_lengths.shape, doc_lengths.dtype),
            pltpu.VMEM(query.shape, query.dtype),
            pltpu.VMEM(dout.shape, dout.dtype),
            pltpu.SemaphoreType.DMA((3,)),
        ],
        compiler_params=pltpu.CompilerParams(vmem_limit_bytes=VMEM_LIMIT),
        cost_estimate=pl.CostEstimate(flops=0, bytes_accessed=4 * 2**20, transcendentals=0),
        name="prepare",
    )(far_kv, near_kv, *(in_hbm(array) for array in (doc_lengths, query, dout)))


class Window:
    def __init__(self, rows, slot):
        self.tiles = rows // TQ
        self.chunks = 2 * self.tiles + 1
        self.steps = range(self.tiles)
        self.late = [self.tiles - step for step in self.steps]
        self.middle = [(1 - slot) * self.tiles for step in self.steps]
        self.early = [
            self.chunks - late - middle for late, middle in zip(self.late, self.middle)
        ]


def chunk_rows(counts, step, first=0, count=None):
    start = sum(counts[:step]) + first
    count = counts[step] - first if count is None else count
    return slice(start * CHUNK, (start + count) * CHUNK)


def run_length(run):
    return run[-1].stop - run[-1].start


def runs_of(chunks):
    runs = []
    for chunk in chunks:
        if runs:
            last = runs[-1]
            length = run_length(last)
            if last[1] is chunk[1] and last[2] + length == chunk[2] and length < RUN * CHUNK:
                runs[-1] = (*last[:-1], slice(last[-1].start, chunk[-1].stop))
                continue
        runs.append(chunk)
    return runs


def exponentials(jobs, rows, heads, scores, scores_first=False):
    back = 2 * rows
    wide = heads * TQ
    base2 = SCALE * math.log2(math.e)

    def score(job, index, row_max):
        step, chunks, (query_t, _, documents), _, _ = jobs[job]
        chunk, keys, row = chunks[index][0:3]
        tile = slice(step * wide, (step + 1) * wide)
        length = run_length(chunks[index])
        window = slice(step * TQ + chunk * CHUNK, step * TQ + chunk * CHUNK + length)
        product = dot_nn(
            jnp.concatenate([keys[row : row + length, :], documents[window, :]], axis=1),
            query_t[:, tile],
        )
        for start in range(0, length, GROUP):
            place = chunk * CHUNK + start
            for h in range(heads):
                lanes = slice(h * TQ, (h + 1) * TQ)
                part = product[start : start + GROUP, lanes]
                if place >= back:
                    key_at = lax.broadcasted_iota(jnp.int32, (GROUP, TQ), 0) + (place - back)
                    query_at = lax.broadcasted_iota(jnp.int32, (GROUP, TQ), 1)
                    part = jnp.where(key_at <= query_at, part, masked_score)
                scores[job % scores.shape[0], place : place + GROUP, lanes] = part
                for row8 in range(0, GROUP, 8):
                    row_max[h] = jnp.maximum(row_max[h], part[row8 : row8 + 8, :])

    def start_max():
        return [jnp.full((8, TQ), masked_score, jnp.float32)] * heads

    pending = None
    every = [start_max() for _ in jobs]
    for job in range(len(jobs) if scores_first else 1):
        for index in range(len(jobs[job][1])):
            score(job, index, every[job])
    for job, (step, chunks, (_, dout_t, _), first_max, end) in enumerate(jobs):
        tile = slice(step * wide, (step + 1) * wide)
        row_max = jnp.concatenate(
            [jnp.max(part, axis=0, keepdims=True) * base2 for part in every[job]], axis=1
        )
        if first_max is not None:
            row_max = jnp.maximum(row_max, first_max)
        ahead = len(jobs[job + 1][1]) if job + 1 < len(jobs) and not scores_first else 0
        done = 0
        total = jnp.zeros((8, wide), jnp.float32)
        delta = jnp.zeros((8, wide), jnp.float32)
        for index, (chunk, keys, row, weights, dprobs, kept) in enumerate(chunks):
            length = kept.stop - kept.start
            product = dot_nn(keys[rows + row : rows + row + length, :], dout_t[:, tile])
            for start in range(0, length, GROUP):
                place = chunk * CHUNK + start
                there = slice(kept.start + start, kept.start + start + GROUP)
                dprob = product[start : start + GROUP, :]
                dprobs[there, :] = dprob.astype(jnp.bfloat16)
                part = jnp.exp2(scores[job % scores.shape[0], place : place + GROUP, :] * base2 - row_max)
                weights[there, :] = part.astype(jnp.bfloat16)
                term = part * dprob
                for row8 in range(0, GROUP, 8):
                    total = total + part[row8 : row8 + 8, :]
                    delta = delta + term[row8 : row8 + 8, :]
            while done * len(chunks) < ahead * (index + 1):
                score(job + 1, done, every[job + 1])
                done += 1
            if index == 0 and pending is not None:
                pending()
        sums = [jnp.sum(part, axis=0, keepdims=True) for part in (total, delta)]
        pending = functools.partial(end, row_max, *sums)
    pending()


def group_kernel(rows, heads, slot, middle, query_t, dout_t, documents, *refs):
    (weights, dprobs, stats, scores) = refs[-4:]
    prev1 = refs[0] if middle or slot == 1 else None
    own_kv = None if middle else refs[slot]
    window = Window(rows, slot)
    counts = window.middle if middle else window.early
    jobs = []
    for step in window.steps:
        chunks = []
        for index in range(counts[step]):
            chunk = window.late[step] + (0 if middle else window.middle[step]) + index
            row = step * TQ + chunk * CHUNK
            keys = own_kv if row >= 2 * rows else prev1
            kept = chunk_rows(counts, step, index, 1)
            chunks.append((chunk, keys, row % rows, weights, dprobs, kept))

        def end(*found, step=step):
            for kind, value in enumerate(found):
                stats[8 * kind + step : 8 * kind + step + 1, :] = value

        first_max = refs[1][step : step + 1, :] if middle else None
        jobs.append((step, runs_of(chunks), (query_t, dout_t, documents), first_max, end))
    exponentials(jobs, rows, heads, scores)


def group_scores(slot, middle, ready, *operands):
    rows = ready[0].shape[0] // 2
    heads = ready[1].shape[1] // rows
    wide = heads * TQ
    window = Window(rows, slot)
    counts = window.middle if middle else window.early
    kept = jax.ShapeDtypeStruct((sum(counts) * CHUNK, wide), jnp.bfloat16)
    cost = (0 if slot else 2**33) if not middle else 0
    return pl.pallas_call(
        functools.partial(group_kernel, rows, heads, slot, middle),
        out_shape=(kept, kept, jax.ShapeDtypeStruct((24, wide), jnp.float32)),
        in_specs=[VMEM] * (3 + len(operands)),
        out_specs=[VMEM] * 3,
        scratch_shapes=[pltpu.VMEM((2, 2 * rows + TQ, wide), jnp.float32)],
        compiler_params=pltpu.CompilerParams(vmem_limit_bytes=VMEM_LIMIT),
        cost_estimate=pl.CostEstimate(flops=cost, bytes_accessed=0, transcendentals=0),
        name="middle_far" if middle else "early_far" if slot == 0 else "early_near",
    )(*ready[1:4], *operands)


def scaled_by(array, tile, factor):
    return (array[0:HD, tile].astype(jnp.float32) * factor).astype(jnp.bfloat16)


def dscore_rows(dscores, there, weights, dprobs, kept, delta):
    delta = jnp.broadcast_to(delta, (16, delta.shape[1]))
    for start in range(0, there.stop - there.start, 16):
        out = slice(there.start + start, there.start + start + 16)
        place = slice(kept.start + start, kept.start + start + 16)
        dscores[out, :] = weights[place, :] * (dprobs[place, :] - delta)


def add_products(new, columns, products):
    for total_ref, side, terms in products:
        term = dot_nt(side, terms)
        if new:
            total_ref[:, columns] = term
        else:
            total_ref[:, columns] += term


def late_kernel(rows, heads, slot, query_t, dout_t, documents, prev2, *refs):
    groups = refs[0 : 2 - slot]
    (weights, dscores, stats, prev2_out, scores, dprobs) = refs[2 - slot :]
    wide = heads * TQ
    window = Window(rows, slot)
    jobs = []
    key_terms, value_terms = [], []
    for step in window.steps:
        chunks = []
        for chunk in range(window.late[step]):
            kept = chunk_rows(window.late, step, chunk, 1)
            chunks.append((chunk, prev2, step * TQ + chunk * CHUNK, weights, dprobs, kept))

        def end(row_max, total, delta, step=step):
            tile = slice(step * wide, (step + 1) * wide)
            rows_of = [
                [group[8 * kind + step : 8 * kind + step + 1, :] for kind in range(3)]
                for group in groups
            ]
            shrinks = [jnp.exp2(found[0] - row_max) for found in rows_of]
            for found, shrink in zip(rows_of, shrinks):
                total = total + found[1] * shrink
                delta = delta + found[2] * shrink
            late_factor = 1.0 / total
            delta = delta * late_factor
            factors = [late_factor * shrink for shrink in shrinks]
            for kind, value in enumerate((late_factor, factors[0], delta, factors[-1])):
                stats[8 * kind + step : 8 * kind + step + 1, :] = value
            there = chunk_rows(window.late, step)
            dscore_rows(dscores, there, weights, dprobs, there, delta.astype(jnp.bfloat16))
            value_terms.append(dot_nt(scaled_by(dout_t, tile, late_factor), weights[there, :]))
            key_terms.append(dot_nt(scaled_by(query_t, tile, late_factor), dscores[there, :]))

        first_max = groups[-1][step : step + 1, :]
        jobs.append((step, runs_of(chunks), (query_t, dout_t, documents), first_max, end))
    exponentials(jobs, rows, heads, scores, True)
    for first, terms, scale in ((0, key_terms, SCALE), (HD, value_terms, 1.0)):
        for tile in range(window.tiles):
            parts = [
                terms[step][:, (tile - step) * TQ : (tile - step + 1) * TQ]
                for step in range(tile + 1)
            ]
            prev2_out[first : first + HD, tile * TQ : (tile + 1) * TQ] = (
                sum(parts[1:], parts[0]) * scale
            ).astype(prev2_out.dtype)


def late_scores(slot, ready, groups, prev2):
    rows = prev2.shape[0] // 2
    heads = ready[1].shape[1] // rows
    wide = heads * TQ
    late = jax.ShapeDtypeStruct((sum(Window(rows, slot).late) * CHUNK, wide), jnp.bfloat16)
    return pl.pallas_call(
        functools.partial(late_kernel, rows, heads, slot),
        out_shape=(
            late,
            late,
            jax.ShapeDtypeStruct((32, wide), jnp.float32),
            jax.ShapeDtypeStruct((2 * HD, rows), jnp.bfloat16),
        ),
        in_specs=[VMEM] * (4 + len(groups)),
        out_specs=[VMEM] * 4,
        scratch_shapes=[
            pltpu.VMEM((rows // TQ, rows, wide), jnp.float32),
            pltpu.VMEM(late.shape, late.dtype),
        ],
        compiler_params=pltpu.CompilerParams(vmem_limit_bytes=VMEM_LIMIT),
        cost_estimate=pl.CostEstimate(flops=2**31, bytes_accessed=0, transcendentals=0),
        name="late_far" if slot == 0 else "late_near",
    )(*ready[1:4], prev2, *groups)


def grads_kernel(rows, heads, slots, *refs):
    wide = heads * TQ
    outs = list(refs[5 * len(slots) : -2])
    (dk, dv) = refs[-2:]
    for part, (slot, middle) in enumerate(slots):
        (query_t, dout_t, stats, weights, dprobs) = refs[5 * part : 5 * part + 5]
        dscores = outs.pop(0)
        window = Window(rows, slot)
        counts = window.middle if middle else window.early
        for step in reversed(window.steps):
            tile = slice(step * wide, (step + 1) * wide)
            _, early_factor, delta, middle_factor = (
                stats[8 * kind + step : 8 * kind + step + 1, :] for kind in range(4)
            )
            factor = middle_factor if middle else early_factor
            there = chunk_rows(counts, step)
            dscore_rows(dscores, there, weights, dprobs, there, delta.astype(jnp.bfloat16))
            add_products(
                step == window.tiles - 1,
                slice(0, counts[step] * CHUNK),
                (
                    (dv, scaled_by(dout_t, tile, factor), weights[there, :]),
                    (dk, scaled_by(query_t, tile, factor), dscores[there, :]),
                ),
            )
        for block in range(counts[-1] // window.tiles):
            out = outs.pop(0)
            place = slice(block * rows, (block + 1) * rows)
            out[0:HD] = (dk[:, place] * SCALE).astype(out.dtype)
            out[HD : 2 * HD] = dv[:, place].astype(out.dtype)


def rest_grads(name, cost, parts):
    rows = parts[0][2][0].shape[0] // 2
    heads = parts[0][2][1].shape[1] // rows
    operands, out_shape = [], []
    for slot, middle, (_, query_t, dout_t, _, stats, weights, dprobs), sent in parts:
        window = Window(rows, slot)
        kept = (sum(window.middle if middle else window.early) * CHUNK, heads * TQ)
        operands += [query_t, dout_t, stats, weights, dprobs]
        out_shape.append(jax.ShapeDtypeStruct(kept, jnp.bfloat16))
        for one in sent:
            kind = jnp.bfloat16 if one else jnp.float32
            out_shape.append(jax.ShapeDtypeStruct((2 * HD, rows), kind))
    slots = tuple(part[0:2] for part in parts)
    return pl.pallas_call(
        functools.partial(grads_kernel, rows, heads, slots),
        out_shape=out_shape,
        in_specs=[VMEM] * len(operands),
        out_specs=[VMEM] * len(out_shape),
        scratch_shapes=[pltpu.VMEM((HD, 2 * rows), jnp.float32)] * 2,
        compiler_params=pltpu.CompilerParams(vmem_limit_bytes=VMEM_LIMIT),
        cost_estimate=pl.CostEstimate(flops=cost, bytes_accessed=0, transcendentals=0),
        name=name,
    )(*operands)


def outputs_kernel(rows, heads, *refs):
    blocks = (refs[0:3], refs[3:6], refs[6:9], refs[9]), (refs[10:13], refs[13:15], refs[15:17], refs[17])
    (attended_hbm, grad_query_hbm, attended, grad_query, keys_t, values_t, sems) = refs[18:]
    copies = []
    for slot, (sources, weights, dscores, stats) in enumerate(blocks):
        window = Window(rows, slot)
        groups = [(window.late, 0), (window.early, 1)]
        if slot == 0:
            groups.insert(1, (window.middle, 3))
        own_rows = half_start(rows, slot)
        for place, source in enumerate(sources):
            for tile in range(rows // TQ):
                part = slice(place * rows + tile * TQ, place * rows + (tile + 1) * TQ)
                row = tile * TQ
                keys_t[:, part] = jnp.transpose(source[row : row + TQ, :])
                values_t[:, part] = jnp.transpose(source[rows + row : rows + row + TQ, :])
        for step in window.steps:
            place = pl.ds(own_rows + step * TQ, TQ)
            for out, side, terms, scale in (
                (0, values_t, weights, 1.0),
                (1, keys_t, dscores, SCALE),
            ):
                found = None
                start = step * TQ
                for (counts, kind), term in zip(groups, terms):
                    columns = slice(start, start + counts[step] * CHUNK)
                    start = columns.stop
                    factor = stats[8 * kind + step : 8 * kind + step + 1, :] * scale
                    part = dot_nn(side[:, columns], term[chunk_rows(counts, step), :]) * factor
                    found = part if found is None else found + part
                target = (attended_hbm, grad_query_hbm)[out]
                source = (attended, grad_query)[out]
                for h in range(heads):
                    part = jnp.transpose(found[:, h * TQ : (h + 1) * TQ])
                    source[place, h * HD : (h + 1) * HD] = part.astype(source.dtype)
                copy = pltpu.make_async_copy(
                    source.at[place], target.at[place], sems.at[slot, step, out]
                )
                copy.start()
                copies.append(copy)
    for copy in copies:
        copy.wait()


def block_outputs(query, far, near):
    rows = query.shape[0] // 2
    heads = query.shape[1] // HD
    shape = jax.ShapeDtypeStruct(query.shape, query.dtype)
    return pl.pallas_call(
        functools.partial(outputs_kernel, rows, heads),
        out_shape=(shape, shape),
        in_specs=[VMEM] * 18,
        out_specs=[HBM] * 2,
        scratch_shapes=[pltpu.VMEM(query.shape, query.dtype)] * 2
        + [pltpu.VMEM((HD, 3 * rows), jnp.bfloat16)] * 2
        + [pltpu.SemaphoreType.DMA((2, rows // TQ, 2))],
        compiler_params=pltpu.CompilerParams(vmem_limit_bytes=VMEM_LIMIT),
        cost_estimate=pl.CostEstimate(flops=0, bytes_accessed=0, transcendentals=0),
        name="block_outputs",
    )(*far, *near)


def total_kernel(rows, far_own, far_1, far_2, near, *refs):
    (key_hbm, value_hbm, grad_key, grad_value, sems) = refs
    copies = []
    for slot in (0, 1):
        total = near[...]
        if slot == 0:
            total = far_own[...] + far_1[...].astype(jnp.float32) + far_2[...].astype(jnp.float32)
        place = pl.ds(half_start(rows, slot), rows)
        for side, (source, out) in enumerate(((grad_key, key_hbm), (grad_value, value_hbm))):
            part = jnp.transpose(total[side * HD : (side + 1) * HD])
            source[place, :] = part.astype(source.dtype)
            copy = pltpu.make_async_copy(source.at[place], out.at[place], sems.at[slot, side])
            copy.start()
            copies.append(copy)
    for copy in copies:
        copy.wait()


def total_grads(*parts):
    rows = parts[0].shape[1]
    shape = jax.ShapeDtypeStruct((2 * rows, HD), jnp.bfloat16)
    return pl.pallas_call(
        functools.partial(total_kernel, rows),
        out_shape=(shape, shape),
        in_specs=[VMEM] * 4,
        out_specs=[HBM] * 2,
        scratch_shapes=[pltpu.VMEM(shape.shape, shape.dtype)] * 2
        + [pltpu.SemaphoreType.DMA((2, 2))],
        compiler_params=pltpu.CompilerParams(vmem_limit_bytes=VMEM_LIMIT),
        name="total_grads",
    )(*parts)


def body(query, key, value, d_out, doc_lengths):
    count = lax.axis_size("ctx")

    def holder(block):
        return block if block < count else 2 * count - 1 - block

    def move(array, pairs):
        return lax.ppermute(array, "ctx", pairs)

    near_on = [(holder(b), holder(b + 2)) for b in range(1, 2 * count - 2, 2)]
    far_on = [(holder(b), holder(b + 2)) for b in range(0, 2 * count - 2, 2)]
    near_to_far = [(holder(b), holder(b + 1)) for b in range(1, 2 * count - 2, 2)]
    swap = [(d, d ^ 1) for d in range(count)]
    near_back = [(t, s) for s, t in near_on]
    far_back = [(t, s) for s, t in far_on]

    rows = key.shape[0] // 2
    odd = lax.axis_index("ctx") % 2 == 1
    near_kv, far_kv = (
        jnp.concatenate([jnp.where(first, part[:rows], part[rows:]) for part in (key, value)], axis=0)
        for first in (odd, jnp.logical_not(odd))
    )
    far_1 = move(near_kv, near_to_far)
    far_2 = move(far_kv, far_on)
    prepared = prepare(count, doc_lengths, query, d_out, far_kv, near_kv)
    far_ready, near_ready = prepared[0:4], prepared[4:8]
    near_1 = move(far_ready[0], swap)
    far_early = group_scores(0, False, far_ready, far_ready[0])
    near_early = group_scores(1, False, near_ready, near_1, near_ready[0])
    far_1, near_early = lax.optimization_barrier((far_1, near_early))
    far_middle = group_scores(0, True, far_ready, far_1, far_early[2])
    far_late = late_scores(0, far_ready, (far_early[2], far_middle[2]), far_2)
    from_far_2 = move(far_late[3], far_back)
    near_2 = move(far_1, swap)
    near_2, far_stats = lax.optimization_barrier((near_2, far_late[2]))
    far_middle_d, far_g1 = rest_grads(
        "grads_far", 0, [(0, True, (*far_ready, far_stats, *far_middle[0:2]), (True,))]
    )
    relayed = move(far_g1, swap)
    near_late = late_scores(1, near_ready, (near_early[2],), near_2)
    near_sum = near_late[3].astype(jnp.float32) + relayed.astype(jnp.float32)
    from_near_2 = move(near_sum.astype(jnp.bfloat16), near_back)
    near_early_d, near_g1, near_own, far_early_d, far_own = rest_grads(
        "grads_near",
        2**31,
        [
            (1, False, (*near_ready, near_late[2], *near_early[0:2]), (True, False)),
            (0, False, (*far_ready, far_late[2], *far_early[0:2]), (False,)),
        ],
    )
    near_g1, from_far_2 = lax.optimization_barrier((near_g1, from_far_2))
    from_near_1 = move(near_g1, swap)
    attended, grad_query = block_outputs(
        query,
        (
            *(far_2, far_1, far_ready[0]),
            *(far_late[0], far_middle[0], far_early[0]),
            *(far_late[1], far_middle_d, far_early_d),
            far_late[2],
        ),
        (
            *(near_2, near_1, near_ready[0]),
            *(near_late[0], near_early[0]),
            *(near_late[1], near_early_d),
            near_late[2],
        ),
    )
    near_total = near_own + from_near_2.astype(jnp.float32)
    grad_key, grad_value = total_grads(far_own, from_near_1, from_far_2, near_total)
    return (attended, grad_query, grad_key, grad_value)


def solution(mesh):
    rows = P(("dp", "ctx"), None)
    return jax.shard_map(
        body,
        mesh=mesh,
        in_specs=(rows, rows, rows, rows, P("dp")),
        out_specs=(rows, rows, rows, rows),
        check_vma=False,
    )
```
